32 devices in a mesh: genome: 16 (over z, y, x), sample: 2 (over core).
Axes of the slice: x: 2, y: 2, z: 4, core: 2. Of those that a mesh axis runs over, the one named last changes fastest.
Arguments:
- genotypes: bfloat16 [8192, 8192], P('genome', 'sample'), may hold values from 0.049804688 to 2
- phenotypes: bfloat16 [1024, 8192], P('genome', 'sample'), may hold values from -60 to 60
- environment: float32 [8192], P('sample'), may hold values from 0.3 to 3
- shuffles: int32 [4, 8192], P(None, 'sample'), may hold values from 0 to 8191, each once within a row
- window_start: int32 [1024], replicated, may hold values from 0 to 31, as said below
- window_end: int32 [1024], replicated, may hold values from 1 to 32, as said below
- chrom_bounds: int32 [15], replicated, may hold values from 1 to 31, as said below
Outputs:
- maxima: float32 [5, 1024], P(None, 'genome')
The draws below stay inside these ranges and needn't reach their ends.
Inputs may be any that keep to these rules, and one draw needn't show every extreme that they name: `window_start`: for gene g on genome index d = g // 64 the window is [c - l, c + r + 1) cut to [0, 32), where d * 2 <= c < (d + 1) * 2 and 1 <= l, r <= 7; the first gene of every index has c = d * 2 and l = 7, the last has c = (d + 1) * 2 - 1 and r = 7. `window_end`: the end of the window described for window_start. `chrom_bounds`: strictly increasing.
All inputs are finite; a program needn't handle non-finite values.
Results may differ from the reference program's by a relative error of at most 0.0024.
Values may be sent and summed in bfloat16 or wider, within the bound.
No kernel may reach another device: no remote copies, remote signals or barrier semaphores. Data moves between devices by JAX's collectives and lax.ppermute only.
A program may use at most 128 MiB of HBM per device.

```python
import math
import jax
import jax.numpy as jnp
from jax import lax

SNP_BLOCK = 256
SNP_DEV = 512
GENE_DEV = 64
PERMS = 4
HALF_BLK = 7
P1 = 5
BLK_DEV = 2
REACH = 4
BAND = 9
SNPS = 8192
GENES = 1024
SAMPLES = 8192
NBLK = 32
CHROMS = 16
N_GENOME = 16


def window_pair(key):
    center_key, left_key, right_key = jax.random.split(jax.random.fold_in(key, 11), 3)
    genes = jnp.arange(GENES, dtype=jnp.int32)
    owner = genes // GENE_DEV
    within = genes % GENE_DEV
    shifted = jax.random.randint(center_key, (GENES,), 0, BLK_DEV, dtype=jnp.int32)
    shifted = jnp.where(within == 0, 0, jnp.where(within == GENE_DEV - 1, BLK_DEV - 1, shifted))
    center = owner * BLK_DEV + shifted
    left_reach = jax.random.randint(left_key, (GENES,), 1, HALF_BLK + 1, dtype=jnp.int32)
    right_reach = jax.random.randint(right_key, (GENES,), 1, HALF_BLK + 1, dtype=jnp.int32)
    left_reach = jnp.where(within == 0, HALF_BLK, left_reach)
    right_reach = jnp.where(within == GENE_DEV - 1, HALF_BLK, right_reach)
    starts = jnp.maximum(center - left_reach, 0)
    ends = jnp.minimum(center + right_reach + 1, NBLK)
    return (starts, ends)


def draw_window_start(key, part):
    return window_pair(key)[0]


def draw_window_end(key, part):
    return window_pair(key)[1]


def draw_chrom_bounds(key, part):
    order = jax.random.permutation(jax.random.fold_in(key, 5), NBLK - 1) + 1
    return jnp.sort(order[:CHROMS - 1]).astype(jnp.int32)


def draw_phenotypes(key, part):
    base_key, column_key = jax.random.split(jax.random.fold_in(key, 3), 2)
    base = jax.random.normal(base_key, (GENES, SAMPLES), jnp.float32)
    column_scale = jnp.exp(jax.random.uniform(column_key, (1, SAMPLES), jnp.float32, math.log(0.3), math.log(3.0)))
    values = base * column_scale
    return jnp.clip(values, -60.0, 60.0).astype(jnp.bfloat16)


def level_of(key, dims, pieces, low, top_value):
    def one(axis_at, blocks):
        steps = jax.random.uniform(jax.random.fold_in(jax.random.fold_in(key, 6), axis_at), (blocks,), jnp.float32, low / len(pieces), top_value / len(pieces))
        return jnp.repeat(jnp.exp(steps), dims[axis_at] // blocks).reshape((-1,) + (1,) * (len(dims) - axis_at - 1))

    gain = one(*pieces[0])
    for cut in pieces[1:]:
        gain = gain * one(*cut)
    return gain


def setup_inputs(seed: int = 0) -> dict:
    streams_of = jax.random.split(jax.random.key(seed), 8)
    return {
        "genotypes": jnp.clip(0.049804688 + 1.9501953 * jax.random.uniform(streams_of[0], (SNPS, SAMPLES), jnp.float32) ** level_of(streams_of[0], (SNPS, SAMPLES), ((0, 16), (1, 2)), -0.2, 0.2), 0.049804688, 2.0).astype(jnp.bfloat16),
        "phenotypes": draw_phenotypes(jax.random.fold_in(streams_of[7], 71), 0),
        "environment": jnp.clip(jnp.exp(math.log(3.0) - 2.3025851 * jax.random.uniform(streams_of[2], (SAMPLES,), jnp.float32) ** level_of(streams_of[2], (SAMPLES,), ((0, 2),), -0.2, 0.2)), 0.3, 3.0),
        "shuffles": jax.vmap(lambda own: jax.random.permutation(own, SAMPLES))(jax.random.split(streams_of[3], PERMS)).reshape((PERMS, SAMPLES)).astype(jnp.int32),
        "window_start": draw_window_start(jax.random.fold_in(streams_of[7], 71), 0),
        "window_end": draw_window_end(jax.random.fold_in(streams_of[7], 71), 0),
        "chrom_bounds": draw_chrom_bounds(jax.random.fold_in(streams_of[7], 71), 0),
    }


def window_bounds(window_start, window_end, chrom_bounds, total_blocks):
    middle = (window_start + window_end - 1) // 2
    before = chrom_bounds[None, :] <= middle[:, None]
    lower_edge = lax.optimization_barrier(jnp.max(jnp.where(before, chrom_bounds[None, :], 0), axis=1))
    upper_edge = lax.optimization_barrier(jnp.min(jnp.where(before, total_blocks, chrom_bounds[None, :]), axis=1))
    return (jnp.maximum(window_start, lower_edge), jnp.minimum(window_end, upper_edge))

def window_scores(reduced, square_sum, cross_sum, inter_sum):
    half_cols = reduced.shape[1] // 2
    marginal = reduced[:, :half_cols]
    interact = reduced[:, half_cols:]
    regression = cross_sum / square_sum
    resid_norm = inter_sum - cross_sum * regression
    divisor = resid_norm + 0.1 * inter_sum
    numerator = interact - regression[:, None] * marginal
    return numerator * numerator / divisor[:, None]

def reference(genotypes, phenotypes, environment, shuffles, window_start, window_end, chrom_bounds):
    lower_edge, upper_edge = window_bounds(window_start, window_end, chrom_bounds, NBLK)
    geno_float = genotypes.astype(jnp.float32)
    squares = geno_float * geno_float
    square_sum = lax.optimization_barrier(jnp.sum(squares, axis=1))
    cross_sum = lax.optimization_barrier(jnp.sum(squares * environment[None, :], axis=1))
    inter_sum = lax.optimization_barrier(jnp.sum(squares * (environment * environment)[None, :], axis=1))
    margin_rows = REACH * SNP_DEV
    pad_square = jnp.full((margin_rows,), 1.0, jnp.float32) * SAMPLES
    pad_cross = jnp.full((margin_rows,), 1.0, jnp.float32) * jnp.sum(environment)
    pad_inter = jnp.full((margin_rows,), 1.0, jnp.float32) * jnp.sum(environment * environment)
    square_pad = jnp.concatenate([pad_square, square_sum, pad_square])
    cross_pad = jnp.concatenate([pad_cross, cross_sum, pad_cross])
    inter_pad = jnp.concatenate([pad_inter, inter_sum, pad_inter])
    ones_rows = jnp.ones((margin_rows, SAMPLES), jnp.bfloat16)
    padded_geno = jnp.concatenate([ones_rows, genotypes, ones_rows], axis=0)
    row_power = lax.optimization_barrier(jnp.sum(jnp.square(phenotypes.astype(jnp.float32)), axis=1))

    def gene_block(block_index):
        gene_slab = lax.dynamic_slice_in_dim(phenotypes, block_index * GENE_DEV, GENE_DEV, 0)
        shuffled = jnp.take(gene_slab, shuffles, axis=1)
        stacked = jnp.concatenate([gene_slab[None], jnp.transpose(shuffled, (1, 0, 2))], axis=0)
        stacked = stacked.reshape(P1 * GENE_DEV, SAMPLES)
        weighted = (stacked.astype(jnp.float32) * environment[None, :]).astype(jnp.bfloat16)
        operand = jnp.concatenate([stacked, weighted], axis=0)
        first_row = block_index * SNP_DEV
        geno_slab = lax.dynamic_slice_in_dim(padded_geno, first_row, BAND * SNP_DEV, 0)
        reduced = lax.dot_general(geno_slab, operand, (((1,), (1,)), ((), ())), preferred_element_type=jnp.float32)
        scores = window_scores(reduced, lax.dynamic_slice_in_dim(square_pad, first_row, BAND * SNP_DEV, 0), lax.dynamic_slice_in_dim(cross_pad, first_row, BAND * SNP_DEV, 0), lax.dynamic_slice_in_dim(inter_pad, first_row, BAND * SNP_DEV, 0)).reshape(BAND * SNP_DEV, P1, GENE_DEV)
        row_blocks = ((block_index - REACH) * SNP_DEV + jnp.arange(BAND * SNP_DEV, dtype=jnp.int32)) // SNP_BLOCK
        lower_band = lax.dynamic_slice_in_dim(lower_edge, block_index * GENE_DEV, GENE_DEV, 0)
        upper_band = lax.dynamic_slice_in_dim(upper_edge, block_index * GENE_DEV, GENE_DEV, 0)
        inside = (row_blocks[:, None] >= lower_band[None, :]) & (row_blocks[:, None] < upper_band[None, :])
        best_peak = lax.optimization_barrier(jnp.max(jnp.where(inside[:, None, :], scores, 0.0), axis=0))
        power_band = lax.dynamic_slice_in_dim(row_power, block_index * GENE_DEV, GENE_DEV, 0)
        return jnp.sqrt(best_peak / (power_band[None, :] / SAMPLES + 1e-05))
    blocks_out = lax.map(gene_block, jnp.arange(N_GENOME, dtype=jnp.int32))
    return jnp.transpose(blocks_out, (1, 0, 2)).reshape(P1, GENES)
```

```python
import functools

import jax
import jax.numpy as jnp
from jax import lax
from jax.experimental import pallas as pl
from jax.experimental.pallas import tpu as pltpu
from jax.sharding import PartitionSpec as P

SNP_BLOCK = 256
HALF_BLK = 7
LANES = 128
ROWS_STEP = 16
UNROLL = 16
MIB = 2**20


def passed_along(x, axis, by):
    count = lax.axis_size(axis)
    pairs = [(i, i + by) for i in range(count) if 0 <= i + by < count]
    return lax.ppermute(x, axis, pairs)


def swapped(x):
    count = lax.axis_size("sample")
    return lax.ppermute(x, "sample", [(i, (i + 1) % count) for i in range(count)])


def window_bounds(window_start, window_end, chrom_bounds, total_blocks):
    middle = (window_start + window_end - 1) // 2
    before = chrom_bounds[None, :] <= middle[:, None]
    lower_edge = jnp.max(jnp.where(before, chrom_bounds[None, :], 0), axis=1)
    upper_edge = jnp.min(jnp.where(before, total_blocks, chrom_bounds[None, :]), axis=1)
    return (jnp.maximum(window_start, lower_edge), jnp.minimum(window_end, upper_edge))


def snp_side_kernel(
    idx_ref, core_ref, env_ref, own_ref, other_ref, out_ref, inv_ref,
    geno, table, dest, stage, moments, slope, in_sems, out_sems,
):
    snp_rows, all_samples = geno.shape
    half = all_samples // 2
    chunk = 1024
    chunks = all_samples // chunk
    words = snp_rows // LANES
    labels = out_ref.shape[1] // snp_rows

    def load(k):
        source = own_ref if k * chunk < half else other_ref
        return pltpu.make_async_copy(
            source.at[:, pl.ds((k * chunk) % half, chunk)],
            geno.at[:, pl.ds(k * chunk, chunk)],
            in_sems.at[k],
        )

    for k in range(chunks):
        load(k).start()
    moments[...] = jnp.zeros_like(moments)
    for k in range(chunks):
        load(k).wait()

        def add_rows(i, carry, k=k):
            first = pl.multiple_of(i * ROWS_STEP, ROWS_STEP)
            sums = [moments[m, pl.ds(first, ROWS_STEP), :] for m in range(3)]
            for t in range(chunk // LANES):
                at = k * chunk + t * LANES
                x = geno[pl.ds(first, ROWS_STEP), pl.ds(at, LANES)].astype(jnp.float32)
                e = env_ref[:, pl.ds(at, LANES)]
                x = x * x
                sums[0] = sums[0] + x
                x = x * e
                sums[1] = sums[1] + x
                sums[2] = sums[2] + x * e
            for m in range(3):
                moments[m, pl.ds(first, ROWS_STEP), :] = sums[m]
            return carry

        lax.fori_loop(0, snp_rows // ROWS_STEP, add_rows, 0)
    square_sum = jnp.sum(moments[0], axis=1, keepdims=True)
    cross_sum = jnp.sum(moments[1], axis=1, keepdims=True)
    inter_sum = jnp.sum(moments[2], axis=1, keepdims=True)
    regression = cross_sum / square_sum
    divisor = inter_sum - cross_sum * regression + 0.1 * inter_sum
    slope[...] = jnp.broadcast_to(regression, slope.shape)
    inv_ref[...] = jnp.broadcast_to(1.0 / divisor, slope.shape).T[: inv_ref.shape[0]]

    side = 2 * LANES
    unit = (
        lax.broadcasted_iota(jnp.int32, (side, side), 0)
        == lax.broadcasted_iota(jnp.int32, (side, side), 1)
    ).astype(jnp.bfloat16)
    share = snp_rows // 2

    def turn(k, carry):
        at = pl.multiple_of(k * side, side)
        e = env_ref[:, pl.ds(at, side)]
        turned = []
        for j in range(snp_rows // side):
            rows = pl.ds(j * side, side)
            x = geno[rows, pl.ds(at, side)].astype(jnp.float32)
            r = slope[rows, :]
            a = x * (e - jnp.concatenate([r, r], axis=1))
            t = lax.dot_general(
                unit, a.astype(jnp.bfloat16), (((1,), (1,)), ((), ())),
                preferred_element_type=jnp.float32,
            )
            for c in range(side // LANES):
                table[pl.ds(k * (side * words) + j * (side // LANES) + c, side, stride=words), :] = (
                    t[:, c * LANES : (c + 1) * LANES]
                )
            turned.append(t)
        turned = jnp.concatenate(turned, axis=1)
        kept = jnp.where(core_ref[0] == 0, turned[:, :share], turned[:, share:])
        stage[pl.ds(at, side), pl.ds(0, share)] = kept.astype(jnp.bfloat16)
        return carry

    lax.fori_loop(0, all_samples // side, turn, 0)
    first_out = pltpu.make_async_copy(
        stage.at[:, pl.ds(0, share)],
        out_ref.at[:, pl.ds(labels * snp_rows, share)],
        out_sems.at[0],
    )
    first_out.start()

    parts = out_sems.shape[0]
    part_rows = all_samples // parts

    def save(q, part):
        rows = pl.ds(part * part_rows, part_rows)
        return pltpu.make_async_copy(
            stage.at[rows], out_ref.at[rows, pl.ds(q * snp_rows, snp_rows)], out_sems.at[part]
        )

    for q in range(labels):

        def scatter(i, carry, q=q):
            first = pl.multiple_of(i * UNROLL, UNROLL)
            base = pl.multiple_of(first * words, UNROLL * words)
            held = [table[pl.ds(base + u * words, words), :] for u in range(UNROLL)]
            for u in range(UNROLL):
                to = pl.multiple_of(idx_ref[q * all_samples + first + u], words)
                dest[pl.ds(to, words), :] = held[u]
            return carry

        lax.fori_loop(0, all_samples // UNROLL, scatter, 0)
        if q == 0:
            first_out.wait()
        for part in range(parts):
            if q > 0:
                save(q - 1, part).wait()

            def narrow(k, carry, part=part):
                at = pl.multiple_of(part * part_rows + k * side, side)
                for c in range(words):
                    v = dest[pl.ds(at * words + c, side, stride=words), :]
                    stage[pl.ds(at, side), pl.ds(c * LANES, LANES)] = v.astype(jnp.bfloat16)
                return carry

            lax.fori_loop(0, part_rows // side, narrow, 0)
            save(q, part).start()
    for part in range(parts):
        save(labels - 1, part).wait()


def snp_side(idx, core, env, own, other, labels):
    snp_rows, half = own.shape
    all_samples = 2 * half
    words = snp_rows // LANES
    width = labels * snp_rows + snp_rows // 2
    any_spec = pl.BlockSpec(memory_space=pl.ANY)
    smem = pl.BlockSpec(memory_space=pltpu.SMEM)
    vmem = pl.BlockSpec(memory_space=pltpu.VMEM)
    return pl.pallas_call(
        snp_side_kernel,
        out_shape=(
            jax.ShapeDtypeStruct((all_samples, width), jnp.bfloat16),
            jax.ShapeDtypeStruct((8, snp_rows), jnp.float32),
        ),
        in_specs=[smem, smem, vmem, any_spec, any_spec],
        out_specs=(any_spec, vmem),
        scratch_shapes=[
            pltpu.VMEM((snp_rows, all_samples), jnp.bfloat16),
            pltpu.VMEM((all_samples * words, LANES), jnp.float32),
            pltpu.VMEM((all_samples * words, LANES), jnp.float32),
            pltpu.VMEM((all_samples, snp_rows), jnp.bfloat16),
            pltpu.VMEM((3, snp_rows, LANES), jnp.float32),
            pltpu.VMEM((snp_rows, LANES), jnp.float32),
            pltpu.SemaphoreType.DMA((all_samples // 1024,)),
            pltpu.SemaphoreType.DMA((4,)),
        ],
        compiler_params=pltpu.CompilerParams(vmem_limit_bytes=60 * MIB),
        cost_estimate=pl.CostEstimate(
            flops=40 * 10**9, bytes_accessed=60 * 10**6, transcendentals=0
        ),
        name="snp_side",
    )(idx, core, env, own, other)


def product_kernel(
    pos_ref, inv_ref, low_ref, high_ref, own_ref, other_ref, weights_ref, out_ref, total, power,
    *, labels, snp_rows, power_row,
):
    step = pl.program_id(0)
    steps = pl.num_programs(0)
    genes = own_ref.shape[0]
    width = weights_ref.shape[1]
    block = SNP_BLOCK

    @pl.when(step == 0)
    def _():
        total[...] = jnp.zeros_like(total)
        power[...] = jnp.zeros_like(power)

    def add(rows_ref):
        rows = rows_ref[...]
        for n in range(width // block):
            cols = pl.ds(n * block, block)
            total[pl.ds(0, genes), cols] += jnp.dot(
                rows, weights_ref[:, cols], preferred_element_type=jnp.float32
            )
        x = rows_ref[pl.ds(power_row, LANES), :].astype(jnp.float32)
        x = x * x
        kept = power[...]
        for t in range(x.shape[1] // LANES):
            kept = kept + x[:, t * LANES : (t + 1) * LANES]
        power[...] = kept

    @pl.when(step < steps // 2)
    def _():
        add(own_ref)

    @pl.when(step >= steps // 2)
    def _():
        add(other_ref)

    @pl.when(step == steps - 1)
    def _():
        first_block = pos_ref[0] * (snp_rows // block)
        share_blocks = snp_rows // 2 // block
        low = low_ref[...]
        high = high_ref[...]

        def peak(col, inv_col, snp_block):
            v = total[:, pl.ds(col, block)]
            v = v * v * inv_ref[0:1, pl.ds(inv_col, block)]
            best = v[:, :LANES]
            for t in range(1, block // LANES):
                best = jnp.maximum(best, v[:, t * LANES : (t + 1) * LANES])
            best = jnp.max(best.T, axis=0, keepdims=True)
            inside = (snp_block >= low) & (snp_block < high)
            return jnp.where(inside, best, 0.0)

        rows = []
        for q in range(labels):
            best = jnp.zeros_like(low, jnp.float32)
            for b in range(snp_rows // block):
                best = jnp.maximum(
                    best, peak(q * snp_rows + b * block, b * block, first_block + b)
                )
            rows.append(best)
        best = jnp.zeros_like(low, jnp.float32)
        for b in range(share_blocks):
            start = pos_ref[1] * share_blocks + b
            best = jnp.maximum(
                best,
                peak(
                    labels * snp_rows + b * block,
                    pl.multiple_of(start * block, block),
                    first_block + start,
                ),
            )
        rows.append(best)
        powers = jnp.sum(power[...].T, axis=0, keepdims=True)
        rows.append(jnp.concatenate([powers] * (low.shape[1] // LANES), axis=1))
        while len(rows) < out_ref.shape[0]:
            rows.append(jnp.zeros_like(low, jnp.float32))
        out_ref[...] = jnp.concatenate(rows, axis=0)


def products(pos, inv, low, high, own, other, weights, labels, snp_rows, power_row):
    genes, half = own.shape
    all_samples, width = weights.shape
    padded = low.shape[1]
    depth = 1024
    own_steps = half // depth
    smem = pl.BlockSpec(memory_space=pltpu.SMEM)
    return pl.pallas_call(
        functools.partial(product_kernel, labels=labels, snp_rows=snp_rows, power_row=power_row),
        grid=(all_samples // depth,),
        out_shape=jax.ShapeDtypeStruct((8, padded), jnp.float32),
        in_specs=[
            smem,
            pl.BlockSpec((8, snp_rows), lambda k: (0, 0)),
            pl.BlockSpec((1, padded), lambda k: (0, 0)),
            pl.BlockSpec((1, padded), lambda k: (0, 0)),
            pl.BlockSpec((genes, depth), lambda k: (0, jnp.minimum(k, own_steps - 1))),
            pl.BlockSpec((genes, depth), lambda k: (0, jnp.maximum(k - own_steps, 0))),
            pl.BlockSpec((depth, width), lambda k: (k, 0)),
        ],
        out_specs=pl.BlockSpec((8, padded), lambda k: (0, 0)),
        scratch_shapes=[
            pltpu.VMEM((padded, width), jnp.float32),
            pltpu.VMEM((LANES, LANES), jnp.float32),
        ],
        compiler_params=pltpu.CompilerParams(vmem_limit_bytes=48 * MIB),
        cost_estimate=pl.CostEstimate(
            flops=2 * genes * all_samples * width,
            bytes_accessed=2 * all_samples * (width + genes),
            transcendentals=0,
        ),
        name="products",
    )(pos, inv, low, high, own, other, weights)


def shards(genotypes, phenotypes, environment, shuffles, window_start, window_end, chrom_bounds):
    snp_rows, half = genotypes.shape
    gene_rows = phenotypes.shape[0]
    perms = shuffles.shape[0]
    genome_size = lax.axis_size("genome")
    sample_size = lax.axis_size("sample")
    genome_pos = lax.axis_index("genome")
    sample_pos = lax.axis_index("sample")
    blocks_dev = snp_rows // SNP_BLOCK
    reach_dev = (HALF_BLK + blocks_dev - 1) // blocks_dev
    total_blocks = snp_rows * genome_size // SNP_BLOCK
    all_samples = half * sample_size
    labels = perms // sample_size
    band_slots = 2 * reach_dev + 1

    other_geno = swapped(genotypes)
    small = jnp.concatenate([shuffles.astype(jnp.float32), environment[None]], axis=0)
    other_small = swapped(small)
    pieces = []
    for offset in range(-reach_dev, reach_dev + 1):
        pieces.append(
            phenotypes if offset == 0 else passed_along(phenotypes, "genome", -offset)
        )

    env = jnp.concatenate([environment, other_small[perms]])[None]
    first_label = sample_pos * labels
    idx = jnp.concatenate(
        [
            lax.dynamic_slice_in_dim(shuffles, first_label, labels, 0),
            lax.dynamic_slice_in_dim(other_small, first_label, labels, 0).astype(jnp.int32),
        ],
        axis=1,
    )
    idx = idx - sample_pos * half
    idx = jnp.where(idx < 0, idx + all_samples, idx) * (snp_rows // LANES)
    core = jnp.full((1,), sample_pos, jnp.int32)
    weights, inv = snp_side(idx.reshape(-1), core, env, genotypes, other_geno, labels)

    lower_edge, upper_edge = window_bounds(window_start, window_end, chrom_bounds, total_blocks)
    band_genes = band_slots * gene_rows
    padded = -(-band_genes // LANES) * LANES
    margin = reach_dev * gene_rows
    edges = jnp.pad(
        jnp.stack([lower_edge, upper_edge]), ((0, 0), (margin, margin + padded - band_genes))
    )
    band = lax.dynamic_slice_in_dim(edges, genome_pos * gene_rows, padded, 1)
    low, high = band[0:1], band[1:2]
    high = jnp.where(lax.broadcasted_iota(jnp.int32, high.shape, 1) < band_genes, high, 0)

    own_stack = jnp.concatenate(pieces, axis=0)
    other_stack = swapped(own_stack)
    pos = jnp.stack([genome_pos, sample_pos]).astype(jnp.int32)
    found = products(
        pos, inv, low, high, own_stack, other_stack, weights, labels, snp_rows,
        reach_dev * gene_rows,
    )

    peaks = jnp.zeros((perms + 1, genome_size * gene_rows + 2 * margin), jnp.float32)
    at = genome_pos * gene_rows
    peaks = lax.dynamic_update_slice(peaks, found[:labels, :band_genes], (1 + first_label, at))
    peaks = lax.dynamic_update_slice(peaks, found[labels : labels + 1, :band_genes], (0, at))
    peaks = lax.pmax(peaks[:, margin : margin + genome_size * gene_rows], ("genome", "sample"))
    peak = lax.dynamic_slice_in_dim(peaks, at, gene_rows, 1)
    row_power = found[labels + 1, :gene_rows]
    return jnp.sqrt(peak / (row_power[None, :] / all_samples + 1e-05))


def solution(mesh):
    placed = (
        P("genome", "sample"),
        P("genome", "sample"),
        P("sample"),
        P(None, "sample"),
        P(),
        P(),
        P(),
    )
    return jax.shard_map(
        shards, mesh=mesh, in_specs=placed, out_specs=P(None, "genome"), check_vma=False
    )
```

```python
import functools

import jax
import jax.numpy as jnp
from jax import lax
from jax.experimental import pallas as pl
from jax.experimental.pallas import tpu as pltpu
from jax.sharding import PartitionSpec as P

SNP_BLOCK = 256
HALF_BLK = 7
LANES = 128
ROWS_STEP = 16
UNROLL = 16
MIB = 2**20


def passed_along(x, axis, by):
    count = lax.axis_size(axis)
    pairs = [(i, i + by) for i in range(count) if 0 <= i + by < count]
    return lax.ppermute(x, axis, pairs)


def swapped(x):
    count = lax.axis_size("sample")
    return lax.ppermute(x, "sample", [(i, (i + 1) % count) for i in range(count)])


def moments_kernel(geno_ref, env_ref, out_ref, sums):
    step = pl.program_id(0)
    snp_rows, chunk = geno_ref.shape

    @pl.when(step == 0)
    def _():
        sums[...] = jnp.zeros_like(sums)

    def add_rows(i, carry):
        first = pl.multiple_of(i * ROWS_STEP, ROWS_STEP)
        held = [sums[m, pl.ds(first, ROWS_STEP), :] for m in range(3)]
        for t in range(chunk // LANES):
            x = geno_ref[pl.ds(first, ROWS_STEP), pl.ds(t * LANES, LANES)].astype(jnp.float32)
            e = env_ref[:, pl.ds(t * LANES, LANES)]
            x = x * x
            held[0] = held[0] + x
            x = x * e
            held[1] = held[1] + x
            held[2] = held[2] + x * e
        for m in range(3):
            sums[m, pl.ds(first, ROWS_STEP), :] = held[m]
        return carry

    lax.fori_loop(0, snp_rows // ROWS_STEP, add_rows, 0, unroll=2)

    @pl.when(step == pl.num_programs(0) - 1)
    def _():
        rows = [jnp.sum(sums[m].T, axis=0, keepdims=True) for m in range(3)]
        rows.append(jnp.zeros((out_ref.shape[0] - 3, snp_rows), jnp.float32))
        out_ref[...] = jnp.concatenate(rows, axis=0)


def local_moments(geno, env):
    snp_rows, half = geno.shape
    chunk = 1024
    return pl.pallas_call(
        moments_kernel,
        grid=(half // chunk,),
        out_shape=jax.ShapeDtypeStruct((8, snp_rows), jnp.float32),
        in_specs=[
            pl.BlockSpec((snp_rows, chunk), lambda k: (0, k)),
            pl.BlockSpec((1, chunk), lambda k: (0, k)),
        ],
        out_specs=pl.BlockSpec((8, snp_rows), lambda k: (0, 0)),
        scratch_shapes=[pltpu.VMEM((3, snp_rows, LANES), jnp.float32)],
        compiler_params=pltpu.CompilerParams(vmem_limit_bytes=60 * MIB),
        cost_estimate=pl.CostEstimate(
            flops=5 * 10**9, bytes_accessed=2 * snp_rows * half, transcendentals=0
        ),
        name="local_moments",
    )(geno, env)


def snp_side_kernel(
    idx_ref, core_ref, env_ref, sums_ref, own_ref, other_ref, out_ref,
    geno, table, dest, stage, slope, in_sems, out_sems,
):
    snp_rows, all_samples = geno.shape
    half = all_samples // 2
    chunk = 1024
    chunks = all_samples // chunk
    words = snp_rows // LANES
    labels = out_ref.shape[1] // snp_rows

    def load(k):
        source = own_ref if k * chunk < half else other_ref
        return pltpu.make_async_copy(
            source.at[:, pl.ds((k * chunk) % half, chunk)],
            geno.at[:, pl.ds(k * chunk, chunk)],
            in_sems.at[k],
        )

    for k in range(chunks):
        load(k).start()
    regression = sums_ref[1:2, :] / sums_ref[0:1, :]
    slope[...] = jnp.broadcast_to(regression, (LANES, snp_rows)).T
    for k in range(chunks):
        load(k).wait()

    side = 2 * LANES
    unit = (
        lax.broadcasted_iota(jnp.int32, (side, side), 0)
        == lax.broadcasted_iota(jnp.int32, (side, side), 1)
    ).astype(jnp.bfloat16)
    share = snp_rows // 2

    def turn(k, carry):
        at = pl.multiple_of(k * side, side)
        e = env_ref[:, pl.ds(at, side)]
        turned = []
        for j in range(snp_rows // side):
            rows = pl.ds(j * side, side)
            x = geno[rows, pl.ds(at, side)].astype(jnp.float32)
            r = slope[rows, :]
            a = x * (e - jnp.concatenate([r, r], axis=1))
            t = lax.dot_general(
                unit, a.astype(jnp.bfloat16), (((1,), (1,)), ((), ())),
                preferred_element_type=jnp.float32,
            )
            for c in range(side // LANES):
                table[pl.ds(k * (side * words) + j * (side // LANES) + c, side, stride=words), :] = (
                    t[:, c * LANES : (c + 1) * LANES]
                )
            turned.append(t)
        turned = jnp.concatenate(turned, axis=1)
        kept = jnp.where(core_ref[0] == 0, turned[:, :share], turned[:, share:])
        stage[pl.ds(at, side), pl.ds(0, share)] = kept.astype(jnp.bfloat16)
        return carry

    lax.fori_loop(0, all_samples // side, turn, 0)
    def save_first(h):
        to = pl.multiple_of(jnp.where(core_ref[0] == h, 0, half), half)
        return pltpu.make_async_copy(
            stage.at[pl.ds(h * half, half), pl.ds(0, share)],
            out_ref.at[pl.ds(to, half), pl.ds(labels * snp_rows, share)],
            out_sems.at[h],
        )

    save_first(0).start()
    save_first(1).start()

    parts = out_sems.shape[0]
    part_rows = all_samples // parts

    def save(q, part):
        rows = pl.ds(part * part_rows, part_rows)
        return pltpu.make_async_copy(
            stage.at[rows], out_ref.at[rows, pl.ds(q * snp_rows, snp_rows)], out_sems.at[part]
        )

    for q in range(labels):

        def scatter(i, carry, q=q):
            first = pl.multiple_of(i * UNROLL, UNROLL)
            base = pl.multiple_of(first * words, UNROLL * words)
            held = [table[pl.ds(base + u * words, words), :] for u in range(UNROLL)]
            for u in range(UNROLL):
                to = pl.multiple_of(idx_ref[q * all_samples + first + u], words)
                dest[pl.ds(to, words), :] = held[u]
            return carry

        lax.fori_loop(0, all_samples // UNROLL, scatter, 0)
        if q == 0:
            save_first(0).wait()
            save_first(1).wait()
        for part in range(parts):
            if q > 0:
                save(q - 1, part).wait()

            def narrow(k, carry, part=part):
                at = pl.multiple_of(part * part_rows + k * side, side)
                for c in range(words):
                    v = dest[pl.ds(at * words + c, side, stride=words), :]
                    stage[pl.ds(at, side), pl.ds(c * LANES, LANES)] = v.astype(jnp.bfloat16)
                return carry

            lax.fori_loop(0, part_rows // side, narrow, 0)
            save(q, part).start()
    for part in range(parts):
        save(labels - 1, part).wait()


def snp_side(idx, core, env, sums, own, other, labels):
    snp_rows, half = own.shape
    all_samples = 2 * half
    words = snp_rows // LANES
    width = labels * snp_rows + snp_rows // 2
    any_spec = pl.BlockSpec(memory_space=pl.ANY)
    smem = pl.BlockSpec(memory_space=pltpu.SMEM)
    vmem = pl.BlockSpec(memory_space=pltpu.VMEM)
    return pl.pallas_call(
        snp_side_kernel,
        out_shape=jax.ShapeDtypeStruct((all_samples, width), jnp.bfloat16),
        in_specs=[smem, smem, vmem, vmem, any_spec, any_spec],
        out_specs=any_spec,
        scratch_shapes=[
            pltpu.VMEM((snp_rows, all_samples), jnp.bfloat16),
            pltpu.VMEM((all_samples * words, LANES), jnp.float32),
            pltpu.VMEM((all_samples * words, LANES), jnp.float32),
            pltpu.VMEM((all_samples, snp_rows), jnp.bfloat16),
            pltpu.VMEM((snp_rows, LANES), jnp.float32),
            pltpu.SemaphoreType.DMA((all_samples // 1024,)),
            pltpu.SemaphoreType.DMA((4,)),
        ],
        compiler_params=pltpu.CompilerParams(vmem_limit_bytes=60 * MIB),
        cost_estimate=pl.CostEstimate(
            flops=40 * 10**9, bytes_accessed=60 * 10**6, transcendentals=0
        ),
        name="snp_side",
    )(idx, core, env, sums, own, other)


def window_plan(start, end, bounds_ref, n_bounds, total_blocks):
    middle = (start + end - 1) // 2
    lower_edge = jnp.zeros_like(start)
    upper_edge = jnp.full_like(end, total_blocks)
    for i in range(n_bounds):
        edge = bounds_ref[i]
        before = edge <= middle
        lower_edge = jnp.where(before, jnp.maximum(lower_edge, edge), lower_edge)
        upper_edge = jnp.where(before, upper_edge, jnp.minimum(upper_edge, edge))
    return jnp.maximum(start, lower_edge), jnp.minimum(end, upper_edge)


def select_kernel(
    round_ref, pos_ref, bounds_ref, start_ref, end_ref, own_ref, other_ref, order_ref,
    rounds_ref, plan_ref, full_ref, *rest, caps, blocks_dev,
):
    del order_ref
    pay_refs, (slots, edges) = rest[: len(caps)], rest[len(caps) :]
    reach = len(caps)
    chips, genes = start_ref.shape
    half = own_ref.shape[1]
    chip, core = pos_ref[0], pos_ref[1]
    turn = round_ref[0]
    low, high = window_plan(
        start_ref[...], end_ref[...], bounds_ref, bounds_ref.shape[0], chips * blocks_dev
    )
    edges[0] = low
    edges[1] = high
    at = lax.broadcasted_iota(jnp.int32, (chips, genes), 0)
    upto = (
        lax.broadcasted_iota(jnp.int32, (genes, genes), 0)
        <= lax.broadcasted_iota(jnp.int32, (genes, genes), 1)
    ).astype(jnp.bfloat16)
    rounds = jnp.int32(0)
    for way in range(2):
        for k in range(1, reach + 1):
            to = at + (k if way == 0 else -k)
            need = (
                (low < (to + 1) * blocks_dev) & (high > to * blocks_dev)
                & (low < high) & (to >= 0) & (to < chips)
            )
            rank = jnp.dot(
                need.astype(jnp.float32).astype(jnp.bfloat16), upto,
                preferred_element_type=jnp.float32,
            ).astype(jnp.int32)
            cap = caps[k - 1]
            slot = rank - 1 - turn * cap
            slots[way * reach + k - 1] = jnp.where(
                need & (slot >= 0) & (slot < cap), slot, -1
            )
            rounds = jnp.maximum(rounds, (jnp.max(rank) + cap - 1) // cap)
    rounds_ref[0] = rounds

    plan_ref[...] = jnp.zeros_like(plan_ref)
    plan_ref[0, pl.ds(0, 1), :] = lax.broadcasted_iota(jnp.int32, (1, genes), 1)
    plan_ref[1, pl.ds(0, 1), :] = edges[0, pl.ds(chip, 1), :]
    plan_ref[2, pl.ds(0, 1), :] = edges[1, pl.ds(chip, 1), :]
    for side in range(2):
        way = core if side == 0 else 1 - core
        for k in range(1, reach + 1):
            source = chip + (2 * way - 1) * k
            valid = (source >= 0) & (source < chips)
            row = jnp.clip(source, 0, chips - 1)
            to = pl.ds(1 + side * reach + k - 1, 1)
            slot = slots[way * reach + k - 1, pl.ds(row, 1), :]
            plan_ref[0, to, :] = jnp.where(valid, slot, -1)
            plan_ref[1, to, :] = edges[0, pl.ds(row, 1), :]
            plan_ref[2, to, :] = jnp.where(valid, edges[1, pl.ds(row, 1), :], 0)

    picks = []
    for k in range(1, reach + 1):
        slot = slots[core * reach + k - 1, pl.ds(chip, 1), :]
        rows = lax.broadcasted_iota(jnp.int32, (caps[k - 1], genes), 0)
        picks.append((rows == slot).astype(jnp.float32).astype(jnp.bfloat16))
    step = 1024

    def copy(i, carry):
        cols = pl.ds(pl.multiple_of(i * step, step), step)
        late = pl.ds(pl.multiple_of(half + i * step, step), step)
        a, b = own_ref[:, cols], other_ref[:, cols]
        first = jnp.where(core == 0, a, b)
        second = jnp.where(core == 0, b, a)
        full_ref[:, cols] = first
        full_ref[:, late] = second
        for pick, pay in zip(picks, pay_refs):
            for part, to in ((first, cols), (second, late)):
                pay[:, to] = jnp.dot(
                    pick, part, preferred_element_type=jnp.float32
                ).astype(jnp.bfloat16)
        return carry

    lax.fori_loop(0, half // step, copy, 0)


def select(turn, pos, bounds, start, end, own, other, order, caps, blocks_dev):
    genes, half = own.shape
    chips = start.shape[0]
    reach = len(caps)
    smem = pl.BlockSpec(memory_space=pltpu.SMEM)
    vmem = pl.BlockSpec(memory_space=pltpu.VMEM)
    plan_rows = -(-(2 * reach + 1) // 8) * 8
    return pl.pallas_call(
        functools.partial(select_kernel, caps=caps, blocks_dev=blocks_dev),
        out_shape=(
            jax.ShapeDtypeStruct((1,), jnp.int32),
            jax.ShapeDtypeStruct((3, plan_rows, genes), jnp.int32),
            jax.ShapeDtypeStruct((genes, 2 * half), jnp.bfloat16),
            *[jax.ShapeDtypeStruct((cap, 2 * half), jnp.bfloat16) for cap in caps],
        ),
        in_specs=[smem, smem, smem, vmem, vmem, vmem, vmem, pl.BlockSpec(memory_space=pl.ANY)],
        out_specs=(smem, vmem, vmem, *[vmem for _ in caps]),
        scratch_shapes=[
            pltpu.VMEM((2 * reach, chips, genes), jnp.int32),
            pltpu.VMEM((2, chips, genes), jnp.int32),
        ],
        compiler_params=pltpu.CompilerParams(vmem_limit_bytes=24 * MIB),
        name="select",
    )(turn, pos, bounds, start, end, own, other, order)


def product_kernel(
    pos_ref, sums_ref, plan_ref, *rest, caps, labels, genes, blocks_dev
):
    reach = len(caps)
    n_in = 1 + 2 * reach
    gene_refs = rest[:n_in]
    weights_ref, out_ref, power_ref, rows, total, power = rest[n_in:]
    step = pl.program_id(0)
    steps = pl.num_programs(0)
    snp_rows = sums_ref.shape[1]
    depth, width = weights_ref.shape
    block = SNP_BLOCK
    sizes = (genes,) + tuple(caps) + tuple(caps)
    starts = [sum(sizes[:i]) for i in range(n_in)]
    used = sum(sizes)

    @pl.when(step == 0)
    def _():
        total[...] = jnp.zeros_like(total)
        power[...] = jnp.zeros_like(power)

    for ref, start, size in zip(gene_refs, starts, sizes):
        rows[pl.ds(start, size), :] = ref[...]
    for n in range(width // block):
        cols = pl.ds(n * block, block)
        total[pl.ds(0, used), cols] += jnp.dot(
            rows[...], weights_ref[:, cols], preferred_element_type=jnp.float32
        )
    kept = power[...]
    for t in range(depth // LANES):
        x = gene_refs[0][:, pl.ds(t * LANES, LANES)].astype(jnp.float32)
        kept = kept + x * x
    power[...] = kept

    @pl.when(step == steps - 1)
    def _():
        chip, core = pos_ref[0], pos_ref[1]
        share_blocks = blocks_dev // 2
        cross = sums_ref[1:2, :]
        inter = sums_ref[2:3, :]
        inv = 1.0 / (inter - cross * (cross / sums_ref[0:1, :]) + 0.1 * inter)

        def peak(col, inv_block):
            v = total[:, pl.ds(col, block)]
            v = v * v * inv_block
            best = v[:, :LANES]
            for t in range(1, block // LANES):
                best = jnp.maximum(best, v[:, t * LANES : (t + 1) * LANES])
            return jnp.max(best.T, axis=0, keepdims=True)

        peaks = []
        for q in range(labels):
            for b in range(blocks_dev):
                peaks.append(
                    peak(q * snp_rows + b * block, inv[:, b * block : (b + 1) * block])
                )
        for b in range(share_blocks):
            mine = inv[:, b * block : (b + 1) * block]
            late = inv[:, (share_blocks + b) * block : (share_blocks + b + 1) * block]
            peaks.append(
                peak(labels * snp_rows + b * block, jnp.where(core == 0, mine, late))
            )
        while len(peaks) % 8:
            peaks.append(jnp.zeros_like(peaks[0]))
        peaks = jnp.concatenate(peaks, axis=0)
        out_ref[...] = jnp.zeros_like(out_ref)
        slot_of = lax.broadcasted_iota(jnp.int32, (total.shape[0], genes), 0)
        for i in range(n_in):
            slot = plan_ref[0, pl.ds(i, 1), :]
            slot = jnp.where(slot >= 0, slot + starts[i], -1)
            low = plan_ref[1, pl.ds(i, 1), :]
            high = plan_ref[2, pl.ds(i, 1), :]
            spread = jnp.dot(
                peaks, (slot_of == slot).astype(jnp.float32),
                precision=lax.Precision.HIGHEST, preferred_element_type=jnp.float32,
            )

            def masked(row, snp_block):
                inside = (snp_block >= low) & (snp_block < high)
                return jnp.where(inside, spread[row : row + 1], 0.0)

            found = []
            for q in range(labels):
                best = jnp.zeros((1, genes), jnp.float32)
                for b in range(blocks_dev):
                    best = jnp.maximum(best, masked(q * blocks_dev + b, chip * blocks_dev + b))
                found.append(best)
            best = jnp.zeros((1, genes), jnp.float32)
            for b in range(share_blocks):
                best = jnp.maximum(
                    best,
                    masked(
                        labels * blocks_dev + b, chip * blocks_dev + core * share_blocks + b
                    ),
                )
            out_rows = [best]
            for c in range(2):
                out_rows += [jnp.where(core == c, v, 0.0) for v in found]
            while len(out_rows) % 8:
                out_rows.append(jnp.zeros_like(best))
            if i == 0:
                target = chip
            else:
                way = core if i <= reach else 1 - core
                target = chip + (2 * way - 1) * ((i - 1) % reach + 1)
            out_ref[target + reach] = jnp.concatenate(out_rows, axis=0)
        powers = jnp.sum(power[...].T, axis=0, keepdims=True)
        power_ref[...] = jnp.broadcast_to(powers, power_ref.shape)


def products(pos, sums, plan, full, mine, other, weights, caps, labels, chips, blocks_dev):
    genes, all_samples = full.shape
    width = weights.shape[1]
    snp_rows = sums.shape[1]
    reach = len(caps)
    depth = 1024
    used = genes + 2 * sum(caps)
    padded = -(-used // LANES) * LANES
    out_rows = -(-(1 + 2 * labels) // 8) * 8

    def blocked(x):
        return pl.BlockSpec((x.shape[0], depth), lambda k: (0, k))

    arrays = (full, *mine, *other)
    return pl.pallas_call(
        functools.partial(
            product_kernel, caps=caps, labels=labels, genes=genes, blocks_dev=blocks_dev
        ),
        grid=(all_samples // depth,),
        out_shape=(
            jax.ShapeDtypeStruct((chips + 2 * reach, out_rows, genes), jnp.float32),
            jax.ShapeDtypeStruct((8, genes), jnp.float32),
        ),
        in_specs=[
            pl.BlockSpec(memory_space=pltpu.SMEM),
            pl.BlockSpec(sums.shape, lambda k: (0, 0)),
            pl.BlockSpec(plan.shape, lambda k: (0, 0, 0)),
            *[blocked(x) for x in arrays],
            pl.BlockSpec((depth, width), lambda k: (k, 0)),
        ],
        out_specs=(
            pl.BlockSpec((chips + 2 * reach, out_rows, genes), lambda k: (0, 0, 0)),
            pl.BlockSpec((8, genes), lambda k: (0, 0)),
        ),
        scratch_shapes=[
            pltpu.VMEM((used, depth), jnp.bfloat16),
            pltpu.VMEM((padded, width), jnp.float32),
            pltpu.VMEM((genes, LANES), jnp.float32),
        ],
        compiler_params=pltpu.CompilerParams(vmem_limit_bytes=48 * MIB),
        cost_estimate=pl.CostEstimate(
            flops=2 * used * all_samples * width,
            bytes_accessed=2 * all_samples * (width + used),
            transcendentals=0,
        ),
        name="products",
    )(pos, sums, plan, *arrays, weights)


def shards(genotypes, phenotypes, environment, shuffles, window_start, window_end, chrom_bounds):
    snp_rows, half = genotypes.shape
    genes = phenotypes.shape[0]
    perms = shuffles.shape[0]
    chips = lax.axis_size("genome")
    cores = lax.axis_size("sample")
    genome_pos = lax.axis_index("genome")
    sample_pos = lax.axis_index("sample")
    blocks_dev = snp_rows // SNP_BLOCK
    reach = (HALF_BLK + blocks_dev - 1) // blocks_dev
    all_samples = half * cores
    labels = perms // cores
    caps = tuple(min(genes, genes * 4 >> k) for k in range(1, reach + 1))

    small = jnp.concatenate([shuffles.astype(jnp.float32), environment[None]], axis=0)
    other_small = swapped(small)
    other_pheno = swapped(phenotypes)
    other_geno = swapped(genotypes)
    pos = jnp.stack([genome_pos, sample_pos]).astype(jnp.int32)
    start = window_start.reshape(chips, genes)
    end = window_end.reshape(chips, genes)

    def chosen(turn):
        return select(
            turn, pos, chrom_bounds, start, end, phenotypes, other_pheno, other_small, caps,
            blocks_dev,
        )

    def travel(payloads):
        mine = []
        for k, payload in enumerate(payloads, 1):
            pairs = [(i * cores, (i + k) * cores) for i in range(chips - k)]
            pairs += [((i + k) * cores + 1, i * cores + 1) for i in range(chips - k)]
            mine.append(lax.ppermute(payload, ("genome", "sample"), pairs))
        return mine

    rounds, plan, full, *payloads = chosen(jnp.zeros((1,), jnp.int32))
    mine = travel(payloads)

    sums = lax.psum(local_moments(genotypes, environment[None]), "sample")
    env = jnp.concatenate([environment, other_small[perms]])[None]
    first_label = sample_pos * labels
    idx = jnp.concatenate(
        [
            lax.dynamic_slice_in_dim(shuffles, first_label, labels, 0),
            lax.dynamic_slice_in_dim(other_small, first_label, labels, 0).astype(jnp.int32),
        ],
        axis=1,
    ) * (snp_rows // LANES)
    weights = snp_side(
        idx.reshape(-1), pos[1:], env, sums, genotypes, other_geno, labels
    )

    def met(plan, full, mine):
        other = [swapped(x) for x in mine]
        return products(
            pos, sums, plan, full, mine, other, weights, caps, labels, chips, blocks_dev
        )

    *mine, weights = lax.optimization_barrier((*mine, weights))
    found, power = met(plan, full, mine)

    def more(carry):
        return carry[0] < rounds[0]

    def again(carry):
        turn, best = carry
        _, plan, full, *payloads = chosen(jnp.full((1,), turn, jnp.int32))
        return turn + 1, jnp.maximum(best, met(plan, full, travel(payloads))[0])

    _, found = lax.while_loop(more, again, (jnp.int32(1), found))
    found = found[reach : reach + chips]
    sent = jnp.broadcast_to(found[:, None], (chips, cores) + found.shape[1:])
    sent = sent.reshape((chips * cores,) + found.shape[1:])
    peak = jnp.max(lax.all_to_all(sent, ("genome", "sample"), 0, 0, tiled=True), axis=0)
    return jnp.sqrt(peak[: perms + 1] / (power[0:1] / all_samples + 1e-05))


def solution(mesh):
    placed = (
        P("genome", "sample"),
        P("genome", "sample"),
        P("sample"),
        P(None, "sample"),
        P(),
        P(),
        P(),
    )
    return jax.shard_map(
        shards, mesh=mesh, in_specs=placed, out_specs=P(None, "genome"), check_vma=False
    )
```

```python
import functools

import jax
import jax.numpy as jnp
from jax import lax
from jax.experimental import pallas as pl
from jax.experimental.pallas import tpu as pltpu
from jax.sharding import PartitionSpec as P

SNP_BLOCK = 256
HALF_BLK = 7
LANES = 128
ROWS_STEP = 16
UNROLL = 16
SLOT = 8
CHUNK = 1024
MIB = 2**20


def passed_along(x, axis, by):
    count = lax.axis_size(axis)
    pairs = [(i, i + by) for i in range(count) if 0 <= i + by < count]
    return lax.ppermute(x, axis, pairs)


def swapped(x):
    count = lax.axis_size("sample")
    return lax.ppermute(x, "sample", [(i, (i + 1) % count) for i in range(count)])


def moments_kernel(geno_ref, env_ref, out_ref, sums):
    step = pl.program_id(0)
    snp_rows, chunk = geno_ref.shape

    @pl.when(step == 0)
    def _():
        sums[...] = jnp.zeros_like(sums)

    def add_rows(i, carry):
        first = pl.multiple_of(i * ROWS_STEP, ROWS_STEP)
        held = [sums[m, pl.ds(first, ROWS_STEP), :] for m in range(3)]
        for t in range(chunk // LANES):
            x = geno_ref[pl.ds(first, ROWS_STEP), pl.ds(t * LANES, LANES)].astype(jnp.float32)
            e = env_ref[:, pl.ds(t * LANES, LANES)]
            x = x * x
            held[0] = held[0] + x
            x = x * e
            held[1] = held[1] + x
            held[2] = held[2] + x * e
        for m in range(3):
            sums[m, pl.ds(first, ROWS_STEP), :] = held[m]
        return carry

    lax.fori_loop(0, snp_rows // ROWS_STEP, add_rows, 0, unroll=4)

    @pl.when(step == pl.num_programs(0) - 1)
    def _():
        rows = [jnp.sum(sums[m].T, axis=0, keepdims=True) for m in range(3)]
        rows.append(jnp.zeros((out_ref.shape[0] - 3, snp_rows), jnp.float32))
        out_ref[...] = jnp.concatenate(rows, axis=0)


def local_moments(geno, env):
    snp_rows, half = geno.shape
    chunk = CHUNK
    return pl.pallas_call(
        moments_kernel,
        grid=(half // chunk,),
        out_shape=jax.ShapeDtypeStruct((8, snp_rows), jnp.float32),
        in_specs=[
            pl.BlockSpec((snp_rows, chunk), lambda k: (0, k)),
            pl.BlockSpec((1, chunk), lambda k: (0, k)),
        ],
        out_specs=pl.BlockSpec((8, snp_rows), lambda k: (0, 0)),
        scratch_shapes=[pltpu.VMEM((3, snp_rows, LANES), jnp.float32)],
        compiler_params=pltpu.CompilerParams(vmem_limit_bytes=60 * MIB),
        cost_estimate=pl.CostEstimate(
            flops=5 * 10**9, bytes_accessed=2 * snp_rows * half, transcendentals=0
        ),
        name="local_moments",
    )(geno, env)


def snp_side_kernel(
    core_ref, env_own, env_other, sums_own, sums_other, shuf_own, shuf_other, own_ref, other_ref,
    out_ref,
    idx, geno, table, dest, stage, first_stage, slope, idx_sems, in_sems, out_sems, first_sems,
    *, labels,
):
    snp_rows, half = own_ref.shape
    all_samples = 2 * half
    chunks = all_samples // CHUNK
    words = snp_rows // LANES
    share = snp_rows // 2
    side = 2 * LANES
    core = core_ref[0]
    depth = geno.shape[0]

    def load(k):
        source = own_ref if k * CHUNK < half else other_ref
        return pltpu.make_async_copy(
            source.at[:, pl.ds((k * CHUNK) % half, CHUNK)], geno.at[k % depth],
            in_sems.at[k % depth],
        )

    def load_idx(q, h):
        source = shuf_own if h == 0 else shuf_other
        return pltpu.make_async_copy(
            source.at[core * labels + q],
            idx.at[pl.ds(q * all_samples + h * half, half)],
            idx_sems.at[2 * q + h],
        )

    def save_first(k):
        there = jnp.where(core == 0, k * CHUNK, (k * CHUNK + half) % all_samples)
        rows = pl.ds(pl.multiple_of(there, CHUNK), CHUNK)
        return pltpu.make_async_copy(
            first_stage.at[k % 2], out_ref.at[rows, pl.ds(labels * snp_rows, share)],
            first_sems.at[k % 2],
        )

    def save(q, k):
        return pltpu.make_async_copy(
            stage.at[k % 2],
            out_ref.at[pl.ds(k * CHUNK, CHUNK), pl.ds(q * snp_rows, snp_rows)],
            out_sems.at[k % 2],
        )

    for k in range(depth):
        load(k).start()
    for q in range(labels):
        for h in range(2):
            load_idx(q, h).start()
    sums = sums_own[...] + sums_other[...]
    slope[...] = jnp.broadcast_to(sums[1:2, :] / sums[0:1, :], (LANES, snp_rows)).T
    unit = (
        lax.broadcasted_iota(jnp.int32, (side, side), 0)
        == lax.broadcasted_iota(jnp.int32, (side, side), 1)
    ).astype(jnp.bfloat16)

    for k in range(chunks):
        load(k).wait()
        if k >= 2:
            save_first(k - 2).wait()
        env_ref = env_own if k * CHUNK < half else env_other

        def turn(i, carry, k=k, env_ref=env_ref):
            at = pl.multiple_of(i * side, side)
            e = env_ref[:, pl.ds((k * CHUNK) % half + at, side)]
            turned = []
            for j in range(snp_rows // side):
                rows = pl.ds(j * side, side)
                x = geno[k % depth, rows, pl.ds(at, side)].astype(jnp.float32)
                r = slope[rows, :]
                a = x * (e - jnp.concatenate([r] * (side // LANES), axis=1))
                t = lax.dot_general(
                    unit, a.astype(jnp.bfloat16), (((1,), (1,)), ((), ())),
                    preferred_element_type=jnp.float32,
                )
                for c in range(side // LANES):
                    word = j * (side // LANES) + c
                    table[pl.ds((k * CHUNK + at) * words + word, side, stride=words), :] = (
                        t[:, c * LANES : (c + 1) * LANES]
                    )
                turned.append(t)
            turned = jnp.concatenate(turned, axis=1)
            kept = jnp.where(core == 0, turned[:, :share], turned[:, share:])
            first_stage[k % 2, pl.ds(at, side), :] = kept.astype(jnp.bfloat16)
            return carry

        lax.fori_loop(0, CHUNK // side, turn, 0, unroll=2)
        save_first(k).start()
        if k + depth < chunks:
            load(k + depth).start()

    for q in range(labels):
        for h in range(2):
            load_idx(q, h).wait()

        def scatter(i, carry, q=q):
            first = pl.multiple_of(i * UNROLL, UNROLL)
            base = pl.multiple_of(first * words, UNROLL * words)
            held = [table[pl.ds(base + u * words, SLOT), :] for u in range(UNROLL)]
            for u in range(UNROLL):
                to = pl.multiple_of(idx[q * all_samples + first + u] * SLOT, SLOT)
                dest[pl.ds(to, SLOT), :] = held[u]
            return carry

        lax.fori_loop(0, all_samples // UNROLL, scatter, 0)
        for k in range(chunks):
            if q * chunks + k >= 2:
                save((q * chunks + k - 2) // chunks, (k - 2) % chunks).wait()

            def narrow(i, carry, k=k):
                at = pl.multiple_of(i * side, side)
                for c in range(words):
                    v = dest[pl.ds((k * CHUNK + at) * SLOT + c, side, stride=SLOT), :]
                    stage[k % 2, pl.ds(at, side), pl.ds(c * LANES, LANES)] = v.astype(jnp.bfloat16)
                return carry

            lax.fori_loop(0, CHUNK // side, narrow, 0)
            save(q, k).start()
    for k in range(chunks - 2, chunks):
        save_first(k).wait()
        save(labels - 1, k).wait()


def snp_side(core, env_own, env_other, sums_own, sums_other, shuf_own, shuf_other, own, other,
             labels):
    snp_rows, half = own.shape
    all_samples = 2 * half
    words = snp_rows // LANES
    width = labels * snp_rows + snp_rows // 2
    any_spec = pl.BlockSpec(memory_space=pl.ANY)
    smem = pl.BlockSpec(memory_space=pltpu.SMEM)
    vmem = pl.BlockSpec(memory_space=pltpu.VMEM)
    return pl.pallas_call(
        functools.partial(snp_side_kernel, labels=labels),
        out_shape=jax.ShapeDtypeStruct((all_samples, width), jnp.bfloat16),
        in_specs=[smem, vmem, vmem, vmem, vmem, any_spec, any_spec, any_spec, any_spec],
        out_specs=any_spec,
        scratch_shapes=[
            pltpu.SMEM((labels * all_samples,), jnp.int32),
            pltpu.VMEM((3, snp_rows, CHUNK), jnp.bfloat16),
            pltpu.VMEM((all_samples * words + SLOT, LANES), jnp.float32),
            pltpu.VMEM((all_samples * SLOT, LANES), jnp.float32),
            pltpu.VMEM((2, CHUNK, snp_rows), jnp.bfloat16),
            pltpu.VMEM((2, CHUNK, snp_rows // 2), jnp.bfloat16),
            pltpu.VMEM((snp_rows, LANES), jnp.float32),
            pltpu.SemaphoreType.DMA((2 * labels,)),
            pltpu.SemaphoreType.DMA((3,)),
            pltpu.SemaphoreType.DMA((2,)),
            pltpu.SemaphoreType.DMA((2,)),
        ],
        compiler_params=pltpu.CompilerParams(vmem_limit_bytes=61 * MIB),
        cost_estimate=pl.CostEstimate(
            flops=40 * 10**9, bytes_accessed=60 * 10**6, transcendentals=0
        ),
        name="snp_side",
    )(core, env_own, env_other, sums_own, sums_other, shuf_own, shuf_other, own, other)


def window_plan(start, end, bounds_ref, n_bounds, total_blocks):
    middle = (start + end - 1) // 2
    lower_edge = jnp.zeros_like(start)
    upper_edge = jnp.full_like(end, total_blocks)
    for i in range(n_bounds):
        edge = bounds_ref[i]
        before = edge <= middle
        lower_edge = jnp.where(before, jnp.maximum(lower_edge, edge), lower_edge)
        upper_edge = jnp.where(before, upper_edge, jnp.minimum(upper_edge, edge))
    return jnp.maximum(start, lower_edge), jnp.minimum(end, upper_edge)


def select_kernel(
    round_ref, pos_ref, bounds_ref, start_ref, end_ref, own_ref, other_ref,
    rounds_ref, plan_ref, full_ref, *rest, caps, blocks_dev,
):
    pay_refs, (slots, edges) = rest[: len(caps)], rest[len(caps) :]
    reach = len(caps)
    genes, half = own_ref.shape
    shape = start_ref.shape
    per_row = LANES // genes
    chips = shape[0] * per_row
    chip, core = pos_ref[0], pos_ref[1]
    turn = round_ref[0]
    low, high = window_plan(
        start_ref[...], end_ref[...], bounds_ref, bounds_ref.shape[0], chips * blocks_dev
    )
    edges[0] = low
    edges[1] = high
    at = lax.broadcasted_iota(jnp.int32, shape, 0) * per_row
    at = at + lax.broadcasted_iota(jnp.int32, shape, 1) // genes
    a = lax.broadcasted_iota(jnp.int32, (LANES, LANES), 0)
    b = lax.broadcasted_iota(jnp.int32, (LANES, LANES), 1)
    upto = ((a <= b) & (a // genes == b // genes)).astype(jnp.float32).astype(jnp.bfloat16)
    rounds = jnp.int32(0)
    for way in range(2):
        for k in range(1, reach + 1):
            to = at + (k if way == 0 else -k)
            need = (
                (low < (to + 1) * blocks_dev) & (high > to * blocks_dev)
                & (low < high) & (to >= 0) & (to < chips)
            )
            rank = jnp.dot(
                need.astype(jnp.float32).astype(jnp.bfloat16), upto,
                preferred_element_type=jnp.float32,
            ).astype(jnp.int32)
            cap = caps[k - 1]
            slot = rank - 1 - turn * cap
            slots[way * reach + k - 1] = jnp.where(
                need & (slot >= 0) & (slot < cap), slot, -1
            )
            rounds = jnp.maximum(rounds, (jnp.max(rank) + cap - 1) // cap)
    rounds_ref[0] = rounds

    def of_chip(ref, index, which):
        row = ref[index, pl.ds(which // per_row, 1), :]
        out = row[:, :genes]
        for part in range(1, per_row):
            out = jnp.where(
                which % per_row == part, row[:, part * genes : (part + 1) * genes], out
            )
        return out

    plan_ref[...] = jnp.zeros_like(plan_ref)
    plan_ref[0, pl.ds(0, 1), :] = lax.broadcasted_iota(jnp.int32, (1, genes), 1)
    plan_ref[1, pl.ds(0, 1), :] = of_chip(edges, 0, chip)
    plan_ref[2, pl.ds(0, 1), :] = of_chip(edges, 1, chip)
    for side in range(2):
        way = core if side == 0 else 1 - core
        for k in range(1, reach + 1):
            source = chip + (2 * way - 1) * k
            valid = (source >= 0) & (source < chips)
            source = jnp.clip(source, 0, chips - 1)
            to = pl.ds(1 + side * reach + k - 1, 1)
            slot = of_chip(slots, way * reach + k - 1, source)
            plan_ref[0, to, :] = jnp.where(valid, slot, -1)
            plan_ref[1, to, :] = of_chip(edges, 0, source)
            plan_ref[2, to, :] = jnp.where(valid, of_chip(edges, 1, source), 0)

    picks = []
    for k in range(1, reach + 1):
        slot = of_chip(slots, core * reach + k - 1, chip)
        rows = lax.broadcasted_iota(jnp.int32, (caps[k - 1], genes), 0)
        picks.append((rows == slot).astype(jnp.float32))
    picks = jnp.concatenate(picks, axis=0).astype(jnp.bfloat16)
    step = 1024

    def copy(i, carry):
        cols = pl.ds(pl.multiple_of(i * step, step), step)
        late = pl.ds(pl.multiple_of(half + i * step, step), step)
        a, b = own_ref[:, cols], other_ref[:, cols]
        first = jnp.where(core == 0, a, b)
        second = jnp.where(core == 0, b, a)
        full_ref[:, cols] = first
        full_ref[:, late] = second
        for part, to in ((first, cols), (second, late)):
            chosen = jnp.dot(picks, part, preferred_element_type=jnp.float32)
            chosen = chosen.astype(jnp.bfloat16)
            row = 0
            for pay in pay_refs:
                pay[:, to] = chosen[row : row + pay.shape[0]]
                row += pay.shape[0]
        return carry

    lax.fori_loop(0, half // step, copy, 0)


def select(turn, pos, bounds, start, end, own, other, caps, blocks_dev):
    genes, half = own.shape
    reach = len(caps)
    smem = pl.BlockSpec(memory_space=pltpu.SMEM)
    vmem = pl.BlockSpec(memory_space=pltpu.VMEM)
    plan_rows = -(-(2 * reach + 1) // 8) * 8
    return pl.pallas_call(
        functools.partial(select_kernel, caps=caps, blocks_dev=blocks_dev),
        out_shape=(
            jax.ShapeDtypeStruct((1,), jnp.int32),
            jax.ShapeDtypeStruct((3, plan_rows, genes), jnp.int32),
            jax.ShapeDtypeStruct((genes, 2 * half), jnp.bfloat16),
            *[jax.ShapeDtypeStruct((cap, 2 * half), jnp.bfloat16) for cap in caps],
        ),
        in_specs=[smem, smem, smem, vmem, vmem, vmem, vmem],
        out_specs=(smem, vmem, vmem, *[vmem for _ in caps]),
        scratch_shapes=[
            pltpu.VMEM((2 * reach,) + start.shape, jnp.int32),
            pltpu.VMEM((2,) + start.shape, jnp.int32),
        ],
        compiler_params=pltpu.CompilerParams(vmem_limit_bytes=24 * MIB),
        name="select",
    )(turn, pos, bounds, start, end, own, other)


def product_kernel(
    pos_ref, sums_own, sums_other, *rest, n_in, sizes, labels, blocks_dev, last
):
    if last:
        plan_ref, before_ref = rest[:2]
        rest = rest[2:]
    gene_refs = rest[:n_in]
    weights_ref, out_ref, *rest = rest[n_in:]
    if not last:
        power_ref, *rest = rest
    rows, total, *rest = rest
    step = pl.program_id(0)
    steps = pl.num_programs(0)
    snp_rows = sums_own.shape[1]
    depth, width = weights_ref.shape
    block = SNP_BLOCK
    used = rows.shape[0]

    @pl.when(step == 0)
    def _():
        total[...] = jnp.zeros_like(total)

    at = 0
    for ref in gene_refs:
        rows[pl.ds(at, ref.shape[0]), :] = ref[...]
        at += ref.shape[0]
    for n in range(width // block):
        cols = pl.ds(n * block, block)
        total[pl.ds(0, used), cols] += jnp.dot(
            rows[...], weights_ref[:, cols], preferred_element_type=jnp.float32
        )
    if not last:
        power = rest[0]
        kept = jnp.where(step == 0, 0.0, power[...])
        for t in range(depth // LANES):
            x = gene_refs[0][:, pl.ds(t * LANES, LANES)].astype(jnp.float32)
            kept = kept + x * x
        power[...] = kept

    @pl.when(step == steps - 1)
    def _():
        chip, core = pos_ref[0], pos_ref[1]
        share_blocks = blocks_dev // 2
        sums = sums_own[...] + sums_other[...]
        cross = sums[1:2, :]
        inter = sums[2:3, :]
        inv = 1.0 / (inter - cross * (cross / sums[0:1, :]) + 0.1 * inter)

        def peak(col, inv_block):
            v = total[:, pl.ds(col, block)]
            v = v * v * inv_block
            best = v[:, :LANES]
            for t in range(1, block // LANES):
                best = jnp.maximum(best, v[:, t * LANES : (t + 1) * LANES])
            return jnp.max(best.T, axis=0, keepdims=True)

        peaks = []
        for q in range(labels):
            for b in range(blocks_dev):
                peaks.append(
                    peak(q * snp_rows + b * block, inv[:, b * block : (b + 1) * block])
                )
        for b in range(share_blocks):
            mine = inv[:, b * block : (b + 1) * block]
            late = inv[:, (share_blocks + b) * block : (share_blocks + b + 1) * block]
            peaks.append(
                peak(labels * snp_rows + b * block, jnp.where(core == 0, mine, late))
            )
        while len(peaks) % 8:
            peaks.append(jnp.zeros_like(peaks[0]))
        peaks = jnp.concatenate(peaks, axis=0)
        if not last:
            out_ref[...] = peaks
            powers = jnp.sum(rest[0][...].T, axis=0, keepdims=True)
            power_ref[...] = jnp.broadcast_to(powers, power_ref.shape)
            return

        genes = plan_ref.shape[2]
        chips = out_ref.shape[0] // 2
        reach = (len(sizes) - 1) // 2
        before = before_ref[...]
        out_ref[...] = jnp.zeros_like(out_ref)
        start = 0
        for i, size in enumerate(sizes):
            if i == n_in + 1:
                start = 0
            values = before if i <= reach else peaks
            slot = plan_ref[0, pl.ds(i, 1), :]
            slot = jnp.where(slot >= 0, slot + start, -1)
            start += size
            low = plan_ref[1, pl.ds(i, 1), :]
            high = plan_ref[2, pl.ds(i, 1), :]
            slot_of = lax.broadcasted_iota(jnp.int32, (values.shape[1], genes), 0)
            spread = jnp.dot(
                values, (slot_of == slot).astype(jnp.float32),
                precision=lax.Precision.HIGHEST, preferred_element_type=jnp.float32,
            )

            def masked(row, snp_block):
                inside = (snp_block >= low) & (snp_block < high)
                return jnp.where(inside, spread[row : row + 1], 0.0)

            found = []
            for q in range(labels):
                best = jnp.zeros((1, genes), jnp.float32)
                for b in range(blocks_dev):
                    best = jnp.maximum(best, masked(q * blocks_dev + b, chip * blocks_dev + b))
                found.append(best)
            best = jnp.zeros((1, genes), jnp.float32)
            for b in range(share_blocks):
                best = jnp.maximum(
                    best,
                    masked(
                        labels * blocks_dev + b, chip * blocks_dev + core * share_blocks + b
                    ),
                )
            out_rows = [best]
            for c in range(2):
                out_rows += [jnp.where(core == c, v, 0.0) for v in found]
            while len(out_rows) % 8:
                out_rows.append(jnp.zeros_like(best))
            if i == 0:
                target = chip
            else:
                way = core if i <= reach else 1 - core
                target = chip + (2 * way - 1) * ((i - 1) % reach + 1)

            @pl.when((target >= 0) & (target < chips))
            def _(out_rows=out_rows, target=target):
                for c in range(2):
                    out_ref[2 * target + c, :, pl.ds(0, genes)] = jnp.concatenate(
                        out_rows, axis=0
                    )


def products(pos, sums, arrays, weights, caps, labels, blocks_dev, before=None, plan=None,
             chips=None):
    all_samples, width = weights.shape
    genes = arrays[0].shape[0] if plan is None else plan.shape[2]
    sizes = (genes,) + tuple(caps) + tuple(caps)
    used = sum(x.shape[0] for x in arrays)
    padded = -(-used // LANES) * LANES
    out_rows = -(-(1 + 2 * labels) // 8) * 8
    peak_rows = -(-(labels * blocks_dev + blocks_dev // 2) // 8) * 8
    last = plan is not None
    extra = (plan, before) if last else ()

    def whole(x):
        return pl.BlockSpec(x.shape, lambda k: (0,) * x.ndim)

    if last:
        outs = (jax.ShapeDtypeStruct((2 * chips, out_rows, LANES), jnp.float32),)
    else:
        outs = (
            jax.ShapeDtypeStruct((peak_rows, padded), jnp.float32),
            jax.ShapeDtypeStruct((8, genes), jnp.float32),
        )
    scratch = [
        pltpu.VMEM((used, CHUNK), jnp.bfloat16),
        pltpu.VMEM((padded, width), jnp.float32),
    ]
    if not last:
        scratch.append(pltpu.VMEM((genes, LANES), jnp.float32))
    return pl.pallas_call(
        functools.partial(
            product_kernel, n_in=len(arrays), sizes=sizes, labels=labels,
            blocks_dev=blocks_dev, last=last,
        ),
        grid=(all_samples // CHUNK,),
        out_shape=outs,
        in_specs=[
            pl.BlockSpec(memory_space=pltpu.SMEM),
            *[whole(x) for x in (*sums, *extra)],
            *[pl.BlockSpec((x.shape[0], CHUNK), lambda k: (0, k)) for x in arrays],
            pl.BlockSpec((CHUNK, width), lambda k: (k, 0)),
        ],
        out_specs=tuple(whole(x) for x in outs),
        scratch_shapes=scratch,
        compiler_params=pltpu.CompilerParams(vmem_limit_bytes=48 * MIB),
        cost_estimate=pl.CostEstimate(
            flops=2 * used * all_samples * width,
            bytes_accessed=2 * all_samples * (width + used),
            transcendentals=0,
        ),
        name="products_last" if last else "products",
    )(pos, *sums, *extra, *arrays, weights)


def finish_kernel(gathered_ref, power_ref, out_ref, *, samples):
    best = gathered_ref[0]
    for i in range(1, gathered_ref.shape[0]):
        best = jnp.maximum(best, gathered_ref[i])
    labels, genes = out_ref.shape
    peak = best[:labels, :genes]
    out_ref[...] = jnp.sqrt(peak / (power_ref[0:1, :] / samples + 1e-05))


def shards(genotypes, phenotypes, environment, shuffles, window_start, window_end, chrom_bounds):
    snp_rows, half = genotypes.shape
    genes = phenotypes.shape[0]
    perms = shuffles.shape[0]
    chips = lax.axis_size("genome")
    cores = lax.axis_size("sample")
    genome_pos = lax.axis_index("genome")
    sample_pos = lax.axis_index("sample")
    blocks_dev = snp_rows // SNP_BLOCK
    reach = (HALF_BLK + blocks_dev - 1) // blocks_dev
    all_samples = half * cores
    labels = perms // cores
    caps = tuple(min(genes, genes * 4 >> k) for k in range(1, reach + 1))

    other_pheno = swapped(phenotypes)
    other_geno = swapped(genotypes)
    env = environment[None]
    other_env = swapped(env)
    other_shuffles = swapped(shuffles)
    pos = jnp.stack([genome_pos, sample_pos]).astype(jnp.int32)
    start = window_start.reshape(-1, LANES)
    end = window_end.reshape(-1, LANES)

    def chosen(turn):
        return select(
            turn, pos, chrom_bounds, start, end, phenotypes, other_pheno, caps, blocks_dev
        )

    def travel(payloads):
        mine = []
        for k, payload in enumerate(payloads, 1):
            pairs = [(i * cores, (i + k) * cores) for i in range(chips - k)]
            pairs += [((i + k) * cores + 1, i * cores + 1) for i in range(chips - k)]
            mine.append(lax.ppermute(payload, ("genome", "sample"), pairs))
        return mine

    rounds, plan, full, *payloads = chosen(jnp.zeros((1,), jnp.int32))
    mine = travel(payloads)
    own_sums = local_moments(genotypes, env)
    sums = (own_sums, swapped(own_sums))
    weights = snp_side(
        pos[1:], env, other_env, *sums, shuffles, other_shuffles, genotypes, other_geno, labels
    )

    def met(plan, full, mine):
        other = [swapped(x) for x in mine]
        before, power = products(
            pos, sums, (full, *mine), weights, caps, labels, blocks_dev
        )
        (found,) = products(
            pos, sums, other, weights, caps, labels, blocks_dev, before, plan, chips
        )
        return found, power

    *mine, weights = lax.optimization_barrier((*mine, weights))
    found, power = met(plan, full, mine)

    def more(carry):
        return carry[0] < rounds[0]

    def again(carry):
        turn, best = carry
        _, plan, full, *payloads = chosen(jnp.full((1,), turn, jnp.int32))
        return turn + 1, jnp.maximum(best, met(plan, full, travel(payloads))[0])

    _, found = lax.while_loop(more, again, (jnp.int32(1), found))
    gathered = lax.all_to_all(found, ("genome", "sample"), 0, 0, tiled=True)
    return pl.pallas_call(
        functools.partial(finish_kernel, samples=all_samples),
        out_shape=jax.ShapeDtypeStruct((perms + 1, genes), jnp.float32),
        name="finish",
    )(gathered, power)


def solution(mesh):
    placed = (
        P("genome", "sample"),
        P("genome", "sample"),
        P("sample"),
        P(None, "sample"),
        P(),
        P(),
        P(),
    )
    return jax.shard_map(
        shards, mesh=mesh, in_specs=placed, out_specs=P(None, "genome"), check_vma=False
    )
```

```python
import functools

import jax
import jax.numpy as jnp
from jax import lax
from jax.experimental import pallas as pl
from jax.experimental.pallas import tpu as pltpu
from jax.sharding import PartitionSpec as P

SNP_BLOCK = 256
HALF_BLK = 7
LANES = 128
ROWS_STEP = 16
UNROLL = 32
CHUNK = 1024
MIB = 2**20


def passed_along(x, axis, by):
    count = lax.axis_size(axis)
    pairs = [(i, i + by) for i in range(count) if 0 <= i + by < count]
    return lax.ppermute(x, axis, pairs)


def swapped(x):
    count = lax.axis_size("sample")
    return lax.ppermute(x, "sample", [(i, (i + 1) % count) for i in range(count)])


def moments_kernel(geno_ref, env_ref, out_ref, sums):
    step = pl.program_id(0)
    snp_rows, chunk = geno_ref.shape

    @pl.when(step == 0)
    def _():
        sums[...] = jnp.zeros_like(sums)

    def add_rows(i, carry):
        first = pl.multiple_of(i * ROWS_STEP, ROWS_STEP)
        held = [sums[m, pl.ds(first, ROWS_STEP), :] for m in range(3)]
        for t in range(chunk // LANES):
            x = geno_ref[pl.ds(first, ROWS_STEP), pl.ds(t * LANES, LANES)].astype(jnp.float32)
            e = env_ref[:, pl.ds(t * LANES, LANES)]
            x = x * x
            held[0] = held[0] + x
            x = x * e
            held[1] = held[1] + x
            held[2] = held[2] + x * e
        for m in range(3):
            sums[m, pl.ds(first, ROWS_STEP), :] = held[m]
        return carry

    lax.fori_loop(0, snp_rows // ROWS_STEP, add_rows, 0, unroll=4)

    @pl.when(step == pl.num_programs(0) - 1)
    def _():
        rows = [jnp.sum(sums[m].T, axis=0, keepdims=True) for m in range(3)]
        rows.append(jnp.zeros((out_ref.shape[0] - 3, snp_rows), jnp.float32))
        out_ref[...] = jnp.concatenate(rows, axis=0)


def local_moments(geno, env):
    snp_rows, half = geno.shape
    chunk = CHUNK
    return pl.pallas_call(
        moments_kernel,
        grid=(half // chunk,),
        out_shape=jax.ShapeDtypeStruct((8, snp_rows), jnp.float32),
        in_specs=[
            pl.BlockSpec((snp_rows, chunk), lambda k: (0, k)),
            pl.BlockSpec((1, chunk), lambda k: (0, k)),
        ],
        out_specs=pl.BlockSpec((8, snp_rows), lambda k: (0, 0)),
        scratch_shapes=[pltpu.VMEM((3, snp_rows, LANES), jnp.float32)],
        compiler_params=pltpu.CompilerParams(vmem_limit_bytes=60 * MIB),
        cost_estimate=pl.CostEstimate(
            flops=5 * 10**9, bytes_accessed=2 * snp_rows * half, transcendentals=0
        ),
        name="local_moments",
    )(geno, env)


def snp_side_kernel(
    core_ref, env_own, env_other, sums_own, sums_other, shuf_own, shuf_other, own_ref, other_ref,
    out_ref,
    idx, geno, table, dest, stage, first_stage, slope, idx_sems, in_sems, out_sems, first_sems,
    *, labels,
):
    snp_rows, half = own_ref.shape
    all_samples = 2 * half
    chunks = all_samples // CHUNK
    words = snp_rows // LANES
    slot = words | 1
    share = snp_rows // 2
    side = 2 * LANES
    core = core_ref[0]
    depth = geno.shape[0]

    def load(k):
        source = own_ref if k * CHUNK < half else other_ref
        return pltpu.make_async_copy(
            source.at[:, pl.ds((k * CHUNK) % half, CHUNK)], geno.at[k % depth],
            in_sems.at[k % depth],
        )

    def load_idx(q, h):
        source = shuf_own if h == 0 else shuf_other
        return pltpu.make_async_copy(
            source.at[core * labels + q],
            idx.at[pl.ds(q * all_samples + h * half, half)],
            idx_sems.at[2 * q + h],
        )

    def save_first(k):
        there = jnp.where(core == 0, k * CHUNK, (k * CHUNK + half) % all_samples)
        rows = pl.ds(pl.multiple_of(there, CHUNK), CHUNK)
        return pltpu.make_async_copy(
            first_stage.at[k % 2], out_ref.at[rows, pl.ds(labels * snp_rows, share)],
            first_sems.at[k % 2],
        )

    def save(q, k):
        return pltpu.make_async_copy(
            stage.at[k % 2],
            out_ref.at[pl.ds(k * CHUNK, CHUNK), pl.ds(q * snp_rows, snp_rows)],
            out_sems.at[k % 2],
        )

    for k in range(depth):
        load(k).start()
    for q in range(labels):
        for h in range(2):
            load_idx(q, h).start()
    sums = sums_own[...] + sums_other[...]
    slope[...] = jnp.broadcast_to(sums[1:2, :] / sums[0:1, :], (LANES, snp_rows)).T
    unit = (
        lax.broadcasted_iota(jnp.int32, (side, side), 0)
        == lax.broadcasted_iota(jnp.int32, (side, side), 1)
    ).astype(jnp.bfloat16)

    for k in range(chunks):
        load(k).wait()
        if k >= 2:
            save_first(k - 2).wait()
        env_ref = env_own if k * CHUNK < half else env_other

        def turn(i, carry, k=k, env_ref=env_ref):
            at = pl.multiple_of(i * side, side)
            e = env_ref[:, pl.ds((k * CHUNK) % half + at, side)]
            turned = []
            for j in range(snp_rows // side):
                rows = pl.ds(j * side, side)
                x = geno[k % depth, rows, pl.ds(at, side)].astype(jnp.float32)
                r = slope[rows, :]
                a = x * (e - jnp.concatenate([r] * (side // LANES), axis=1))
                t = lax.dot_general(
                    unit, a.astype(jnp.bfloat16), (((1,), (1,)), ((), ())),
                    preferred_element_type=jnp.float32,
                )
                for c in range(side // LANES):
                    word = j * (side // LANES) + c
                    table[pl.ds((k * CHUNK + at) * slot + word, side, stride=slot), :] = (
                        t[:, c * LANES : (c + 1) * LANES]
                    )
                turned.append(t)
            turned = jnp.concatenate(turned, axis=1)
            kept = jnp.where(core == 0, turned[:, :share], turned[:, share:])
            first_stage[k % 2, pl.ds(at, side), :] = kept.astype(jnp.bfloat16)
            return carry

        lax.fori_loop(0, CHUNK // side, turn, 0, unroll=2)
        save_first(k).start()
        if k + depth < chunks:
            load(k + depth).start()

    for q in range(labels):
        for h in range(2):
            load_idx(q, h).wait()

        def scatter(i, carry, q=q):
            first = pl.multiple_of(i * UNROLL, UNROLL)
            base = pl.multiple_of(first * slot, UNROLL * slot)
            held = [table[pl.ds(base + u * slot, words), :] for u in range(UNROLL)]
            for u in range(UNROLL):
                to = idx[q * all_samples + first + u] * slot
                dest[pl.ds(to, words), :] = held[u]
            return carry

        lax.fori_loop(0, all_samples // UNROLL, scatter, 0)
        for k in range(chunks):
            if q * chunks + k >= 2:
                save((q * chunks + k - 2) // chunks, (k - 2) % chunks).wait()

            def narrow(i, carry, k=k):
                at = pl.multiple_of(i * side, side)
                for c in range(words):
                    v = dest[pl.ds((k * CHUNK + at) * slot + c, side, stride=slot), :]
                    stage[k % 2, pl.ds(at, side), pl.ds(c * LANES, LANES)] = v.astype(jnp.bfloat16)
                return carry

            lax.fori_loop(0, CHUNK // side, narrow, 0)
            save(q, k).start()
    for k in range(chunks - 2, chunks):
        save_first(k).wait()
        save(labels - 1, k).wait()


def snp_side(core, env_own, env_other, sums_own, sums_other, shuf_own, shuf_other, own, other,
             labels):
    snp_rows, half = own.shape
    all_samples = 2 * half
    words = snp_rows // LANES
    width = labels * snp_rows + snp_rows // 2
    any_spec = pl.BlockSpec(memory_space=pl.ANY)
    smem = pl.BlockSpec(memory_space=pltpu.SMEM)
    vmem = pl.BlockSpec(memory_space=pltpu.VMEM)
    return pl.pallas_call(
        functools.partial(snp_side_kernel, labels=labels),
        out_shape=jax.ShapeDtypeStruct((all_samples, width), jnp.bfloat16),
        in_specs=[smem, vmem, vmem, vmem, vmem, any_spec, any_spec, any_spec, any_spec],
        out_specs=any_spec,
        scratch_shapes=[
            pltpu.SMEM((labels * all_samples,), jnp.int32),
            pltpu.VMEM((3, snp_rows, CHUNK), jnp.bfloat16),
            pltpu.VMEM((all_samples * (words | 1), LANES), jnp.float32),
            pltpu.VMEM((all_samples * (words | 1), LANES), jnp.float32),
            pltpu.VMEM((2, CHUNK, snp_rows), jnp.bfloat16),
            pltpu.VMEM((2, CHUNK, snp_rows // 2), jnp.bfloat16),
            pltpu.VMEM((snp_rows, LANES), jnp.float32),
            pltpu.SemaphoreType.DMA((2 * labels,)),
            pltpu.SemaphoreType.DMA((3,)),
            pltpu.SemaphoreType.DMA((2,)),
            pltpu.SemaphoreType.DMA((2,)),
        ],
        compiler_params=pltpu.CompilerParams(vmem_limit_bytes=61 * MIB),
        cost_estimate=pl.CostEstimate(
            flops=40 * 10**9, bytes_accessed=60 * 10**6, transcendentals=0
        ),
        name="snp_side",
    )(core, env_own, env_other, sums_own, sums_other, shuf_own, shuf_other, own, other)


def window_plan(start, end, bounds_ref, n_bounds, total_blocks):
    middle = (start + end - 1) // 2
    lower_edge = jnp.zeros_like(start)
    upper_edge = jnp.full_like(end, total_blocks)
    for i in range(n_bounds):
        edge = bounds_ref[i]
        before = edge <= middle
        lower_edge = jnp.where(before, jnp.maximum(lower_edge, edge), lower_edge)
        upper_edge = jnp.where(before, upper_edge, jnp.minimum(upper_edge, edge))
    return jnp.maximum(start, lower_edge), jnp.minimum(end, upper_edge)


def select_kernel(
    round_ref, pos_ref, bounds_ref, start_ref, end_ref, own_ref, other_ref,
    rounds_ref, plan_ref, full_ref, *rest, caps, blocks_dev,
):
    pay_refs, (slots, edges) = rest[: len(caps)], rest[len(caps) :]
    reach = len(caps)
    genes, half = own_ref.shape
    shape = start_ref.shape
    per_row = LANES // genes
    chips = shape[0] * per_row
    chip, core = pos_ref[0], pos_ref[1]
    turn = round_ref[0]
    low, high = window_plan(
        start_ref[...], end_ref[...], bounds_ref, bounds_ref.shape[0], chips * blocks_dev
    )
    edges[0] = low
    edges[1] = high
    at = lax.broadcasted_iota(jnp.int32, shape, 0) * per_row
    at = at + lax.broadcasted_iota(jnp.int32, shape, 1) // genes
    a = lax.broadcasted_iota(jnp.int32, (LANES, LANES), 0)
    b = lax.broadcasted_iota(jnp.int32, (LANES, LANES), 1)
    upto = ((a <= b) & (a // genes == b // genes)).astype(jnp.float32).astype(jnp.bfloat16)
    rounds = jnp.int32(0)
    for way in range(2):
        for k in range(1, reach + 1):
            to = at + (k if way == 0 else -k)
            need = (
                (low < (to + 1) * blocks_dev) & (high > to * blocks_dev)
                & (low < high) & (to >= 0) & (to < chips)
            )
            rank = jnp.dot(
                need.astype(jnp.float32).astype(jnp.bfloat16), upto,
                preferred_element_type=jnp.float32,
            ).astype(jnp.int32)
            cap = caps[k - 1]
            slot = rank - 1 - turn * cap
            slots[way * reach + k - 1] = jnp.where(
                need & (slot >= 0) & (slot < cap), slot, -1
            )
            rounds = jnp.maximum(rounds, (jnp.max(rank) + cap - 1) // cap)
    rounds_ref[0] = rounds

    def of_chip(ref, index, which):
        row = ref[index, pl.ds(which // per_row, 1), :]
        out = row[:, :genes]
        for part in range(1, per_row):
            out = jnp.where(
                which % per_row == part, row[:, part * genes : (part + 1) * genes], out
            )
        return out

    plan_ref[...] = jnp.zeros_like(plan_ref)
    plan_ref[0, pl.ds(0, 1), :] = lax.broadcasted_iota(jnp.int32, (1, genes), 1)
    plan_ref[1, pl.ds(0, 1), :] = of_chip(edges, 0, chip)
    plan_ref[2, pl.ds(0, 1), :] = of_chip(edges, 1, chip)
    for side in range(2):
        way = core if side == 0 else 1 - core
        for k in range(1, reach + 1):
            source = chip + (2 * way - 1) * k
            valid = (source >= 0) & (source < chips)
            source = jnp.clip(source, 0, chips - 1)
            to = pl.ds(1 + side * reach + k - 1, 1)
            slot = of_chip(slots, way * reach + k - 1, source)
            plan_ref[0, to, :] = jnp.where(valid, slot, -1)
            plan_ref[1, to, :] = of_chip(edges, 0, source)
            plan_ref[2, to, :] = jnp.where(valid, of_chip(edges, 1, source), 0)

    picks = []
    for k in range(1, reach + 1):
        slot = of_chip(slots, core * reach + k - 1, chip)
        rows = lax.broadcasted_iota(jnp.int32, (caps[k - 1], genes), 0)
        picks.append((rows == slot).astype(jnp.float32))
    picks = jnp.concatenate(picks, axis=0).astype(jnp.bfloat16)
    step = 1024

    def copy(i, carry):
        cols = pl.ds(pl.multiple_of(i * step, step), step)
        late = pl.ds(pl.multiple_of(half + i * step, step), step)
        a, b = own_ref[:, cols], other_ref[:, cols]
        first = jnp.where(core == 0, a, b)
        second = jnp.where(core == 0, b, a)
        full_ref[:, cols] = first
        full_ref[:, late] = second
        for part, to in ((first, cols), (second, late)):
            chosen = jnp.dot(picks, part, preferred_element_type=jnp.float32)
            chosen = chosen.astype(jnp.bfloat16)
            row = 0
            for pay in pay_refs:
                pay[:, to] = chosen[row : row + pay.shape[0]]
                row += pay.shape[0]
        return carry

    lax.fori_loop(0, half // step, copy, 0)


def select(turn, pos, bounds, start, end, own, other, caps, blocks_dev):
    genes, half = own.shape
    reach = len(caps)
    smem = pl.BlockSpec(memory_space=pltpu.SMEM)
    vmem = pl.BlockSpec(memory_space=pltpu.VMEM)
    plan_rows = -(-(2 * reach + 1) // 8) * 8
    return pl.pallas_call(
        functools.partial(select_kernel, caps=caps, blocks_dev=blocks_dev),
        out_shape=(
            jax.ShapeDtypeStruct((1,), jnp.int32),
            jax.ShapeDtypeStruct((3, plan_rows, genes), jnp.int32),
            jax.ShapeDtypeStruct((genes, 2 * half), jnp.bfloat16),
            *[jax.ShapeDtypeStruct((cap, 2 * half), jnp.bfloat16) for cap in caps],
        ),
        in_specs=[smem, smem, smem, vmem, vmem, vmem, vmem],
        out_specs=(smem, vmem, vmem, *[vmem for _ in caps]),
        scratch_shapes=[
            pltpu.VMEM((2 * reach,) + start.shape, jnp.int32),
            pltpu.VMEM((2,) + start.shape, jnp.int32),
        ],
        compiler_params=pltpu.CompilerParams(vmem_limit_bytes=24 * MIB),
        name="select",
    )(turn, pos, bounds, start, end, own, other)


def product_kernel(
    pos_ref, sums_own, sums_other, plan_ref, *rest, caps, labels, genes, blocks_dev
):
    reach = len(caps)
    n_in = 1 + 2 * reach
    gene_refs = rest[:n_in]
    weights_ref, out_ref, power_ref, rows, total, power = rest[n_in:]
    step = pl.program_id(0)
    steps = pl.num_programs(0)
    snp_rows = sums_own.shape[1]
    depth, width = weights_ref.shape
    block = SNP_BLOCK
    sizes = (genes,) + tuple(caps) + tuple(caps)
    starts = [sum(sizes[:i]) for i in range(n_in)]
    used = sum(sizes)

    @pl.when(step == 0)
    def _():
        total[...] = jnp.zeros_like(total)
        power[...] = jnp.zeros_like(power)

    for ref, start, size in zip(gene_refs, starts, sizes):
        rows[pl.ds(start, size), :] = ref[...]
    for n in range(width // block):
        cols = pl.ds(n * block, block)
        total[pl.ds(0, used), cols] += jnp.dot(
            rows[...], weights_ref[:, cols], preferred_element_type=jnp.float32
        )
    kept = power[...]
    for t in range(depth // LANES):
        x = gene_refs[0][:, pl.ds(t * LANES, LANES)].astype(jnp.float32)
        kept = kept + x * x
    power[...] = kept

    @pl.when(step == steps - 1)
    def _():
        chip, core = pos_ref[0], pos_ref[1]
        share_blocks = blocks_dev // 2
        sums = sums_own[...] + sums_other[...]
        cross = sums[1:2, :]
        inter = sums[2:3, :]
        inv = 1.0 / (inter - cross * (cross / sums[0:1, :]) + 0.1 * inter)

        def peak(col, inv_block):
            v = total[:, pl.ds(col, block)]
            v = v * v * inv_block
            best = v[:, :LANES]
            for t in range(1, block // LANES):
                best = jnp.maximum(best, v[:, t * LANES : (t + 1) * LANES])
            return jnp.max(best.T, axis=0, keepdims=True)

        peaks = []
        for q in range(labels):
            for b in range(blocks_dev):
                peaks.append(
                    peak(q * snp_rows + b * block, inv[:, b * block : (b + 1) * block])
                )
        for b in range(share_blocks):
            mine = inv[:, b * block : (b + 1) * block]
            late = inv[:, (share_blocks + b) * block : (share_blocks + b + 1) * block]
            peaks.append(
                peak(labels * snp_rows + b * block, jnp.where(core == 0, mine, late))
            )
        while len(peaks) % 8:
            peaks.append(jnp.zeros_like(peaks[0]))
        peaks = jnp.concatenate(peaks, axis=0)
        out_ref[...] = jnp.zeros_like(out_ref)
        slot_of = lax.broadcasted_iota(jnp.int32, (total.shape[0], genes), 0)
        for i in range(n_in):
            slot = plan_ref[0, pl.ds(i, 1), :]
            slot = jnp.where(slot >= 0, slot + starts[i], -1)
            low = plan_ref[1, pl.ds(i, 1), :]
            high = plan_ref[2, pl.ds(i, 1), :]
            spread = jnp.dot(
                peaks, (slot_of == slot).astype(jnp.float32),
                precision=lax.Precision.HIGHEST, preferred_element_type=jnp.float32,
            )

            def masked(row, snp_block):
                inside = (snp_block >= low) & (snp_block < high)
                return jnp.where(inside, spread[row : row + 1], 0.0)

            found = []
            for q in range(labels):
                best = jnp.zeros((1, genes), jnp.float32)
                for b in range(blocks_dev):
                    best = jnp.maximum(best, masked(q * blocks_dev + b, chip * blocks_dev + b))
                found.append(best)
            best = jnp.zeros((1, genes), jnp.float32)
            for b in range(share_blocks):
                best = jnp.maximum(
                    best,
                    masked(
                        labels * blocks_dev + b, chip * blocks_dev + core * share_blocks + b
                    ),
                )
            out_rows = [best]
            for c in range(2):
                out_rows += [jnp.where(core == c, v, 0.0) for v in found]
            while len(out_rows) % 8:
                out_rows.append(jnp.zeros_like(best))
            if i == 0:
                target = chip
            else:
                way = core if i <= reach else 1 - core
                target = chip + (2 * way - 1) * ((i - 1) % reach + 1)

            @pl.when((target >= 0) & (target < out_ref.shape[0] // 2))
            def _(out_rows=out_rows, target=target):
                for c in range(2):
                    out_ref[2 * target + c, :, pl.ds(0, genes)] = jnp.concatenate(
                        out_rows, axis=0
                    )

        powers = jnp.sum(power[...].T, axis=0, keepdims=True)
        power_ref[...] = jnp.broadcast_to(powers, power_ref.shape)


def products(pos, sums, plan, full, mine, other, weights, caps, labels, chips, blocks_dev):
    genes, all_samples = full.shape
    width = weights.shape[1]
    snp_rows = sums[0].shape[1]
    depth = CHUNK
    used = genes + 2 * sum(caps)
    padded = -(-used // LANES) * LANES
    out_rows = -(-(1 + 2 * labels) // 8) * 8

    def blocked(x):
        return pl.BlockSpec((x.shape[0], depth), lambda k: (0, k))

    arrays = (full, *mine, *other)
    return pl.pallas_call(
        functools.partial(
            product_kernel, caps=caps, labels=labels, genes=genes, blocks_dev=blocks_dev
        ),
        grid=(all_samples // depth,),
        out_shape=(
            jax.ShapeDtypeStruct((2 * chips, out_rows, LANES), jnp.float32),
            jax.ShapeDtypeStruct((8, genes), jnp.float32),
        ),
        in_specs=[
            pl.BlockSpec(memory_space=pltpu.SMEM),
            pl.BlockSpec((8, snp_rows), lambda k: (0, 0)),
            pl.BlockSpec((8, snp_rows), lambda k: (0, 0)),
            pl.BlockSpec(plan.shape, lambda k: (0, 0, 0)),
            *[blocked(x) for x in arrays],
            pl.BlockSpec((depth, width), lambda k: (k, 0)),
        ],
        out_specs=(
            pl.BlockSpec((2 * chips, out_rows, LANES), lambda k: (0, 0, 0)),
            pl.BlockSpec((8, genes), lambda k: (0, 0)),
        ),
        scratch_shapes=[
            pltpu.VMEM((used, depth), jnp.bfloat16),
            pltpu.VMEM((padded, width), jnp.float32),
            pltpu.VMEM((genes, LANES), jnp.float32),
        ],
        compiler_params=pltpu.CompilerParams(vmem_limit_bytes=48 * MIB),
        cost_estimate=pl.CostEstimate(
            flops=2 * used * all_samples * width,
            bytes_accessed=2 * all_samples * (width + used),
            transcendentals=0,
        ),
        name="products",
    )(pos, *sums, plan, *arrays, weights)


def finish_kernel(gathered_ref, power_ref, out_ref, *, samples):
    best = gathered_ref[0]
    for i in range(1, gathered_ref.shape[0]):
        best = jnp.maximum(best, gathered_ref[i])
    labels, genes = out_ref.shape
    peak = best[:labels, :genes]
    out_ref[...] = jnp.sqrt(peak / (power_ref[0:1, :] / samples + 1e-05))


def shards(genotypes, phenotypes, environment, shuffles, window_start, window_end, chrom_bounds):
    snp_rows, half = genotypes.shape
    genes = phenotypes.shape[0]
    perms = shuffles.shape[0]
    chips = lax.axis_size("genome")
    cores = lax.axis_size("sample")
    genome_pos = lax.axis_index("genome")
    sample_pos = lax.axis_index("sample")
    blocks_dev = snp_rows // SNP_BLOCK
    reach = (HALF_BLK + blocks_dev - 1) // blocks_dev
    all_samples = half * cores
    labels = perms // cores
    caps = tuple(min(genes, genes * 4 >> k) for k in range(1, reach + 1))

    other_pheno = swapped(phenotypes)
    env = environment[None]
    own_sums = local_moments(genotypes, env)
    sums = (own_sums, swapped(own_sums))
    late_geno, _ = lax.optimization_barrier((genotypes, other_pheno))
    other_geno = swapped(late_geno)
    other_env = swapped(env)
    other_shuffles = swapped(shuffles)
    pos = jnp.stack([genome_pos, sample_pos]).astype(jnp.int32)
    start = window_start.reshape(-1, LANES)
    end = window_end.reshape(-1, LANES)

    def chosen(turn):
        return select(
            turn, pos, chrom_bounds, start, end, phenotypes, other_pheno, caps, blocks_dev
        )

    def travel(payloads):
        mine = []
        for k, payload in enumerate(payloads, 1):
            pairs = [(i * cores, (i + k) * cores) for i in range(chips - k)]
            pairs += [((i + k) * cores + 1, i * cores + 1) for i in range(chips - k)]
            mine.append(lax.ppermute(payload, ("genome", "sample"), pairs))
        return mine

    rounds, plan, full, *payloads = chosen(jnp.zeros((1,), jnp.int32))
    mine = travel(payloads)
    weights = snp_side(
        pos[1:], env, other_env, *sums, shuffles, other_shuffles, genotypes, other_geno, labels
    )

    def met(plan, full, mine):
        other = [swapped(x) for x in mine]
        return products(
            pos, sums, plan, full, mine, other, weights, caps, labels, chips, blocks_dev
        )

    *mine, weights = lax.optimization_barrier((*mine, weights))
    found, power = met(plan, full, mine)

    def more(carry):
        return carry[0] < rounds[0]

    def again(carry):
        turn, best = carry
        _, plan, full, *payloads = chosen(jnp.full((1,), turn, jnp.int32))
        return turn + 1, jnp.maximum(best, met(plan, full, travel(payloads))[0])

    _, found = lax.while_loop(more, again, (jnp.int32(1), found))
    gathered = lax.all_to_all(found, ("genome", "sample"), 0, 0, tiled=True)
    return pl.pallas_call(
        functools.partial(finish_kernel, samples=all_samples),
        out_shape=jax.ShapeDtypeStruct((perms + 1, genes), jnp.float32),
        name="finish",
    )(gathered, power)


def solution(mesh):
    placed = (
        P("genome", "sample"),
        P("genome", "sample"),
        P("sample"),
        P(None, "sample"),
        P(),
        P(),
        P(),
    )
    return jax.shard_map(
        shards, mesh=mesh, in_specs=placed, out_specs=P(None, "genome"), check_vma=False
    )
```

```python
import functools

import jax
import jax.numpy as jnp
from jax import lax
from jax.experimental import pallas as pl
from jax.experimental.pallas import tpu as pltpu
from jax.sharding import PartitionSpec as P

SNP_BLOCK = 256
HALF_BLK = 7
LANES = 128
ROWS_STEP = 16
CHUNK = 1024
MIB = 2**20


def passed_along(x, axis, by):
    count = lax.axis_size(axis)
    pairs = [(i, i + by) for i in range(count) if 0 <= i + by < count]
    return lax.ppermute(x, axis, pairs)


def swapped(x):
    count = lax.axis_size("sample")
    return lax.ppermute(x, "sample", [(i, (i + 1) % count) for i in range(count)])


def moments_kernel(geno_ref, env_ref, out_ref, sums):
    step = pl.program_id(0)
    snp_rows, chunk = geno_ref.shape

    @pl.when(step == 0)
    def _():
        sums[...] = jnp.zeros_like(sums)

    def add_rows(i, carry):
        first = pl.multiple_of(i * ROWS_STEP, ROWS_STEP)
        held = [sums[m, pl.ds(first, ROWS_STEP), :] for m in range(3)]
        for t in range(chunk // LANES):
            x = geno_ref[pl.ds(first, ROWS_STEP), pl.ds(t * LANES, LANES)].astype(jnp.float32)
            e = env_ref[:, pl.ds(t * LANES, LANES)]
            x = x * x
            held[0] = held[0] + x
            x = x * e
            held[1] = held[1] + x
            held[2] = held[2] + x * e
        for m in range(3):
            sums[m, pl.ds(first, ROWS_STEP), :] = held[m]
        return carry

    lax.fori_loop(0, snp_rows // ROWS_STEP, add_rows, 0, unroll=4)

    @pl.when(step == pl.num_programs(0) - 1)
    def _():
        rows = [jnp.sum(sums[m].T, axis=0, keepdims=True) for m in range(3)]
        rows.append(jnp.zeros((out_ref.shape[0] - 3, snp_rows), jnp.float32))
        out_ref[...] = jnp.concatenate(rows, axis=0)


def local_moments(geno, env):
    snp_rows, half = geno.shape
    chunk = CHUNK
    return pl.pallas_call(
        moments_kernel,
        grid=(half // chunk,),
        out_shape=jax.ShapeDtypeStruct((8, snp_rows), jnp.float32),
        in_specs=[
            pl.BlockSpec((snp_rows, chunk), lambda k: (0, k)),
            pl.BlockSpec((1, chunk), lambda k: (0, k)),
        ],
        out_specs=pl.BlockSpec((8, snp_rows), lambda k: (0, 0)),
        scratch_shapes=[pltpu.VMEM((3, snp_rows, LANES), jnp.float32)],
        compiler_params=pltpu.CompilerParams(vmem_limit_bytes=60 * MIB),
        cost_estimate=pl.CostEstimate(
            flops=5 * 10**9, bytes_accessed=2 * snp_rows * half, transcendentals=0
        ),
        name="local_moments",
    )(geno, env)


def snp_side_kernel(
    core_ref, env_own, env_other, sums_own, sums_other, shuf_own, shuf_other, own_ref, other_ref,
    out_ref,
    idx, geno, env, even, odd, dests, stage, first_stage, slope,
    idx_sems, in_sems, out_sems, first_sems,
    *, labels,
):
    snp_rows, half = own_ref.shape
    all_samples = 2 * half
    chunks = all_samples // CHUNK
    words = snp_rows // LANES
    share = snp_rows // 2
    side = even.shape[0]
    blocks = all_samples // side
    per_chunk = CHUNK // side
    core = core_ref[0]

    def load(k):
        source = own_ref if k * CHUNK < half else other_ref
        return pltpu.make_async_copy(
            source.at[:, pl.ds((k * CHUNK) % half, CHUNK)], geno.at[k], in_sems.at[k]
        )

    def load_idx(q, h):
        source = shuf_own if h == 0 else shuf_other
        return pltpu.make_async_copy(
            source.at[core * labels + q],
            idx.at[pl.ds(q * all_samples + h * half, half)],
            idx_sems.at[2 * q + h],
        )

    def save_first(h):
        to = pl.multiple_of(jnp.where(core == h, 0, half), half)
        return pltpu.make_async_copy(
            first_stage.at[pl.ds(h * half, half)],
            out_ref.at[pl.ds(to, half), pl.ds(labels * snp_rows, share)],
            first_sems.at[h],
        )

    def save(q, k):
        return pltpu.make_async_copy(
            stage.at[k % 2],
            out_ref.at[pl.ds(k * CHUNK, CHUNK), pl.ds(q * snp_rows, snp_rows)],
            out_sems.at[k % 2],
        )

    for k in range(chunks):
        load(k).start()
    for q in range(labels):
        for h in range(2):
            load_idx(q, h).start()
    env[:, pl.ds(0, half)] = env_own[...]
    env[:, pl.ds(half, half)] = env_other[...]
    sums = sums_own[...] + sums_other[...]
    slope[...] = jnp.broadcast_to(sums[1:2, :] / sums[0:1, :], (LANES, snp_rows)).T
    unit = (
        lax.broadcasted_iota(jnp.int32, (side, side), 0)
        == lax.broadcasted_iota(jnp.int32, (side, side), 1)
    ).astype(jnp.bfloat16)

    def turn(b, held):
        k = b // per_chunk
        at = pl.multiple_of((b % per_chunk) * side, side)
        e = env[:, pl.ds(pl.multiple_of(b * side, side), side)]
        flat = held.reshape(side * words, LANES)
        kept = None
        for j in range(snp_rows // side):
            rows = pl.ds(j * side, side)
            x = geno[k, rows, pl.ds(at, side)].astype(jnp.float32)
            r = slope[rows, :]
            a = x * (e - jnp.concatenate([r] * (side // LANES), axis=1))
            t = lax.dot_general(
                unit, a.astype(jnp.bfloat16), (((1,), (1,)), ((), ())),
                preferred_element_type=jnp.float32,
            )
            for c in range(side // LANES):
                word = j * (side // LANES) + c
                flat[pl.ds(word, side, stride=words), :] = t[:, c * LANES : (c + 1) * LANES]
            kept = t if j == 0 else jnp.where(core == 0, kept, t)
        first_stage[pl.ds(pl.multiple_of(b * side, side), side), :] = kept.astype(jnp.bfloat16)

    def scatter(b, held):
        first = pl.multiple_of(b * side, side)
        for u in range(side):
            row = held[u]
            for q in range(labels):
                dests[q][idx[q * all_samples + first + u]] = row

    load(0).wait()
    turn(0, even)
    for q in range(labels):
        for h in range(2):
            load_idx(q, h).wait()

    def arrive(b):
        for k in range(1, chunks):

            @pl.when(b == k * per_chunk)
            def _(k=k):
                load(k).wait()

    def pair(i, carry):
        arrive(2 * i + 2)
        scatter(2 * i, even)
        turn(2 * i + 1, odd)
        scatter(2 * i + 1, odd)
        turn(jnp.minimum(2 * i + 2, blocks - 1), even)
        return carry

    lax.fori_loop(0, blocks // 2, pair, 0)
    for h in range(2):
        save_first(h).start()

    for q in range(labels):
        flat = dests[q].reshape(all_samples * words, LANES)
        for k in range(chunks):
            if q * chunks + k >= 2:
                save((q * chunks + k - 2) // chunks, (k - 2) % chunks).wait()

            def narrow(i, carry, k=k, flat=flat):
                at = pl.multiple_of(i * side, side)
                for c in range(words):
                    v = flat[pl.ds((k * CHUNK + at) * words + c, side, stride=words), :]
                    stage[k % 2, pl.ds(at, side), pl.ds(c * LANES, LANES)] = v.astype(jnp.bfloat16)
                return carry

            lax.fori_loop(0, CHUNK // side, narrow, 0)
            save(q, k).start()
    for k in range(chunks - 2, chunks):
        save(labels - 1, k).wait()
    for h in range(2):
        save_first(h).wait()


def snp_side(core, env_own, env_other, sums_own, sums_other, shuf_own, shuf_other, own, other,
             labels):
    snp_rows, half = own.shape
    all_samples = 2 * half
    words = snp_rows // LANES
    width = labels * snp_rows + snp_rows // 2
    side = 2 * LANES
    any_spec = pl.BlockSpec(memory_space=pl.ANY)
    smem = pl.BlockSpec(memory_space=pltpu.SMEM)
    vmem = pl.BlockSpec(memory_space=pltpu.VMEM)
    return pl.pallas_call(
        functools.partial(snp_side_kernel, labels=labels),
        out_shape=jax.ShapeDtypeStruct((all_samples, width), jnp.bfloat16),
        in_specs=[smem, vmem, vmem, vmem, vmem, any_spec, any_spec, any_spec, any_spec],
        out_specs=any_spec,
        scratch_shapes=[
            pltpu.SMEM((labels * all_samples,), jnp.int32),
            pltpu.VMEM((all_samples // CHUNK, snp_rows, CHUNK), jnp.bfloat16),
            pltpu.VMEM((1, all_samples), jnp.float32),
            pltpu.VMEM((side, words, LANES), jnp.float32),
            pltpu.VMEM((side, words, LANES), jnp.float32),
            [pltpu.VMEM((all_samples, words, LANES), jnp.float32) for _ in range(labels)],
            pltpu.VMEM((2, CHUNK, snp_rows), jnp.bfloat16),
            pltpu.VMEM((all_samples, snp_rows // 2), jnp.bfloat16),
            pltpu.VMEM((snp_rows, LANES), jnp.float32),
            pltpu.SemaphoreType.DMA((2 * labels,)),
            pltpu.SemaphoreType.DMA((all_samples // CHUNK,)),
            pltpu.SemaphoreType.DMA((2,)),
            pltpu.SemaphoreType.DMA((2,)),
        ],
        compiler_params=pltpu.CompilerParams(vmem_limit_bytes=60 * MIB),
        cost_estimate=pl.CostEstimate(
            flops=40 * 10**9, bytes_accessed=60 * 10**6, transcendentals=0
        ),
        name="snp_side",
    )(core, env_own, env_other, sums_own, sums_other, shuf_own, shuf_other, own, other)


def window_plan(start, end, bounds_ref, n_bounds, total_blocks):
    middle = (start + end - 1) // 2
    lower_edge = jnp.zeros_like(start)
    upper_edge = jnp.full_like(end, total_blocks)
    for i in range(n_bounds):
        edge = bounds_ref[i]
        before = edge <= middle
        lower_edge = jnp.where(before, jnp.maximum(lower_edge, edge), lower_edge)
        upper_edge = jnp.where(before, upper_edge, jnp.minimum(upper_edge, edge))
    return jnp.maximum(start, lower_edge), jnp.minimum(end, upper_edge)


def select_kernel(
    round_ref, pos_ref, bounds_ref, start_ref, end_ref, own_ref, other_ref,
    rounds_ref, plan_ref, full_ref, *rest, caps, blocks_dev,
):
    pay_refs, (slots, edges) = rest[: len(caps)], rest[len(caps) :]
    reach = len(caps)
    genes, half = own_ref.shape
    shape = start_ref.shape
    per_row = LANES // genes
    chips = shape[0] * per_row
    chip, core = pos_ref[0], pos_ref[1]
    turn = round_ref[0]
    low, high = window_plan(
        start_ref[...], end_ref[...], bounds_ref, bounds_ref.shape[0], chips * blocks_dev
    )
    edges[0] = low
    edges[1] = high
    at = lax.broadcasted_iota(jnp.int32, shape, 0) * per_row
    at = at + lax.broadcasted_iota(jnp.int32, shape, 1) // genes
    a = lax.broadcasted_iota(jnp.int32, (LANES, LANES), 0)
    b = lax.broadcasted_iota(jnp.int32, (LANES, LANES), 1)
    upto = ((a <= b) & (a // genes == b // genes)).astype(jnp.float32).astype(jnp.bfloat16)
    rounds = jnp.int32(0)
    for way in range(2):
        for k in range(1, reach + 1):
            to = at + (k if way == 0 else -k)
            need = (
                (low < (to + 1) * blocks_dev) & (high > to * blocks_dev)
                & (low < high) & (to >= 0) & (to < chips)
            )
            rank = jnp.dot(
                need.astype(jnp.float32).astype(jnp.bfloat16), upto,
                preferred_element_type=jnp.float32,
            ).astype(jnp.int32)
            cap = caps[k - 1]
            slot = rank - 1 - turn * cap
            slots[way * reach + k - 1] = jnp.where(
                need & (slot >= 0) & (slot < cap), slot, -1
            )
            rounds = jnp.maximum(rounds, (jnp.max(rank) + cap - 1) // cap)
    rounds_ref[0] = rounds

    def of_chip(ref, index, which):
        row = ref[index, pl.ds(which // per_row, 1), :]
        out = row[:, :genes]
        for part in range(1, per_row):
            out = jnp.where(
                which % per_row == part, row[:, part * genes : (part + 1) * genes], out
            )
        return out

    plan_ref[...] = jnp.zeros_like(plan_ref)
    plan_ref[0, pl.ds(0, 1), :] = lax.broadcasted_iota(jnp.int32, (1, genes), 1)
    plan_ref[1, pl.ds(0, 1), :] = of_chip(edges, 0, chip)
    plan_ref[2, pl.ds(0, 1), :] = of_chip(edges, 1, chip)
    for side in range(2):
        way = core if side == 0 else 1 - core
        for k in range(1, reach + 1):
            source = chip + (2 * way - 1) * k
            valid = (source >= 0) & (source < chips)
            source = jnp.clip(source, 0, chips - 1)
            to = pl.ds(1 + side * reach + k - 1, 1)
            slot = of_chip(slots, way * reach + k - 1, source)
            plan_ref[0, to, :] = jnp.where(valid, slot, -1)
            plan_ref[1, to, :] = of_chip(edges, 0, source)
            plan_ref[2, to, :] = jnp.where(valid, of_chip(edges, 1, source), 0)

    picks = []
    for k in range(1, reach + 1):
        slot = of_chip(slots, core * reach + k - 1, chip)
        rows = lax.broadcasted_iota(jnp.int32, (caps[k - 1], genes), 0)
        picks.append((rows == slot).astype(jnp.float32))
    picks = jnp.concatenate(picks, axis=0).astype(jnp.bfloat16)
    step = 1024

    def copy(i, carry):
        cols = pl.ds(pl.multiple_of(i * step, step), step)
        late = pl.ds(pl.multiple_of(half + i * step, step), step)
        a, b = own_ref[:, cols], other_ref[:, cols]
        first = jnp.where(core == 0, a, b)
        second = jnp.where(core == 0, b, a)
        full_ref[:, cols] = first
        full_ref[:, late] = second
        for part, to in ((first, cols), (second, late)):
            chosen = jnp.dot(picks, part, preferred_element_type=jnp.float32)
            chosen = chosen.astype(jnp.bfloat16)
            row = 0
            for pay in pay_refs:
                pay[:, to] = chosen[row : row + pay.shape[0]]
                row += pay.shape[0]
        return carry

    lax.fori_loop(0, half // step, copy, 0)


def select(turn, pos, bounds, start, end, own, other, caps, blocks_dev):
    genes, half = own.shape
    reach = len(caps)
    smem = pl.BlockSpec(memory_space=pltpu.SMEM)
    vmem = pl.BlockSpec(memory_space=pltpu.VMEM)
    plan_rows = -(-(2 * reach + 1) // 8) * 8
    return pl.pallas_call(
        functools.partial(select_kernel, caps=caps, blocks_dev=blocks_dev),
        out_shape=(
            jax.ShapeDtypeStruct((1,), jnp.int32),
            jax.ShapeDtypeStruct((3, plan_rows, genes), jnp.int32),
            jax.ShapeDtypeStruct((genes, 2 * half), jnp.bfloat16),
            *[jax.ShapeDtypeStruct((cap, 2 * half), jnp.bfloat16) for cap in caps],
        ),
        in_specs=[smem, smem, smem, vmem, vmem, vmem, vmem],
        out_specs=(smem, vmem, vmem, *[vmem for _ in caps]),
        scratch_shapes=[
            pltpu.VMEM((2 * reach,) + start.shape, jnp.int32),
            pltpu.VMEM((2,) + start.shape, jnp.int32),
        ],
        compiler_params=pltpu.CompilerParams(vmem_limit_bytes=24 * MIB),
        name="select",
    )(turn, pos, bounds, start, end, own, other)


def product_kernel(
    pos_ref, sums_own, sums_other, plan_ref, *rest, caps, labels, genes, blocks_dev
):
    reach = len(caps)
    n_in = 1 + 2 * reach
    gene_refs = rest[:n_in]
    weights_ref, out_ref, power_ref, rows, total, power = rest[n_in:]
    step = pl.program_id(0)
    steps = pl.num_programs(0)
    snp_rows = sums_own.shape[1]
    depth, width = weights_ref.shape
    block = SNP_BLOCK
    sizes = (genes,) + tuple(caps) + tuple(caps)
    starts = [sum(sizes[:i]) for i in range(n_in)]
    used = sum(sizes)

    @pl.when(step == 0)
    def _():
        total[...] = jnp.zeros_like(total)
        power[...] = jnp.zeros_like(power)

    for ref, start, size in zip(gene_refs, starts, sizes):
        rows[pl.ds(start, size), :] = ref[...]
    for n in range(width // block):
        cols = pl.ds(n * block, block)
        total[pl.ds(0, used), cols] += jnp.dot(
            rows[...], weights_ref[:, cols], preferred_element_type=jnp.float32
        )
    kept = power[...]
    for t in range(depth // LANES):
        x = gene_refs[0][:, pl.ds(t * LANES, LANES)].astype(jnp.float32)
        kept = kept + x * x
    power[...] = kept

    @pl.when(step == steps - 1)
    def _():
        chip, core = pos_ref[0], pos_ref[1]
        share_blocks = blocks_dev // 2
        sums = sums_own[...] + sums_other[...]
        cross = sums[1:2, :]
        inter = sums[2:3, :]
        inv = 1.0 / (inter - cross * (cross / sums[0:1, :]) + 0.1 * inter)

        def peak(col, inv_block):
            v = total[:, pl.ds(col, block)]
            v = v * v * inv_block
            best = v[:, :LANES]
            for t in range(1, block // LANES):
                best = jnp.maximum(best, v[:, t * LANES : (t + 1) * LANES])
            return jnp.max(best.T, axis=0, keepdims=True)

        peaks = []
        for q in range(labels):
            for b in range(blocks_dev):
                peaks.append(
                    peak(q * snp_rows + b * block, inv[:, b * block : (b + 1) * block])
                )
        for b in range(share_blocks):
            mine = inv[:, b * block : (b + 1) * block]
            late = inv[:, (share_blocks + b) * block : (share_blocks + b + 1) * block]
            peaks.append(
                peak(labels * snp_rows + b * block, jnp.where(core == 0, mine, late))
            )
        while len(peaks) % 8:
            peaks.append(jnp.zeros_like(peaks[0]))
        peaks = jnp.concatenate(peaks, axis=0)
        out_ref[...] = jnp.zeros_like(out_ref)
        slot_of = lax.broadcasted_iota(jnp.int32, (total.shape[0], genes), 0)
        for i in range(n_in):
            slot = plan_ref[0, pl.ds(i, 1), :]
            slot = jnp.where(slot >= 0, slot + starts[i], -1)
            low = plan_ref[1, pl.ds(i, 1), :]
            high = plan_ref[2, pl.ds(i, 1), :]
            spread = jnp.dot(
                peaks, (slot_of == slot).astype(jnp.float32),
                precision=lax.Precision.HIGHEST, preferred_element_type=jnp.float32,
            )

            def masked(row, snp_block):
                inside = (snp_block >= low) & (snp_block < high)
                return jnp.where(inside, spread[row : row + 1], 0.0)

            found = []
            for q in range(labels):
                best = jnp.zeros((1, genes), jnp.float32)
                for b in range(blocks_dev):
                    best = jnp.maximum(best, masked(q * blocks_dev + b, chip * blocks_dev + b))
                found.append(best)
            best = jnp.zeros((1, genes), jnp.float32)
            for b in range(share_blocks):
                best = jnp.maximum(
                    best,
                    masked(
                        labels * blocks_dev + b, chip * blocks_dev + core * share_blocks + b
                    ),
                )
            out_rows = [best]
            for c in range(2):
                out_rows += [jnp.where(core == c, v, 0.0) for v in found]
            while len(out_rows) % 8:
                out_rows.append(jnp.zeros_like(best))
            if i == 0:
                target = chip
            else:
                way = core if i <= reach else 1 - core
                target = chip + (2 * way - 1) * ((i - 1) % reach + 1)

            @pl.when((target >= 0) & (target < out_ref.shape[0] // 2))
            def _(out_rows=out_rows, target=target):
                for c in range(2):
                    out_ref[2 * target + c, :, pl.ds(0, genes)] = jnp.concatenate(
                        out_rows, axis=0
                    )

        powers = jnp.sum(power[...].T, axis=0, keepdims=True)
        power_ref[...] = jnp.broadcast_to(powers, power_ref.shape)


def products(pos, sums, plan, full, mine, other, weights, caps, labels, chips, blocks_dev):
    genes, all_samples = full.shape
    width = weights.shape[1]
    snp_rows = sums[0].shape[1]
    depth = CHUNK
    used = genes + 2 * sum(caps)
    padded = -(-used // LANES) * LANES
    out_rows = -(-(1 + 2 * labels) // 8) * 8

    def blocked(x):
        return pl.BlockSpec((x.shape[0], depth), lambda k: (0, k))

    arrays = (full, *mine, *other)
    return pl.pallas_call(
        functools.partial(
            product_kernel, caps=caps, labels=labels, genes=genes, blocks_dev=blocks_dev
        ),
        grid=(all_samples // depth,),
        out_shape=(
            jax.ShapeDtypeStruct((2 * chips, out_rows, LANES), jnp.float32),
            jax.ShapeDtypeStruct((8, genes), jnp.float32),
        ),
        in_specs=[
            pl.BlockSpec(memory_space=pltpu.SMEM),
            pl.BlockSpec((8, snp_rows), lambda k: (0, 0)),
            pl.BlockSpec((8, snp_rows), lambda k: (0, 0)),
            pl.BlockSpec(plan.shape, lambda k: (0, 0, 0)),
            *[blocked(x) for x in arrays],
            pl.BlockSpec((depth, width), lambda k: (k, 0)),
        ],
        out_specs=(
            pl.BlockSpec((2 * chips, out_rows, LANES), lambda k: (0, 0, 0)),
            pl.BlockSpec((8, genes), lambda k: (0, 0)),
        ),
        scratch_shapes=[
            pltpu.VMEM((used, depth), jnp.bfloat16),
            pltpu.VMEM((padded, width), jnp.float32),
            pltpu.VMEM((genes, LANES), jnp.float32),
        ],
        compiler_params=pltpu.CompilerParams(vmem_limit_bytes=48 * MIB),
        cost_estimate=pl.CostEstimate(
            flops=2 * used * all_samples * width,
            bytes_accessed=2 * all_samples * (width + used),
            transcendentals=0,
        ),
        name="products",
    )(pos, *sums, plan, *arrays, weights)


def finish_kernel(gathered_ref, power_ref, out_ref, *, samples):
    best = gathered_ref[0]
    for i in range(1, gathered_ref.shape[0]):
        best = jnp.maximum(best, gathered_ref[i])
    labels, genes = out_ref.shape
    peak = best[:labels, :genes]
    out_ref[...] = jnp.sqrt(peak / (power_ref[0:1, :] / samples + 1e-05))


def shards(genotypes, phenotypes, environment, shuffles, window_start, window_end, chrom_bounds):
    snp_rows, half = genotypes.shape
    genes = phenotypes.shape[0]
    perms = shuffles.shape[0]
    chips = lax.axis_size("genome")
    cores = lax.axis_size("sample")
    genome_pos = lax.axis_index("genome")
    sample_pos = lax.axis_index("sample")
    blocks_dev = snp_rows // SNP_BLOCK
    reach = (HALF_BLK + blocks_dev - 1) // blocks_dev
    all_samples = half * cores
    labels = perms // cores
    caps = tuple(min(genes, genes * 4 >> k) for k in range(1, reach + 1))

    other_pheno = swapped(phenotypes)
    env = environment[None]
    own_sums = local_moments(genotypes, env)
    sums = (own_sums, swapped(own_sums))
    late_geno, _ = lax.optimization_barrier((genotypes, other_pheno))
    other_geno = swapped(late_geno)
    other_env = swapped(env)
    other_shuffles = swapped(shuffles)
    pos = jnp.stack([genome_pos, sample_pos]).astype(jnp.int32)
    start = window_start.reshape(-1, LANES)
    end = window_end.reshape(-1, LANES)

    def chosen(turn):
        return select(
            turn, pos, chrom_bounds, start, end, phenotypes, other_pheno, caps, blocks_dev
        )

    def travel(payloads):
        mine = []
        for k, payload in enumerate(payloads, 1):
            pairs = [(i * cores, (i + k) * cores) for i in range(chips - k)]
            pairs += [((i + k) * cores + 1, i * cores + 1) for i in range(chips - k)]
            mine.append(lax.ppermute(payload, ("genome", "sample"), pairs))
        return mine

    rounds, plan, full, *payloads = chosen(jnp.zeros((1,), jnp.int32))
    mine = travel(payloads)
    weights = snp_side(
        pos[1:], env, other_env, *sums, shuffles, other_shuffles, genotypes, other_geno, labels
    )

    def met(plan, full, mine):
        other = [swapped(x) for x in mine]
        return products(
            pos, sums, plan, full, mine, other, weights, caps, labels, chips, blocks_dev
        )

    *mine, weights = lax.optimization_barrier((*mine, weights))
    found, power = met(plan, full, mine)

    def more(carry):
        return carry[0] < rounds[0]

    def again(carry):
        turn, best = carry
        _, plan, full, *payloads = chosen(jnp.full((1,), turn, jnp.int32))
        return turn + 1, jnp.maximum(best, met(plan, full, travel(payloads))[0])

    _, found = lax.while_loop(more, again, (jnp.int32(1), found))
    gathered = lax.all_to_all(found, ("genome", "sample"), 0, 0, tiled=True)
    return pl.pallas_call(
        functools.partial(finish_kernel, samples=all_samples),
        out_shape=jax.ShapeDtypeStruct((perms + 1, genes), jnp.float32),
        name="finish",
    )(gathered, power)


def solution(mesh):
    placed = (
        P("genome", "sample"),
        P("genome", "sample"),
        P("sample"),
        P(None, "sample"),
        P(),
        P(),
        P(),
    )
    return jax.shard_map(
        shards, mesh=mesh, in_specs=placed, out_specs=P(None, "genome"), check_vma=False
    )
```

```python
import functools

import jax
import jax.numpy as jnp
from jax import lax
from jax.experimental import pallas as pl
from jax.experimental.pallas import tpu as pltpu
from jax.sharding import PartitionSpec as P

SNP_BLOCK = 256
HALF_BLK = 7
LANES = 128
ROWS_STEP = 16
UNROLL = 32
CHUNK = 1024
MIB = 2**20


def passed_along(x, axis, by):
    count = lax.axis_size(axis)
    pairs = [(i, i + by) for i in range(count) if 0 <= i + by < count]
    return lax.ppermute(x, axis, pairs)


def swapped(x):
    count = lax.axis_size("sample")
    return lax.ppermute(x, "sample", [(i, (i + 1) % count) for i in range(count)])


def moments_kernel(geno_ref, env_ref, out_ref, sums):
    step = pl.program_id(0)
    snp_rows, chunk = geno_ref.shape

    @pl.when(step == 0)
    def _():
        sums[...] = jnp.zeros_like(sums)

    def add_rows(i, carry):
        first = pl.multiple_of(i * ROWS_STEP, ROWS_STEP)
        held = [sums[m, pl.ds(first, ROWS_STEP), :] for m in range(3)]
        for t in range(chunk // LANES):
            x = geno_ref[pl.ds(first, ROWS_STEP), pl.ds(t * LANES, LANES)].astype(jnp.float32)
            e = env_ref[:, pl.ds(t * LANES, LANES)]
            x = x * x
            held[0] = held[0] + x
            x = x * e
            held[1] = held[1] + x
            held[2] = held[2] + x * e
        for m in range(3):
            sums[m, pl.ds(first, ROWS_STEP), :] = held[m]
        return carry

    lax.fori_loop(0, snp_rows // ROWS_STEP, add_rows, 0, unroll=4)

    @pl.when(step == pl.num_programs(0) - 1)
    def _():
        rows = [jnp.sum(sums[m].T, axis=0, keepdims=True) for m in range(3)]
        rows.append(jnp.zeros((out_ref.shape[0] - 3, snp_rows), jnp.float32))
        out_ref[...] = jnp.concatenate(rows, axis=0)


def local_moments(geno, env):
    snp_rows, half = geno.shape
    chunk = CHUNK
    return pl.pallas_call(
        moments_kernel,
        grid=(half // chunk,),
        out_shape=jax.ShapeDtypeStruct((8, snp_rows), jnp.float32),
        in_specs=[
            pl.BlockSpec((snp_rows, chunk), lambda k: (0, k)),
            pl.BlockSpec((1, chunk), lambda k: (0, k)),
        ],
        out_specs=pl.BlockSpec((8, snp_rows), lambda k: (0, 0)),
        scratch_shapes=[pltpu.VMEM((3, snp_rows, LANES), jnp.float32)],
        compiler_params=pltpu.CompilerParams(vmem_limit_bytes=60 * MIB),
        cost_estimate=pl.CostEstimate(
            flops=5 * 10**9, bytes_accessed=2 * snp_rows * half, transcendentals=0
        ),
        name="local_moments",
    )(geno, env)


def snp_side_kernel(
    core_ref, env_own, env_other, sums_own, sums_other, shuf_own, shuf_other, own_ref, other_ref,
    out_ref,
    idx, geno, env, even, dests, stage, first_stage, slope,
    idx_sems, in_sems, out_sems, first_sems,
    *, labels,
):
    snp_rows, half = own_ref.shape
    all_samples = 2 * half
    chunks = all_samples // CHUNK
    words = snp_rows // LANES
    share = snp_rows // 2
    side = even.shape[0]
    blocks = all_samples // side
    per_chunk = CHUNK // side
    core = core_ref[0]

    def load(k):
        source = own_ref if k * CHUNK < half else other_ref
        return pltpu.make_async_copy(
            source.at[:, pl.ds((k * CHUNK) % half, CHUNK)], geno.at[k], in_sems.at[k]
        )

    def load_idx(q, h):
        source = shuf_own if h == 0 else shuf_other
        return pltpu.make_async_copy(
            source.at[core * labels + q],
            idx.at[pl.ds(q * all_samples + h * half, half)],
            idx_sems.at[2 * q + h],
        )

    def save_first(h):
        to = pl.multiple_of(jnp.where(core == h, 0, half), half)
        return pltpu.make_async_copy(
            first_stage.at[pl.ds(h * half, half)],
            out_ref.at[pl.ds(to, half), pl.ds(labels * snp_rows, share)],
            first_sems.at[h],
        )

    def save(q, k):
        return pltpu.make_async_copy(
            stage.at[k % 2],
            out_ref.at[pl.ds(k * CHUNK, CHUNK), pl.ds(q * snp_rows, snp_rows)],
            out_sems.at[k % 2],
        )

    for k in range(chunks):
        load(k).start()
    for q in range(labels):
        for h in range(2):
            load_idx(q, h).start()
    env[:, pl.ds(0, half)] = env_own[...]
    env[:, pl.ds(half, half)] = env_other[...]
    sums = sums_own[...] + sums_other[...]
    slope[...] = jnp.broadcast_to(sums[1:2, :] / sums[0:1, :], (LANES, snp_rows)).T
    unit = (
        lax.broadcasted_iota(jnp.int32, (side, side), 0)
        == lax.broadcasted_iota(jnp.int32, (side, side), 1)
    ).astype(jnp.bfloat16)

    def turn(b, held):
        k = b // per_chunk
        at = pl.multiple_of((b % per_chunk) * side, side)
        e = env[:, pl.ds(pl.multiple_of(b * side, side), side)]
        flat = held.reshape(side * words, LANES)
        kept = None
        for j in range(snp_rows // side):
            rows = pl.ds(j * side, side)
            x = geno[k, rows, pl.ds(at, side)].astype(jnp.float32)
            r = slope[rows, :]
            a = x * (e - jnp.concatenate([r] * (side // LANES), axis=1))
            t = lax.dot_general(
                unit, a.astype(jnp.bfloat16), (((1,), (1,)), ((), ())),
                preferred_element_type=jnp.float32,
            )
            for c in range(side // LANES):
                word = j * (side // LANES) + c
                flat[pl.ds(word, side, stride=words), :] = t[:, c * LANES : (c + 1) * LANES]
            kept = t if j == 0 else jnp.where(core == 0, kept, t)
        first_stage[pl.ds(pl.multiple_of(b * side, side), side), :] = kept.astype(jnp.bfloat16)

    def scatter(b, held):
        def group(i, carry):
            low = pl.multiple_of(i * UNROLL, UNROLL)
            first = pl.multiple_of(b * side + low, UNROLL)
            rows = [held[low + u] for u in range(UNROLL)]
            for q in range(labels):
                for u in range(UNROLL):
                    dests[q][idx[q * all_samples + first + u]] = rows[u]
            return carry

        lax.fori_loop(0, side // UNROLL, group, 0)

    load(0).wait()
    for q in range(labels):
        for h in range(2):
            load_idx(q, h).wait()

    def arrive(b):
        for k in range(1, chunks):

            @pl.when(b == k * per_chunk)
            def _(k=k):
                load(k).wait()

    def one(b, carry):
        arrive(b)
        turn(b, even)
        scatter(b, even)
        return carry

    lax.fori_loop(0, blocks, one, 0)
    for h in range(2):
        save_first(h).start()

    for q in range(labels):
        flat = dests[q].reshape(all_samples * words, LANES)
        for k in range(chunks):
            if q * chunks + k >= 2:
                save((q * chunks + k - 2) // chunks, (k - 2) % chunks).wait()

            def narrow(i, carry, k=k, flat=flat):
                at = pl.multiple_of(i * side, side)
                for c in range(words):
                    v = flat[pl.ds((k * CHUNK + at) * words + c, side, stride=words), :]
                    stage[k % 2, pl.ds(at, side), pl.ds(c * LANES, LANES)] = v.astype(jnp.bfloat16)
                return carry

            lax.fori_loop(0, CHUNK // side, narrow, 0)
            save(q, k).start()
    for k in range(chunks - 2, chunks):
        save(labels - 1, k).wait()
    for h in range(2):
        save_first(h).wait()


def snp_side(core, env_own, env_other, sums_own, sums_other, shuf_own, shuf_other, own, other,
             labels):
    snp_rows, half = own.shape
    all_samples = 2 * half
    words = snp_rows // LANES
    width = labels * snp_rows + snp_rows // 2
    side = 2 * LANES
    any_spec = pl.BlockSpec(memory_space=pl.ANY)
    smem = pl.BlockSpec(memory_space=pltpu.SMEM)
    vmem = pl.BlockSpec(memory_space=pltpu.VMEM)
    return pl.pallas_call(
        functools.partial(snp_side_kernel, labels=labels),
        out_shape=jax.ShapeDtypeStruct((all_samples, width), jnp.bfloat16),
        in_specs=[smem, vmem, vmem, vmem, vmem, any_spec, any_spec, any_spec, any_spec],
        out_specs=any_spec,
        scratch_shapes=[
            pltpu.SMEM((labels * all_samples,), jnp.int32),
            pltpu.VMEM((all_samples // CHUNK, snp_rows, CHUNK), jnp.bfloat16),
            pltpu.VMEM((1, all_samples), jnp.float32),
            pltpu.VMEM((side, words, LANES), jnp.float32),
            [pltpu.VMEM((all_samples, words, LANES), jnp.float32) for _ in range(labels)],
            pltpu.VMEM((2, CHUNK, snp_rows), jnp.bfloat16),
            pltpu.VMEM((all_samples, snp_rows // 2), jnp.bfloat16),
            pltpu.VMEM((snp_rows, LANES), jnp.float32),
            pltpu.SemaphoreType.DMA((2 * labels,)),
            pltpu.SemaphoreType.DMA((all_samples // CHUNK,)),
            pltpu.SemaphoreType.DMA((2,)),
            pltpu.SemaphoreType.DMA((2,)),
        ],
        compiler_params=pltpu.CompilerParams(vmem_limit_bytes=60 * MIB),
        cost_estimate=pl.CostEstimate(
            flops=40 * 10**9, bytes_accessed=60 * 10**6, transcendentals=0
        ),
        name="snp_side",
    )(core, env_own, env_other, sums_own, sums_other, shuf_own, shuf_other, own, other)


def window_plan(start, end, bounds_ref, n_bounds, total_blocks):
    middle = (start + end - 1) // 2
    lower_edge = jnp.zeros_like(start)
    upper_edge = jnp.full_like(end, total_blocks)
    for i in range(n_bounds):
        edge = bounds_ref[i]
        before = edge <= middle
        lower_edge = jnp.where(before, jnp.maximum(lower_edge, edge), lower_edge)
        upper_edge = jnp.where(before, upper_edge, jnp.minimum(upper_edge, edge))
    return jnp.maximum(start, lower_edge), jnp.minimum(end, upper_edge)


def select_kernel(
    round_ref, pos_ref, bounds_ref, start_ref, end_ref, own_ref, other_ref,
    rounds_ref, plan_ref, full_ref, *rest, caps, blocks_dev,
):
    pay_refs, (slots, edges) = rest[: len(caps)], rest[len(caps) :]
    reach = len(caps)
    genes, half = own_ref.shape
    shape = start_ref.shape
    per_row = LANES // genes
    chips = shape[0] * per_row
    chip, core = pos_ref[0], pos_ref[1]
    turn = round_ref[0]
    low, high = window_plan(
        start_ref[...], end_ref[...], bounds_ref, bounds_ref.shape[0], chips * blocks_dev
    )
    edges[0] = low
    edges[1] = high
    at = lax.broadcasted_iota(jnp.int32, shape, 0) * per_row
    at = at + lax.broadcasted_iota(jnp.int32, shape, 1) // genes
    a = lax.broadcasted_iota(jnp.int32, (LANES, LANES), 0)
    b = lax.broadcasted_iota(jnp.int32, (LANES, LANES), 1)
    upto = ((a <= b) & (a // genes == b // genes)).astype(jnp.float32).astype(jnp.bfloat16)
    rounds = jnp.int32(0)
    for way in range(2):
        for k in range(1, reach + 1):
            to = at + (k if way == 0 else -k)
            need = (
                (low < (to + 1) * blocks_dev) & (high > to * blocks_dev)
                & (low < high) & (to >= 0) & (to < chips)
            )
            rank = jnp.dot(
                need.astype(jnp.float32).astype(jnp.bfloat16), upto,
                preferred_element_type=jnp.float32,
            ).astype(jnp.int32)
            cap = caps[k - 1]
            slot = rank - 1 - turn * cap
            slots[way * reach + k - 1] = jnp.where(
                need & (slot >= 0) & (slot < cap), slot, -1
            )
            rounds = jnp.maximum(rounds, (jnp.max(rank) + cap - 1) // cap)
    rounds_ref[0] = rounds

    def of_chip(ref, index, which):
        row = ref[index, pl.ds(which // per_row, 1), :]
        out = row[:, :genes]
        for part in range(1, per_row):
            out = jnp.where(
                which % per_row == part, row[:, part * genes : (part + 1) * genes], out
            )
        return out

    plan_ref[...] = jnp.zeros_like(plan_ref)
    plan_ref[0, pl.ds(0, 1), :] = lax.broadcasted_iota(jnp.int32, (1, genes), 1)
    plan_ref[1, pl.ds(0, 1), :] = of_chip(edges, 0, chip)
    plan_ref[2, pl.ds(0, 1), :] = of_chip(edges, 1, chip)
    for side in range(2):
        way = core if side == 0 else 1 - core
        for k in range(1, reach + 1):
            source = chip + (2 * way - 1) * k
            valid = (source >= 0) & (source < chips)
            source = jnp.clip(source, 0, chips - 1)
            to = pl.ds(1 + side * reach + k - 1, 1)
            slot = of_chip(slots, way * reach + k - 1, source)
            plan_ref[0, to, :] = jnp.where(valid, slot, -1)
            plan_ref[1, to, :] = of_chip(edges, 0, source)
            plan_ref[2, to, :] = jnp.where(valid, of_chip(edges, 1, source), 0)

    picks = []
    for k in range(1, reach + 1):
        slot = of_chip(slots, core * reach + k - 1, chip)
        rows = lax.broadcasted_iota(jnp.int32, (caps[k - 1], genes), 0)
        picks.append((rows == slot).astype(jnp.float32))
    picks = jnp.concatenate(picks, axis=0).astype(jnp.bfloat16)
    step = 1024

    def copy(i, carry):
        cols = pl.ds(pl.multiple_of(i * step, step), step)
        late = pl.ds(pl.multiple_of(half + i * step, step), step)
        a, b = own_ref[:, cols], other_ref[:, cols]
        first = jnp.where(core == 0, a, b)
        second = jnp.where(core == 0, b, a)
        full_ref[:, cols] = first
        full_ref[:, late] = second
        for part, to in ((first, cols), (second, late)):
            chosen = jnp.dot(picks, part, preferred_element_type=jnp.float32)
            chosen = chosen.astype(jnp.bfloat16)
            row = 0
            for pay in pay_refs:
                pay[:, to] = chosen[row : row + pay.shape[0]]
                row += pay.shape[0]
        return carry

    lax.fori_loop(0, half // step, copy, 0)


def select(turn, pos, bounds, start, end, own, other, caps, blocks_dev):
    genes, half = own.shape
    reach = len(caps)
    smem = pl.BlockSpec(memory_space=pltpu.SMEM)
    vmem = pl.BlockSpec(memory_space=pltpu.VMEM)
    plan_rows = -(-(2 * reach + 1) // 8) * 8
    return pl.pallas_call(
        functools.partial(select_kernel, caps=caps, blocks_dev=blocks_dev),
        out_shape=(
            jax.ShapeDtypeStruct((1,), jnp.int32),
            jax.ShapeDtypeStruct((3, plan_rows, genes), jnp.int32),
            jax.ShapeDtypeStruct((genes, 2 * half), jnp.bfloat16),
            *[jax.ShapeDtypeStruct((cap, 2 * half), jnp.bfloat16) for cap in caps],
        ),
        in_specs=[smem, smem, smem, vmem, vmem, vmem, vmem],
        out_specs=(smem, vmem, vmem, *[vmem for _ in caps]),
        scratch_shapes=[
            pltpu.VMEM((2 * reach,) + start.shape, jnp.int32),
            pltpu.VMEM((2,) + start.shape, jnp.int32),
        ],
        compiler_params=pltpu.CompilerParams(vmem_limit_bytes=24 * MIB),
        name="select",
    )(turn, pos, bounds, start, end, own, other)


def product_kernel(
    pos_ref, sums_own, sums_other, plan_ref, *rest, caps, labels, genes, blocks_dev
):
    reach = len(caps)
    n_in = 1 + 2 * reach
    gene_refs = rest[:n_in]
    weights_ref, out_ref, power_ref, rows, total, power = rest[n_in:]
    step = pl.program_id(0)
    steps = pl.num_programs(0)
    snp_rows = sums_own.shape[1]
    depth, width = weights_ref.shape
    block = SNP_BLOCK
    sizes = (genes,) + tuple(caps) + tuple(caps)
    starts = [sum(sizes[:i]) for i in range(n_in)]
    used = sum(sizes)

    @pl.when(step == 0)
    def _():
        total[...] = jnp.zeros_like(total)
        power[...] = jnp.zeros_like(power)

    for ref, start, size in zip(gene_refs, starts, sizes):
        rows[pl.ds(start, size), :] = ref[...]
    for n in range(width // block):
        cols = pl.ds(n * block, block)
        total[pl.ds(0, used), cols] += jnp.dot(
            rows[...], weights_ref[:, cols], preferred_element_type=jnp.float32
        )
    kept = power[...]
    for t in range(depth // LANES):
        x = gene_refs[0][:, pl.ds(t * LANES, LANES)].astype(jnp.float32)
        kept = kept + x * x
    power[...] = kept

    @pl.when(step == steps - 1)
    def _():
        chip, core = pos_ref[0], pos_ref[1]
        share_blocks = blocks_dev // 2
        sums = sums_own[...] + sums_other[...]
        cross = sums[1:2, :]
        inter = sums[2:3, :]
        inv = 1.0 / (inter - cross * (cross / sums[0:1, :]) + 0.1 * inter)

        def peak(col, inv_block):
            v = total[:, pl.ds(col, block)]
            v = v * v * inv_block
            best = v[:, :LANES]
            for t in range(1, block // LANES):
                best = jnp.maximum(best, v[:, t * LANES : (t + 1) * LANES])
            return jnp.max(best.T, axis=0, keepdims=True)

        peaks = []
        for q in range(labels):
            for b in range(blocks_dev):
                peaks.append(
                    peak(q * snp_rows + b * block, inv[:, b * block : (b + 1) * block])
                )
        for b in range(share_blocks):
            mine = inv[:, b * block : (b + 1) * block]
            late = inv[:, (share_blocks + b) * block : (share_blocks + b + 1) * block]
            peaks.append(
                peak(labels * snp_rows + b * block, jnp.where(core == 0, mine, late))
            )
        while len(peaks) % 8:
            peaks.append(jnp.zeros_like(peaks[0]))
        peaks = jnp.concatenate(peaks, axis=0)
        out_ref[...] = jnp.zeros_like(out_ref)
        slot_of = lax.broadcasted_iota(jnp.int32, (total.shape[0], genes), 0)
        for i in range(n_in):
            slot = plan_ref[0, pl.ds(i, 1), :]
            slot = jnp.where(slot >= 0, slot + starts[i], -1)
            low = plan_ref[1, pl.ds(i, 1), :]
            high = plan_ref[2, pl.ds(i, 1), :]
            spread = jnp.dot(
                peaks, (slot_of == slot).astype(jnp.float32),
                precision=lax.Precision.HIGHEST, preferred_element_type=jnp.float32,
            )

            def masked(row, snp_block):
                inside = (snp_block >= low) & (snp_block < high)
                return jnp.where(inside, spread[row : row + 1], 0.0)

            found = []
            for q in range(labels):
                best = jnp.zeros((1, genes), jnp.float32)
                for b in range(blocks_dev):
                    best = jnp.maximum(best, masked(q * blocks_dev + b, chip * blocks_dev + b))
                found.append(best)
            best = jnp.zeros((1, genes), jnp.float32)
            for b in range(share_blocks):
                best = jnp.maximum(
                    best,
                    masked(
                        labels * blocks_dev + b, chip * blocks_dev + core * share_blocks + b
                    ),
                )
            out_rows = [best]
            for c in range(2):
                out_rows += [jnp.where(core == c, v, 0.0) for v in found]
            while len(out_rows) % 8:
                out_rows.append(jnp.zeros_like(best))
            if i == 0:
                target = chip
            else:
                way = core if i <= reach else 1 - core
                target = chip + (2 * way - 1) * ((i - 1) % reach + 1)

            @pl.when((target >= 0) & (target < out_ref.shape[0] // 2))
            def _(out_rows=out_rows, target=target):
                for c in range(2):
                    out_ref[2 * target + c, :, pl.ds(0, genes)] = jnp.concatenate(
                        out_rows, axis=0
                    )

        powers = jnp.sum(power[...].T, axis=0, keepdims=True)
        power_ref[...] = jnp.broadcast_to(powers, power_ref.shape)


def products(pos, sums, plan, full, mine, other, weights, caps, labels, chips, blocks_dev):
    genes, all_samples = full.shape
    width = weights.shape[1]
    snp_rows = sums[0].shape[1]
    depth = CHUNK
    used = genes + 2 * sum(caps)
    padded = -(-used // LANES) * LANES
    out_rows = -(-(1 + 2 * labels) // 8) * 8

    def blocked(x):
        return pl.BlockSpec((x.shape[0], depth), lambda k: (0, k))

    arrays = (full, *mine, *other)
    return pl.pallas_call(
        functools.partial(
            product_kernel, caps=caps, labels=labels, genes=genes, blocks_dev=blocks_dev
        ),
        grid=(all_samples // depth,),
        out_shape=(
            jax.ShapeDtypeStruct((2 * chips, out_rows, LANES), jnp.float32),
            jax.ShapeDtypeStruct((8, genes), jnp.float32),
        ),
        in_specs=[
            pl.BlockSpec(memory_space=pltpu.SMEM),
            pl.BlockSpec((8, snp_rows), lambda k: (0, 0)),
            pl.BlockSpec((8, snp_rows), lambda k: (0, 0)),
            pl.BlockSpec(plan.shape, lambda k: (0, 0, 0)),
            *[blocked(x) for x in arrays],
            pl.BlockSpec((depth, width), lambda k: (k, 0)),
        ],
        out_specs=(
            pl.BlockSpec((2 * chips, out_rows, LANES), lambda k: (0, 0, 0)),
            pl.BlockSpec((8, genes), lambda k: (0, 0)),
        ),
        scratch_shapes=[
            pltpu.VMEM((used, depth), jnp.bfloat16),
            pltpu.VMEM((padded, width), jnp.float32),
            pltpu.VMEM((genes, LANES), jnp.float32),
        ],
        compiler_params=pltpu.CompilerParams(vmem_limit_bytes=48 * MIB),
        cost_estimate=pl.CostEstimate(
            flops=2 * used * all_samples * width,
            bytes_accessed=2 * all_samples * (width + used),
            transcendentals=0,
        ),
        name="products",
    )(pos, *sums, plan, *arrays, weights)


def finish_kernel(gathered_ref, power_ref, out_ref, *, samples):
    best = gathered_ref[0]
    for i in range(1, gathered_ref.shape[0]):
        best = jnp.maximum(best, gathered_ref[i])
    labels, genes = out_ref.shape
    peak = best[:labels, :genes]
    out_ref[...] = jnp.sqrt(peak / (power_ref[0:1, :] / samples + 1e-05))


def shards(genotypes, phenotypes, environment, shuffles, window_start, window_end, chrom_bounds):
    snp_rows, half = genotypes.shape
    genes = phenotypes.shape[0]
    perms = shuffles.shape[0]
    chips = lax.axis_size("genome")
    cores = lax.axis_size("sample")
    genome_pos = lax.axis_index("genome")
    sample_pos = lax.axis_index("sample")
    blocks_dev = snp_rows // SNP_BLOCK
    reach = (HALF_BLK + blocks_dev - 1) // blocks_dev
    all_samples = half * cores
    labels = perms // cores
    caps = tuple(min(genes, genes * 4 >> k) for k in range(1, reach + 1))

    other_pheno = swapped(phenotypes)
    env = environment[None]
    own_sums = local_moments(genotypes, env)
    sums = (own_sums, swapped(own_sums))
    late_geno, _ = lax.optimization_barrier((genotypes, other_pheno))
    other_geno = swapped(late_geno)
    other_env = swapped(env)
    other_shuffles = swapped(shuffles)
    pos = jnp.stack([genome_pos, sample_pos]).astype(jnp.int32)
    start = window_start.reshape(-1, LANES)
    end = window_end.reshape(-1, LANES)

    def chosen(turn):
        return select(
            turn, pos, chrom_bounds, start, end, phenotypes, other_pheno, caps, blocks_dev
        )

    def travel(payloads):
        mine = []
        for k, payload in enumerate(payloads, 1):
            pairs = [(i * cores, (i + k) * cores) for i in range(chips - k)]
            pairs += [((i + k) * cores + 1, i * cores + 1) for i in range(chips - k)]
            mine.append(lax.ppermute(payload, ("genome", "sample"), pairs))
        return mine

    rounds, plan, full, *payloads = chosen(jnp.zeros((1,), jnp.int32))
    mine = travel(payloads)
    weights = snp_side(
        pos[1:], env, other_env, *sums, shuffles, other_shuffles, genotypes, other_geno, labels
    )

    def met(plan, full, mine):
        other = [swapped(x) for x in mine]
        return products(
            pos, sums, plan, full, mine, other, weights, caps, labels, chips, blocks_dev
        )

    *mine, weights = lax.optimization_barrier((*mine, weights))
    found, power = met(plan, full, mine)

    def more(carry):
        return carry[0] < rounds[0]

    def again(carry):
        turn, best = carry
        _, plan, full, *payloads = chosen(jnp.full((1,), turn, jnp.int32))
        return turn + 1, jnp.maximum(best, met(plan, full, travel(payloads))[0])

    _, found = lax.while_loop(more, again, (jnp.int32(1), found))
    gathered = lax.all_to_all(found, ("genome", "sample"), 0, 0, tiled=True)
    return pl.pallas_call(
        functools.partial(finish_kernel, samples=all_samples),
        out_shape=jax.ShapeDtypeStruct((perms + 1, genes), jnp.float32),
        name="finish",
    )(gathered, power)


def solution(mesh):
    placed = (
        P("genome", "sample"),
        P("genome", "sample"),
        P("sample"),
        P(None, "sample"),
        P(),
        P(),
        P(),
    )
    return jax.shard_map(
        shards, mesh=mesh, in_specs=placed, out_specs=P(None, "genome"), check_vma=False
    )
```

```python
import functools

import jax
import jax.numpy as jnp
from jax import lax
from jax.experimental import pallas as pl
from jax.experimental.pallas import tpu as pltpu
from jax.sharding import PartitionSpec as P

SNP_BLOCK = 256
HALF_BLK = 7
LANES = 128
ROWS_STEP = 16
UNROLL = 32
SIDE = 2 * LANES
CHUNK = 1024
MIB = 2**20


def passed_along(x, axis, by):
    count = lax.axis_size(axis)
    pairs = [(i, i + by) for i in range(count) if 0 <= i + by < count]
    return lax.ppermute(x, axis, pairs)


def swapped(x):
    count = lax.axis_size("sample")
    return lax.ppermute(x, "sample", [(i, (i + 1) % count) for i in range(count)])


def moments_kernel(geno_ref, env_ref, out_ref, sums):
    step = pl.program_id(0)
    snp_rows, chunk = geno_ref.shape

    @pl.when(step == 0)
    def _():
        sums[...] = jnp.zeros_like(sums)

    def add_rows(i, carry):
        first = pl.multiple_of(i * ROWS_STEP, ROWS_STEP)
        held = [sums[m, pl.ds(first, ROWS_STEP), :] for m in range(3)]
        for t in range(chunk // LANES):
            x = geno_ref[pl.ds(first, ROWS_STEP), pl.ds(t * LANES, LANES)].astype(jnp.float32)
            e = env_ref[:, pl.ds(t * LANES, LANES)]
            x = x * x
            held[0] = held[0] + x
            x = x * e
            held[1] = held[1] + x
            held[2] = held[2] + x * e
        for m in range(3):
            sums[m, pl.ds(first, ROWS_STEP), :] = held[m]
        return carry

    lax.fori_loop(0, snp_rows // ROWS_STEP, add_rows, 0, unroll=4)

    @pl.when(step == pl.num_programs(0) - 1)
    def _():
        rows = [jnp.sum(sums[m].T, axis=0, keepdims=True) for m in range(3)]
        rows.append(jnp.zeros((out_ref.shape[0] - 3, snp_rows), jnp.float32))
        out_ref[...] = jnp.concatenate(rows, axis=0)


def local_moments(geno, env):
    snp_rows, half = geno.shape
    chunk = CHUNK
    return pl.pallas_call(
        moments_kernel,
        grid=(half // chunk,),
        out_shape=jax.ShapeDtypeStruct((8, snp_rows), jnp.float32),
        in_specs=[
            pl.BlockSpec((snp_rows, chunk), lambda k: (0, k)),
            pl.BlockSpec((1, chunk), lambda k: (0, k)),
        ],
        out_specs=pl.BlockSpec((8, snp_rows), lambda k: (0, 0)),
        scratch_shapes=[pltpu.VMEM((3, snp_rows, LANES), jnp.float32)],
        compiler_params=pltpu.CompilerParams(vmem_limit_bytes=60 * MIB),
        cost_estimate=pl.CostEstimate(
            flops=5 * 10**9, bytes_accessed=2 * snp_rows * half, transcendentals=0
        ),
        name="local_moments",
    )(geno, env)


def turned_kernel(geno_ref, env_ref, sums_own, sums_other, out_ref, slope):
    snp_rows, chunk = geno_ref.shape

    @pl.when(pl.program_id(0) == 0)
    def _():
        sums = sums_own[...] + sums_other[...]
        slope[...] = jnp.broadcast_to(sums[1:2, :] / sums[0:1, :], (LANES, snp_rows)).T

    unit = (
        lax.broadcasted_iota(jnp.int32, (SIDE, SIDE), 0)
        == lax.broadcasted_iota(jnp.int32, (SIDE, SIDE), 1)
    ).astype(jnp.bfloat16)
    for i in range(chunk // SIDE):
        cols = pl.ds(i * SIDE, SIDE)
        e = env_ref[:, cols]
        for j in range(snp_rows // SIDE):
            rows = pl.ds(j * SIDE, SIDE)
            x = geno_ref[rows, cols].astype(jnp.float32)
            r = slope[rows, :]
            a = x * (e - jnp.concatenate([r] * (SIDE // LANES), axis=1))
            t = lax.dot_general(
                unit, a.astype(jnp.bfloat16), (((1,), (1,)), ((), ())),
                preferred_element_type=jnp.float32,
            )
            out_ref[cols, rows] = t.astype(jnp.bfloat16)


def turned(geno, env, sums):
    snp_rows, half = geno.shape
    return pl.pallas_call(
        turned_kernel,
        grid=(half // CHUNK,),
        out_shape=jax.ShapeDtypeStruct((half, snp_rows), jnp.bfloat16),
        in_specs=[
            pl.BlockSpec((snp_rows, CHUNK), lambda k: (0, k)),
            pl.BlockSpec((1, CHUNK), lambda k: (0, k)),
            pl.BlockSpec((8, snp_rows), lambda k: (0, 0)),
            pl.BlockSpec((8, snp_rows), lambda k: (0, 0)),
        ],
        out_specs=pl.BlockSpec((CHUNK, snp_rows), lambda k: (k, 0)),
        scratch_shapes=[pltpu.VMEM((snp_rows, LANES), jnp.float32)],
        compiler_params=pltpu.CompilerParams(vmem_limit_bytes=60 * MIB),
        cost_estimate=pl.CostEstimate(
            flops=5 * 10**9, bytes_accessed=4 * snp_rows * half, transcendentals=0
        ),
        name="turned",
    )(geno, env, *sums)


def permute_kernel(
    core_ref, shuf_own, shuf_other, own_ref, other_ref, out_ref,
    idx, source, rows, dests, stage, idx_sems, in_sems, out_sems, first_sems,
    *, labels,
):
    half, snp_rows = own_ref.shape
    all_samples = 2 * half
    chunks = all_samples // CHUNK
    words = snp_rows // LANES
    slot = words | 1
    share = snp_rows // 2
    core = core_ref[0]

    def load(k):
        ref = own_ref if k * CHUNK < half else other_ref
        return pltpu.make_async_copy(
            ref.at[pl.ds((k * CHUNK) % half, CHUNK)], source.at[k], in_sems.at[k]
        )

    def load_idx(q, h):
        ref = shuf_own if h == 0 else shuf_other
        return pltpu.make_async_copy(
            ref.at[core * labels + q],
            idx.at[pl.ds(q * all_samples + h * half, half)],
            idx_sems.at[2 * q + h],
        )

    def save_first(k):
        there = jnp.where(core == 0, k * CHUNK, (k * CHUNK + half) % all_samples)
        return pltpu.make_async_copy(
            source.at[k, :, pl.ds(pl.multiple_of(core * share, share), share)],
            out_ref.at[
                pl.ds(pl.multiple_of(there, CHUNK), CHUNK), pl.ds(labels * snp_rows, share)
            ],
            first_sems.at[k],
        )

    def save(q, k):
        return pltpu.make_async_copy(
            stage.at[k % 2],
            out_ref.at[pl.ds(k * CHUNK, CHUNK), pl.ds(q * snp_rows, snp_rows)],
            out_sems.at[k % 2],
        )

    for k in range(chunks):
        load(k).start()
    for q in range(labels):
        for h in range(2):
            load_idx(q, h).start()
    for q in range(labels):
        for h in range(2):
            load_idx(q, h).wait()
    for k in range(chunks):
        load(k).wait()
        save_first(k).start()

        def block(b, carry, k=k):
            at = pl.multiple_of(b * SIDE, SIDE)
            for c in range(words):
                x = source[k, pl.ds(at, SIDE), pl.ds(c * LANES, LANES)]
                rows[pl.ds(c, SIDE, stride=slot), :] = x.astype(jnp.float32)

            def group(i, carry):
                low = pl.multiple_of(i * UNROLL, UNROLL)
                first = pl.multiple_of(k * CHUNK + at + low, UNROLL)
                base = pl.multiple_of(low * slot, UNROLL * slot)
                held = [rows[pl.ds(base + u * slot, words), :] for u in range(UNROLL)]
                for q in range(labels):
                    for u in range(UNROLL):
                        to = idx[q * all_samples + first + u] * slot
                        dests[q][pl.ds(to, words), :] = held[u]
                return carry

            lax.fori_loop(0, SIDE // UNROLL, group, 0)
            return carry

        lax.fori_loop(0, CHUNK // SIDE, block, 0)

    for q in range(labels):
        for k in range(chunks):
            if q * chunks + k >= 2:
                save((q * chunks + k - 2) // chunks, (k - 2) % chunks).wait()

            def narrow(i, carry, k=k, q=q):
                at = pl.multiple_of(i * SIDE, SIDE)
                for c in range(words):
                    v = dests[q][pl.ds((k * CHUNK + at) * slot + c, SIDE, stride=slot), :]
                    stage[k % 2, pl.ds(at, SIDE), pl.ds(c * LANES, LANES)] = v.astype(jnp.bfloat16)
                return carry

            lax.fori_loop(0, CHUNK // SIDE, narrow, 0)
            save(q, k).start()
    for k in range(chunks - 2, chunks):
        save(labels - 1, k).wait()
    for k in range(chunks):
        save_first(k).wait()


def permuted(core, shuf_own, shuf_other, own, other, labels):
    half, snp_rows = own.shape
    all_samples = 2 * half
    slot = (snp_rows // LANES) | 1
    width = labels * snp_rows + snp_rows // 2
    any_spec = pl.BlockSpec(memory_space=pl.ANY)
    return pl.pallas_call(
        functools.partial(permute_kernel, labels=labels),
        out_shape=jax.ShapeDtypeStruct((all_samples, width), jnp.bfloat16),
        in_specs=[pl.BlockSpec(memory_space=pltpu.SMEM)] + [any_spec] * 4,
        out_specs=any_spec,
        scratch_shapes=[
            pltpu.SMEM((labels * all_samples,), jnp.int32),
            pltpu.VMEM((all_samples // CHUNK, CHUNK, snp_rows), jnp.bfloat16),
            pltpu.VMEM((SIDE * slot, LANES), jnp.float32),
            [pltpu.VMEM((all_samples * slot, LANES), jnp.float32) for _ in range(labels)],
            pltpu.VMEM((2, CHUNK, snp_rows), jnp.bfloat16),
            pltpu.SemaphoreType.DMA((2 * labels,)),
            pltpu.SemaphoreType.DMA((all_samples // CHUNK,)),
            pltpu.SemaphoreType.DMA((2,)),
            pltpu.SemaphoreType.DMA((all_samples // CHUNK,)),
        ],
        compiler_params=pltpu.CompilerParams(vmem_limit_bytes=61 * MIB),
        cost_estimate=pl.CostEstimate(
            flops=40 * 10**9, bytes_accessed=60 * 10**6, transcendentals=0
        ),
        name="permuted",
    )(core, shuf_own, shuf_other, own, other)


def window_plan(start, end, bounds_ref, n_bounds, total_blocks):
    middle = (start + end - 1) // 2
    lower_edge = jnp.zeros_like(start)
    upper_edge = jnp.full_like(end, total_blocks)
    for i in range(n_bounds):
        edge = bounds_ref[i]
        before = edge <= middle
        lower_edge = jnp.where(before, jnp.maximum(lower_edge, edge), lower_edge)
        upper_edge = jnp.where(before, upper_edge, jnp.minimum(upper_edge, edge))
    return jnp.maximum(start, lower_edge), jnp.minimum(end, upper_edge)


def select_kernel(
    round_ref, pos_ref, bounds_ref, start_ref, end_ref, own_ref, other_ref,
    rounds_ref, plan_ref, full_ref, *rest, caps, blocks_dev,
):
    pay_refs, (slots, edges) = rest[: len(caps)], rest[len(caps) :]
    reach = len(caps)
    genes, half = own_ref.shape
    shape = start_ref.shape
    per_row = LANES // genes
    chips = shape[0] * per_row
    chip, core = pos_ref[0], pos_ref[1]
    turn = round_ref[0]
    low, high = window_plan(
        start_ref[...], end_ref[...], bounds_ref, bounds_ref.shape[0], chips * blocks_dev
    )
    edges[0] = low
    edges[1] = high
    at = lax.broadcasted_iota(jnp.int32, shape, 0) * per_row
    at = at + lax.broadcasted_iota(jnp.int32, shape, 1) // genes
    a = lax.broadcasted_iota(jnp.int32, (LANES, LANES), 0)
    b = lax.broadcasted_iota(jnp.int32, (LANES, LANES), 1)
    upto = ((a <= b) & (a // genes == b // genes)).astype(jnp.float32).astype(jnp.bfloat16)
    rounds = jnp.int32(0)
    for way in range(2):
        for k in range(1, reach + 1):
            to = at + (k if way == 0 else -k)
            need = (
                (low < (to + 1) * blocks_dev) & (high > to * blocks_dev)
                & (low < high) & (to >= 0) & (to < chips)
            )
            rank = jnp.dot(
                need.astype(jnp.float32).astype(jnp.bfloat16), upto,
                preferred_element_type=jnp.float32,
            ).astype(jnp.int32)
            cap = caps[k - 1]
            slot = rank - 1 - turn * cap
            slots[way * reach + k - 1] = jnp.where(
                need & (slot >= 0) & (slot < cap), slot, -1
            )
            rounds = jnp.maximum(rounds, (jnp.max(rank) + cap - 1) // cap)
    rounds_ref[0] = rounds

    def of_chip(ref, index, which):
        row = ref[index, pl.ds(which // per_row, 1), :]
        out = row[:, :genes]
        for part in range(1, per_row):
            out = jnp.where(
                which % per_row == part, row[:, part * genes : (part + 1) * genes], out
            )
        return out

    plan_ref[...] = jnp.zeros_like(plan_ref)
    plan_ref[0, pl.ds(0, 1), :] = lax.broadcasted_iota(jnp.int32, (1, genes), 1)
    plan_ref[1, pl.ds(0, 1), :] = of_chip(edges, 0, chip)
    plan_ref[2, pl.ds(0, 1), :] = of_chip(edges, 1, chip)
    for side in range(2):
        way = core if side == 0 else 1 - core
        for k in range(1, reach + 1):
            source = chip + (2 * way - 1) * k
            valid = (source >= 0) & (source < chips)
            source = jnp.clip(source, 0, chips - 1)
            to = pl.ds(1 + side * reach + k - 1, 1)
            slot = of_chip(slots, way * reach + k - 1, source)
            plan_ref[0, to, :] = jnp.where(valid, slot, -1)
            plan_ref[1, to, :] = of_chip(edges, 0, source)
            plan_ref[2, to, :] = jnp.where(valid, of_chip(edges, 1, source), 0)

    picks = []
    for k in range(1, reach + 1):
        slot = of_chip(slots, core * reach + k - 1, chip)
        rows = lax.broadcasted_iota(jnp.int32, (caps[k - 1], genes), 0)
        picks.append((rows == slot).astype(jnp.float32))
    picks = jnp.concatenate(picks, axis=0).astype(jnp.bfloat16)
    step = 1024

    def copy(i, carry):
        cols = pl.ds(pl.multiple_of(i * step, step), step)
        late = pl.ds(pl.multiple_of(half + i * step, step), step)
        a, b = own_ref[:, cols], other_ref[:, cols]
        first = jnp.where(core == 0, a, b)
        second = jnp.where(core == 0, b, a)
        full_ref[:, cols] = first
        full_ref[:, late] = second
        for part, to in ((first, cols), (second, late)):
            chosen = jnp.dot(picks, part, preferred_element_type=jnp.float32)
            chosen = chosen.astype(jnp.bfloat16)
            row = 0
            for pay in pay_refs:
                pay[:, to] = chosen[row : row + pay.shape[0]]
                row += pay.shape[0]
        return carry

    lax.fori_loop(0, half // step, copy, 0)


def select(turn, pos, bounds, start, end, own, other, caps, blocks_dev):
    genes, half = own.shape
    reach = len(caps)
    smem = pl.BlockSpec(memory_space=pltpu.SMEM)
    vmem = pl.BlockSpec(memory_space=pltpu.VMEM)
    plan_rows = -(-(2 * reach + 1) // 8) * 8
    return pl.pallas_call(
        functools.partial(select_kernel, caps=caps, blocks_dev=blocks_dev),
        out_shape=(
            jax.ShapeDtypeStruct((1,), jnp.int32),
            jax.ShapeDtypeStruct((3, plan_rows, genes), jnp.int32),
            jax.ShapeDtypeStruct((genes, 2 * half), jnp.bfloat16),
            *[jax.ShapeDtypeStruct((cap, 2 * half), jnp.bfloat16) for cap in caps],
        ),
        in_specs=[smem, smem, smem, vmem, vmem, vmem, vmem],
        out_specs=(smem, vmem, vmem, *[vmem for _ in caps]),
        scratch_shapes=[
            pltpu.VMEM((2 * reach,) + start.shape, jnp.int32),
            pltpu.VMEM((2,) + start.shape, jnp.int32),
        ],
        compiler_params=pltpu.CompilerParams(vmem_limit_bytes=24 * MIB),
        name="select",
    )(turn, pos, bounds, start, end, own, other)


def product_kernel(
    pos_ref, sums_own, sums_other, plan_ref, *rest, caps, labels, genes, blocks_dev
):
    reach = len(caps)
    n_in = 1 + 2 * reach
    gene_refs = rest[:n_in]
    weights_ref, out_ref, power_ref, rows, total, power = rest[n_in:]
    step = pl.program_id(0)
    steps = pl.num_programs(0)
    snp_rows = sums_own.shape[1]
    depth, width = weights_ref.shape
    block = SNP_BLOCK
    sizes = (genes,) + tuple(caps) + tuple(caps)
    starts = [sum(sizes[:i]) for i in range(n_in)]
    used = sum(sizes)

    @pl.when(step == 0)
    def _():
        total[...] = jnp.zeros_like(total)
        power[...] = jnp.zeros_like(power)

    for ref, start, size in zip(gene_refs, starts, sizes):
        rows[pl.ds(start, size), :] = ref[...]
    for n in range(width // block):
        cols = pl.ds(n * block, block)
        total[pl.ds(0, used), cols] += jnp.dot(
            rows[...], weights_ref[:, cols], preferred_element_type=jnp.float32
        )
    kept = power[...]
    for t in range(depth // LANES):
        x = gene_refs[0][:, pl.ds(t * LANES, LANES)].astype(jnp.float32)
        kept = kept + x * x
    power[...] = kept

    @pl.when(step == steps - 1)
    def _():
        chip, core = pos_ref[0], pos_ref[1]
        share_blocks = blocks_dev // 2
        sums = sums_own[...] + sums_other[...]
        cross = sums[1:2, :]
        inter = sums[2:3, :]
        inv = 1.0 / (inter - cross * (cross / sums[0:1, :]) + 0.1 * inter)

        def peak(col, inv_block):
            v = total[:, pl.ds(col, block)]
            v = v * v * inv_block
            best = v[:, :LANES]
            for t in range(1, block // LANES):
                best = jnp.maximum(best, v[:, t * LANES : (t + 1) * LANES])
            return jnp.max(best.T, axis=0, keepdims=True)

        peaks = []
        for q in range(labels):
            for b in range(blocks_dev):
                peaks.append(
                    peak(q * snp_rows + b * block, inv[:, b * block : (b + 1) * block])
                )
        for b in range(share_blocks):
            mine = inv[:, b * block : (b + 1) * block]
            late = inv[:, (share_blocks + b) * block : (share_blocks + b + 1) * block]
            peaks.append(
                peak(labels * snp_rows + b * block, jnp.where(core == 0, mine, late))
            )
        while len(peaks) % 8:
            peaks.append(jnp.zeros_like(peaks[0]))
        peaks = jnp.concatenate(peaks, axis=0)
        out_ref[...] = jnp.zeros_like(out_ref)
        slot_of = lax.broadcasted_iota(jnp.int32, (total.shape[0], genes), 0)
        for i in range(n_in):
            slot = plan_ref[0, pl.ds(i, 1), :]
            slot = jnp.where(slot >= 0, slot + starts[i], -1)
            low = plan_ref[1, pl.ds(i, 1), :]
            high = plan_ref[2, pl.ds(i, 1), :]
            spread = jnp.dot(
                peaks, (slot_of == slot).astype(jnp.float32),
                precision=lax.Precision.HIGHEST, preferred_element_type=jnp.float32,
            )

            def masked(row, snp_block):
                inside = (snp_block >= low) & (snp_block < high)
                return jnp.where(inside, spread[row : row + 1], 0.0)

            found = []
            for q in range(labels):
                best = jnp.zeros((1, genes), jnp.float32)
                for b in range(blocks_dev):
                    best = jnp.maximum(best, masked(q * blocks_dev + b, chip * blocks_dev + b))
                found.append(best)
            best = jnp.zeros((1, genes), jnp.float32)
            for b in range(share_blocks):
                best = jnp.maximum(
                    best,
                    masked(
                        labels * blocks_dev + b, chip * blocks_dev + core * share_blocks + b
                    ),
                )
            out_rows = [best]
            for c in range(2):
                out_rows += [jnp.where(core == c, v, 0.0) for v in found]
            while len(out_rows) % 8:
                out_rows.append(jnp.zeros_like(best))
            if i == 0:
                target = chip
            else:
                way = core if i <= reach else 1 - core
                target = chip + (2 * way - 1) * ((i - 1) % reach + 1)

            @pl.when((target >= 0) & (target < out_ref.shape[0] // 2))
            def _(out_rows=out_rows, target=target):
                for c in range(2):
                    out_ref[2 * target + c, :, pl.ds(0, genes)] = jnp.concatenate(
                        out_rows, axis=0
                    )

        powers = jnp.sum(power[...].T, axis=0, keepdims=True)
        power_ref[...] = jnp.broadcast_to(powers, power_ref.shape)


def products(pos, sums, plan, full, mine, other, weights, caps, labels, chips, blocks_dev):
    genes, all_samples = full.shape
    width = weights.shape[1]
    snp_rows = sums[0].shape[1]
    depth = CHUNK
    used = genes + 2 * sum(caps)
    padded = -(-used // LANES) * LANES
    out_rows = -(-(1 + 2 * labels) // 8) * 8

    def blocked(x):
        return pl.BlockSpec((x.shape[0], depth), lambda k: (0, k))

    arrays = (full, *mine, *other)
    return pl.pallas_call(
        functools.partial(
            product_kernel, caps=caps, labels=labels, genes=genes, blocks_dev=blocks_dev
        ),
        grid=(all_samples // depth,),
        out_shape=(
            jax.ShapeDtypeStruct((2 * chips, out_rows, LANES), jnp.float32),
            jax.ShapeDtypeStruct((8, genes), jnp.float32),
        ),
        in_specs=[
            pl.BlockSpec(memory_space=pltpu.SMEM),
            pl.BlockSpec((8, snp_rows), lambda k: (0, 0)),
            pl.BlockSpec((8, snp_rows), lambda k: (0, 0)),
            pl.BlockSpec(plan.shape, lambda k: (0, 0, 0)),
            *[blocked(x) for x in arrays],
            pl.BlockSpec((depth, width), lambda k: (k, 0)),
        ],
        out_specs=(
            pl.BlockSpec((2 * chips, out_rows, LANES), lambda k: (0, 0, 0)),
            pl.BlockSpec((8, genes), lambda k: (0, 0)),
        ),
        scratch_shapes=[
            pltpu.VMEM((used, depth), jnp.bfloat16),
            pltpu.VMEM((padded, width), jnp.float32),
            pltpu.VMEM((genes, LANES), jnp.float32),
        ],
        compiler_params=pltpu.CompilerParams(vmem_limit_bytes=48 * MIB),
        cost_estimate=pl.CostEstimate(
            flops=2 * used * all_samples * width,
            bytes_accessed=2 * all_samples * (width + used),
            transcendentals=0,
        ),
        name="products",
    )(pos, *sums, plan, *arrays, weights)


def finish_kernel(gathered_ref, power_ref, out_ref, *, samples):
    best = gathered_ref[0]
    for i in range(1, gathered_ref.shape[0]):
        best = jnp.maximum(best, gathered_ref[i])
    labels, genes = out_ref.shape
    peak = best[:labels, :genes]
    out_ref[...] = jnp.sqrt(peak / (power_ref[0:1, :] / samples + 1e-05))


def shards(genotypes, phenotypes, environment, shuffles, window_start, window_end, chrom_bounds):
    snp_rows, half = genotypes.shape
    genes = phenotypes.shape[0]
    perms = shuffles.shape[0]
    chips = lax.axis_size("genome")
    cores = lax.axis_size("sample")
    genome_pos = lax.axis_index("genome")
    sample_pos = lax.axis_index("sample")
    blocks_dev = snp_rows // SNP_BLOCK
    reach = (HALF_BLK + blocks_dev - 1) // blocks_dev
    all_samples = half * cores
    labels = perms // cores
    caps = tuple(min(genes, genes * 4 >> k) for k in range(1, reach + 1))

    env = environment[None]
    other_pheno = swapped(phenotypes)
    own_sums = local_moments(genotypes, env)
    sums = (own_sums, swapped(own_sums))
    other_shuffles = swapped(shuffles)
    pos = jnp.stack([genome_pos, sample_pos]).astype(jnp.int32)
    start = window_start.reshape(-1, LANES)
    end = window_end.reshape(-1, LANES)

    def chosen(turn):
        return select(
            turn, pos, chrom_bounds, start, end, phenotypes, other_pheno, caps, blocks_dev
        )

    def travel(payloads):
        mine = []
        for k, payload in enumerate(payloads, 1):
            pairs = [(i * cores, (i + k) * cores) for i in range(chips - k)]
            pairs += [((i + k) * cores + 1, i * cores + 1) for i in range(chips - k)]
            mine.append(lax.ppermute(payload, ("genome", "sample"), pairs))
        return mine

    rounds, plan, full, *payloads = chosen(jnp.zeros((1,), jnp.int32))
    late_env, *payloads = lax.optimization_barrier((env, *payloads))
    own_turned = turned(genotypes, late_env, sums)
    own_turned, *payloads = lax.optimization_barrier((own_turned, *payloads))
    other_turned = swapped(own_turned)
    mine = travel(payloads)
    weights = permuted(pos[1:], shuffles, other_shuffles, own_turned, other_turned, labels)

    def met(plan, full, mine):
        other = [swapped(x) for x in mine]
        return products(
            pos, sums, plan, full, mine, other, weights, caps, labels, chips, blocks_dev
        )

    *mine, weights = lax.optimization_barrier((*mine, weights))
    found, power = met(plan, full, mine)

    def more(carry):
        return carry[0] < rounds[0]

    def again(carry):
        turn, best = carry
        _, plan, full, *payloads = chosen(jnp.full((1,), turn, jnp.int32))
        return turn + 1, jnp.maximum(best, met(plan, full, travel(payloads))[0])

    _, found = lax.while_loop(more, again, (jnp.int32(1), found))
    gathered = lax.all_to_all(found, ("genome", "sample"), 0, 0, tiled=True)
    return pl.pallas_call(
        functools.partial(finish_kernel, samples=all_samples),
        out_shape=jax.ShapeDtypeStruct((perms + 1, genes), jnp.float32),
        name="finish",
    )(gathered, power)


def solution(mesh):
    placed = (
        P("genome", "sample"),
        P("genome", "sample"),
        P("sample"),
        P(None, "sample"),
        P(),
        P(),
        P(),
    )
    return jax.shard_map(
        shards, mesh=mesh, in_specs=placed, out_specs=P(None, "genome"), check_vma=False
    )
```

```python
import functools

import jax
import jax.numpy as jnp
from jax import lax
from jax.experimental import pallas as pl
from jax.experimental.pallas import tpu as pltpu
from jax.sharding import PartitionSpec as P

SNP_BLOCK = 256
HALF_BLK = 7
LANES = 128
ROWS_STEP = 16
UNROLL = 32
SIDE = 2 * LANES
CHUNK = 1024
MIB = 2**20


def passed_along(x, axis, by):
    count = lax.axis_size(axis)
    pairs = [(i, i + by) for i in range(count) if 0 <= i + by < count]
    return lax.ppermute(x, axis, pairs)


def swapped(x):
    count = lax.axis_size("sample")
    return lax.ppermute(x, "sample", [(i, (i + 1) % count) for i in range(count)])


def moments_kernel(geno_ref, env_ref, out_ref, sums):
    step = pl.program_id(0)
    snp_rows, chunk = geno_ref.shape

    @pl.when(step == 0)
    def _():
        sums[...] = jnp.zeros_like(sums)

    def add_rows(i, carry):
        first = pl.multiple_of(i * ROWS_STEP, ROWS_STEP)
        held = [sums[m, pl.ds(first, ROWS_STEP), :] for m in range(3)]
        for t in range(chunk // LANES):
            x = geno_ref[pl.ds(first, ROWS_STEP), pl.ds(t * LANES, LANES)].astype(jnp.float32)
            e = env_ref[:, pl.ds(t * LANES, LANES)]
            x = x * x
            held[0] = held[0] + x
            x = x * e
            held[1] = held[1] + x
            held[2] = held[2] + x * e
        for m in range(3):
            sums[m, pl.ds(first, ROWS_STEP), :] = held[m]
        return carry

    lax.fori_loop(0, snp_rows // ROWS_STEP, add_rows, 0, unroll=4)

    @pl.when(step == pl.num_programs(0) - 1)
    def _():
        rows = [jnp.sum(sums[m].T, axis=0, keepdims=True) for m in range(3)]
        rows.append(jnp.zeros((out_ref.shape[0] - 3, snp_rows), jnp.float32))
        out_ref[...] = jnp.concatenate(rows, axis=0)


def local_moments(geno, env):
    snp_rows, half = geno.shape
    chunk = CHUNK
    return pl.pallas_call(
        moments_kernel,
        grid=(half // chunk,),
        out_shape=jax.ShapeDtypeStruct((8, snp_rows), jnp.float32),
        in_specs=[
            pl.BlockSpec((snp_rows, chunk), lambda k: (0, k)),
            pl.BlockSpec((1, chunk), lambda k: (0, k)),
        ],
        out_specs=pl.BlockSpec((8, snp_rows), lambda k: (0, 0)),
        scratch_shapes=[pltpu.VMEM((3, snp_rows, LANES), jnp.float32)],
        compiler_params=pltpu.CompilerParams(vmem_limit_bytes=60 * MIB),
        cost_estimate=pl.CostEstimate(
            flops=5 * 10**9, bytes_accessed=2 * snp_rows * half, transcendentals=0
        ),
        name="local_moments",
    )(geno, env)


def snp_side_kernel(
    core_ref, env_own, env_other, sums_own, sums_other, shuf_own, shuf_other, own_ref, other_ref,
    out_ref,
    idx, geno, table, dest, stage, first_stage, slope, idx_sems, in_sems, out_sems, first_sems,
    *, labels,
):
    snp_rows, half = own_ref.shape
    all_samples = 2 * half
    chunks = all_samples // CHUNK
    words = snp_rows // LANES
    slot = words
    share = snp_rows // 2
    side = 2 * LANES
    core = core_ref[0]
    depth = geno.shape[0]

    def load(k):
        source = own_ref if k * CHUNK < half else other_ref
        return pltpu.make_async_copy(
            source.at[:, pl.ds((k * CHUNK) % half, CHUNK)], geno.at[k % depth],
            in_sems.at[k % depth],
        )

    def load_idx(q, h):
        source = shuf_own if h == 0 else shuf_other
        return pltpu.make_async_copy(
            source.at[core * labels + q],
            idx.at[pl.ds(q * all_samples + h * half, half)],
            idx_sems.at[2 * q + h],
        )

    def save_first(k):
        there = jnp.where(core == 0, k * CHUNK, (k * CHUNK + half) % all_samples)
        rows = pl.ds(pl.multiple_of(there, CHUNK), CHUNK)
        return pltpu.make_async_copy(
            first_stage.at[k % 2], out_ref.at[rows, pl.ds(labels * snp_rows, share)],
            first_sems.at[k % 2],
        )

    def save(q, k):
        return pltpu.make_async_copy(
            stage.at[k % 2],
            out_ref.at[pl.ds(k * CHUNK, CHUNK), pl.ds(q * snp_rows, snp_rows)],
            out_sems.at[k % 2],
        )

    for k in range(depth):
        load(k).start()
    for q in range(labels):
        for h in range(2):
            load_idx(q, h).start()
    sums = sums_own[...] + sums_other[...]
    slope[...] = jnp.broadcast_to(sums[1:2, :] / sums[0:1, :], (LANES, snp_rows)).T
    unit = (
        lax.broadcasted_iota(jnp.int32, (side, side), 0)
        == lax.broadcasted_iota(jnp.int32, (side, side), 1)
    ).astype(jnp.bfloat16)

    for k in range(chunks):
        load(k).wait()
        if k >= 2:
            save_first(k - 2).wait()
        env_ref = env_own if k * CHUNK < half else env_other

        def turn(i, carry, k=k, env_ref=env_ref):
            at = pl.multiple_of(i * side, side)
            e = env_ref[:, pl.ds((k * CHUNK) % half + at, side)]
            turned = []
            for j in range(snp_rows // side):
                rows = pl.ds(j * side, side)
                x = geno[k % depth, rows, pl.ds(at, side)].astype(jnp.float32)
                r = slope[rows, :]
                a = x * (e - jnp.concatenate([r] * (side // LANES), axis=1))
                t = lax.dot_general(
                    unit, a.astype(jnp.bfloat16), (((1,), (1,)), ((), ())),
                    preferred_element_type=jnp.float32,
                )
                for c in range(side // LANES):
                    word = j * (side // LANES) + c
                    table[pl.ds((k * CHUNK + at) * slot + word, side, stride=slot), :] = (
                        t[:, c * LANES : (c + 1) * LANES]
                    )
                turned.append(t)
            turned = jnp.concatenate(turned, axis=1)
            kept = jnp.where(core == 0, turned[:, :share], turned[:, share:])
            first_stage[k % 2, pl.ds(at, side), :] = kept.astype(jnp.bfloat16)
            return carry

        lax.fori_loop(0, CHUNK // side, turn, 0, unroll=2)
        save_first(k).start()
        if k + depth < chunks:
            load(k + depth).start()

    for q in range(labels):
        for h in range(2):
            load_idx(q, h).wait()

        def scatter(i, carry, q=q):
            first = pl.multiple_of(i * UNROLL, UNROLL)
            base = pl.multiple_of(first * slot, UNROLL * slot)
            held = [table[pl.ds(base + u * slot, words), :] for u in range(UNROLL)]
            for u in range(UNROLL):
                to = pl.multiple_of(idx[q * all_samples + first + u] * slot, slot)
                dest[pl.ds(to, words), :] = held[u]
            return carry

        lax.fori_loop(0, all_samples // UNROLL, scatter, 0)
        for k in range(chunks):
            if q * chunks + k >= 2:
                save((q * chunks + k - 2) // chunks, (k - 2) % chunks).wait()

            def narrow(i, carry, k=k):
                at = pl.multiple_of(i * side, side)
                for c in range(words):
                    v = dest[pl.ds((k * CHUNK + at) * slot + c, side, stride=slot), :]
                    stage[k % 2, pl.ds(at, side), pl.ds(c * LANES, LANES)] = v.astype(jnp.bfloat16)
                return carry

            lax.fori_loop(0, CHUNK // side, narrow, 0)
            save(q, k).start()
    for k in range(chunks - 2, chunks):
        save_first(k).wait()
        save(labels - 1, k).wait()


def snp_side(core, env_own, env_other, sums_own, sums_other, shuf_own, shuf_other, own, other,
             labels):
    snp_rows, half = own.shape
    all_samples = 2 * half
    words = snp_rows // LANES
    width = labels * snp_rows + snp_rows // 2
    any_spec = pl.BlockSpec(memory_space=pl.ANY)
    smem = pl.BlockSpec(memory_space=pltpu.SMEM)
    vmem = pl.BlockSpec(memory_space=pltpu.VMEM)
    return pl.pallas_call(
        functools.partial(snp_side_kernel, labels=labels),
        out_shape=jax.ShapeDtypeStruct((all_samples, width), jnp.bfloat16),
        in_specs=[smem, vmem, vmem, vmem, vmem, any_spec, any_spec, any_spec, any_spec],
        out_specs=any_spec,
        scratch_shapes=[
            pltpu.SMEM((labels * all_samples,), jnp.int32),
            pltpu.VMEM((3, snp_rows, CHUNK), jnp.bfloat16),
            pltpu.VMEM((all_samples * words, LANES), jnp.float32),
            pltpu.VMEM((all_samples * words, LANES), jnp.float32),
            pltpu.VMEM((2, CHUNK, snp_rows), jnp.bfloat16),
            pltpu.VMEM((2, CHUNK, snp_rows // 2), jnp.bfloat16),
            pltpu.VMEM((snp_rows, LANES), jnp.float32),
            pltpu.SemaphoreType.DMA((2 * labels,)),
            pltpu.SemaphoreType.DMA((3,)),
            pltpu.SemaphoreType.DMA((2,)),
            pltpu.SemaphoreType.DMA((2,)),
        ],
        compiler_params=pltpu.CompilerParams(vmem_limit_bytes=61 * MIB),
        cost_estimate=pl.CostEstimate(
            flops=40 * 10**9, bytes_accessed=60 * 10**6, transcendentals=0
        ),
        name="snp_side",
    )(core, env_own, env_other, sums_own, sums_other, shuf_own, shuf_other, own, other)


def window_plan(start, end, bounds_ref, n_bounds, total_blocks):
    middle = (start + end - 1) // 2
    lower_edge = jnp.zeros_like(start)
    upper_edge = jnp.full_like(end, total_blocks)
    for i in range(n_bounds):
        edge = bounds_ref[i]
        before = edge <= middle
        lower_edge = jnp.where(before, jnp.maximum(lower_edge, edge), lower_edge)
        upper_edge = jnp.where(before, upper_edge, jnp.minimum(upper_edge, edge))
    return jnp.maximum(start, lower_edge), jnp.minimum(end, upper_edge)


def select_kernel(
    round_ref, pos_ref, bounds_ref, start_ref, end_ref, own_ref, other_ref,
    rounds_ref, plan_ref, full_ref, *rest, caps, blocks_dev,
):
    reach = len(caps)
    genes, half = own_ref.shape
    chosen_from = sum(cap == genes for cap in caps)
    (slots, edges), pay_refs = rest[-2:], rest[:-2]
    shape = start_ref.shape
    per_row = LANES // genes
    chips = shape[0] * per_row
    chip, core = pos_ref[0], pos_ref[1]
    turn = round_ref[0]
    low, high = window_plan(
        start_ref[...], end_ref[...], bounds_ref, bounds_ref.shape[0], chips * blocks_dev
    )
    edges[0] = low
    edges[1] = high
    at = lax.broadcasted_iota(jnp.int32, shape, 0) * per_row
    at = at + lax.broadcasted_iota(jnp.int32, shape, 1) // genes
    a = lax.broadcasted_iota(jnp.int32, (LANES, LANES), 0)
    b = lax.broadcasted_iota(jnp.int32, (LANES, LANES), 1)
    upto = ((a <= b) & (a // genes == b // genes)).astype(jnp.float32).astype(jnp.bfloat16)
    rounds = jnp.int32(0)
    for way in range(2):
        for k in range(1, reach + 1):
            to = at + (k if way == 0 else -k)
            need = (
                (low < (to + 1) * blocks_dev) & (high > to * blocks_dev)
                & (low < high) & (to >= 0) & (to < chips)
            )
            rank = jnp.dot(
                need.astype(jnp.float32).astype(jnp.bfloat16), upto,
                preferred_element_type=jnp.float32,
            ).astype(jnp.int32)
            cap = caps[k - 1]
            if cap == genes:
                which = lax.broadcasted_iota(jnp.int32, shape, 1) % genes
                slots[way * reach + k - 1] = jnp.where(need, which, -1)
                continue
            slot = rank - 1 - turn * cap
            slots[way * reach + k - 1] = jnp.where(
                need & (slot >= 0) & (slot < cap), slot, -1
            )
            rounds = jnp.maximum(rounds, (jnp.max(rank) + cap - 1) // cap)
    rounds_ref[0] = rounds

    def of_chip(ref, index, which):
        row = ref[index, pl.ds(which // per_row, 1), :]
        out = row[:, :genes]
        for part in range(1, per_row):
            out = jnp.where(
                which % per_row == part, row[:, part * genes : (part + 1) * genes], out
            )
        return out

    used = [lax.broadcasted_iota(jnp.int32, (1, genes), 1)]
    lows = [of_chip(edges, 0, chip)]
    highs = [of_chip(edges, 1, chip)]
    first = genes
    for side in range(2):
        way = core if side == 0 else 1 - core
        for k in range(1, reach + 1):
            source = chip + (2 * way - 1) * k
            valid = (source >= 0) & (source < chips)
            source = jnp.clip(source, 0, chips - 1)
            slot = of_chip(slots, way * reach + k - 1, source)
            used.append(jnp.where(valid & (slot >= 0), slot + first, -1))
            lows.append(of_chip(edges, 0, source))
            highs.append(jnp.where(valid, of_chip(edges, 1, source), 0))
            first += caps[k - 1]
    while len(used) * genes < plan_ref.shape[1]:
        used.append(jnp.full_like(used[0], -1))
        lows.append(jnp.zeros_like(used[0]))
        highs.append(jnp.zeros_like(used[0]))
    plan_ref[...] = jnp.zeros_like(plan_ref)
    for row, parts in enumerate((used, lows, highs)):
        plan_ref[pl.ds(row, 1), :] = jnp.concatenate(parts, axis=1)

    picks = []
    for k in range(chosen_from + 1, reach + 1):
        slot = of_chip(slots, core * reach + k - 1, chip)
        rows = lax.broadcasted_iota(jnp.int32, (caps[k - 1], genes), 0)
        picks.append((rows == slot).astype(jnp.float32))
    if picks:
        picks = jnp.concatenate(picks, axis=0).astype(jnp.bfloat16)
    step = 1024

    def copy(i, carry):
        cols = pl.ds(pl.multiple_of(i * step, step), step)
        late = pl.ds(pl.multiple_of(half + i * step, step), step)
        a, b = own_ref[:, cols], other_ref[:, cols]
        for part, to in ((jnp.where(core == 0, a, b), cols), (jnp.where(core == 0, b, a), late)):
            full_ref[:, to] = part
            if pay_refs:
                chosen = jnp.dot(picks, part, preferred_element_type=jnp.float32)
                chosen = chosen.astype(jnp.bfloat16)
                row = 0
                for pay in pay_refs:
                    pay[:, to] = chosen[row : row + pay.shape[0]]
                    row += pay.shape[0]
        return carry

    lax.fori_loop(0, half // step, copy, 0)


def select(turn, pos, bounds, start, end, own, other, caps, blocks_dev):
    genes, half = own.shape
    all_samples = 2 * half
    reach = len(caps)
    smem = pl.BlockSpec(memory_space=pltpu.SMEM)
    vmem = pl.BlockSpec(memory_space=pltpu.VMEM)
    width = -(-(2 * reach + 1) * genes // LANES) * LANES
    chosen = [cap for cap in caps if cap < genes]
    return pl.pallas_call(
        functools.partial(select_kernel, caps=caps, blocks_dev=blocks_dev),
        out_shape=(
            jax.ShapeDtypeStruct((1,), jnp.int32),
            jax.ShapeDtypeStruct((8, width), jnp.int32),
            jax.ShapeDtypeStruct((genes, all_samples), jnp.bfloat16),
            *[jax.ShapeDtypeStruct((cap, all_samples), jnp.bfloat16) for cap in chosen],
        ),
        in_specs=[smem, smem, smem, vmem, vmem, vmem, vmem],
        out_specs=(smem, vmem, vmem, *[vmem for _ in chosen]),
        scratch_shapes=[
            pltpu.VMEM((2 * reach,) + start.shape, jnp.int32),
            pltpu.VMEM((2,) + start.shape, jnp.int32),
        ],
        compiler_params=pltpu.CompilerParams(vmem_limit_bytes=24 * MIB),
        name="select",
    )(turn, pos, bounds, start, end, own, other)


def product_kernel(
    pos_ref, sums_own, sums_other, plan_ref, *rest, caps, labels, genes, blocks_dev
):
    reach = len(caps)
    n_in = 1 + 2 * reach
    gene_refs = rest[:n_in]
    weights_ref, out_ref, power_ref, rows, total, power, held, sems = rest[n_in:]
    snp_rows = sums_own.shape[1]
    all_samples, width = weights_ref.shape
    block = SNP_BLOCK
    used = rows.shape[0]
    chip, core = pos_ref[0], pos_ref[1]

    def load(k):
        return pltpu.make_async_copy(
            weights_ref.at[pl.ds(k * CHUNK, CHUNK)], held.at[k], sems.at[k]
        )

    for k in range(all_samples // CHUNK):
        load(k).start()
    power[...] = jnp.zeros_like(power)
    total[...] = jnp.zeros_like(total)
    for k in range(all_samples // CHUNK):
        depth = pl.ds(k * CHUNK, CHUNK)
        at = 0
        for ref in gene_refs:
            rows[pl.ds(at, ref.shape[0]), :] = ref[:, depth]
            at += ref.shape[0]
        kept = power[...]
        for t in range(CHUNK // LANES):
            x = rows[pl.ds(0, genes), pl.ds(t * LANES, LANES)].astype(jnp.float32)
            kept = kept + x * x
        power[...] = kept
        load(k).wait()

        def step(n, carry, k=k):
            cols = pl.ds(pl.multiple_of(n * block, block), block)
            total[pl.ds(0, used), cols] += jnp.dot(
                rows[...], held[k, :, cols], preferred_element_type=jnp.float32
            )
            return carry

        lax.fori_loop(0, width // block, step, 0)

    share_blocks = blocks_dev // 2
    sums = sums_own[...] + sums_other[...]
    cross = sums[1:2, :]
    inter = sums[2:3, :]
    inv = 1.0 / (inter - cross * (cross / sums[0:1, :]) + 0.1 * inter)

    def peak(col, inv_block):
        best = None
        for t in range(block // LANES):
            v = total[:, pl.ds(col + t * LANES, LANES)]
            v = v * v * inv_block[:, t * LANES : (t + 1) * LANES]
            best = v if best is None else jnp.maximum(best, v)
        return jnp.max(best.T, axis=0, keepdims=True)

    peaks = []
    for q in range(labels):
        for b in range(blocks_dev):
            peaks.append(peak(q * snp_rows + b * block, inv[:, b * block : (b + 1) * block]))
    for b in range(share_blocks):
        mine = inv[:, b * block : (b + 1) * block]
        late = inv[:, (share_blocks + b) * block : (share_blocks + b + 1) * block]
        peaks.append(peak(labels * snp_rows + b * block, jnp.where(core == 0, mine, late)))
    while len(peaks) % 8:
        peaks.append(jnp.zeros_like(peaks[0]))
    peaks = jnp.concatenate(peaks, axis=0)
    count = peaks.shape[0]
    terms = []
    left = peaks
    for _ in range(3):
        terms.append(left.astype(jnp.bfloat16).astype(jnp.float32))
        left = left - terms[-1]
    terms = jnp.concatenate(terms, axis=0).astype(jnp.bfloat16)
    band = plan_ref.shape[1]
    slot = plan_ref[0:1, :]
    low = plan_ref[1:2, :]
    high = plan_ref[2:3, :]
    place = lax.broadcasted_iota(jnp.int32, (total.shape[0], band), 0) == slot
    spread = jnp.dot(
        terms, place.astype(jnp.float32).astype(jnp.bfloat16),
        preferred_element_type=jnp.float32,
    )
    spread = spread[:count] + spread[count : 2 * count] + spread[2 * count :]

    def masked(row, snp_block):
        inside = (snp_block >= low) & (snp_block < high)
        return jnp.where(inside, spread[row : row + 1], 0.0)

    def highest(row, blocks, first_block):
        best = masked(row, first_block)
        for b in range(1, blocks):
            best = jnp.maximum(best, masked(row + b, first_block + b))
        return best

    out_rows = [highest(labels * blocks_dev, share_blocks, chip * blocks_dev + core * share_blocks)]
    found = [highest(q * blocks_dev, blocks_dev, chip * blocks_dev) for q in range(labels)]
    for c in range(2):
        out_rows += [jnp.where(core == c, v, 0.0) for v in found]
    while len(out_rows) % 8:
        out_rows.append(jnp.zeros_like(out_rows[0]))
    dense = jnp.concatenate(out_rows, axis=0)
    out_ref[...] = jnp.zeros_like(out_ref)
    chips = out_ref.shape[0]
    for i in range(n_in):
        if i == 0:
            target = chip
        else:
            way = core if i <= reach else 1 - core
            target = chip + (2 * way - 1) * ((i - 1) % reach + 1)

        @pl.when((target >= 0) & (target < chips))
        def _(i=i, target=target):
            out_ref[target, :, pl.ds(0, genes)] = dense[:, i * genes : (i + 1) * genes]

    powers = jnp.sum(power[...].T, axis=0, keepdims=True)
    power_ref[...] = jnp.broadcast_to(powers, power_ref.shape)


def products(pos, sums, plan, full, mine, other, weights, caps, labels, chips, blocks_dev):
    genes, all_samples = full.shape
    used = genes + 2 * sum(caps)
    padded = -(-used // LANES) * LANES
    out_rows = -(-(1 + 2 * labels) // 8) * 8
    width = weights.shape[1]
    arrays = (full, *mine, *other)
    vmem = pl.BlockSpec(memory_space=pltpu.VMEM)
    return pl.pallas_call(
        functools.partial(
            product_kernel, caps=caps, labels=labels, genes=genes, blocks_dev=blocks_dev
        ),
        out_shape=(
            jax.ShapeDtypeStruct((chips, out_rows, LANES), jnp.float32),
            jax.ShapeDtypeStruct((8, genes), jnp.float32),
        ),
        in_specs=[
            pl.BlockSpec(memory_space=pltpu.SMEM), vmem, vmem, vmem, *[vmem for _ in arrays],
            pl.BlockSpec(memory_space=pl.ANY),
        ],
        out_specs=(vmem, vmem),
        scratch_shapes=[
            pltpu.VMEM((used, CHUNK), jnp.bfloat16),
            pltpu.VMEM((padded, width), jnp.float32),
            pltpu.VMEM((genes, LANES), jnp.float32),
            pltpu.VMEM((all_samples // CHUNK, CHUNK, width), jnp.bfloat16),
            pltpu.SemaphoreType.DMA((all_samples // CHUNK,)),
        ],
        compiler_params=pltpu.CompilerParams(vmem_limit_bytes=48 * MIB),
        cost_estimate=pl.CostEstimate(
            flops=2 * used * all_samples * width,
            bytes_accessed=2 * all_samples * (width + used),
            transcendentals=0,
        ),
        name="products",
    )(pos, *sums, plan, *arrays, weights)


def finish_kernel(own_ref, other_ref, power_ref, out_ref, *, samples):
    best = jnp.maximum(own_ref[0], other_ref[0])
    for i in range(1, own_ref.shape[0]):
        best = jnp.maximum(best, jnp.maximum(own_ref[i], other_ref[i]))
    labels, genes = out_ref.shape
    peak = best[:labels, :genes]
    out_ref[...] = jnp.sqrt(peak / (power_ref[0:1, :] / samples + 1e-05))


def shards(genotypes, phenotypes, environment, shuffles, window_start, window_end, chrom_bounds):
    snp_rows, half = genotypes.shape
    genes = phenotypes.shape[0]
    perms = shuffles.shape[0]
    chips = lax.axis_size("genome")
    cores = lax.axis_size("sample")
    blocks_dev = snp_rows // SNP_BLOCK
    reach = (HALF_BLK + blocks_dev - 1) // blocks_dev
    all_samples = half * cores
    labels = perms // cores
    caps = tuple(min(genes, genes * 4 >> k) for k in range(1, reach + 1))
    env = environment[None]
    start = window_start.reshape(-1, LANES)
    end = window_end.reshape(-1, LANES)
    pos = jnp.stack([lax.axis_index("genome"), lax.axis_index("sample")]).astype(jnp.int32)

    def travel(k, payload):
        pairs = [(i * cores, (i + k) * cores) for i in range(chips - k)]
        pairs += [((i + k) * cores + 1, i * cores + 1) for i in range(chips - k)]
        return lax.ppermute(payload, ("genome", "sample"), pairs)

    def one_round(turn, pos):
        core = pos[1:]
        other_pheno = swapped(phenotypes)
        own_sums = local_moments(genotypes, env)
        sums = (own_sums, swapped(own_sums))
        late_geno, _ = lax.optimization_barrier((genotypes, other_pheno))
        other_geno = swapped(late_geno)
        other_env = swapped(env)
        other_shuffles = swapped(shuffles)
        rounds, plan, full, *payloads = select(
            turn, pos, chrom_bounds, start, end, phenotypes, other_pheno, caps, blocks_dev
        )
        payloads = [full] * (reach - len(payloads)) + payloads
        mine = [travel(k, x) for k, x in enumerate(payloads, 1)]
        weights = snp_side(
            core, env, other_env, *sums, shuffles, other_shuffles, genotypes, other_geno, labels
        )
        *mine, weights = lax.optimization_barrier((*mine, weights))
        other = [swapped(x) for x in mine]
        found, power = products(
            pos, sums, plan, full, mine, other, weights, caps, labels, chips, blocks_dev
        )
        return rounds, found, power

    rounds, found, power = one_round(jnp.zeros((1,), jnp.int32), pos)

    def more(carry):
        return carry[0] < rounds[0]

    def again(carry):
        turn, best = carry
        turns, place = lax.optimization_barrier((jnp.full((1,), turn, jnp.int32), pos))
        return turn + 1, jnp.maximum(best, one_round(turns, place)[1])

    _, found = lax.while_loop(more, again, (jnp.int32(1), found))
    gathered = lax.all_to_all(found, "genome", 0, 0, tiled=True)
    return pl.pallas_call(
        functools.partial(finish_kernel, samples=all_samples),
        out_shape=jax.ShapeDtypeStruct((perms + 1, genes), jnp.float32),
        name="finish",
    )(gathered, swapped(gathered), power)


def solution(mesh):
    placed = (
        P("genome", "sample"),
        P("genome", "sample"),
        P("sample"),
        P(None, "sample"),
        P(),
        P(),
        P(),
    )
    return jax.shard_map(
        shards, mesh=mesh, in_specs=placed, out_specs=P(None, "genome"), check_vma=False
    )
```

```python
import functools

import jax
import jax.numpy as jnp
from jax import lax
from jax.experimental import pallas as pl
from jax.experimental.pallas import tpu as pltpu
from jax.sharding import PartitionSpec as P

SNP_BLOCK = 256
HALF_BLK = 7
LANES = 128
ROWS_STEP = 16
UNROLL = 32
SIDE = 2 * LANES
CHUNK = 1024
MIB = 2**20


def passed_along(x, axis, by):
    count = lax.axis_size(axis)
    pairs = [(i, i + by) for i in range(count) if 0 <= i + by < count]
    return lax.ppermute(x, axis, pairs)


def swapped(x):
    count = lax.axis_size("sample")
    return lax.ppermute(x, "sample", [(i, (i + 1) % count) for i in range(count)])


def moments_kernel(geno_ref, env_ref, out_ref, sums):
    step = pl.program_id(0)
    snp_rows, chunk = geno_ref.shape

    @pl.when(step == 0)
    def _():
        sums[...] = jnp.zeros_like(sums)

    def add_rows(i, carry):
        first = pl.multiple_of(i * ROWS_STEP, ROWS_STEP)
        held = [sums[m, pl.ds(first, ROWS_STEP), :] for m in range(3)]
        for t in range(chunk // LANES):
            x = geno_ref[pl.ds(first, ROWS_STEP), pl.ds(t * LANES, LANES)].astype(jnp.float32)
            e = env_ref[:, pl.ds(t * LANES, LANES)]
            x = x * x
            held[0] = held[0] + x
            x = x * e
            held[1] = held[1] + x
            held[2] = held[2] + x * e
        for m in range(3):
            sums[m, pl.ds(first, ROWS_STEP), :] = held[m]
        return carry

    lax.fori_loop(0, snp_rows // ROWS_STEP, add_rows, 0, unroll=4)

    @pl.when(step == pl.num_programs(0) - 1)
    def _():
        rows = [jnp.sum(sums[m].T, axis=0, keepdims=True) for m in range(3)]
        rows.append(jnp.zeros((out_ref.shape[0] - 3, snp_rows), jnp.float32))
        out_ref[...] = jnp.concatenate(rows, axis=0)


def local_moments(geno, env):
    snp_rows, half = geno.shape
    chunk = CHUNK
    return pl.pallas_call(
        moments_kernel,
        grid=(half // chunk,),
        out_shape=jax.ShapeDtypeStruct((8, snp_rows), jnp.float32),
        in_specs=[
            pl.BlockSpec((snp_rows, chunk), lambda k: (0, k)),
            pl.BlockSpec((1, chunk), lambda k: (0, k)),
        ],
        out_specs=pl.BlockSpec((8, snp_rows), lambda k: (0, 0)),
        scratch_shapes=[pltpu.VMEM((3, snp_rows, LANES), jnp.float32)],
        compiler_params=pltpu.CompilerParams(vmem_limit_bytes=60 * MIB),
        cost_estimate=pl.CostEstimate(
            flops=10**6, bytes_accessed=10**6, transcendentals=0
        ),
        name="local_moments",
    )(geno, env)


def snp_side_kernel(
    core_ref, env_own, env_other, sums_own, sums_other, shuf_own, shuf_other, own_ref, other_ref,
    out_ref,
    idx, geno, table, dest, stage, first_stage, slope, idx_sems, in_sems, out_sems, first_sems,
    *, labels,
):
    snp_rows, half = own_ref.shape
    all_samples = 2 * half
    chunks = all_samples // CHUNK
    words = snp_rows // LANES
    slot = words
    share = snp_rows // 2
    side = 2 * LANES
    core = core_ref[0]
    depth = geno.shape[0]

    def load(k):
        source = own_ref if k * CHUNK < half else other_ref
        return pltpu.make_async_copy(
            source.at[:, pl.ds((k * CHUNK) % half, CHUNK)], geno.at[k % depth],
            in_sems.at[k % depth],
        )

    def load_idx(q, h):
        source = shuf_own if h == 0 else shuf_other
        return pltpu.make_async_copy(
            source.at[core * labels + q],
            idx.at[pl.ds(q * all_samples + h * half, half)],
            idx_sems.at[2 * q + h],
        )

    def save_first(k):
        there = jnp.where(core == 0, k * CHUNK, (k * CHUNK + half) % all_samples)
        rows = pl.ds(pl.multiple_of(there, CHUNK), CHUNK)
        return pltpu.make_async_copy(
            first_stage.at[k % 2], out_ref.at[rows, pl.ds(labels * snp_rows, share)],
            first_sems.at[k % 2],
        )

    def save(q, k):
        return pltpu.make_async_copy(
            stage.at[k % 2],
            out_ref.at[pl.ds(k * CHUNK, CHUNK), pl.ds(q * snp_rows, snp_rows)],
            out_sems.at[k % 2],
        )

    for k in range(depth):
        load(k).start()
    for q in range(labels):
        for h in range(2):
            load_idx(q, h).start()
    sums = sums_own[...] + sums_other[...]
    slope[...] = jnp.broadcast_to(sums[1:2, :] / sums[0:1, :], (LANES, snp_rows)).T
    unit = (
        lax.broadcasted_iota(jnp.int32, (side, side), 0)
        == lax.broadcasted_iota(jnp.int32, (side, side), 1)
    ).astype(jnp.bfloat16)

    for k in range(chunks):
        load(k).wait()
        if k >= 2:
            save_first(k - 2).wait()
        env_ref = env_own if k * CHUNK < half else env_other

        def turn(i, carry, k=k, env_ref=env_ref):
            at = pl.multiple_of(i * side, side)
            e = env_ref[:, pl.ds((k * CHUNK) % half + at, side)]
            turned = []
            for j in range(snp_rows // side):
                rows = pl.ds(j * side, side)
                x = geno[k % depth, rows, pl.ds(at, side)].astype(jnp.float32)
                r = slope[rows, :]
                a = x * (e - jnp.concatenate([r] * (side // LANES), axis=1))
                t = lax.dot_general(
                    unit, a.astype(jnp.bfloat16), (((1,), (1,)), ((), ())),
                    preferred_element_type=jnp.float32,
                )
                for c in range(side // LANES):
                    word = j * (side // LANES) + c
                    table[pl.ds((k * CHUNK + at) * slot + word, side, stride=slot), :] = (
                        t[:, c * LANES : (c + 1) * LANES]
                    )
                turned.append(t)
            turned = jnp.concatenate(turned, axis=1)
            kept = jnp.where(core == 0, turned[:, :share], turned[:, share:])
            first_stage[k % 2, pl.ds(at, side), :] = kept.astype(jnp.bfloat16)
            return carry

        lax.fori_loop(0, CHUNK // side, turn, 0, unroll=2)
        save_first(k).start()
        if k + depth < chunks:
            load(k + depth).start()

    for q in range(labels):
        for h in range(2):
            load_idx(q, h).wait()

        def scatter(i, carry, q=q):
            first = pl.multiple_of(i * UNROLL, UNROLL)
            base = pl.multiple_of(first * slot, UNROLL * slot)
            held = [table[pl.ds(base + u * slot, words), :] for u in range(UNROLL)]
            for u in range(UNROLL):
                to = pl.multiple_of(idx[q * all_samples + first + u] * slot, slot)
                dest[pl.ds(to, words), :] = held[u]
            return carry

        lax.fori_loop(0, all_samples // UNROLL, scatter, 0)
        for k in range(chunks):
            if q * chunks + k >= 2:
                save((q * chunks + k - 2) // chunks, (k - 2) % chunks).wait()

            def narrow(i, carry, k=k):
                at = pl.multiple_of(i * side, side)
                for c in range(words):
                    v = dest[pl.ds((k * CHUNK + at) * slot + c, side, stride=slot), :]
                    stage[k % 2, pl.ds(at, side), pl.ds(c * LANES, LANES)] = v.astype(jnp.bfloat16)
                return carry

            lax.fori_loop(0, CHUNK // side, narrow, 0)
            save(q, k).start()
    for k in range(chunks - 2, chunks):
        save_first(k).wait()
        save(labels - 1, k).wait()


def snp_side(core, env_own, env_other, sums_own, sums_other, shuf_own, shuf_other, own, other,
             labels):
    snp_rows, half = own.shape
    all_samples = 2 * half
    words = snp_rows // LANES
    width = labels * snp_rows + snp_rows // 2
    any_spec = pl.BlockSpec(memory_space=pl.ANY)
    smem = pl.BlockSpec(memory_space=pltpu.SMEM)
    vmem = pl.BlockSpec(memory_space=pltpu.VMEM)
    return pl.pallas_call(
        functools.partial(snp_side_kernel, labels=labels),
        out_shape=jax.ShapeDtypeStruct((all_samples, width), jnp.bfloat16),
        in_specs=[smem, vmem, vmem, vmem, vmem, any_spec, any_spec, any_spec, any_spec],
        out_specs=any_spec,
        scratch_shapes=[
            pltpu.SMEM((labels * all_samples,), jnp.int32),
            pltpu.VMEM((3, snp_rows, CHUNK), jnp.bfloat16),
            pltpu.VMEM((all_samples * words, LANES), jnp.float32),
            pltpu.VMEM((all_samples * words, LANES), jnp.float32),
            pltpu.VMEM((2, CHUNK, snp_rows), jnp.bfloat16),
            pltpu.VMEM((2, CHUNK, snp_rows // 2), jnp.bfloat16),
            pltpu.VMEM((snp_rows, LANES), jnp.float32),
            pltpu.SemaphoreType.DMA((2 * labels,)),
            pltpu.SemaphoreType.DMA((3,)),
            pltpu.SemaphoreType.DMA((2,)),
            pltpu.SemaphoreType.DMA((2,)),
        ],
        compiler_params=pltpu.CompilerParams(vmem_limit_bytes=61 * MIB),
        cost_estimate=pl.CostEstimate(
            flops=10**6, bytes_accessed=10**6, transcendentals=0
        ),
        name="snp_side",
    )(core, env_own, env_other, sums_own, sums_other, shuf_own, shuf_other, own, other)


def merge_kernel(core_ref, own_ref, other_ref, *rest):
    full_ref, sems = rest[-2:]
    half = own_ref.shape[1]
    core = core_ref[0]
    own = pltpu.make_async_copy(
        own_ref, full_ref.at[:, pl.ds(pl.multiple_of(core * half, half), half)], sems.at[0]
    )
    other = pltpu.make_async_copy(
        other_ref, full_ref.at[:, pl.ds(pl.multiple_of((1 - core) * half, half), half)], sems.at[1]
    )
    own.start()
    other.start()
    own.wait()
    other.wait()


def merged(core, own, other, *after):
    any_spec = pl.BlockSpec(memory_space=pl.ANY)
    return pl.pallas_call(
        merge_kernel,
        out_shape=jax.ShapeDtypeStruct((own.shape[0], 2 * own.shape[1]), own.dtype),
        in_specs=[pl.BlockSpec(memory_space=pltpu.SMEM)] + [any_spec] * (2 + len(after)),
        out_specs=any_spec,
        scratch_shapes=[pltpu.SemaphoreType.DMA((2,))],
        name="merged",
    )(core, own, other, *after)


def window_plan(start, end, bounds_ref, n_bounds, total_blocks):
    middle = (start + end - 1) // 2
    lower_edge = jnp.zeros_like(start)
    upper_edge = jnp.full_like(end, total_blocks)
    for i in range(n_bounds):
        edge = bounds_ref[i]
        before = edge <= middle
        lower_edge = jnp.where(before, jnp.maximum(lower_edge, edge), lower_edge)
        upper_edge = jnp.where(before, upper_edge, jnp.minimum(upper_edge, edge))
    return jnp.maximum(start, lower_edge), jnp.minimum(end, upper_edge)


def select_kernel(
    round_ref, pos_ref, bounds_ref, start_ref, end_ref, full_ref,
    rounds_ref, plan_ref, *rest, caps, blocks_dev,
):
    reach = len(caps)
    genes, all_samples = full_ref.shape
    chosen_from = sum(cap == genes for cap in caps)
    (slots, edges), pay_refs = rest[-2:], rest[:-2]
    shape = start_ref.shape
    per_row = LANES // genes
    chips = shape[0] * per_row
    chip, core = pos_ref[0], pos_ref[1]
    turn = round_ref[0]
    low, high = window_plan(
        start_ref[...], end_ref[...], bounds_ref, bounds_ref.shape[0], chips * blocks_dev
    )
    edges[0] = low
    edges[1] = high
    at = lax.broadcasted_iota(jnp.int32, shape, 0) * per_row
    at = at + lax.broadcasted_iota(jnp.int32, shape, 1) // genes
    a = lax.broadcasted_iota(jnp.int32, (LANES, LANES), 0)
    b = lax.broadcasted_iota(jnp.int32, (LANES, LANES), 1)
    upto = ((a <= b) & (a // genes == b // genes)).astype(jnp.float32).astype(jnp.bfloat16)
    rounds = jnp.int32(0)
    for way in range(2):
        for k in range(1, reach + 1):
            to = at + (k if way == 0 else -k)
            need = (
                (low < (to + 1) * blocks_dev) & (high > to * blocks_dev)
                & (low < high) & (to >= 0) & (to < chips)
            )
            rank = jnp.dot(
                need.astype(jnp.float32).astype(jnp.bfloat16), upto,
                preferred_element_type=jnp.float32,
            ).astype(jnp.int32)
            cap = caps[k - 1]
            if cap == genes:
                which = lax.broadcasted_iota(jnp.int32, shape, 1) % genes
                slots[way * reach + k - 1] = jnp.where(need, which, -1)
                continue
            slot = rank - 1 - turn * cap
            slots[way * reach + k - 1] = jnp.where(
                need & (slot >= 0) & (slot < cap), slot, -1
            )
            rounds = jnp.maximum(rounds, (jnp.max(rank) + cap - 1) // cap)
    rounds_ref[0] = rounds

    def of_chip(ref, index, which):
        row = ref[index, pl.ds(which // per_row, 1), :]
        out = row[:, :genes]
        for part in range(1, per_row):
            out = jnp.where(
                which % per_row == part, row[:, part * genes : (part + 1) * genes], out
            )
        return out

    used = [lax.broadcasted_iota(jnp.int32, (1, genes), 1)]
    lows = [of_chip(edges, 0, chip)]
    highs = [of_chip(edges, 1, chip)]
    first = genes
    for side in range(2):
        way = core if side == 0 else 1 - core
        for k in range(1, reach + 1):
            source = chip + (2 * way - 1) * k
            valid = (source >= 0) & (source < chips)
            source = jnp.clip(source, 0, chips - 1)
            slot = of_chip(slots, way * reach + k - 1, source)
            used.append(jnp.where(valid & (slot >= 0), slot + first, -1))
            lows.append(of_chip(edges, 0, source))
            highs.append(jnp.where(valid, of_chip(edges, 1, source), 0))
            first += caps[k - 1]
    while len(used) * genes < plan_ref.shape[1]:
        used.append(jnp.full_like(used[0], -1))
        lows.append(jnp.zeros_like(used[0]))
        highs.append(jnp.zeros_like(used[0]))
    plan_ref[...] = jnp.zeros_like(plan_ref)
    for row, parts in enumerate((used, lows, highs)):
        plan_ref[pl.ds(row, 1), :] = jnp.concatenate(parts, axis=1)

    picks = []
    for k in range(chosen_from + 1, reach + 1):
        slot = of_chip(slots, core * reach + k - 1, chip)
        rows = lax.broadcasted_iota(jnp.int32, (caps[k - 1], genes), 0)
        picks.append((rows == slot).astype(jnp.float32))
    if picks:
        picks = jnp.concatenate(picks, axis=0).astype(jnp.bfloat16)
        step = 1024

        def copy(i, carry):
            cols = pl.ds(pl.multiple_of(i * step, step), step)
            chosen = jnp.dot(picks, full_ref[:, cols], preferred_element_type=jnp.float32)
            chosen = chosen.astype(jnp.bfloat16)
            row = 0
            for pay in pay_refs:
                pay[:, cols] = chosen[row : row + pay.shape[0]]
                row += pay.shape[0]
            return carry

        lax.fori_loop(0, all_samples // step, copy, 0)


def select(turn, pos, bounds, start, end, full, caps, blocks_dev):
    genes, all_samples = full.shape
    reach = len(caps)
    smem = pl.BlockSpec(memory_space=pltpu.SMEM)
    vmem = pl.BlockSpec(memory_space=pltpu.VMEM)
    width = -(-(2 * reach + 1) * genes // LANES) * LANES
    chosen = [cap for cap in caps if cap < genes]
    return pl.pallas_call(
        functools.partial(select_kernel, caps=caps, blocks_dev=blocks_dev),
        out_shape=(
            jax.ShapeDtypeStruct((1,), jnp.int32),
            jax.ShapeDtypeStruct((8, width), jnp.int32),
            *[jax.ShapeDtypeStruct((cap, all_samples), jnp.bfloat16) for cap in chosen],
        ),
        in_specs=[smem, smem, smem, vmem, vmem, vmem],
        out_specs=(smem, vmem, *[vmem for _ in chosen]),
        scratch_shapes=[
            pltpu.VMEM((2 * reach,) + start.shape, jnp.int32),
            pltpu.VMEM((2,) + start.shape, jnp.int32),
        ],
        compiler_params=pltpu.CompilerParams(vmem_limit_bytes=24 * MIB),
        name="select",
    )(turn, pos, bounds, start, end, full)


def product_kernel(
    pos_ref, sums_own, sums_other, plan_ref, *rest, caps, labels, genes, blocks_dev
):
    reach = len(caps)
    n_in = 1 + 2 * reach
    gene_refs = rest[:n_in]
    weights_ref, out_ref, power_ref, rows, total, power = rest[n_in:]
    step = pl.program_id(0)
    snp_rows = sums_own.shape[1]
    depth, width = weights_ref.shape
    block = SNP_BLOCK
    used = rows.shape[0]
    chip, core = pos_ref[0], pos_ref[1]

    @pl.when(step == 0)
    def _():
        total[...] = jnp.zeros_like(total)
        power[...] = jnp.zeros_like(power)

    at = 0
    for ref in gene_refs:
        rows[pl.ds(at, ref.shape[0]), :] = ref[...]
        at += ref.shape[0]
    for at in range(0, width, snp_rows):
        cols = pl.ds(at, min(snp_rows, width - at))
        total[pl.ds(0, used), cols] += jnp.dot(
            rows[...], weights_ref[:, cols], preferred_element_type=jnp.float32
        )
    kept = power[...]
    for t in range(depth // LANES):
        x = rows[pl.ds(0, genes), pl.ds(t * LANES, LANES)].astype(jnp.float32)
        kept = kept + x * x
    power[...] = kept

    @pl.when(step == pl.num_programs(0) - 1)
    def _():
        summed_up(
            chip, core, sums_own, sums_other, plan_ref, out_ref, power_ref, total, power,
            reach=reach, labels=labels, genes=genes, blocks_dev=blocks_dev,
        )


def summed_up(
    chip, core, sums_own, sums_other, plan_ref, out_ref, power_ref, total, power,
    *, reach, labels, genes, blocks_dev,
):
    snp_rows = sums_own.shape[1]
    block = SNP_BLOCK
    n_in = 1 + 2 * reach
    share_blocks = blocks_dev // 2
    sums = sums_own[...] + sums_other[...]
    cross = sums[1:2, :]
    inter = sums[2:3, :]
    inv = 1.0 / (inter - cross * (cross / sums[0:1, :]) + 0.1 * inter)

    def peak(col, inv_block):
        best = None
        for t in range(block // LANES):
            v = total[:, pl.ds(col + t * LANES, LANES)]
            v = v * v * inv_block[:, t * LANES : (t + 1) * LANES]
            best = v if best is None else jnp.maximum(best, v)
        return jnp.max(best.T, axis=0, keepdims=True)

    peaks = []
    for q in range(labels):
        for b in range(blocks_dev):
            peaks.append(peak(q * snp_rows + b * block, inv[:, b * block : (b + 1) * block]))
    for b in range(share_blocks):
        mine = inv[:, b * block : (b + 1) * block]
        late = inv[:, (share_blocks + b) * block : (share_blocks + b + 1) * block]
        peaks.append(peak(labels * snp_rows + b * block, jnp.where(core == 0, mine, late)))
    while len(peaks) % 8:
        peaks.append(jnp.zeros_like(peaks[0]))
    peaks = jnp.concatenate(peaks, axis=0)
    count = peaks.shape[0]
    terms = []
    left = peaks
    for _ in range(3):
        terms.append(left.astype(jnp.bfloat16).astype(jnp.float32))
        left = left - terms[-1]
    terms = jnp.concatenate(terms, axis=0).astype(jnp.bfloat16)
    band = plan_ref.shape[1]
    slot = plan_ref[0:1, :]
    low = plan_ref[1:2, :]
    high = plan_ref[2:3, :]
    place = lax.broadcasted_iota(jnp.int32, (total.shape[0], band), 0) == slot
    spread = jnp.dot(
        terms, place.astype(jnp.float32).astype(jnp.bfloat16),
        preferred_element_type=jnp.float32,
    )
    spread = spread[:count] + spread[count : 2 * count] + spread[2 * count :]

    def masked(row, snp_block):
        inside = (snp_block >= low) & (snp_block < high)
        return jnp.where(inside, spread[row : row + 1], 0.0)

    def highest(row, blocks, first_block):
        best = masked(row, first_block)
        for b in range(1, blocks):
            best = jnp.maximum(best, masked(row + b, first_block + b))
        return best

    out_rows = [highest(labels * blocks_dev, share_blocks, chip * blocks_dev + core * share_blocks)]
    found = [highest(q * blocks_dev, blocks_dev, chip * blocks_dev) for q in range(labels)]
    for c in range(2):
        out_rows += [jnp.where(core == c, v, 0.0) for v in found]
    while len(out_rows) % 8:
        out_rows.append(jnp.zeros_like(out_rows[0]))
    dense = jnp.concatenate(out_rows, axis=0)
    out_ref[...] = jnp.zeros_like(out_ref)
    chips = out_ref.shape[0]
    for i in range(n_in):
        if i == 0:
            target = chip
        else:
            way = core if i <= reach else 1 - core
            target = chip + (2 * way - 1) * ((i - 1) % reach + 1)

        @pl.when((target >= 0) & (target < chips))
        def _(i=i, target=target):
            out_ref[target, :, pl.ds(0, genes)] = dense[:, i * genes : (i + 1) * genes]

    powers = jnp.sum(power[...].T, axis=0, keepdims=True)
    power_ref[...] = jnp.broadcast_to(powers, power_ref.shape)


def products(pos, sums, plan, full, mine, other, weights, caps, labels, chips, blocks_dev):
    genes, all_samples = full.shape
    used = genes + 2 * sum(caps)
    padded = -(-used // LANES) * LANES
    out_rows = -(-(1 + 2 * labels) // 8) * 8
    width = weights.shape[1]
    arrays = (full, *mine, *other)

    def whole(x):
        return pl.BlockSpec(x.shape, lambda k: (0,) * len(x.shape))

    outs = (
        jax.ShapeDtypeStruct((chips, out_rows, LANES), jnp.float32),
        jax.ShapeDtypeStruct((8, genes), jnp.float32),
    )
    return pl.pallas_call(
        functools.partial(
            product_kernel, caps=caps, labels=labels, genes=genes, blocks_dev=blocks_dev
        ),
        grid=(all_samples // CHUNK,),
        out_shape=outs,
        in_specs=[
            pl.BlockSpec(memory_space=pltpu.SMEM),
            *[whole(x) for x in (*sums, plan)],
            *[pl.BlockSpec((x.shape[0], CHUNK), lambda k: (0, k)) for x in arrays],
            pl.BlockSpec((CHUNK, width), lambda k: (k, 0)),
        ],
        out_specs=tuple(whole(x) for x in outs),
        scratch_shapes=[
            pltpu.VMEM((used, CHUNK), jnp.bfloat16),
            pltpu.VMEM((padded, width), jnp.float32),
            pltpu.VMEM((genes, LANES), jnp.float32),
        ],
        compiler_params=pltpu.CompilerParams(vmem_limit_bytes=48 * MIB),
        cost_estimate=pl.CostEstimate(
            flops=2 * used * all_samples * width,
            bytes_accessed=2 * all_samples * (width + used),
            transcendentals=0,
        ),
        name="products",
    )(pos, *sums, plan, *arrays, weights)


def finish_kernel(own_ref, other_ref, power_ref, out_ref, *, samples):
    best = jnp.maximum(own_ref[0], other_ref[0])
    for i in range(1, own_ref.shape[0]):
        best = jnp.maximum(best, jnp.maximum(own_ref[i], other_ref[i]))
    labels, genes = out_ref.shape
    peak = best[:labels, :genes]
    out_ref[...] = jnp.sqrt(peak / (power_ref[0:1, :] / samples + 1e-05))


def shards(genotypes, phenotypes, environment, shuffles, window_start, window_end, chrom_bounds):
    snp_rows, half = genotypes.shape
    genes = phenotypes.shape[0]
    perms = shuffles.shape[0]
    chips = lax.axis_size("genome")
    cores = lax.axis_size("sample")
    blocks_dev = snp_rows // SNP_BLOCK
    reach = (HALF_BLK + blocks_dev - 1) // blocks_dev
    all_samples = half * cores
    labels = perms // cores
    caps = tuple(min(genes, genes * 4 >> k) for k in range(1, reach + 1))
    env = environment[None]
    start = window_start.reshape(-1, LANES)
    end = window_end.reshape(-1, LANES)
    pos = jnp.stack([lax.axis_index("genome"), lax.axis_index("sample")]).astype(jnp.int32)

    def travel(k, payload):
        pairs = [(i * cores, (i + k) * cores) for i in range(chips - k)]
        pairs += [((i + k) * cores + 1, i * cores + 1) for i in range(chips - k)]
        return lax.ppermute(payload, ("genome", "sample"), pairs)

    def one_round(turn, pos):
        core = pos[1:]
        other_pheno = swapped(phenotypes)
        other_env = swapped(env)
        other_shuffles = swapped(shuffles)
        full = merged(core, phenotypes, other_pheno, other_env, other_shuffles)
        whole = [travel(k, full) for k in range(1, reach + 1) if caps[k - 1] == genes]
        late_geno, late_env, _ = lax.optimization_barrier((genotypes, env, full))
        other_geno = swapped(late_geno)
        own_sums = local_moments(genotypes, late_env)
        late_full, _ = lax.optimization_barrier((full, own_sums))
        sums = (own_sums, swapped(own_sums))
        rounds, plan, *payloads = select(
            turn, pos, chrom_bounds, start, end, late_full, caps, blocks_dev
        )
        mine = whole + [travel(len(whole) + i, x) for i, x in enumerate(payloads, 1)]
        weights = snp_side(
            core, env, other_env, *sums, shuffles, other_shuffles, genotypes, other_geno, labels
        )
        *mine, weights = lax.optimization_barrier((*mine, weights))
        other = [swapped(x) for x in mine]
        found, power = products(
            pos, sums, plan, full, mine, other, weights, caps, labels, chips, blocks_dev
        )
        return rounds, found, power

    rounds, found, power = one_round(jnp.zeros((1,), jnp.int32), pos)

    def more(carry):
        return carry[0] < rounds[0]

    def again(carry):
        turn, best = carry
        turns, place = lax.optimization_barrier((jnp.full((1,), turn, jnp.int32), pos))
        return turn + 1, jnp.maximum(best, one_round(turns, place)[1])

    _, found = lax.while_loop(more, again, (jnp.int32(1), found))
    gathered = lax.all_to_all(found, "genome", 0, 0, tiled=True)
    return pl.pallas_call(
        functools.partial(finish_kernel, samples=all_samples),
        out_shape=jax.ShapeDtypeStruct((perms + 1, genes), jnp.float32),
        name="finish",
    )(gathered, swapped(gathered), power)


def solution(mesh):
    placed = (
        P("genome", "sample"),
        P("genome", "sample"),
        P("sample"),
        P(None, "sample"),
        P(),
        P(),
        P(),
    )
    return jax.shard_map(
        shards, mesh=mesh, in_specs=placed, out_specs=P(None, "genome"), check_vma=False
    )
```

```python
import functools

import jax
import jax.numpy as jnp
from jax import lax
from jax.experimental import pallas as pl
from jax.experimental.pallas import tpu as pltpu
from jax.sharding import PartitionSpec as P

SNP_BLOCK = 256
HALF_BLK = 7
LANES = 128
ROWS_STEP = 16
UNROLL = 32
SIDE = 2 * LANES
CHUNK = 1024
MIB = 2**20


def passed_along(x, axis, by):
    count = lax.axis_size(axis)
    pairs = [(i, i + by) for i in range(count) if 0 <= i + by < count]
    return lax.ppermute(x, axis, pairs)


def swapped(x):
    count = lax.axis_size("sample")
    return lax.ppermute(x, "sample", [(i, (i + 1) % count) for i in range(count)])


def moments_kernel(geno_ref, env_ref, out_ref, sums):
    step = pl.program_id(0)
    snp_rows, chunk = geno_ref.shape

    @pl.when(step == 0)
    def _():
        sums[...] = jnp.zeros_like(sums)

    def add_rows(i, carry):
        first = pl.multiple_of(i * ROWS_STEP, ROWS_STEP)
        held = [sums[m, pl.ds(first, ROWS_STEP), :] for m in range(3)]
        for t in range(chunk // LANES):
            x = geno_ref[pl.ds(first, ROWS_STEP), pl.ds(t * LANES, LANES)].astype(jnp.float32)
            e = env_ref[:, pl.ds(t * LANES, LANES)]
            x = x * x
            held[0] = held[0] + x
            x = x * e
            held[1] = held[1] + x
            held[2] = held[2] + x * e
        for m in range(3):
            sums[m, pl.ds(first, ROWS_STEP), :] = held[m]
        return carry

    lax.fori_loop(0, snp_rows // ROWS_STEP, add_rows, 0, unroll=4)

    @pl.when(step == pl.num_programs(0) - 1)
    def _():
        rows = [jnp.sum(sums[m].T, axis=0, keepdims=True) for m in range(3)]
        rows.append(jnp.zeros((out_ref.shape[0] - 3, snp_rows), jnp.float32))
        out_ref[...] = jnp.concatenate(rows, axis=0)


def local_moments(geno, env):
    snp_rows, half = geno.shape
    chunk = CHUNK
    return pl.pallas_call(
        moments_kernel,
        grid=(half // chunk,),
        out_shape=jax.ShapeDtypeStruct((8, snp_rows), jnp.float32),
        in_specs=[
            pl.BlockSpec((snp_rows, chunk), lambda k: (0, k)),
            pl.BlockSpec((1, chunk), lambda k: (0, k)),
        ],
        out_specs=pl.BlockSpec((8, snp_rows), lambda k: (0, 0)),
        scratch_shapes=[pltpu.VMEM((3, snp_rows, LANES), jnp.float32)],
        compiler_params=pltpu.CompilerParams(vmem_limit_bytes=60 * MIB),
        cost_estimate=pl.CostEstimate(
            flops=5 * 10**9, bytes_accessed=2 * snp_rows * half, transcendentals=0
        ),
        name="local_moments",
    )(geno, env)


def snp_side_kernel(
    core_ref, env_own, env_other, sums_own, sums_other, shuf_own, shuf_other, own_ref, other_ref,
    out_ref,
    idx, geno, table, dests, stage, first_stage, slope, idx_sems, in_sems, out_sems, first_sems,
    *, labels,
):
    snp_rows, half = own_ref.shape
    all_samples = 2 * half
    chunks = all_samples // CHUNK
    words = snp_rows // LANES
    share = snp_rows // 2
    side = SIDE
    per_chunk = CHUNK // side
    core = core_ref[0]
    depth = geno.shape[0]

    def load(k):
        source = own_ref if k * CHUNK < half else other_ref
        return pltpu.make_async_copy(
            source.at[:, pl.ds((k * CHUNK) % half, CHUNK)], geno.at[k % depth],
            in_sems.at[k % depth],
        )

    def load_idx(q, h):
        source = shuf_own if h == 0 else shuf_other
        return pltpu.make_async_copy(
            source.at[core * labels + q],
            idx.at[pl.ds(q * all_samples + h * half, half)],
            idx_sems.at[2 * q + h],
        )

    def save_first(k):
        there = jnp.where(core == 0, k * CHUNK, (k * CHUNK + half) % all_samples)
        rows = pl.ds(pl.multiple_of(there, CHUNK), CHUNK)
        return pltpu.make_async_copy(
            first_stage.at[k % 2, :, pl.ds(pl.multiple_of(core * share, share), share)],
            out_ref.at[rows, pl.ds(labels * snp_rows, share)],
            first_sems.at[k % 2],
        )

    def save(q, k):
        return pltpu.make_async_copy(
            stage.at[k % 2],
            out_ref.at[pl.ds(k * CHUNK, CHUNK), pl.ds(q * snp_rows, snp_rows)],
            out_sems.at[k % 2],
        )

    def read_rows(first):
        base = pl.multiple_of(first * words, UNROLL * words)
        return [table[pl.ds(base + u * words, words), :] for u in range(UNROLL)]

    def write_rows(q, first, held):
        for u in range(UNROLL):
            to = pl.multiple_of(idx[q * all_samples + first + u] * words, words)
            dests[q][pl.ds(to, words), :] = held[u]

    def narrowed(q, at, rows):
        return [
            dests[q][pl.ds(at * words + c, rows, stride=words), :].astype(jnp.bfloat16)
            for c in range(words)
        ]

    for k in range(depth):
        load(k).start()
    for q in range(labels):
        for h in range(2):
            load_idx(q, h).start()
    sums = sums_own[...] + sums_other[...]
    slope[...] = jnp.broadcast_to(sums[1:2, :] / sums[0:1, :], (LANES, snp_rows)).T
    unit = (
        lax.broadcasted_iota(jnp.int32, (side, side), 0)
        == lax.broadcasted_iota(jnp.int32, (side, side), 1)
    ).astype(jnp.bfloat16)
    for q in range(labels):
        for h in range(2):
            load_idx(q, h).wait()

    groups = side // UNROLL // words
    for k in range(chunks):
        load(k).wait()
        if k >= 2:
            save_first(k - 2).wait()
        env_ref = env_own if k * CHUNK < half else env_other

        def turn(i, carry, k=k, env_ref=env_ref):
            at = pl.multiple_of(i * side, side)
            e = env_ref[:, pl.ds((k * CHUNK) % half + at, side)]
            behind = pl.multiple_of(jnp.maximum(k * CHUNK + at - side, 0), side)
            for c in range(words):
                rows = pl.ds(c * LANES, LANES)
                x = geno[k % depth, rows, pl.ds(at, side)].astype(jnp.float32)
                r = slope[rows, :]
                a = x * (e - jnp.concatenate([r] * (side // LANES), axis=1))
                t = lax.dot_general(
                    unit, a.astype(jnp.bfloat16), (((1,), (1,)), ((), ())),
                    preferred_element_type=jnp.float32,
                )
                for g in range(groups):
                    first = pl.multiple_of(behind + (c * groups + g) * UNROLL, UNROLL)
                    write_rows(0, first, read_rows(first))
                table[pl.ds((k * CHUNK + at) * words + c, side, stride=words), :] = t
                first_stage[k % 2, pl.ds(at, side), pl.ds(c * LANES, LANES)] = t.astype(
                    jnp.bfloat16
                )
            return carry

        lax.fori_loop(0, per_chunk, turn, 0)
        save_first(k).start()
        if k + depth < chunks:
            load(k + depth).start()

    def rest(i, carry):
        first = pl.multiple_of(all_samples - side + i * UNROLL, UNROLL)
        write_rows(0, first, read_rows(first))
        return carry

    lax.fori_loop(0, side // UNROLL, rest, 0)

    count = 0
    for q in range(1, labels + 1):
        for k in range(chunks):
            if count >= 2:
                save((count - 2) // chunks, (count - 2) % chunks).wait()

            def step(i, carry, k=k, q=q):
                at = pl.multiple_of(i * UNROLL, UNROLL)
                first = pl.multiple_of(k * CHUNK + at, UNROLL)
                if q < labels:
                    held = read_rows(first)
                parts = narrowed(q - 1, first, UNROLL)
                if q < labels:
                    write_rows(q, first, held)
                for c in range(words):
                    stage[k % 2, pl.ds(at, UNROLL), pl.ds(c * LANES, LANES)] = parts[c]
                return carry

            def wide(i, carry, k=k, q=q):
                at = pl.multiple_of(i * side, side)
                parts = narrowed(q - 1, k * CHUNK + at, side)
                for c in range(words):
                    stage[k % 2, pl.ds(at, side), pl.ds(c * LANES, LANES)] = parts[c]
                return carry

            if q < labels:
                lax.fori_loop(0, CHUNK // UNROLL, step, 0)
            else:
                lax.fori_loop(0, CHUNK // side, wide, 0)
            save(q - 1, k).start()
            count += 1
    for k in range(chunks - 2, chunks):
        save_first(k).wait()
        save(labels - 1, k).wait()


def snp_side(core, env_own, env_other, sums_own, sums_other, shuf_own, shuf_other, own, other,
             labels):
    snp_rows, half = own.shape
    all_samples = 2 * half
    words = snp_rows // LANES
    width = labels * snp_rows + snp_rows // 2
    any_spec = pl.BlockSpec(memory_space=pl.ANY)
    smem = pl.BlockSpec(memory_space=pltpu.SMEM)
    vmem = pl.BlockSpec(memory_space=pltpu.VMEM)
    return pl.pallas_call(
        functools.partial(snp_side_kernel, labels=labels),
        out_shape=jax.ShapeDtypeStruct((all_samples, width), jnp.bfloat16),
        in_specs=[smem, vmem, vmem, vmem, vmem, any_spec, any_spec, any_spec, any_spec],
        out_specs=any_spec,
        scratch_shapes=[
            pltpu.SMEM((labels * all_samples,), jnp.int32),
            pltpu.VMEM((2, snp_rows, CHUNK), jnp.bfloat16),
            pltpu.VMEM((all_samples * words, LANES), jnp.float32),
            [pltpu.VMEM((all_samples * words, LANES), jnp.float32) for _ in range(labels)],
            pltpu.VMEM((2, CHUNK, snp_rows), jnp.bfloat16),
            pltpu.VMEM((2, CHUNK, snp_rows), jnp.bfloat16),
            pltpu.VMEM((snp_rows, LANES), jnp.float32),
            pltpu.SemaphoreType.DMA((2 * labels,)),
            pltpu.SemaphoreType.DMA((2,)),
            pltpu.SemaphoreType.DMA((2,)),
            pltpu.SemaphoreType.DMA((2,)),
        ],
        compiler_params=pltpu.CompilerParams(vmem_limit_bytes=61 * MIB),
        cost_estimate=pl.CostEstimate(
            flops=40 * 10**9, bytes_accessed=60 * 10**6, transcendentals=0
        ),
        name="snp_side",
    )(core, env_own, env_other, sums_own, sums_other, shuf_own, shuf_other, own, other)


def window_plan(start, end, bounds_ref, n_bounds, total_blocks):
    middle = (start + end - 1) // 2
    lower_edge = jnp.zeros_like(start)
    upper_edge = jnp.full_like(end, total_blocks)
    for i in range(n_bounds):
        edge = bounds_ref[i]
        before = edge <= middle
        lower_edge = jnp.where(before, jnp.maximum(lower_edge, edge), lower_edge)
        upper_edge = jnp.where(before, upper_edge, jnp.minimum(upper_edge, edge))
    return jnp.maximum(start, lower_edge), jnp.minimum(end, upper_edge)


def select_kernel(
    round_ref, pos_ref, bounds_ref, start_ref, end_ref, own_ref, other_ref,
    rounds_ref, plan_ref, full_ref, *rest, caps, blocks_dev,
):
    reach = len(caps)
    genes, half = own_ref.shape
    chosen_from = sum(cap == genes for cap in caps)
    (slots, edges), pay_refs = rest[-2:], rest[:-2]
    shape = start_ref.shape
    per_row = LANES // genes
    chips = shape[0] * per_row
    chip, core = pos_ref[0], pos_ref[1]
    turn = round_ref[0]
    low, high = window_plan(
        start_ref[...], end_ref[...], bounds_ref, bounds_ref.shape[0], chips * blocks_dev
    )
    edges[0] = low
    edges[1] = high
    at = lax.broadcasted_iota(jnp.int32, shape, 0) * per_row
    at = at + lax.broadcasted_iota(jnp.int32, shape, 1) // genes
    a = lax.broadcasted_iota(jnp.int32, (LANES, LANES), 0)
    b = lax.broadcasted_iota(jnp.int32, (LANES, LANES), 1)
    upto = ((a <= b) & (a // genes == b // genes)).astype(jnp.float32).astype(jnp.bfloat16)
    rounds = jnp.int32(0)
    for way in range(2):
        for k in range(1, reach + 1):
            to = at + (k if way == 0 else -k)
            need = (
                (low < (to + 1) * blocks_dev) & (high > to * blocks_dev)
                & (low < high) & (to >= 0) & (to < chips)
            )
            rank = jnp.dot(
                need.astype(jnp.float32).astype(jnp.bfloat16), upto,
                preferred_element_type=jnp.float32,
            ).astype(jnp.int32)
            cap = caps[k - 1]
            if cap == genes:
                which = lax.broadcasted_iota(jnp.int32, shape, 1) % genes
                slots[way * reach + k - 1] = jnp.where(need, which, -1)
                continue
            slot = rank - 1 - turn * cap
            slots[way * reach + k - 1] = jnp.where(
                need & (slot >= 0) & (slot < cap), slot, -1
            )
            rounds = jnp.maximum(rounds, (jnp.max(rank) + cap - 1) // cap)
    rounds_ref[0] = rounds

    def of_chip(ref, index, which):
        row = ref[index, pl.ds(which // per_row, 1), :]
        out = row[:, :genes]
        for part in range(1, per_row):
            out = jnp.where(
                which % per_row == part, row[:, part * genes : (part + 1) * genes], out
            )
        return out

    used = [lax.broadcasted_iota(jnp.int32, (1, genes), 1)]
    lows = [of_chip(edges, 0, chip)]
    highs = [of_chip(edges, 1, chip)]
    first = genes
    for side in range(2):
        way = core if side == 0 else 1 - core
        for k in range(1, reach + 1):
            source = chip + (2 * way - 1) * k
            valid = (source >= 0) & (source < chips)
            source = jnp.clip(source, 0, chips - 1)
            slot = of_chip(slots, way * reach + k - 1, source)
            used.append(jnp.where(valid & (slot >= 0), slot + first, -1))
            lows.append(of_chip(edges, 0, source))
            highs.append(jnp.where(valid, of_chip(edges, 1, source), 0))
            first += caps[k - 1]
    while len(used) * genes < plan_ref.shape[1]:
        used.append(jnp.full_like(used[0], -1))
        lows.append(jnp.zeros_like(used[0]))
        highs.append(jnp.zeros_like(used[0]))
    plan_ref[...] = jnp.zeros_like(plan_ref)
    for row, parts in enumerate((used, lows, highs)):
        plan_ref[pl.ds(row, 1), :] = jnp.concatenate(parts, axis=1)

    picks = []
    for k in range(chosen_from + 1, reach + 1):
        slot = of_chip(slots, core * reach + k - 1, chip)
        rows = lax.broadcasted_iota(jnp.int32, (caps[k - 1], genes), 0)
        picks.append((rows == slot).astype(jnp.float32))
    if picks:
        picks = jnp.concatenate(picks, axis=0).astype(jnp.bfloat16)
    step = 1024

    def copy(i, carry):
        cols = pl.ds(pl.multiple_of(i * step, step), step)
        late = pl.ds(pl.multiple_of(half + i * step, step), step)
        a, b = own_ref[:, cols], other_ref[:, cols]
        for part, to in ((jnp.where(core == 0, a, b), cols), (jnp.where(core == 0, b, a), late)):
            full_ref[:, to] = part
            if pay_refs:
                chosen = jnp.dot(picks, part, preferred_element_type=jnp.float32)
                chosen = chosen.astype(jnp.bfloat16)
                row = 0
                for pay in pay_refs:
                    pay[:, to] = chosen[row : row + pay.shape[0]]
                    row += pay.shape[0]
        return carry

    lax.fori_loop(0, half // step, copy, 0)


def select(turn, pos, bounds, start, end, own, other, caps, blocks_dev):
    genes, half = own.shape
    all_samples = 2 * half
    reach = len(caps)
    smem = pl.BlockSpec(memory_space=pltpu.SMEM)
    vmem = pl.BlockSpec(memory_space=pltpu.VMEM)
    width = -(-(2 * reach + 1) * genes // LANES) * LANES
    chosen = [cap for cap in caps if cap < genes]
    return pl.pallas_call(
        functools.partial(select_kernel, caps=caps, blocks_dev=blocks_dev),
        out_shape=(
            jax.ShapeDtypeStruct((1,), jnp.int32),
            jax.ShapeDtypeStruct((8, width), jnp.int32),
            jax.ShapeDtypeStruct((genes, all_samples), jnp.bfloat16),
            *[jax.ShapeDtypeStruct((cap, all_samples), jnp.bfloat16) for cap in chosen],
        ),
        in_specs=[smem, smem, smem, vmem, vmem, vmem, vmem],
        out_specs=(smem, vmem, vmem, *[vmem for _ in chosen]),
        scratch_shapes=[
            pltpu.VMEM((2 * reach,) + start.shape, jnp.int32),
            pltpu.VMEM((2,) + start.shape, jnp.int32),
        ],
        compiler_params=pltpu.CompilerParams(vmem_limit_bytes=24 * MIB),
        name="select",
    )(turn, pos, bounds, start, end, own, other)


def product_kernel(
    pos_ref, sums_own, sums_other, plan_ref, *rest, caps, labels, genes, blocks_dev
):
    reach = len(caps)
    n_in = 1 + 2 * reach
    gene_refs = rest[:n_in]
    weights_ref, out_ref, power_ref, rows, total, power = rest[n_in:]
    step = pl.program_id(0)
    snp_rows = sums_own.shape[1]
    depth, width = weights_ref.shape
    block = SNP_BLOCK
    used = rows.shape[0]
    chip, core = pos_ref[0], pos_ref[1]

    @pl.when(step == 0)
    def _():
        total[...] = jnp.zeros_like(total)
        power[...] = jnp.zeros_like(power)

    at = 0
    for ref in gene_refs:
        rows[pl.ds(at, ref.shape[0]), :] = ref[...]
        at += ref.shape[0]
    for at in range(0, width, snp_rows):
        cols = pl.ds(at, min(snp_rows, width - at))
        total[pl.ds(0, used), cols] += jnp.dot(
            rows[...], weights_ref[:, cols], preferred_element_type=jnp.float32
        )
    kept = power[...]
    for t in range(depth // LANES):
        x = rows[pl.ds(0, genes), pl.ds(t * LANES, LANES)].astype(jnp.float32)
        kept = kept + x * x
    power[...] = kept

    @pl.when(step == pl.num_programs(0) - 1)
    def _():
        summed_up(
            chip, core, sums_own, sums_other, plan_ref, out_ref, power_ref, total, power,
            reach=reach, labels=labels, genes=genes, blocks_dev=blocks_dev,
        )


def summed_up(
    chip, core, sums_own, sums_other, plan_ref, out_ref, power_ref, total, power,
    *, reach, labels, genes, blocks_dev,
):
    snp_rows = sums_own.shape[1]
    block = SNP_BLOCK
    n_in = 1 + 2 * reach
    share_blocks = blocks_dev // 2
    sums = sums_own[...] + sums_other[...]
    cross = sums[1:2, :]
    inter = sums[2:3, :]
    inv = 1.0 / (inter - cross * (cross / sums[0:1, :]) + 0.1 * inter)

    def peak(col, inv_block):
        best = None
        for t in range(block // LANES):
            v = total[:, pl.ds(col + t * LANES, LANES)]
            v = v * v * inv_block[:, t * LANES : (t + 1) * LANES]
            best = v if best is None else jnp.maximum(best, v)
        return jnp.max(best.T, axis=0, keepdims=True)

    peaks = []
    for q in range(labels):
        for b in range(blocks_dev):
            peaks.append(peak(q * snp_rows + b * block, inv[:, b * block : (b + 1) * block]))
    for b in range(share_blocks):
        mine = inv[:, b * block : (b + 1) * block]
        late = inv[:, (share_blocks + b) * block : (share_blocks + b + 1) * block]
        peaks.append(peak(labels * snp_rows + b * block, jnp.where(core == 0, mine, late)))
    while len(peaks) % 8:
        peaks.append(jnp.zeros_like(peaks[0]))
    peaks = jnp.concatenate(peaks, axis=0)
    count = peaks.shape[0]
    terms = []
    left = peaks
    for _ in range(3):
        terms.append(left.astype(jnp.bfloat16).astype(jnp.float32))
        left = left - terms[-1]
    terms = jnp.concatenate(terms, axis=0).astype(jnp.bfloat16)
    band = plan_ref.shape[1]
    slot = plan_ref[0:1, :]
    low = plan_ref[1:2, :]
    high = plan_ref[2:3, :]
    place = lax.broadcasted_iota(jnp.int32, (total.shape[0], band), 0) == slot
    spread = jnp.dot(
        terms, place.astype(jnp.float32).astype(jnp.bfloat16),
        preferred_element_type=jnp.float32,
    )
    spread = spread[:count] + spread[count : 2 * count] + spread[2 * count :]

    def masked(row, snp_block):
        inside = (snp_block >= low) & (snp_block < high)
        return jnp.where(inside, spread[row : row + 1], 0.0)

    def highest(row, blocks, first_block):
        best = masked(row, first_block)
        for b in range(1, blocks):
            best = jnp.maximum(best, masked(row + b, first_block + b))
        return best

    out_rows = [highest(labels * blocks_dev, share_blocks, chip * blocks_dev + core * share_blocks)]
    found = [highest(q * blocks_dev, blocks_dev, chip * blocks_dev) for q in range(labels)]
    for c in range(2):
        out_rows += [jnp.where(core == c, v, 0.0) for v in found]
    while len(out_rows) % 8:
        out_rows.append(jnp.zeros_like(out_rows[0]))
    dense = jnp.concatenate(out_rows, axis=0)
    out_ref[...] = jnp.zeros_like(out_ref)
    chips = out_ref.shape[0]
    for i in range(n_in):
        if i == 0:
            target = chip
        else:
            way = core if i <= reach else 1 - core
            target = chip + (2 * way - 1) * ((i - 1) % reach + 1)

        @pl.when((target >= 0) & (target < chips))
        def _(i=i, target=target):
            out_ref[target, :, pl.ds(0, genes)] = dense[:, i * genes : (i + 1) * genes]

    powers = jnp.sum(power[...].T, axis=0, keepdims=True)
    power_ref[...] = jnp.broadcast_to(powers, power_ref.shape)


def products(pos, sums, plan, full, mine, other, weights, caps, labels, chips, blocks_dev):
    genes, all_samples = full.shape
    used = genes + 2 * sum(caps)
    padded = -(-used // LANES) * LANES
    out_rows = -(-(1 + 2 * labels) // 8) * 8
    width = weights.shape[1]
    arrays = (full, *mine, *other)

    def whole(x):
        return pl.BlockSpec(x.shape, lambda k: (0,) * len(x.shape))

    outs = (
        jax.ShapeDtypeStruct((chips, out_rows, LANES), jnp.float32),
        jax.ShapeDtypeStruct((8, genes), jnp.float32),
    )
    return pl.pallas_call(
        functools.partial(
            product_kernel, caps=caps, labels=labels, genes=genes, blocks_dev=blocks_dev
        ),
        grid=(all_samples // CHUNK,),
        out_shape=outs,
        in_specs=[
            pl.BlockSpec(memory_space=pltpu.SMEM),
            *[whole(x) for x in (*sums, plan)],
            *[pl.BlockSpec((x.shape[0], CHUNK), lambda k: (0, k)) for x in arrays],
            pl.BlockSpec((CHUNK, width), lambda k: (k, 0)),
        ],
        out_specs=tuple(whole(x) for x in outs),
        scratch_shapes=[
            pltpu.VMEM((used, CHUNK), jnp.bfloat16),
            pltpu.VMEM((padded, width), jnp.float32),
            pltpu.VMEM((genes, LANES), jnp.float32),
        ],
        compiler_params=pltpu.CompilerParams(vmem_limit_bytes=48 * MIB),
        cost_estimate=pl.CostEstimate(
            flops=2 * used * all_samples * width,
            bytes_accessed=2 * all_samples * (width + used),
            transcendentals=0,
        ),
        name="products",
    )(pos, *sums, plan, *arrays, weights)


def finish_kernel(own_ref, other_ref, power_ref, out_ref, *, samples):
    best = jnp.maximum(own_ref[0], other_ref[0])
    for i in range(1, own_ref.shape[0]):
        best = jnp.maximum(best, jnp.maximum(own_ref[i], other_ref[i]))
    labels, genes = out_ref.shape
    peak = best[:labels, :genes]
    out_ref[...] = jnp.sqrt(peak / (power_ref[0:1, :] / samples + 1e-05))


def shards(genotypes, phenotypes, environment, shuffles, window_start, window_end, chrom_bounds):
    snp_rows, half = genotypes.shape
    genes = phenotypes.shape[0]
    perms = shuffles.shape[0]
    chips = lax.axis_size("genome")
    cores = lax.axis_size("sample")
    blocks_dev = snp_rows // SNP_BLOCK
    reach = (HALF_BLK + blocks_dev - 1) // blocks_dev
    all_samples = half * cores
    labels = perms // cores
    caps = tuple(min(genes, genes * 4 >> k) for k in range(1, reach + 1))
    env = environment[None]
    start = window_start.reshape(-1, LANES)
    end = window_end.reshape(-1, LANES)
    pos = jnp.stack([lax.axis_index("genome"), lax.axis_index("sample")]).astype(jnp.int32)

    def travel(k, payload):
        pairs = [(i * cores, (i + k) * cores) for i in range(chips - k)]
        pairs += [((i + k) * cores + 1, i * cores + 1) for i in range(chips - k)]
        return lax.ppermute(payload, ("genome", "sample"), pairs)

    def one_round(turn, pos):
        core = pos[1:]
        other_pheno = swapped(phenotypes)
        own_sums = local_moments(genotypes, env)
        sums = (own_sums, swapped(own_sums))
        late_geno, _ = lax.optimization_barrier((genotypes, other_pheno))
        other_geno = swapped(late_geno)
        other_env = swapped(env)
        other_shuffles = swapped(shuffles)
        rounds, plan, full, *payloads = select(
            turn, pos, chrom_bounds, start, end, phenotypes, other_pheno, caps, blocks_dev
        )
        payloads = [full] * (reach - len(payloads)) + payloads
        mine = [travel(k, x) for k, x in enumerate(payloads, 1)]
        weights = snp_side(
            core, env, other_env, *sums, shuffles, other_shuffles, genotypes, other_geno, labels
        )
        *mine, weights = lax.optimization_barrier((*mine, weights))
        other = [swapped(x) for x in mine]
        found, power = products(
            pos, sums, plan, full, mine, other, weights, caps, labels, chips, blocks_dev
        )
        return rounds, found, power

    rounds, found, power = one_round(jnp.zeros((1,), jnp.int32), pos)

    def more(carry):
        return carry[0] < rounds[0]

    def again(carry):
        turn, best = carry
        turns, place = lax.optimization_barrier((jnp.full((1,), turn, jnp.int32), pos))
        return turn + 1, jnp.maximum(best, one_round(turns, place)[1])

    _, found = lax.while_loop(more, again, (jnp.int32(1), found))
    gathered = lax.all_to_all(found, "genome", 0, 0, tiled=True)
    return pl.pallas_call(
        functools.partial(finish_kernel, samples=all_samples),
        out_shape=jax.ShapeDtypeStruct((perms + 1, genes), jnp.float32),
        name="finish",
    )(gathered, swapped(gathered), power)


def solution(mesh):
    placed = (
        P("genome", "sample"),
        P("genome", "sample"),
        P("sample"),
        P(None, "sample"),
        P(),
        P(),
        P(),
    )
    return jax.shard_map(
        shards, mesh=mesh, in_specs=placed, out_specs=P(None, "genome"), check_vma=False
    )
```

```python
import functools

import jax
import jax.numpy as jnp
from jax import lax
from jax.experimental import pallas as pl
from jax.experimental.pallas import tpu as pltpu
from jax.sharding import PartitionSpec as P

SNP_BLOCK = 256
HALF_BLK = 7
LANES = 128
ROWS_STEP = 16
UNROLL = 32
SIDE = 2 * LANES
CHUNK = 1024
MIB = 2**20


def passed_along(x, axis, by):
    count = lax.axis_size(axis)
    pairs = [(i, i + by) for i in range(count) if 0 <= i + by < count]
    return lax.ppermute(x, axis, pairs)


def swapped(x):
    count = lax.axis_size("sample")
    return lax.ppermute(x, "sample", [(i, (i + 1) % count) for i in range(count)])


def moments_kernel(geno_ref, env_ref, out_ref, sums):
    step = pl.program_id(0)
    snp_rows, chunk = geno_ref.shape

    @pl.when(step == 0)
    def _():
        sums[...] = jnp.zeros_like(sums)

    def add_rows(i, carry):
        first = pl.multiple_of(i * ROWS_STEP, ROWS_STEP)
        held = [sums[m, pl.ds(first, ROWS_STEP), :] for m in range(3)]
        for t in range(chunk // LANES):
            x = geno_ref[pl.ds(first, ROWS_STEP), pl.ds(t * LANES, LANES)].astype(jnp.float32)
            e = env_ref[:, pl.ds(t * LANES, LANES)]
            x = x * x
            held[0] = held[0] + x
            x = x * e
            held[1] = held[1] + x
            held[2] = held[2] + x * e
        for m in range(3):
            sums[m, pl.ds(first, ROWS_STEP), :] = held[m]
        return carry

    lax.fori_loop(0, snp_rows // ROWS_STEP, add_rows, 0, unroll=4)

    @pl.when(step == pl.num_programs(0) - 1)
    def _():
        rows = [jnp.sum(sums[m].T, axis=0, keepdims=True) for m in range(3)]
        rows.append(jnp.zeros((out_ref.shape[0] - 3, snp_rows), jnp.float32))
        out_ref[...] = jnp.concatenate(rows, axis=0)


def local_moments(geno, env):
    snp_rows, half = geno.shape
    chunk = CHUNK
    return pl.pallas_call(
        moments_kernel,
        grid=(half // chunk,),
        out_shape=jax.ShapeDtypeStruct((8, snp_rows), jnp.float32),
        in_specs=[
            pl.BlockSpec((snp_rows, chunk), lambda k: (0, k)),
            pl.BlockSpec((1, chunk), lambda k: (0, k)),
        ],
        out_specs=pl.BlockSpec((8, snp_rows), lambda k: (0, 0)),
        scratch_shapes=[pltpu.VMEM((3, snp_rows, LANES), jnp.float32)],
        compiler_params=pltpu.CompilerParams(vmem_limit_bytes=60 * MIB),
        cost_estimate=pl.CostEstimate(
            flops=5 * 10**9, bytes_accessed=2 * snp_rows * half, transcendentals=0
        ),
        name="local_moments",
    )(geno, env)


def snp_side_kernel(
    core_ref, env_own, env_other, sums_own, sums_other, shuf_own, shuf_other, own_ref, other_ref,
    out_ref,
    idx, geno, table, dests, stage, first_stage, slope, idx_sems, in_sems, out_sems, first_sems,
    *, labels,
):
    snp_rows, half = own_ref.shape
    all_samples = 2 * half
    chunks = all_samples // CHUNK
    words = snp_rows // LANES
    share = snp_rows // 2
    side = SIDE
    per_chunk = CHUNK // side
    core = core_ref[0]
    depth = geno.shape[0]

    def load(k):
        source = own_ref if k * CHUNK < half else other_ref
        return pltpu.make_async_copy(
            source.at[:, pl.ds((k * CHUNK) % half, CHUNK)], geno.at[k % depth],
            in_sems.at[k % depth],
        )

    def load_idx(q, h):
        source = shuf_own if h == 0 else shuf_other
        return pltpu.make_async_copy(
            source.at[core * labels + q],
            idx.at[pl.ds(q * all_samples + h * half, half)],
            idx_sems.at[2 * q + h],
        )

    def save_first(k):
        there = jnp.where(core == 0, k * CHUNK, (k * CHUNK + half) % all_samples)
        rows = pl.ds(pl.multiple_of(there, CHUNK), CHUNK)
        return pltpu.make_async_copy(
            first_stage.at[k % 2, :, pl.ds(pl.multiple_of(core * share, share), share)],
            out_ref.at[rows, pl.ds(labels * snp_rows, share)],
            first_sems.at[k % 2],
        )

    def save(q, k):
        return pltpu.make_async_copy(
            stage.at[k % 2],
            out_ref.at[pl.ds(k * CHUNK, CHUNK), pl.ds(q * snp_rows, snp_rows)],
            out_sems.at[k % 2],
        )

    def read_rows(first):
        base = pl.multiple_of(first * words, UNROLL * words)
        return [table[pl.ds(base + u * words, words), :] for u in range(UNROLL)]

    def write_rows(q, first, held):
        for u in range(UNROLL):
            dests[q][idx[q * all_samples + first + u]] = held[u]

    def narrowed(q, at, rows):
        flat = dests[q].reshape(all_samples * words, LANES)
        return [
            flat[pl.ds(at * words + c, rows, stride=words), :].astype(jnp.bfloat16)
            for c in range(words)
        ]

    for k in range(depth):
        load(k).start()
    for q in range(labels):
        for h in range(2):
            load_idx(q, h).start()
    sums = sums_own[...] + sums_other[...]
    slope[...] = jnp.broadcast_to(sums[1:2, :] / sums[0:1, :], (LANES, snp_rows)).T
    unit = (
        lax.broadcasted_iota(jnp.int32, (side, side), 0)
        == lax.broadcasted_iota(jnp.int32, (side, side), 1)
    ).astype(jnp.bfloat16)
    for q in range(labels):
        for h in range(2):
            load_idx(q, h).wait()

    groups = side // UNROLL // words
    for k in range(chunks):
        load(k).wait()
        if k >= 2:
            save_first(k - 2).wait()
        env_ref = env_own if k * CHUNK < half else env_other

        def turn(i, carry, k=k, env_ref=env_ref):
            at = pl.multiple_of(i * side, side)
            e = env_ref[:, pl.ds((k * CHUNK) % half + at, side)]
            behind = pl.multiple_of(jnp.maximum(k * CHUNK + at - side, 0), side)
            for c in range(words):
                rows = pl.ds(c * LANES, LANES)
                x = geno[k % depth, rows, pl.ds(at, side)].astype(jnp.float32)
                r = slope[rows, :]
                a = x * (e - jnp.concatenate([r] * (side // LANES), axis=1))
                t = lax.dot_general(
                    unit, a.astype(jnp.bfloat16), (((1,), (1,)), ((), ())),
                    preferred_element_type=jnp.float32,
                )
                for g in range(groups):
                    first = pl.multiple_of(behind + (c * groups + g) * UNROLL, UNROLL)
                    write_rows(0, first, read_rows(first))
                table[pl.ds((k * CHUNK + at) * words + c, side, stride=words), :] = t
                first_stage[k % 2, pl.ds(at, side), pl.ds(c * LANES, LANES)] = t.astype(
                    jnp.bfloat16
                )
            return carry

        lax.fori_loop(0, per_chunk, turn, 0)
        save_first(k).start()
        if k + depth < chunks:
            load(k + depth).start()

    def rest(i, carry):
        first = pl.multiple_of(all_samples - side + i * UNROLL, UNROLL)
        write_rows(0, first, read_rows(first))
        return carry

    lax.fori_loop(0, side // UNROLL, rest, 0)

    count = 0
    for q in range(1, labels + 1):
        for k in range(chunks):
            if count >= 2:
                save((count - 2) // chunks, (count - 2) % chunks).wait()

            def step(i, carry, k=k, q=q):
                at = pl.multiple_of(i * UNROLL, UNROLL)
                first = pl.multiple_of(k * CHUNK + at, UNROLL)
                if q < labels:
                    held = read_rows(first)
                parts = narrowed(q - 1, first, UNROLL)
                if q < labels:
                    write_rows(q, first, held)
                for c in range(words):
                    stage[k % 2, pl.ds(at, UNROLL), pl.ds(c * LANES, LANES)] = parts[c]
                return carry

            def wide(i, carry, k=k, q=q):
                at = pl.multiple_of(i * side, side)
                parts = narrowed(q - 1, k * CHUNK + at, side)
                for c in range(words):
                    stage[k % 2, pl.ds(at, side), pl.ds(c * LANES, LANES)] = parts[c]
                return carry

            if q < labels:
                lax.fori_loop(0, CHUNK // UNROLL, step, 0)
            else:
                lax.fori_loop(0, CHUNK // side, wide, 0)
            save(q - 1, k).start()
            count += 1
    for k in range(chunks - 2, chunks):
        save_first(k).wait()
        save(labels - 1, k).wait()


def snp_side(core, env_own, env_other, sums_own, sums_other, shuf_own, shuf_other, own, other,
             labels):
    snp_rows, half = own.shape
    all_samples = 2 * half
    words = snp_rows // LANES
    width = labels * snp_rows + snp_rows // 2
    any_spec = pl.BlockSpec(memory_space=pl.ANY)
    smem = pl.BlockSpec(memory_space=pltpu.SMEM)
    vmem = pl.BlockSpec(memory_space=pltpu.VMEM)
    return pl.pallas_call(
        functools.partial(snp_side_kernel, labels=labels),
        out_shape=jax.ShapeDtypeStruct((all_samples, width), jnp.bfloat16),
        in_specs=[smem, vmem, vmem, vmem, vmem, any_spec, any_spec, any_spec, any_spec],
        out_specs=any_spec,
        scratch_shapes=[
            pltpu.SMEM((labels * all_samples,), jnp.int32),
            pltpu.VMEM((2, snp_rows, CHUNK), jnp.bfloat16),
            pltpu.VMEM((all_samples * words, LANES), jnp.float32),
            [pltpu.VMEM((all_samples, words, LANES), jnp.float32) for _ in range(labels)],
            pltpu.VMEM((2, CHUNK, snp_rows), jnp.bfloat16),
            pltpu.VMEM((2, CHUNK, snp_rows), jnp.bfloat16),
            pltpu.VMEM((snp_rows, LANES), jnp.float32),
            pltpu.SemaphoreType.DMA((2 * labels,)),
            pltpu.SemaphoreType.DMA((2,)),
            pltpu.SemaphoreType.DMA((2,)),
            pltpu.SemaphoreType.DMA((2,)),
        ],
        compiler_params=pltpu.CompilerParams(vmem_limit_bytes=61 * MIB),
        cost_estimate=pl.CostEstimate(
            flops=40 * 10**9, bytes_accessed=60 * 10**6, transcendentals=0
        ),
        name="snp_side",
    )(core, env_own, env_other, sums_own, sums_other, shuf_own, shuf_other, own, other)


def window_plan(start, end, bounds_ref, n_bounds, total_blocks):
    middle = (start + end - 1) // 2
    lower_edge = jnp.zeros_like(start)
    upper_edge = jnp.full_like(end, total_blocks)
    for i in range(n_bounds):
        edge = bounds_ref[i]
        before = edge <= middle
        lower_edge = jnp.where(before, jnp.maximum(lower_edge, edge), lower_edge)
        upper_edge = jnp.where(before, upper_edge, jnp.minimum(upper_edge, edge))
    return jnp.maximum(start, lower_edge), jnp.minimum(end, upper_edge)


def select_kernel(
    round_ref, pos_ref, bounds_ref, start_ref, end_ref, own_ref, other_ref,
    rounds_ref, plan_ref, full_ref, *rest, caps, blocks_dev,
):
    reach = len(caps)
    genes, half = own_ref.shape
    chosen_from = sum(cap == genes for cap in caps)
    (slots, edges), pay_refs = rest[-2:], rest[:-2]
    shape = start_ref.shape
    per_row = LANES // genes
    chips = shape[0] * per_row
    chip, core = pos_ref[0], pos_ref[1]
    turn = round_ref[0]
    low, high = window_plan(
        start_ref[...], end_ref[...], bounds_ref, bounds_ref.shape[0], chips * blocks_dev
    )
    edges[0] = low
    edges[1] = high
    at = lax.broadcasted_iota(jnp.int32, shape, 0) * per_row
    at = at + lax.broadcasted_iota(jnp.int32, shape, 1) // genes
    a = lax.broadcasted_iota(jnp.int32, (LANES, LANES), 0)
    b = lax.broadcasted_iota(jnp.int32, (LANES, LANES), 1)
    upto = ((a <= b) & (a // genes == b // genes)).astype(jnp.float32).astype(jnp.bfloat16)
    rounds = jnp.int32(0)
    for way in range(2):
        for k in range(1, reach + 1):
            to = at + (k if way == 0 else -k)
            need = (
                (low < (to + 1) * blocks_dev) & (high > to * blocks_dev)
                & (low < high) & (to >= 0) & (to < chips)
            )
            rank = jnp.dot(
                need.astype(jnp.float32).astype(jnp.bfloat16), upto,
                preferred_element_type=jnp.float32,
            ).astype(jnp.int32)
            cap = caps[k - 1]
            if cap == genes:
                which = lax.broadcasted_iota(jnp.int32, shape, 1) % genes
                slots[way * reach + k - 1] = jnp.where(need, which, -1)
                continue
            slot = rank - 1 - turn * cap
            slots[way * reach + k - 1] = jnp.where(
                need & (slot >= 0) & (slot < cap), slot, -1
            )
            rounds = jnp.maximum(rounds, (jnp.max(rank) + cap - 1) // cap)
    rounds_ref[0] = rounds

    def of_chip(ref, index, which):
        row = ref[index, pl.ds(which // per_row, 1), :]
        out = row[:, :genes]
        for part in range(1, per_row):
            out = jnp.where(
                which % per_row == part, row[:, part * genes : (part + 1) * genes], out
            )
        return out

    used = [lax.broadcasted_iota(jnp.int32, (1, genes), 1)]
    lows = [of_chip(edges, 0, chip)]
    highs = [of_chip(edges, 1, chip)]
    first = genes
    for side in range(2):
        way = core if side == 0 else 1 - core
        for k in range(1, reach + 1):
            source = chip + (2 * way - 1) * k
            valid = (source >= 0) & (source < chips)
            source = jnp.clip(source, 0, chips - 1)
            slot = of_chip(slots, way * reach + k - 1, source)
            used.append(jnp.where(valid & (slot >= 0), slot + first, -1))
            lows.append(of_chip(edges, 0, source))
            highs.append(jnp.where(valid, of_chip(edges, 1, source), 0))
            first += caps[k - 1]
    while len(used) * genes < plan_ref.shape[1]:
        used.append(jnp.full_like(used[0], -1))
        lows.append(jnp.zeros_like(used[0]))
        highs.append(jnp.zeros_like(used[0]))
    plan_ref[...] = jnp.zeros_like(plan_ref)
    for row, parts in enumerate((used, lows, highs)):
        plan_ref[pl.ds(row, 1), :] = jnp.concatenate(parts, axis=1)

    picks = []
    for k in range(chosen_from + 1, reach + 1):
        slot = of_chip(slots, core * reach + k - 1, chip)
        rows = lax.broadcasted_iota(jnp.int32, (caps[k - 1], genes), 0)
        picks.append((rows == slot).astype(jnp.float32))
    if picks:
        picks = jnp.concatenate(picks, axis=0).astype(jnp.bfloat16)
    step = 1024

    def copy(i, carry):
        cols = pl.ds(pl.multiple_of(i * step, step), step)
        late = pl.ds(pl.multiple_of(half + i * step, step), step)
        a, b = own_ref[:, cols], other_ref[:, cols]
        for part, to in ((jnp.where(core == 0, a, b), cols), (jnp.where(core == 0, b, a), late)):
            full_ref[:, to] = part
            if pay_refs:
                chosen = jnp.dot(picks, part, preferred_element_type=jnp.float32)
                chosen = chosen.astype(jnp.bfloat16)
                row = 0
                for pay in pay_refs:
                    pay[:, to] = chosen[row : row + pay.shape[0]]
                    row += pay.shape[0]
        return carry

    lax.fori_loop(0, half // step, copy, 0)


def select(turn, pos, bounds, start, end, own, other, caps, blocks_dev):
    genes, half = own.shape
    all_samples = 2 * half
    reach = len(caps)
    smem = pl.BlockSpec(memory_space=pltpu.SMEM)
    vmem = pl.BlockSpec(memory_space=pltpu.VMEM)
    width = -(-(2 * reach + 1) * genes // LANES) * LANES
    chosen = [cap for cap in caps if cap < genes]
    return pl.pallas_call(
        functools.partial(select_kernel, caps=caps, blocks_dev=blocks_dev),
        out_shape=(
            jax.ShapeDtypeStruct((1,), jnp.int32),
            jax.ShapeDtypeStruct((8, width), jnp.int32),
            jax.ShapeDtypeStruct((genes, all_samples), jnp.bfloat16),
            *[jax.ShapeDtypeStruct((cap, all_samples), jnp.bfloat16) for cap in chosen],
        ),
        in_specs=[smem, smem, smem, vmem, vmem, vmem, vmem],
        out_specs=(smem, vmem, vmem, *[vmem for _ in chosen]),
        scratch_shapes=[
            pltpu.VMEM((2 * reach,) + start.shape, jnp.int32),
            pltpu.VMEM((2,) + start.shape, jnp.int32),
        ],
        compiler_params=pltpu.CompilerParams(vmem_limit_bytes=24 * MIB),
        name="select",
    )(turn, pos, bounds, start, end, own, other)


def product_kernel(
    pos_ref, sums_own, sums_other, plan_ref, *rest, caps, labels, genes, blocks_dev
):
    reach = len(caps)
    n_in = 1 + 2 * reach
    gene_refs = rest[:n_in]
    weights_ref, out_ref, power_ref, rows, total, power = rest[n_in:]
    step = pl.program_id(0)
    snp_rows = sums_own.shape[1]
    depth, width = weights_ref.shape
    block = SNP_BLOCK
    used = rows.shape[0]
    chip, core = pos_ref[0], pos_ref[1]

    @pl.when(step == 0)
    def _():
        total[...] = jnp.zeros_like(total)
        power[...] = jnp.zeros_like(power)

    at = 0
    for ref in gene_refs:
        rows[pl.ds(at, ref.shape[0]), :] = ref[...]
        at += ref.shape[0]
    for at in range(0, width, snp_rows):
        cols = pl.ds(at, min(snp_rows, width - at))
        total[pl.ds(0, used), cols] += jnp.dot(
            rows[...], weights_ref[:, cols], preferred_element_type=jnp.float32
        )
    kept = power[...]
    for t in range(depth // LANES):
        x = rows[pl.ds(0, genes), pl.ds(t * LANES, LANES)].astype(jnp.float32)
        kept = kept + x * x
    power[...] = kept

    @pl.when(step == pl.num_programs(0) - 1)
    def _():
        summed_up(
            chip, core, sums_own, sums_other, plan_ref, out_ref, power_ref, total, power,
            reach=reach, labels=labels, genes=genes, blocks_dev=blocks_dev,
        )


def summed_up(
    chip, core, sums_own, sums_other, plan_ref, out_ref, power_ref, total, power,
    *, reach, labels, genes, blocks_dev,
):
    snp_rows = sums_own.shape[1]
    block = SNP_BLOCK
    n_in = 1 + 2 * reach
    share_blocks = blocks_dev // 2
    sums = sums_own[...] + sums_other[...]
    cross = sums[1:2, :]
    inter = sums[2:3, :]
    inv = 1.0 / (inter - cross * (cross / sums[0:1, :]) + 0.1 * inter)

    def peak(col, inv_block):
        best = None
        for t in range(block // LANES):
            v = total[:, pl.ds(col + t * LANES, LANES)]
            v = v * v * inv_block[:, t * LANES : (t + 1) * LANES]
            best = v if best is None else jnp.maximum(best, v)
        return jnp.max(best.T, axis=0, keepdims=True)

    peaks = []
    for q in range(labels):
        for b in range(blocks_dev):
            peaks.append(peak(q * snp_rows + b * block, inv[:, b * block : (b + 1) * block]))
    for b in range(share_blocks):
        mine = inv[:, b * block : (b + 1) * block]
        late = inv[:, (share_blocks + b) * block : (share_blocks + b + 1) * block]
        peaks.append(peak(labels * snp_rows + b * block, jnp.where(core == 0, mine, late)))
    while len(peaks) % 8:
        peaks.append(jnp.zeros_like(peaks[0]))
    peaks = jnp.concatenate(peaks, axis=0)
    count = peaks.shape[0]
    terms = []
    left = peaks
    for _ in range(3):
        terms.append(left.astype(jnp.bfloat16).astype(jnp.float32))
        left = left - terms[-1]
    terms = jnp.concatenate(terms, axis=0).astype(jnp.bfloat16)
    band = plan_ref.shape[1]
    slot = plan_ref[0:1, :]
    low = plan_ref[1:2, :]
    high = plan_ref[2:3, :]
    place = lax.broadcasted_iota(jnp.int32, (total.shape[0], band), 0) == slot
    spread = jnp.dot(
        terms, place.astype(jnp.float32).astype(jnp.bfloat16),
        preferred_element_type=jnp.float32,
    )
    spread = spread[:count] + spread[count : 2 * count] + spread[2 * count :]

    def masked(row, snp_block):
        inside = (snp_block >= low) & (snp_block < high)
        return jnp.where(inside, spread[row : row + 1], 0.0)

    def highest(row, blocks, first_block):
        best = masked(row, first_block)
        for b in range(1, blocks):
            best = jnp.maximum(best, masked(row + b, first_block + b))
        return best

    out_rows = [highest(labels * blocks_dev, share_blocks, chip * blocks_dev + core * share_blocks)]
    found = [highest(q * blocks_dev, blocks_dev, chip * blocks_dev) for q in range(labels)]
    for c in range(2):
        out_rows += [jnp.where(core == c, v, 0.0) for v in found]
    while len(out_rows) % 8:
        out_rows.append(jnp.zeros_like(out_rows[0]))
    dense = jnp.concatenate(out_rows, axis=0)
    out_ref[...] = jnp.zeros_like(out_ref)
    chips = out_ref.shape[0]
    for i in range(n_in):
        if i == 0:
            target = chip
        else:
            way = core if i <= reach else 1 - core
            target = chip + (2 * way - 1) * ((i - 1) % reach + 1)

        @pl.when((target >= 0) & (target < chips))
        def _(i=i, target=target):
            out_ref[target, :, pl.ds(0, genes)] = dense[:, i * genes : (i + 1) * genes]

    powers = jnp.sum(power[...].T, axis=0, keepdims=True)
    power_ref[...] = jnp.broadcast_to(powers, power_ref.shape)


def products(pos, sums, plan, full, mine, other, weights, caps, labels, chips, blocks_dev):
    genes, all_samples = full.shape
    used = genes + 2 * sum(caps)
    padded = -(-used // LANES) * LANES
    out_rows = -(-(1 + 2 * labels) // 8) * 8
    width = weights.shape[1]
    arrays = (full, *mine, *other)

    def whole(x):
        return pl.BlockSpec(x.shape, lambda k: (0,) * len(x.shape))

    outs = (
        jax.ShapeDtypeStruct((chips, out_rows, LANES), jnp.float32),
        jax.ShapeDtypeStruct((8, genes), jnp.float32),
    )
    return pl.pallas_call(
        functools.partial(
            product_kernel, caps=caps, labels=labels, genes=genes, blocks_dev=blocks_dev
        ),
        grid=(all_samples // CHUNK,),
        out_shape=outs,
        in_specs=[
            pl.BlockSpec(memory_space=pltpu.SMEM),
            *[whole(x) for x in (*sums, plan)],
            *[pl.BlockSpec((x.shape[0], CHUNK), lambda k: (0, k)) for x in arrays],
            pl.BlockSpec((CHUNK, width), lambda k: (k, 0)),
        ],
        out_specs=tuple(whole(x) for x in outs),
        scratch_shapes=[
            pltpu.VMEM((used, CHUNK), jnp.bfloat16),
            pltpu.VMEM((padded, width), jnp.float32),
            pltpu.VMEM((genes, LANES), jnp.float32),
        ],
        compiler_params=pltpu.CompilerParams(vmem_limit_bytes=48 * MIB),
        cost_estimate=pl.CostEstimate(
            flops=2 * used * all_samples * width,
            bytes_accessed=2 * all_samples * (width + used),
            transcendentals=0,
        ),
        name="products",
    )(pos, *sums, plan, *arrays, weights)


def finish_kernel(own_ref, other_ref, power_ref, out_ref, *, samples):
    best = jnp.maximum(own_ref[0], other_ref[0])
    for i in range(1, own_ref.shape[0]):
        best = jnp.maximum(best, jnp.maximum(own_ref[i], other_ref[i]))
    labels, genes = out_ref.shape
    peak = best[:labels, :genes]
    out_ref[...] = jnp.sqrt(peak / (power_ref[0:1, :] / samples + 1e-05))


def shards(genotypes, phenotypes, environment, shuffles, window_start, window_end, chrom_bounds):
    snp_rows, half = genotypes.shape
    genes = phenotypes.shape[0]
    perms = shuffles.shape[0]
    chips = lax.axis_size("genome")
    cores = lax.axis_size("sample")
    blocks_dev = snp_rows // SNP_BLOCK
    reach = (HALF_BLK + blocks_dev - 1) // blocks_dev
    all_samples = half * cores
    labels = perms // cores
    caps = tuple(min(genes, genes * 4 >> k) for k in range(1, reach + 1))
    env = environment[None]
    start = window_start.reshape(-1, LANES)
    end = window_end.reshape(-1, LANES)
    pos = jnp.stack([lax.axis_index("genome"), lax.axis_index("sample")]).astype(jnp.int32)

    def travel(k, payload):
        pairs = [(i * cores, (i + k) * cores) for i in range(chips - k)]
        pairs += [((i + k) * cores + 1, i * cores + 1) for i in range(chips - k)]
        return lax.ppermute(payload, ("genome", "sample"), pairs)

    def one_round(turn, pos):
        core = pos[1:]
        other_pheno = swapped(phenotypes)
        own_sums = local_moments(genotypes, env)
        sums = (own_sums, swapped(own_sums))
        late_geno, _ = lax.optimization_barrier((genotypes, other_pheno))
        other_geno = swapped(late_geno)
        other_env = swapped(env)
        other_shuffles = swapped(shuffles)
        rounds, plan, full, *payloads = select(
            turn, pos, chrom_bounds, start, end, phenotypes, other_pheno, caps, blocks_dev
        )
        payloads = [full] * (reach - len(payloads)) + payloads
        mine = [travel(k, x) for k, x in enumerate(payloads, 1)]
        weights = snp_side(
            core, env, other_env, *sums, shuffles, other_shuffles, genotypes, other_geno, labels
        )
        *mine, weights = lax.optimization_barrier((*mine, weights))
        other = [swapped(x) for x in mine]
        found, power = products(
            pos, sums, plan, full, mine, other, weights, caps, labels, chips, blocks_dev
        )
        return rounds, found, power

    rounds, found, power = one_round(jnp.zeros((1,), jnp.int32), pos)

    def more(carry):
        return carry[0] < rounds[0]

    def again(carry):
        turn, best = carry
        turns, place = lax.optimization_barrier((jnp.full((1,), turn, jnp.int32), pos))
        return turn + 1, jnp.maximum(best, one_round(turns, place)[1])

    _, found = lax.while_loop(more, again, (jnp.int32(1), found))
    gathered = lax.all_to_all(found, "genome", 0, 0, tiled=True)
    return pl.pallas_call(
        functools.partial(finish_kernel, samples=all_samples),
        out_shape=jax.ShapeDtypeStruct((perms + 1, genes), jnp.float32),
        name="finish",
    )(gathered, swapped(gathered), power)


def solution(mesh):
    placed = (
        P("genome", "sample"),
        P("genome", "sample"),
        P("sample"),
        P(None, "sample"),
        P(),
        P(),
        P(),
    )
    return jax.shard_map(
        shards, mesh=mesh, in_specs=placed, out_specs=P(None, "genome"), check_vma=False
    )
```

```python
import functools

import jax
import jax.numpy as jnp
from jax import lax
from jax.experimental import pallas as pl
from jax.experimental.pallas import tpu as pltpu
from jax.sharding import PartitionSpec as P

SNP_BLOCK = 256
HALF_BLK = 7
LANES = 128
ROWS_STEP = 16
UNROLL = 32
SIDE = 2 * LANES
CHUNK = 1024
MIB = 2**20


def passed_along(x, axis, by):
    count = lax.axis_size(axis)
    pairs = [(i, i + by) for i in range(count) if 0 <= i + by < count]
    return lax.ppermute(x, axis, pairs)


def swapped(x):
    count = lax.axis_size("sample")
    return lax.ppermute(x, "sample", [(i, (i + 1) % count) for i in range(count)])


def moments_kernel(geno_ref, env_ref, out_ref, sums):
    step = pl.program_id(0)
    snp_rows, chunk = geno_ref.shape

    @pl.when(step == 0)
    def _():
        sums[...] = jnp.zeros_like(sums)

    def add_rows(i, carry):
        first = pl.multiple_of(i * ROWS_STEP, ROWS_STEP)
        held = [sums[m, pl.ds(first, ROWS_STEP), :] for m in range(3)]
        for t in range(chunk // LANES):
            x = geno_ref[pl.ds(first, ROWS_STEP), pl.ds(t * LANES, LANES)].astype(jnp.float32)
            e = env_ref[:, pl.ds(t * LANES, LANES)]
            x = x * x
            held[0] = held[0] + x
            x = x * e
            held[1] = held[1] + x
            held[2] = held[2] + x * e
        for m in range(3):
            sums[m, pl.ds(first, ROWS_STEP), :] = held[m]
        return carry

    lax.fori_loop(0, snp_rows // ROWS_STEP, add_rows, 0, unroll=4)

    @pl.when(step == pl.num_programs(0) - 1)
    def _():
        rows = [jnp.sum(sums[m].T, axis=0, keepdims=True) for m in range(3)]
        rows.append(jnp.zeros((out_ref.shape[0] - 3, snp_rows), jnp.float32))
        out_ref[...] = jnp.concatenate(rows, axis=0)


def local_moments(geno, env):
    snp_rows, half = geno.shape
    chunk = CHUNK
    return pl.pallas_call(
        moments_kernel,
        grid=(half // chunk,),
        out_shape=jax.ShapeDtypeStruct((8, snp_rows), jnp.float32),
        in_specs=[
            pl.BlockSpec((snp_rows, chunk), lambda k: (0, k)),
            pl.BlockSpec((1, chunk), lambda k: (0, k)),
        ],
        out_specs=pl.BlockSpec((8, snp_rows), lambda k: (0, 0)),
        scratch_shapes=[pltpu.VMEM((3, snp_rows, LANES), jnp.float32)],
        compiler_params=pltpu.CompilerParams(vmem_limit_bytes=60 * MIB),
        cost_estimate=pl.CostEstimate(
            flops=5 * 10**9, bytes_accessed=2 * snp_rows * half, transcendentals=0
        ),
        name="local_moments",
    )(geno, env)


def snp_side_kernel(
    core_ref, env_own, env_other, sums_own, sums_other, shuf_own, shuf_other, own_ref, other_ref,
    out_ref,
    idx, places, geno, table, dests, stage, first_stage, slope,
    idx_sem, in_sems, out_sems, first_sems,
    *, labels,
):
    snp_rows, half = own_ref.shape
    all_samples = 2 * half
    chunks = all_samples // CHUNK
    words = snp_rows // LANES
    share = snp_rows // 2
    side = SIDE
    piece = geno.shape[3]
    pieces = half // piece
    group = UNROLL // 2
    core = core_ref[0]

    def load(k, h):
        source = own_ref if h == 0 else other_ref
        return pltpu.make_async_copy(
            source.at[:, pl.ds(k * piece, piece)], geno.at[k % 2, h], in_sems.at[k % 2, h]
        )

    def save_first(k, h):
        there = jnp.where(core == h, k * piece, k * piece + half)
        rows = pl.ds(pl.multiple_of(there, piece), piece)
        return pltpu.make_async_copy(
            first_stage.at[k % 2, h, :, pl.ds(pl.multiple_of(core * share, share), share)],
            out_ref.at[rows, pl.ds(labels * snp_rows, share)],
            first_sems.at[k % 2, h],
        )

    def save(q, k):
        return pltpu.make_async_copy(
            stage.at[k % 2],
            out_ref.at[pl.ds(k * CHUNK, CHUNK), pl.ds(q * snp_rows, snp_rows)],
            out_sems.at[k % 2],
        )

    def read_rows(first):
        base = pl.multiple_of(first * words, group * words)
        late = pl.multiple_of((half + first) * words, group * words)
        return [
            table[pl.ds(at + u * words, words), :] for at in (base, late) for u in range(group)
        ]

    def write_rows(q, first, held):
        for u in range(group):
            both = idx[q * half + first + u]
            dests[q][both & 0xFFFF] = held[u]
            dests[q][lax.shift_right_logical(both, 16)] = held[group + u]

    def narrowed(q, at, rows):
        flat = dests[q].reshape(all_samples * words, LANES)
        return [
            flat[pl.ds(at * words + c, rows, stride=words), :].astype(jnp.bfloat16)
            for c in range(words)
        ]

    for k in range(2):
        for h in range(2):
            load(k, h).start()
    for q in range(labels):
        row = pl.ds(core * labels + q, 1)
        places[:, pl.ds(q * half, half)] = shuf_own[row, :] + shuf_other[row, :] * 65536
    fetch = pltpu.make_async_copy(places.at[0], idx, idx_sem)
    fetch.start()
    sums = sums_own[...] + sums_other[...]
    slope[...] = jnp.broadcast_to(sums[1:2, :] / sums[0:1, :], (LANES, snp_rows)).T
    unit = (
        lax.broadcasted_iota(jnp.int32, (side, side), 0)
        == lax.broadcasted_iota(jnp.int32, (side, side), 1)
    ).astype(jnp.bfloat16)
    fetch.wait()

    groups = side // group // (2 * words)
    for k in range(pieces):
        for h in range(2):
            load(k, h).wait()
            if k >= 2:
                save_first(k - 2, h).wait()

        def turn(i, carry, k=k):
            at = pl.multiple_of(i * side, side)
            behind = pl.multiple_of(jnp.maximum(k * piece + at - side, 0), side)
            for h in range(2):
                env_ref = env_own if h == 0 else env_other
                e = env_ref[:, pl.ds(k * piece + at, side)]
                for c in range(words):
                    rows = pl.ds(c * LANES, LANES)
                    x = geno[k % 2, h, rows, pl.ds(at, side)].astype(jnp.float32)
                    r = slope[rows, :]
                    a = x * (e - jnp.concatenate([r] * (side // LANES), axis=1))
                    t = lax.dot_general(
                        unit, a.astype(jnp.bfloat16), (((1,), (1,)), ((), ())),
                        preferred_element_type=jnp.float32,
                    )
                    for g in range(groups):
                        first = pl.multiple_of(
                            behind + ((h * words + c) * groups + g) * group, group
                        )
                        write_rows(0, first, read_rows(first))
                    start = (h * half + k * piece + at) * words
                    table[pl.ds(start + c, side, stride=words), :] = t
                    first_stage[k % 2, h, pl.ds(at, side), pl.ds(c * LANES, LANES)] = t.astype(
                        jnp.bfloat16
                    )
            return carry

        lax.fori_loop(0, piece // side, turn, 0)
        for h in range(2):
            save_first(k, h).start()
            if k + 2 < pieces:
                load(k + 2, h).start()

    def rest(i, carry):
        first = pl.multiple_of(half - side + i * group, group)
        write_rows(0, first, read_rows(first))
        return carry

    lax.fori_loop(0, side // group, rest, 0)

    count = 0
    for q in range(1, labels + 1):
        for k in range(chunks):
            if count >= 2:
                save((count - 2) // chunks, (count - 2) % chunks).wait()

            def step(i, carry, k=k, q=q):
                at = pl.multiple_of(i * UNROLL, UNROLL)
                first = pl.multiple_of(k * (CHUNK // 2) + i * group, group)
                held = read_rows(first)
                parts = narrowed(q - 1, pl.multiple_of(k * CHUNK + at, UNROLL), UNROLL)
                write_rows(q, first, held)
                for c in range(words):
                    stage[k % 2, pl.ds(at, UNROLL), pl.ds(c * LANES, LANES)] = parts[c]
                return carry

            def wide(i, carry, k=k, q=q):
                at = pl.multiple_of(i * side, side)
                parts = narrowed(q - 1, k * CHUNK + at, side)
                for c in range(words):
                    stage[k % 2, pl.ds(at, side), pl.ds(c * LANES, LANES)] = parts[c]
                return carry

            if q < labels:
                lax.fori_loop(0, CHUNK // UNROLL, step, 0)
            else:
                lax.fori_loop(0, CHUNK // side, wide, 0)
            save(q - 1, k).start()
            count += 1
    for k in range(2):
        for h in range(2):
            save_first(pieces - 2 + k, h).wait()
        save(labels - 1, chunks - 2 + k).wait()


def snp_side(core, env_own, env_other, sums_own, sums_other, shuf_own, shuf_other, own, other,
             labels):
    snp_rows, half = own.shape
    all_samples = 2 * half
    words = snp_rows // LANES
    width = labels * snp_rows + snp_rows // 2
    any_spec = pl.BlockSpec(memory_space=pl.ANY)
    smem = pl.BlockSpec(memory_space=pltpu.SMEM)
    vmem = pl.BlockSpec(memory_space=pltpu.VMEM)
    return pl.pallas_call(
        functools.partial(snp_side_kernel, labels=labels),
        out_shape=jax.ShapeDtypeStruct((all_samples, width), jnp.bfloat16),
        in_specs=[smem, vmem, vmem, vmem, vmem, vmem, vmem, any_spec, any_spec],
        out_specs=any_spec,
        scratch_shapes=[
            pltpu.SMEM((labels * half,), jnp.int32),
            pltpu.VMEM((1, labels * half), jnp.int32),
            pltpu.VMEM((2, 2, snp_rows, CHUNK // 2), jnp.bfloat16),
            pltpu.VMEM((all_samples * words, LANES), jnp.float32),
            [pltpu.VMEM((all_samples, words, LANES), jnp.float32) for _ in range(labels)],
            pltpu.VMEM((2, CHUNK, snp_rows), jnp.bfloat16),
            pltpu.VMEM((2, 2, CHUNK // 2, snp_rows), jnp.bfloat16),
            pltpu.VMEM((snp_rows, LANES), jnp.float32),
            pltpu.SemaphoreType.DMA,
            pltpu.SemaphoreType.DMA((2, 2)),
            pltpu.SemaphoreType.DMA((2,)),
            pltpu.SemaphoreType.DMA((2, 2)),
        ],
        compiler_params=pltpu.CompilerParams(vmem_limit_bytes=61 * MIB),
        cost_estimate=pl.CostEstimate(
            flops=40 * 10**9, bytes_accessed=60 * 10**6, transcendentals=0
        ),
        name="snp_side",
    )(core, env_own, env_other, sums_own, sums_other, shuf_own, shuf_other, own, other)


def window_plan(start, end, bounds_ref, n_bounds, total_blocks):
    middle = (start + end - 1) // 2
    lower_edge = jnp.zeros_like(start)
    upper_edge = jnp.full_like(end, total_blocks)
    for i in range(n_bounds):
        edge = bounds_ref[i]
        before = edge <= middle
        lower_edge = jnp.where(before, jnp.maximum(lower_edge, edge), lower_edge)
        upper_edge = jnp.where(before, upper_edge, jnp.minimum(upper_edge, edge))
    return jnp.maximum(start, lower_edge), jnp.minimum(end, upper_edge)


def select_kernel(
    round_ref, pos_ref, bounds_ref, start_ref, end_ref, own_ref, other_ref,
    rounds_ref, plan_ref, full_ref, *rest, caps, blocks_dev,
):
    reach = len(caps)
    genes, half = own_ref.shape
    chosen_from = sum(cap == genes for cap in caps)
    (slots, edges), pay_refs = rest[-2:], rest[:-2]
    shape = start_ref.shape
    per_row = LANES // genes
    chips = shape[0] * per_row
    chip, core = pos_ref[0], pos_ref[1]
    turn = round_ref[0]
    low, high = window_plan(
        start_ref[...], end_ref[...], bounds_ref, bounds_ref.shape[0], chips * blocks_dev
    )
    edges[0] = low
    edges[1] = high
    at = lax.broadcasted_iota(jnp.int32, shape, 0) * per_row
    at = at + lax.broadcasted_iota(jnp.int32, shape, 1) // genes
    a = lax.broadcasted_iota(jnp.int32, (LANES, LANES), 0)
    b = lax.broadcasted_iota(jnp.int32, (LANES, LANES), 1)
    upto = ((a <= b) & (a // genes == b // genes)).astype(jnp.float32).astype(jnp.bfloat16)
    rounds = jnp.int32(0)
    for way in range(2):
        for k in range(1, reach + 1):
            to = at + (k if way == 0 else -k)
            need = (
                (low < (to + 1) * blocks_dev) & (high > to * blocks_dev)
                & (low < high) & (to >= 0) & (to < chips)
            )
            rank = jnp.dot(
                need.astype(jnp.float32).astype(jnp.bfloat16), upto,
                preferred_element_type=jnp.float32,
            ).astype(jnp.int32)
            cap = caps[k - 1]
            if cap == genes:
                which = lax.broadcasted_iota(jnp.int32, shape, 1) % genes
                slots[way * reach + k - 1] = jnp.where(need, which, -1)
                continue
            slot = rank - 1 - turn * cap
            slots[way * reach + k - 1] = jnp.where(
                need & (slot >= 0) & (slot < cap), slot, -1
            )
            rounds = jnp.maximum(rounds, (jnp.max(rank) + cap - 1) // cap)
    rounds_ref[0] = rounds

    def of_chip(ref, index, which):
        row = ref[index, pl.ds(which // per_row, 1), :]
        out = row[:, :genes]
        for part in range(1, per_row):
            out = jnp.where(
                which % per_row == part, row[:, part * genes : (part + 1) * genes], out
            )
        return out

    used = [lax.broadcasted_iota(jnp.int32, (1, genes), 1)]
    lows = [of_chip(edges, 0, chip)]
    highs = [of_chip(edges, 1, chip)]
    first = genes
    for side in range(2):
        way = core if side == 0 else 1 - core
        for k in range(1, reach + 1):
            source = chip + (2 * way - 1) * k
            valid = (source >= 0) & (source < chips)
            source = jnp.clip(source, 0, chips - 1)
            slot = of_chip(slots, way * reach + k - 1, source)
            used.append(jnp.where(valid & (slot >= 0), slot + first, -1))
            lows.append(of_chip(edges, 0, source))
            highs.append(jnp.where(valid, of_chip(edges, 1, source), 0))
            first += caps[k - 1]
    while len(used) * genes < plan_ref.shape[1]:
        used.append(jnp.full_like(used[0], -1))
        lows.append(jnp.zeros_like(used[0]))
        highs.append(jnp.zeros_like(used[0]))
    plan_ref[...] = jnp.zeros_like(plan_ref)
    for row, parts in enumerate((used, lows, highs)):
        plan_ref[pl.ds(row, 1), :] = jnp.concatenate(parts, axis=1)

    picks = []
    for k in range(chosen_from + 1, reach + 1):
        slot = of_chip(slots, core * reach + k - 1, chip)
        rows = lax.broadcasted_iota(jnp.int32, (caps[k - 1], genes), 0)
        picks.append((rows == slot).astype(jnp.float32))
    if picks:
        picks = jnp.concatenate(picks, axis=0).astype(jnp.bfloat16)
    step = 1024

    def copy(i, carry):
        cols = pl.ds(pl.multiple_of(i * step, step), step)
        late = pl.ds(pl.multiple_of(half + i * step, step), step)
        a, b = own_ref[:, cols], other_ref[:, cols]
        for part, to in ((jnp.where(core == 0, a, b), cols), (jnp.where(core == 0, b, a), late)):
            full_ref[:, to] = part
            if pay_refs:
                chosen = jnp.dot(picks, part, preferred_element_type=jnp.float32)
                chosen = chosen.astype(jnp.bfloat16)
                row = 0
                for pay in pay_refs:
                    pay[:, to] = chosen[row : row + pay.shape[0]]
                    row += pay.shape[0]
        return carry

    lax.fori_loop(0, half // step, copy, 0)


def select(turn, pos, bounds, start, end, own, other, caps, blocks_dev):
    genes, half = own.shape
    all_samples = 2 * half
    reach = len(caps)
    smem = pl.BlockSpec(memory_space=pltpu.SMEM)
    vmem = pl.BlockSpec(memory_space=pltpu.VMEM)
    width = -(-(2 * reach + 1) * genes // LANES) * LANES
    chosen = [cap for cap in caps if cap < genes]
    return pl.pallas_call(
        functools.partial(select_kernel, caps=caps, blocks_dev=blocks_dev),
        out_shape=(
            jax.ShapeDtypeStruct((1,), jnp.int32),
            jax.ShapeDtypeStruct((8, width), jnp.int32),
            jax.ShapeDtypeStruct((genes, all_samples), jnp.bfloat16),
            *[jax.ShapeDtypeStruct((cap, all_samples), jnp.bfloat16) for cap in chosen],
        ),
        in_specs=[smem, smem, smem, vmem, vmem, vmem, vmem],
        out_specs=(smem, vmem, vmem, *[vmem for _ in chosen]),
        scratch_shapes=[
            pltpu.VMEM((2 * reach,) + start.shape, jnp.int32),
            pltpu.VMEM((2,) + start.shape, jnp.int32),
        ],
        compiler_params=pltpu.CompilerParams(vmem_limit_bytes=24 * MIB),
        name="select",
    )(turn, pos, bounds, start, end, own, other)


def product_kernel(
    pos_ref, sums_own, sums_other, plan_ref, *rest, caps, labels, genes, blocks_dev
):
    reach = len(caps)
    n_in = 1 + 2 * reach
    gene_refs = rest[:n_in]
    weights_ref, out_ref, power_ref, rows, total, power = rest[n_in:]
    step = pl.program_id(0)
    snp_rows = sums_own.shape[1]
    depth, width = weights_ref.shape
    block = SNP_BLOCK
    used = rows.shape[0]
    chip, core = pos_ref[0], pos_ref[1]

    @pl.when(step == 0)
    def _():
        total[...] = jnp.zeros_like(total)
        power[...] = jnp.zeros_like(power)

    at = 0
    for ref in gene_refs:
        rows[pl.ds(at, ref.shape[0]), :] = ref[...]
        at += ref.shape[0]
    for at in range(0, width, snp_rows):
        cols = pl.ds(at, min(snp_rows, width - at))
        total[pl.ds(0, used), cols] += jnp.dot(
            rows[...], weights_ref[:, cols], preferred_element_type=jnp.float32
        )
    kept = power[...]
    for t in range(depth // LANES):
        x = rows[pl.ds(0, genes), pl.ds(t * LANES, LANES)].astype(jnp.float32)
        kept = kept + x * x
    power[...] = kept

    @pl.when(step == pl.num_programs(0) - 1)
    def _():
        summed_up(
            chip, core, sums_own, sums_other, plan_ref, out_ref, power_ref, total, power,
            reach=reach, labels=labels, genes=genes, blocks_dev=blocks_dev,
        )


def summed_up(
    chip, core, sums_own, sums_other, plan_ref, out_ref, power_ref, total, power,
    *, reach, labels, genes, blocks_dev,
):
    snp_rows = sums_own.shape[1]
    block = SNP_BLOCK
    n_in = 1 + 2 * reach
    share_blocks = blocks_dev // 2
    sums = sums_own[...] + sums_other[...]
    cross = sums[1:2, :]
    inter = sums[2:3, :]
    inv = 1.0 / (inter - cross * (cross / sums[0:1, :]) + 0.1 * inter)

    def peak(col, inv_block):
        best = None
        for t in range(block // LANES):
            v = total[:, pl.ds(col + t * LANES, LANES)]
            v = v * v * inv_block[:, t * LANES : (t + 1) * LANES]
            best = v if best is None else jnp.maximum(best, v)
        return jnp.max(best.T, axis=0, keepdims=True)

    peaks = []
    for q in range(labels):
        for b in range(blocks_dev):
            peaks.append(peak(q * snp_rows + b * block, inv[:, b * block : (b + 1) * block]))
    for b in range(share_blocks):
        mine = inv[:, b * block : (b + 1) * block]
        late = inv[:, (share_blocks + b) * block : (share_blocks + b + 1) * block]
        peaks.append(peak(labels * snp_rows + b * block, jnp.where(core == 0, mine, late)))
    while len(peaks) % 8:
        peaks.append(jnp.zeros_like(peaks[0]))
    peaks = jnp.concatenate(peaks, axis=0)
    count = peaks.shape[0]
    terms = []
    left = peaks
    for _ in range(3):
        terms.append(left.astype(jnp.bfloat16).astype(jnp.float32))
        left = left - terms[-1]
    terms = jnp.concatenate(terms, axis=0).astype(jnp.bfloat16)
    band = plan_ref.shape[1]
    slot = plan_ref[0:1, :]
    low = plan_ref[1:2, :]
    high = plan_ref[2:3, :]
    place = lax.broadcasted_iota(jnp.int32, (total.shape[0], band), 0) == slot
    spread = jnp.dot(
        terms, place.astype(jnp.float32).astype(jnp.bfloat16),
        preferred_element_type=jnp.float32,
    )
    spread = spread[:count] + spread[count : 2 * count] + spread[2 * count :]

    def masked(row, snp_block):
        inside = (snp_block >= low) & (snp_block < high)
        return jnp.where(inside, spread[row : row + 1], 0.0)

    def highest(row, blocks, first_block):
        best = masked(row, first_block)
        for b in range(1, blocks):
            best = jnp.maximum(best, masked(row + b, first_block + b))
        return best

    out_rows = [highest(labels * blocks_dev, share_blocks, chip * blocks_dev + core * share_blocks)]
    found = [highest(q * blocks_dev, blocks_dev, chip * blocks_dev) for q in range(labels)]
    for c in range(2):
        out_rows += [jnp.where(core == c, v, 0.0) for v in found]
    while len(out_rows) % 8:
        out_rows.append(jnp.zeros_like(out_rows[0]))
    dense = jnp.concatenate(out_rows, axis=0)
    out_ref[...] = jnp.zeros_like(out_ref)
    chips = out_ref.shape[0]
    for i in range(n_in):
        if i == 0:
            target = chip
        else:
            way = core if i <= reach else 1 - core
            target = chip + (2 * way - 1) * ((i - 1) % reach + 1)

        @pl.when((target >= 0) & (target < chips))
        def _(i=i, target=target):
            out_ref[target, :, pl.ds(0, genes)] = dense[:, i * genes : (i + 1) * genes]

    powers = jnp.sum(power[...].T, axis=0, keepdims=True)
    power_ref[...] = jnp.broadcast_to(powers, power_ref.shape)


def products(pos, sums, plan, full, mine, other, weights, caps, labels, chips, blocks_dev):
    genes, all_samples = full.shape
    used = genes + 2 * sum(caps)
    padded = -(-used // LANES) * LANES
    out_rows = -(-(1 + 2 * labels) // 8) * 8
    width = weights.shape[1]
    arrays = (full, *mine, *other)

    def whole(x):
        return pl.BlockSpec(x.shape, lambda k: (0,) * len(x.shape))

    outs = (
        jax.ShapeDtypeStruct((chips, out_rows, LANES), jnp.float32),
        jax.ShapeDtypeStruct((8, genes), jnp.float32),
    )
    return pl.pallas_call(
        functools.partial(
            product_kernel, caps=caps, labels=labels, genes=genes, blocks_dev=blocks_dev
        ),
        grid=(all_samples // CHUNK,),
        out_shape=outs,
        in_specs=[
            pl.BlockSpec(memory_space=pltpu.SMEM),
            *[whole(x) for x in (*sums, plan)],
            *[pl.BlockSpec((x.shape[0], CHUNK), lambda k: (0, k)) for x in arrays],
            pl.BlockSpec((CHUNK, width), lambda k: (k, 0)),
        ],
        out_specs=tuple(whole(x) for x in outs),
        scratch_shapes=[
            pltpu.VMEM((used, CHUNK), jnp.bfloat16),
            pltpu.VMEM((padded, width), jnp.float32),
            pltpu.VMEM((genes, LANES), jnp.float32),
        ],
        compiler_params=pltpu.CompilerParams(vmem_limit_bytes=48 * MIB),
        cost_estimate=pl.CostEstimate(
            flops=2 * used * all_samples * width,
            bytes_accessed=2 * all_samples * (width + used),
            transcendentals=0,
        ),
        name="products",
    )(pos, *sums, plan, *arrays, weights)


def finish_kernel(own_ref, other_ref, power_ref, out_ref, *, samples):
    best = jnp.maximum(own_ref[0], other_ref[0])
    for i in range(1, own_ref.shape[0]):
        best = jnp.maximum(best, jnp.maximum(own_ref[i], other_ref[i]))
    labels, genes = out_ref.shape
    peak = best[:labels, :genes]
    out_ref[...] = jnp.sqrt(peak / (power_ref[0:1, :] / samples + 1e-05))


def shards(genotypes, phenotypes, environment, shuffles, window_start, window_end, chrom_bounds):
    snp_rows, half = genotypes.shape
    genes = phenotypes.shape[0]
    perms = shuffles.shape[0]
    chips = lax.axis_size("genome")
    cores = lax.axis_size("sample")
    blocks_dev = snp_rows // SNP_BLOCK
    reach = (HALF_BLK + blocks_dev - 1) // blocks_dev
    all_samples = half * cores
    labels = perms // cores
    caps = tuple(min(genes, genes * 4 >> k) for k in range(1, reach + 1))
    env = environment[None]
    start = window_start.reshape(-1, LANES)
    end = window_end.reshape(-1, LANES)
    pos = jnp.stack([lax.axis_index("genome"), lax.axis_index("sample")]).astype(jnp.int32)

    def travel(k, payload):
        pairs = [(i * cores, (i + k) * cores) for i in range(chips - k)]
        pairs += [((i + k) * cores + 1, i * cores + 1) for i in range(chips - k)]
        return lax.ppermute(payload, ("genome", "sample"), pairs)

    def one_round(turn, pos):
        core = pos[1:]
        other_pheno = swapped(phenotypes)
        own_sums = local_moments(genotypes, env)
        sums = (own_sums, swapped(own_sums))
        late_geno, _ = lax.optimization_barrier((genotypes, other_pheno))
        other_geno = swapped(late_geno)
        other_env = swapped(env)
        other_shuffles = swapped(shuffles)
        rounds, plan, full, *payloads = select(
            turn, pos, chrom_bounds, start, end, phenotypes, other_pheno, caps, blocks_dev
        )
        payloads = [full] * (reach - len(payloads)) + payloads
        mine = [travel(k, x) for k, x in enumerate(payloads, 1)]
        weights = snp_side(
            core, env, other_env, *sums, shuffles, other_shuffles, genotypes, other_geno, labels
        )
        *mine, weights = lax.optimization_barrier((*mine, weights))
        other = [swapped(x) for x in mine]
        found, power = products(
            pos, sums, plan, full, mine, other, weights, caps, labels, chips, blocks_dev
        )
        return rounds, found, power

    rounds, found, power = one_round(jnp.zeros((1,), jnp.int32), pos)

    def more(carry):
        return carry[0] < rounds[0]

    def again(carry):
        turn, best = carry
        turns, place = lax.optimization_barrier((jnp.full((1,), turn, jnp.int32), pos))
        return turn + 1, jnp.maximum(best, one_round(turns, place)[1])

    _, found = lax.while_loop(more, again, (jnp.int32(1), found))
    gathered = lax.all_to_all(found, "genome", 0, 0, tiled=True)
    return pl.pallas_call(
        functools.partial(finish_kernel, samples=all_samples),
        out_shape=jax.ShapeDtypeStruct((perms + 1, genes), jnp.float32),
        name="finish",
    )(gathered, swapped(gathered), power)


def solution(mesh):
    placed = (
        P("genome", "sample"),
        P("genome", "sample"),
        P("sample"),
        P(None, "sample"),
        P(),
        P(),
        P(),
    )
    return jax.shard_map(
        shards, mesh=mesh, in_specs=placed, out_specs=P(None, "genome"), check_vma=False
    )
```

```python
import functools

import jax
import jax.numpy as jnp
from jax import lax
from jax.experimental import pallas as pl
from jax.experimental.pallas import tpu as pltpu
from jax.sharding import PartitionSpec as P

SNP_BLOCK = 256
HALF_BLK = 7
LANES = 128
ROWS_STEP = 16
UNROLL = 32
SIDE = 2 * LANES
CHUNK = 1024
MIB = 2**20


def passed_along(x, axis, by):
    count = lax.axis_size(axis)
    pairs = [(i, i + by) for i in range(count) if 0 <= i + by < count]
    return lax.ppermute(x, axis, pairs)


def swapped(x):
    count = lax.axis_size("sample")
    return lax.ppermute(x, "sample", [(i, (i + 1) % count) for i in range(count)])


def moments_kernel(geno_ref, env_ref, out_ref, sums):
    step = pl.program_id(0)
    snp_rows, chunk = geno_ref.shape

    @pl.when(step == 0)
    def _():
        sums[...] = jnp.zeros_like(sums)

    def add_rows(i, carry):
        first = pl.multiple_of(i * ROWS_STEP, ROWS_STEP)
        held = [sums[m, pl.ds(first, ROWS_STEP), :] for m in range(3)]
        for t in range(chunk // LANES):
            x = geno_ref[pl.ds(first, ROWS_STEP), pl.ds(t * LANES, LANES)].astype(jnp.float32)
            e = env_ref[:, pl.ds(t * LANES, LANES)]
            x = x * x
            held[0] = held[0] + x
            x = x * e
            held[1] = held[1] + x
            held[2] = held[2] + x * e
        for m in range(3):
            sums[m, pl.ds(first, ROWS_STEP), :] = held[m]
        return carry

    lax.fori_loop(0, snp_rows // ROWS_STEP, add_rows, 0, unroll=4)

    @pl.when(step == pl.num_programs(0) - 1)
    def _():
        rows = [jnp.sum(sums[m].T, axis=0, keepdims=True) for m in range(3)]
        rows.append(jnp.zeros((out_ref.shape[0] - 3, snp_rows), jnp.float32))
        out_ref[...] = jnp.concatenate(rows, axis=0)


def local_moments(geno, env):
    snp_rows, half = geno.shape
    chunk = CHUNK
    return pl.pallas_call(
        moments_kernel,
        grid=(half // chunk,),
        out_shape=jax.ShapeDtypeStruct((8, snp_rows), jnp.float32),
        in_specs=[
            pl.BlockSpec((snp_rows, chunk), lambda k: (0, k)),
            pl.BlockSpec((1, chunk), lambda k: (0, k)),
        ],
        out_specs=pl.BlockSpec((8, snp_rows), lambda k: (0, 0)),
        scratch_shapes=[pltpu.VMEM((3, snp_rows, LANES), jnp.float32)],
        compiler_params=pltpu.CompilerParams(vmem_limit_bytes=60 * MIB),
        cost_estimate=pl.CostEstimate(
            flops=5 * 10**9, bytes_accessed=2 * snp_rows * half, transcendentals=0
        ),
        name="local_moments",
    )(geno, env)


def snp_side_kernel(
    core_ref, env_own, env_other, sums_own, sums_other, shuf_own, shuf_other, own_ref, other_ref,
    *rest, labels,
):
    out_refs, scratch = rest[: labels + 1], rest[labels + 1 :]
    (
        idx, geno, table, dests, stage, first_stage, slope, idx_sems, in_sems, out_sems, first_sems,
    ) = scratch
    snp_rows, half = own_ref.shape
    all_samples = 2 * half
    chunks = all_samples // CHUNK
    words = snp_rows // LANES
    share = snp_rows // 2
    side = SIDE
    per_chunk = CHUNK // side
    core = core_ref[0]
    depth = geno.shape[0]

    def load(k):
        source = own_ref if k * CHUNK < half else other_ref
        return pltpu.make_async_copy(
            source.at[:, pl.ds((k * CHUNK) % half, CHUNK)], geno.at[k % depth],
            in_sems.at[k % depth],
        )

    def load_idx(q, h):
        source = shuf_own if h == 0 else shuf_other
        return pltpu.make_async_copy(
            source.at[core * labels + q],
            idx.at[pl.ds(q * all_samples + h * half, half)],
            idx_sems.at[2 * q + h],
        )

    def save_first(k):
        there = jnp.where(core == 0, k * CHUNK, (k * CHUNK + half) % all_samples)
        rows = pl.ds(pl.multiple_of(there, CHUNK), CHUNK)
        return pltpu.make_async_copy(
            first_stage.at[k % 2, :, pl.ds(pl.multiple_of(core * share, share), share)],
            out_refs[labels].at[rows],
            first_sems.at[k % 2],
        )

    def save(q, k):
        return pltpu.make_async_copy(
            stage.at[k % 2],
            out_refs[q].at[pl.ds(k * CHUNK, CHUNK)],
            out_sems.at[k % 2],
        )

    def read_rows(first):
        base = pl.multiple_of(first * words, UNROLL * words)
        return [table[pl.ds(base + u * words, words), :] for u in range(UNROLL)]

    def write_rows(q, first, held):
        for u in range(UNROLL):
            to = pl.multiple_of(idx[q * all_samples + first + u] * words, words)
            dests[q][pl.ds(to, words), :] = held[u]

    def narrowed(q, at, rows):
        return [
            dests[q][pl.ds(at * words + c, rows, stride=words), :].astype(jnp.bfloat16)
            for c in range(words)
        ]

    for k in range(depth):
        load(k).start()
    for q in range(labels):
        for h in range(2):
            load_idx(q, h).start()
    sums = sums_own[...] + sums_other[...]
    slope[...] = jnp.broadcast_to(sums[1:2, :] / sums[0:1, :], (LANES, snp_rows)).T
    unit = (
        lax.broadcasted_iota(jnp.int32, (side, side), 0)
        == lax.broadcasted_iota(jnp.int32, (side, side), 1)
    ).astype(jnp.bfloat16)
    for q in range(labels):
        for h in range(2):
            load_idx(q, h).wait()

    groups = side // UNROLL // words
    for k in range(chunks):
        load(k).wait()
        if k >= 2:
            save_first(k - 2).wait()
        env_ref = env_own if k * CHUNK < half else env_other

        def turn(i, carry, k=k, env_ref=env_ref):
            at = pl.multiple_of(i * side, side)
            e = env_ref[:, pl.ds((k * CHUNK) % half + at, side)]
            behind = pl.multiple_of(jnp.maximum(k * CHUNK + at - side, 0), side)
            for c in range(words):
                rows = pl.ds(c * LANES, LANES)
                x = geno[k % depth, rows, pl.ds(at, side)].astype(jnp.float32)
                r = slope[rows, :]
                a = x * (e - jnp.concatenate([r] * (side // LANES), axis=1))
                t = lax.dot_general(
                    unit, a.astype(jnp.bfloat16), (((1,), (1,)), ((), ())),
                    preferred_element_type=jnp.float32,
                )
                for g in range(groups):
                    first = pl.multiple_of(behind + (c * groups + g) * UNROLL, UNROLL)
                    write_rows(0, first, read_rows(first))
                table[pl.ds((k * CHUNK + at) * words + c, side, stride=words), :] = t
                first_stage[k % 2, pl.ds(at, side), pl.ds(c * LANES, LANES)] = t.astype(
                    jnp.bfloat16
                )
            return carry

        lax.fori_loop(0, per_chunk, turn, 0)
        save_first(k).start()
        if k + depth < chunks:
            load(k + depth).start()

    def last_block(i, carry):
        first = pl.multiple_of(all_samples - side + i * UNROLL, UNROLL)
        write_rows(0, first, read_rows(first))
        return carry

    lax.fori_loop(0, side // UNROLL, last_block, 0)

    count = 0
    for q in range(1, labels + 1):
        for k in range(chunks):
            if count >= 2:
                save((count - 2) // chunks, (count - 2) % chunks).wait()

            def step(i, carry, k=k, q=q):
                at = pl.multiple_of(i * UNROLL, UNROLL)
                first = pl.multiple_of(k * CHUNK + at, UNROLL)
                if q < labels:
                    held = read_rows(first)
                parts = narrowed(q - 1, first, UNROLL)
                if q < labels:
                    write_rows(q, first, held)
                for c in range(words):
                    stage[k % 2, pl.ds(at, UNROLL), pl.ds(c * LANES, LANES)] = parts[c]
                return carry

            def wide(i, carry, k=k, q=q):
                at = pl.multiple_of(i * side, side)
                parts = narrowed(q - 1, k * CHUNK + at, side)
                for c in range(words):
                    stage[k % 2, pl.ds(at, side), pl.ds(c * LANES, LANES)] = parts[c]
                return carry

            if q < labels:
                lax.fori_loop(0, CHUNK // UNROLL, step, 0)
            else:
                lax.fori_loop(0, CHUNK // side, wide, 0)
            save(q - 1, k).start()
            count += 1
    for k in range(chunks - 2, chunks):
        save_first(k).wait()
        save(labels - 1, k).wait()


def snp_side(core, env_own, env_other, sums_own, sums_other, shuf_own, shuf_other, own, other,
             labels):
    snp_rows, half = own.shape
    all_samples = 2 * half
    words = snp_rows // LANES
    widths = [snp_rows] * labels + [snp_rows // 2]
    any_spec = pl.BlockSpec(memory_space=pl.ANY)
    smem = pl.BlockSpec(memory_space=pltpu.SMEM)
    vmem = pl.BlockSpec(memory_space=pltpu.VMEM)
    return pl.pallas_call(
        functools.partial(snp_side_kernel, labels=labels),
        out_shape=[jax.ShapeDtypeStruct((all_samples, w), jnp.bfloat16) for w in widths],
        in_specs=[smem, vmem, vmem, vmem, vmem, any_spec, any_spec, any_spec, any_spec],
        out_specs=[any_spec for _ in widths],
        scratch_shapes=[
            pltpu.SMEM((labels * all_samples,), jnp.int32),
            pltpu.VMEM((2, snp_rows, CHUNK), jnp.bfloat16),
            pltpu.VMEM((all_samples * words, LANES), jnp.float32),
            [pltpu.VMEM((all_samples * words, LANES), jnp.float32) for _ in range(labels)],
            pltpu.VMEM((2, CHUNK, snp_rows), jnp.bfloat16),
            pltpu.VMEM((2, CHUNK, snp_rows), jnp.bfloat16),
            pltpu.VMEM((snp_rows, LANES), jnp.float32),
            pltpu.SemaphoreType.DMA((2 * labels,)),
            pltpu.SemaphoreType.DMA((2,)),
            pltpu.SemaphoreType.DMA((2,)),
            pltpu.SemaphoreType.DMA((2,)),
        ],
        compiler_params=pltpu.CompilerParams(vmem_limit_bytes=61 * MIB),
        cost_estimate=pl.CostEstimate(
            flops=40 * 10**9, bytes_accessed=60 * 10**6, transcendentals=0
        ),
        name="snp_side",
    )(core, env_own, env_other, sums_own, sums_other, shuf_own, shuf_other, own, other)


def window_plan(start, end, bounds_ref, n_bounds, total_blocks):
    middle = (start + end - 1) // 2
    lower_edge = jnp.zeros_like(start)
    upper_edge = jnp.full_like(end, total_blocks)
    for i in range(n_bounds):
        edge = bounds_ref[i]
        before = edge <= middle
        lower_edge = jnp.where(before, jnp.maximum(lower_edge, edge), lower_edge)
        upper_edge = jnp.where(before, upper_edge, jnp.minimum(upper_edge, edge))
    return jnp.maximum(start, lower_edge), jnp.minimum(end, upper_edge)


def select_kernel(
    round_ref, pos_ref, bounds_ref, start_ref, end_ref, own_ref, other_ref,
    rounds_ref, plan_ref, full_ref, *rest, caps, blocks_dev,
):
    reach = len(caps)
    genes, half = own_ref.shape
    chosen_from = sum(cap == genes for cap in caps)
    (slots, edges), pay_refs = rest[-2:], rest[:-2]
    shape = start_ref.shape
    per_row = LANES // genes
    chips = shape[0] * per_row
    chip, core = pos_ref[0], pos_ref[1]
    turn = round_ref[0]
    low, high = window_plan(
        start_ref[...], end_ref[...], bounds_ref, bounds_ref.shape[0], chips * blocks_dev
    )
    edges[0] = low
    edges[1] = high
    at = lax.broadcasted_iota(jnp.int32, shape, 0) * per_row
    at = at + lax.broadcasted_iota(jnp.int32, shape, 1) // genes
    a = lax.broadcasted_iota(jnp.int32, (LANES, LANES), 0)
    b = lax.broadcasted_iota(jnp.int32, (LANES, LANES), 1)
    upto = ((a <= b) & (a // genes == b // genes)).astype(jnp.float32).astype(jnp.bfloat16)
    rounds = jnp.int32(0)
    for way in range(2):
        for k in range(1, reach + 1):
            to = at + (k if way == 0 else -k)
            need = (
                (low < (to + 1) * blocks_dev) & (high > to * blocks_dev)
                & (low < high) & (to >= 0) & (to < chips)
            )
            rank = jnp.dot(
                need.astype(jnp.float32).astype(jnp.bfloat16), upto,
                preferred_element_type=jnp.float32,
            ).astype(jnp.int32)
            cap = caps[k - 1]
            if cap == genes:
                which = lax.broadcasted_iota(jnp.int32, shape, 1) % genes
                slots[way * reach + k - 1] = jnp.where(need, which, -1)
                continue
            slot = rank - 1 - turn * cap
            slots[way * reach + k - 1] = jnp.where(
                need & (slot >= 0) & (slot < cap), slot, -1
            )
            rounds = jnp.maximum(rounds, (jnp.max(rank) + cap - 1) // cap)
    rounds_ref[0] = rounds

    def of_chip(ref, index, which):
        row = ref[index, pl.ds(which // per_row, 1), :]
        out = row[:, :genes]
        for part in range(1, per_row):
            out = jnp.where(
                which % per_row == part, row[:, part * genes : (part + 1) * genes], out
            )
        return out

    used = [lax.broadcasted_iota(jnp.int32, (1, genes), 1)]
    lows = [of_chip(edges, 0, chip)]
    highs = [of_chip(edges, 1, chip)]
    first = genes
    for side in range(2):
        way = core if side == 0 else 1 - core
        for k in range(1, reach + 1):
            source = chip + (2 * way - 1) * k
            valid = (source >= 0) & (source < chips)
            source = jnp.clip(source, 0, chips - 1)
            slot = of_chip(slots, way * reach + k - 1, source)
            used.append(jnp.where(valid & (slot >= 0), slot + first, -1))
            lows.append(of_chip(edges, 0, source))
            highs.append(jnp.where(valid, of_chip(edges, 1, source), 0))
            first += caps[k - 1]
    while len(used) * genes < plan_ref.shape[1]:
        used.append(jnp.full_like(used[0], -1))
        lows.append(jnp.zeros_like(used[0]))
        highs.append(jnp.zeros_like(used[0]))
    plan_ref[...] = jnp.zeros_like(plan_ref)
    for row, parts in enumerate((used, lows, highs)):
        plan_ref[pl.ds(row, 1), :] = jnp.concatenate(parts, axis=1)

    picks = []
    for k in range(chosen_from + 1, reach + 1):
        slot = of_chip(slots, core * reach + k - 1, chip)
        rows = lax.broadcasted_iota(jnp.int32, (caps[k - 1], genes), 0)
        picks.append((rows == slot).astype(jnp.float32))
    if picks:
        picks = jnp.concatenate(picks, axis=0).astype(jnp.bfloat16)
    step = 1024

    def copy(i, carry):
        cols = pl.ds(pl.multiple_of(i * step, step), step)
        late = pl.ds(pl.multiple_of(half + i * step, step), step)
        a, b = own_ref[:, cols], other_ref[:, cols]
        for part, to in ((jnp.where(core == 0, a, b), cols), (jnp.where(core == 0, b, a), late)):
            full_ref[:, to] = part
            if pay_refs:
                chosen = jnp.dot(picks, part, preferred_element_type=jnp.float32)
                chosen = chosen.astype(jnp.bfloat16)
                row = 0
                for pay in pay_refs:
                    pay[:, to] = chosen[row : row + pay.shape[0]]
                    row += pay.shape[0]
        return carry

    lax.fori_loop(0, half // step, copy, 0)


def select(turn, pos, bounds, start, end, own, other, caps, blocks_dev):
    genes, half = own.shape
    all_samples = 2 * half
    reach = len(caps)
    smem = pl.BlockSpec(memory_space=pltpu.SMEM)
    vmem = pl.BlockSpec(memory_space=pltpu.VMEM)
    width = -(-(2 * reach + 1) * genes // LANES) * LANES
    chosen = [cap for cap in caps if cap < genes]
    return pl.pallas_call(
        functools.partial(select_kernel, caps=caps, blocks_dev=blocks_dev),
        out_shape=(
            jax.ShapeDtypeStruct((1,), jnp.int32),
            jax.ShapeDtypeStruct((8, width), jnp.int32),
            jax.ShapeDtypeStruct((genes, all_samples), jnp.bfloat16),
            *[jax.ShapeDtypeStruct((cap, all_samples), jnp.bfloat16) for cap in chosen],
        ),
        in_specs=[smem, smem, smem, vmem, vmem, vmem, vmem],
        out_specs=(smem, vmem, vmem, *[vmem for _ in chosen]),
        scratch_shapes=[
            pltpu.VMEM((2 * reach,) + start.shape, jnp.int32),
            pltpu.VMEM((2,) + start.shape, jnp.int32),
        ],
        compiler_params=pltpu.CompilerParams(vmem_limit_bytes=24 * MIB),
        name="select",
    )(turn, pos, bounds, start, end, own, other)


def product_kernel(
    pos_ref, sums_own, sums_other, plan_ref, *rest, caps, labels, genes, blocks_dev
):
    reach = len(caps)
    n_in = 1 + 2 * reach
    gene_refs = rest[:n_in]
    weight_refs = rest[n_in : n_in + labels + 1]
    out_ref, power_ref, rows, total, power = rest[n_in + labels + 1 :]
    step = pl.program_id(0)
    snp_rows = sums_own.shape[1]
    depth = rows.shape[1]
    used = rows.shape[0]
    chip, core = pos_ref[0], pos_ref[1]

    @pl.when(step == 0)
    def _():
        total[...] = jnp.zeros_like(total)
        power[...] = jnp.zeros_like(power)

    at = 0
    for ref in gene_refs:
        rows[pl.ds(at, ref.shape[0]), :] = ref[...]
        at += ref.shape[0]
    for q, ref in enumerate(weight_refs):
        cols = pl.ds(q * snp_rows, ref.shape[1])
        total[pl.ds(0, used), cols] += jnp.dot(
            rows[...], ref[...], preferred_element_type=jnp.float32
        )
    kept = power[...]
    for t in range(depth // LANES):
        x = rows[pl.ds(0, genes), pl.ds(t * LANES, LANES)].astype(jnp.float32)
        kept = kept + x * x
    power[...] = kept

    @pl.when(step == pl.num_programs(0) - 1)
    def _():
        summed_up(
            chip, core, sums_own, sums_other, plan_ref, out_ref, power_ref, total, power,
            reach=reach, labels=labels, genes=genes, blocks_dev=blocks_dev,
        )


def summed_up(
    chip, core, sums_own, sums_other, plan_ref, out_ref, power_ref, total, power,
    *, reach, labels, genes, blocks_dev,
):
    snp_rows = sums_own.shape[1]
    block = SNP_BLOCK
    n_in = 1 + 2 * reach
    share_blocks = blocks_dev // 2
    sums = sums_own[...] + sums_other[...]
    cross = sums[1:2, :]
    inter = sums[2:3, :]
    inv = 1.0 / (inter - cross * (cross / sums[0:1, :]) + 0.1 * inter)

    def peak(col, inv_block):
        best = None
        for t in range(block // LANES):
            v = total[:, pl.ds(col + t * LANES, LANES)]
            v = v * v * inv_block[:, t * LANES : (t + 1) * LANES]
            best = v if best is None else jnp.maximum(best, v)
        return jnp.max(best.T, axis=0, keepdims=True)

    peaks = []
    for q in range(labels):
        for b in range(blocks_dev):
            peaks.append(peak(q * snp_rows + b * block, inv[:, b * block : (b + 1) * block]))
    for b in range(share_blocks):
        mine = inv[:, b * block : (b + 1) * block]
        late = inv[:, (share_blocks + b) * block : (share_blocks + b + 1) * block]
        peaks.append(peak(labels * snp_rows + b * block, jnp.where(core == 0, mine, late)))
    while len(peaks) % 8:
        peaks.append(jnp.zeros_like(peaks[0]))
    peaks = jnp.concatenate(peaks, axis=0)
    count = peaks.shape[0]
    terms = []
    left = peaks
    for _ in range(3):
        terms.append(left.astype(jnp.bfloat16).astype(jnp.float32))
        left = left - terms[-1]
    terms = jnp.concatenate(terms, axis=0).astype(jnp.bfloat16)
    band = plan_ref.shape[1]
    slot = plan_ref[0:1, :]
    low = plan_ref[1:2, :]
    high = plan_ref[2:3, :]
    place = lax.broadcasted_iota(jnp.int32, (total.shape[0], band), 0) == slot
    spread = jnp.dot(
        terms, place.astype(jnp.float32).astype(jnp.bfloat16),
        preferred_element_type=jnp.float32,
    )
    spread = spread[:count] + spread[count : 2 * count] + spread[2 * count :]

    def masked(row, snp_block):
        inside = (snp_block >= low) & (snp_block < high)
        return jnp.where(inside, spread[row : row + 1], 0.0)

    def highest(row, blocks, first_block):
        best = masked(row, first_block)
        for b in range(1, blocks):
            best = jnp.maximum(best, masked(row + b, first_block + b))
        return best

    out_rows = [highest(labels * blocks_dev, share_blocks, chip * blocks_dev + core * share_blocks)]
    found = [highest(q * blocks_dev, blocks_dev, chip * blocks_dev) for q in range(labels)]
    for c in range(2):
        out_rows += [jnp.where(core == c, v, 0.0) for v in found]
    while len(out_rows) % 8:
        out_rows.append(jnp.zeros_like(out_rows[0]))
    dense = jnp.concatenate(out_rows, axis=0)
    out_ref[...] = jnp.zeros_like(out_ref)
    chips = out_ref.shape[0]
    for i in range(n_in):
        if i == 0:
            target = chip
        else:
            way = core if i <= reach else 1 - core
            target = chip + (2 * way - 1) * ((i - 1) % reach + 1)

        @pl.when((target >= 0) & (target < chips))
        def _(i=i, target=target):
            out_ref[target, :, pl.ds(0, genes)] = dense[:, i * genes : (i + 1) * genes]

    powers = jnp.sum(power[...].T, axis=0, keepdims=True)
    power_ref[...] = jnp.broadcast_to(powers, power_ref.shape)


def products(pos, sums, plan, full, mine, other, weights, caps, labels, chips, blocks_dev):
    genes, all_samples = full.shape
    used = genes + 2 * sum(caps)
    padded = -(-used // LANES) * LANES
    out_rows = -(-(1 + 2 * labels) // 8) * 8
    width = sum(w.shape[1] for w in weights)
    arrays = (full, *mine, *other)

    def whole(x):
        return pl.BlockSpec(x.shape, lambda k: (0,) * len(x.shape))

    outs = (
        jax.ShapeDtypeStruct((chips, out_rows, LANES), jnp.float32),
        jax.ShapeDtypeStruct((8, genes), jnp.float32),
    )
    return pl.pallas_call(
        functools.partial(
            product_kernel, caps=caps, labels=labels, genes=genes, blocks_dev=blocks_dev
        ),
        grid=(all_samples // CHUNK,),
        out_shape=outs,
        in_specs=[
            pl.BlockSpec(memory_space=pltpu.SMEM),
            *[whole(x) for x in (*sums, plan)],
            *[pl.BlockSpec((x.shape[0], CHUNK), lambda k: (0, k)) for x in arrays],
            *[pl.BlockSpec((CHUNK, w.shape[1]), lambda k: (k, 0)) for w in weights],
        ],
        out_specs=tuple(whole(x) for x in outs),
        scratch_shapes=[
            pltpu.VMEM((used, CHUNK), jnp.bfloat16),
            pltpu.VMEM((padded, width), jnp.float32),
            pltpu.VMEM((genes, LANES), jnp.float32),
        ],
        compiler_params=pltpu.CompilerParams(vmem_limit_bytes=48 * MIB),
        cost_estimate=pl.CostEstimate(
            flops=2 * used * all_samples * width,
            bytes_accessed=2 * all_samples * (width + used),
            transcendentals=0,
        ),
        name="products",
    )(pos, *sums, plan, *arrays, *weights)


def finish_kernel(own_ref, other_ref, power_ref, out_ref, *, samples):
    best = jnp.maximum(own_ref[0], other_ref[0])
    for i in range(1, own_ref.shape[0]):
        best = jnp.maximum(best, jnp.maximum(own_ref[i], other_ref[i]))
    labels, genes = out_ref.shape
    peak = best[:labels, :genes]
    out_ref[...] = jnp.sqrt(peak / (power_ref[0:1, :] / samples + 1e-05))


def shards(genotypes, phenotypes, environment, shuffles, window_start, window_end, chrom_bounds):
    snp_rows, half = genotypes.shape
    genes = phenotypes.shape[0]
    perms = shuffles.shape[0]
    chips = lax.axis_size("genome")
    cores = lax.axis_size("sample")
    blocks_dev = snp_rows // SNP_BLOCK
    reach = (HALF_BLK + blocks_dev - 1) // blocks_dev
    all_samples = half * cores
    labels = perms // cores
    caps = tuple(min(genes, genes * 4 >> k) for k in range(1, reach + 1))
    env = environment[None]
    start = window_start.reshape(-1, LANES)
    end = window_end.reshape(-1, LANES)
    pos = jnp.stack([lax.axis_index("genome"), lax.axis_index("sample")]).astype(jnp.int32)

    def travel(k, payload):
        pairs = [(i * cores, (i + k) * cores) for i in range(chips - k)]
        pairs += [((i + k) * cores + 1, i * cores + 1) for i in range(chips - k)]
        return lax.ppermute(payload, ("genome", "sample"), pairs)

    def one_round(turn, pos):
        core = pos[1:]
        other_pheno = swapped(phenotypes)
        own_sums = local_moments(genotypes, env)
        sums = (own_sums, swapped(own_sums))
        late_geno, _ = lax.optimization_barrier((genotypes, other_pheno))
        other_geno = swapped(late_geno)
        other_env = swapped(env)
        other_shuffles = swapped(shuffles)
        rounds, plan, full, *payloads = select(
            turn, pos, chrom_bounds, start, end, phenotypes, other_pheno, caps, blocks_dev
        )
        payloads = [full] * (reach - len(payloads)) + payloads
        mine = [travel(k, x) for k, x in enumerate(payloads, 1)]
        weights = snp_side(
            core, env, other_env, *sums, shuffles, other_shuffles, genotypes, other_geno, labels
        )
        mine, weights = lax.optimization_barrier((mine, weights))
        other = [swapped(x) for x in mine]
        found, power = products(
            pos, sums, plan, full, mine, other, weights, caps, labels, chips, blocks_dev
        )
        return rounds, found, power

    rounds, found, power = one_round(jnp.zeros((1,), jnp.int32), pos)

    def more(carry):
        return carry[0] < rounds[0]

    def again(carry):
        turn, best = carry
        turns, place = lax.optimization_barrier((jnp.full((1,), turn, jnp.int32), pos))
        return turn + 1, jnp.maximum(best, one_round(turns, place)[1])

    _, found = lax.while_loop(more, again, (jnp.int32(1), found))
    gathered = lax.all_to_all(found, "genome", 0, 0, tiled=True)
    return pl.pallas_call(
        functools.partial(finish_kernel, samples=all_samples),
        out_shape=jax.ShapeDtypeStruct((perms + 1, genes), jnp.float32),
        name="finish",
    )(gathered, swapped(gathered), power)


def solution(mesh):
    placed = (
        P("genome", "sample"),
        P("genome", "sample"),
        P("sample"),
        P(None, "sample"),
        P(),
        P(),
        P(),
    )
    return jax.shard_map(
        shards, mesh=mesh, in_specs=placed, out_specs=P(None, "genome"), check_vma=False
    )
```

```python
import functools

import jax
import jax.numpy as jnp
from jax import lax
from jax.experimental import pallas as pl
from jax.experimental.pallas import tpu as pltpu
from jax.sharding import PartitionSpec as P

SNP_BLOCK = 256
HALF_BLK = 7
LANES = 128
ROWS_STEP = 16
UNROLL = 32
SIDE = 2 * LANES
CHUNK = 1024
MIB = 2**20


def passed_along(x, axis, by):
    count = lax.axis_size(axis)
    pairs = [(i, i + by) for i in range(count) if 0 <= i + by < count]
    return lax.ppermute(x, axis, pairs)


def swapped(x):
    count = lax.axis_size("sample")
    return lax.ppermute(x, "sample", [(i, (i + 1) % count) for i in range(count)])


def moments_kernel(geno_ref, env_ref, out_ref, sums):
    step = pl.program_id(0)
    snp_rows, chunk = geno_ref.shape

    @pl.when(step == 0)
    def _():
        sums[...] = jnp.zeros_like(sums)

    def add_rows(i, carry):
        first = pl.multiple_of(i * ROWS_STEP, ROWS_STEP)
        held = [sums[m, pl.ds(first, ROWS_STEP), :] for m in range(3)]
        for t in range(chunk // LANES):
            x = geno_ref[pl.ds(first, ROWS_STEP), pl.ds(t * LANES, LANES)].astype(jnp.float32)
            e = env_ref[:, pl.ds(t * LANES, LANES)]
            x = x * x
            held[0] = held[0] + x
            x = x * e
            held[1] = held[1] + x
            held[2] = held[2] + x * e
        for m in range(3):
            sums[m, pl.ds(first, ROWS_STEP), :] = held[m]
        return carry

    lax.fori_loop(0, snp_rows // ROWS_STEP, add_rows, 0, unroll=4)

    @pl.when(step == pl.num_programs(0) - 1)
    def _():
        rows = [jnp.sum(sums[m].T, axis=0, keepdims=True) for m in range(3)]
        rows.append(jnp.zeros((out_ref.shape[0] - 3, snp_rows), jnp.float32))
        out_ref[...] = jnp.concatenate(rows, axis=0)


def local_moments(geno, env):
    snp_rows, half = geno.shape
    chunk = CHUNK
    return pl.pallas_call(
        moments_kernel,
        grid=(half // chunk,),
        out_shape=jax.ShapeDtypeStruct((8, snp_rows), jnp.float32),
        in_specs=[
            pl.BlockSpec((snp_rows, chunk), lambda k: (0, k)),
            pl.BlockSpec((1, chunk), lambda k: (0, k)),
        ],
        out_specs=pl.BlockSpec((8, snp_rows), lambda k: (0, 0)),
        scratch_shapes=[pltpu.VMEM((3, snp_rows, LANES), jnp.float32)],
        compiler_params=pltpu.CompilerParams(vmem_limit_bytes=60 * MIB),
        cost_estimate=pl.CostEstimate(
            flops=5 * 10**9, bytes_accessed=2 * snp_rows * half, transcendentals=0
        ),
        name="local_moments",
    )(geno, env)


def snp_side_kernel(
    core_ref, env_own, env_other, sums_own, sums_other, shuf_own, shuf_other, own_ref, other_ref,
    *rest, labels,
):
    out_refs, scratch = rest[: labels + 1], rest[labels + 1 :]
    (
        idx, geno, table, dests, stage, first_stage, slope, idx_sems, in_sems, out_sems, first_sems,
    ) = scratch
    snp_rows, half = own_ref.shape
    all_samples = 2 * half
    chunks = all_samples // CHUNK
    words = snp_rows // LANES
    share = snp_rows // 2
    side = SIDE
    per_chunk = CHUNK // side
    core = core_ref[0]
    depth = geno.shape[0]

    def load(k):
        source = own_ref if k * CHUNK < half else other_ref
        return pltpu.make_async_copy(
            source.at[:, pl.ds((k * CHUNK) % half, CHUNK)], geno.at[k % depth],
            in_sems.at[k % depth],
        )

    def load_idx(q, h):
        source = shuf_own if h == 0 else shuf_other
        return pltpu.make_async_copy(
            source.at[core * labels + q],
            idx.at[pl.ds(q * all_samples + h * half, half)],
            idx_sems.at[2 * q + h],
        )

    def save_first(k):
        there = jnp.where(core == 0, k * CHUNK, (k * CHUNK + half) % all_samples)
        rows = pl.ds(pl.multiple_of(there, CHUNK), CHUNK)
        return pltpu.make_async_copy(
            first_stage.at[k % 2],
            out_refs[labels].at[rows],
            first_sems.at[k % 2],
        )

    def save(q, k):
        return pltpu.make_async_copy(
            stage.at[k % 2],
            out_refs[q].at[pl.ds(k * CHUNK, CHUNK)],
            out_sems.at[k % 2],
        )

    def read_rows(first):
        base = pl.multiple_of(first * words, UNROLL * words)
        return [table[pl.ds(base + u * words, words), :] for u in range(UNROLL)]

    def write_rows(q, first, held):
        for u in range(UNROLL):
            to = pl.multiple_of(idx[q * all_samples + first + u] * words, words)
            dests[q][pl.ds(to, words), :] = held[u]

    def flags(hit):
        return hit.astype(jnp.float32).astype(jnp.bfloat16)

    def narrowed(q, at):
        parts = [
            dests[q][pl.ds(pl.multiple_of((at + n * LANES) * words, LANES * words), LANES * words), :]
            for n in range(side // LANES)
        ]
        whole = jnp.concatenate(parts, axis=1).astype(jnp.bfloat16)
        return jnp.dot(apart, whole, preferred_element_type=jnp.float32)

    def put(k, at, t):
        t = t.astype(jnp.bfloat16)
        for n in range(side // LANES):
            for c in range(words):
                stage[k % 2, pl.ds(at + n * LANES, LANES), pl.ds(c * LANES, LANES)] = t[
                    c * LANES : (c + 1) * LANES, n * LANES : (n + 1) * LANES
                ]

    for k in range(depth):
        load(k).start()
    for q in range(labels):
        for h in range(2):
            load_idx(q, h).start()
    sums = sums_own[...] + sums_other[...]
    slope[...] = jnp.broadcast_to(sums[1:2, :] / sums[0:1, :], (LANES, snp_rows)).T
    row = lax.broadcasted_iota(jnp.int32, (side, side), 0)
    unit = flags(row == lax.broadcasted_iota(jnp.int32, (side, side), 1))
    square = (LANES * words, LANES * words)
    row = lax.broadcasted_iota(jnp.int32, square, 0)
    col = lax.broadcasted_iota(jnp.int32, square, 1)
    woven = flags((row % words) * LANES + row // words == col)
    apart = flags((col % words) * LANES + col // words == row)
    for q in range(labels):
        for h in range(2):
            load_idx(q, h).wait()

    for k in range(chunks):
        load(k).wait()
        if k >= 2:
            save_first(k - 2).wait()
        env_ref = env_own if k * CHUNK < half else env_other

        def turn(i, carry, k=k, env_ref=env_ref):
            at = pl.multiple_of(i * side, side)
            e = env_ref[:, pl.ds((k * CHUNK) % half + at, side)]
            behind = pl.multiple_of(jnp.maximum(k * CHUNK + at - side, 0), side)
            pieces = []
            for c in range(words):
                rows = pl.ds(c * LANES, LANES)
                x = geno[k % depth, rows, pl.ds(at, side)].astype(jnp.float32)
                r = slope[rows, :]
                a = x * (e - jnp.concatenate([r] * (side // LANES), axis=1))
                pieces.append(a.astype(jnp.bfloat16))
            across = (((1,), (1,)), ((), ()))
            wide = jnp.concatenate(
                [
                    jnp.concatenate([a[:, n * LANES : (n + 1) * LANES] for a in pieces], axis=1)
                    for n in range(side // LANES)
                ],
                axis=0,
            )
            t = lax.dot_general(woven, wide, across, preferred_element_type=jnp.float32)
            early = jnp.concatenate(pieces[: words // 2], axis=0)
            late = jnp.concatenate(pieces[words // 2 :], axis=0)
            first = lax.dot_general(
                unit, jnp.where(core == 0, early, late), across,
                preferred_element_type=jnp.float32,
            )
            for g in range(side // UNROLL):
                to = pl.multiple_of(behind + g * UNROLL, UNROLL)
                write_rows(0, to, read_rows(to))
            for n in range(side // LANES):
                start = pl.multiple_of((k * CHUNK + at + n * LANES) * words, LANES * words)
                table[pl.ds(start, LANES * words), :] = t[:, n * LANES : (n + 1) * LANES]
            first_stage[k % 2, pl.ds(at, side), :] = first.astype(jnp.bfloat16)
            return carry

        lax.fori_loop(0, per_chunk, turn, 0)
        save_first(k).start()
        if k + depth < chunks:
            load(k + depth).start()

    def last_block(i, carry):
        first = pl.multiple_of(all_samples - side + i * UNROLL, UNROLL)
        write_rows(0, first, read_rows(first))
        return carry

    lax.fori_loop(0, side // UNROLL, last_block, 0)

    count = 0
    for q in range(1, labels + 1):
        for k in range(chunks):
            if count >= 2:
                save((count - 2) // chunks, (count - 2) % chunks).wait()

            def step(i, carry, k=k, q=q):
                at = pl.multiple_of(i * side, side)
                t = narrowed(q - 1, k * CHUNK + at)
                if q < labels:
                    for g in range(side // UNROLL):
                        first = pl.multiple_of(k * CHUNK + at + g * UNROLL, UNROLL)
                        write_rows(q, first, read_rows(first))
                put(k, at, t)
                return carry

            lax.fori_loop(0, per_chunk, step, 0)
            save(q - 1, k).start()
            count += 1
    for k in range(chunks - 2, chunks):
        save_first(k).wait()
        save(labels - 1, k).wait()


def snp_side(core, env_own, env_other, sums_own, sums_other, shuf_own, shuf_other, own, other,
             labels):
    snp_rows, half = own.shape
    all_samples = 2 * half
    words = snp_rows // LANES
    widths = [snp_rows] * labels + [snp_rows // 2]
    any_spec = pl.BlockSpec(memory_space=pl.ANY)
    smem = pl.BlockSpec(memory_space=pltpu.SMEM)
    vmem = pl.BlockSpec(memory_space=pltpu.VMEM)
    return pl.pallas_call(
        functools.partial(snp_side_kernel, labels=labels),
        out_shape=[jax.ShapeDtypeStruct((all_samples, w), jnp.bfloat16) for w in widths],
        in_specs=[smem, vmem, vmem, vmem, vmem, any_spec, any_spec, any_spec, any_spec],
        out_specs=[any_spec for _ in widths],
        scratch_shapes=[
            pltpu.SMEM((labels * all_samples,), jnp.int32),
            pltpu.VMEM((2, snp_rows, CHUNK), jnp.bfloat16),
            pltpu.VMEM((all_samples * words, LANES), jnp.float32),
            [pltpu.VMEM((all_samples * words, LANES), jnp.float32) for _ in range(labels)],
            pltpu.VMEM((2, CHUNK, snp_rows), jnp.bfloat16),
            pltpu.VMEM((2, CHUNK, snp_rows // 2), jnp.bfloat16),
            pltpu.VMEM((snp_rows, LANES), jnp.float32),
            pltpu.SemaphoreType.DMA((2 * labels,)),
            pltpu.SemaphoreType.DMA((2,)),
            pltpu.SemaphoreType.DMA((2,)),
            pltpu.SemaphoreType.DMA((2,)),
        ],
        compiler_params=pltpu.CompilerParams(vmem_limit_bytes=61 * MIB),
        cost_estimate=pl.CostEstimate(
            flops=40 * 10**9, bytes_accessed=60 * 10**6, transcendentals=0
        ),
        name="snp_side",
    )(core, env_own, env_other, sums_own, sums_other, shuf_own, shuf_other, own, other)


def window_plan(start, end, bounds_ref, n_bounds, total_blocks):
    middle = (start + end - 1) // 2
    lower_edge = jnp.zeros_like(start)
    upper_edge = jnp.full_like(end, total_blocks)
    for i in range(n_bounds):
        edge = bounds_ref[i]
        before = edge <= middle
        lower_edge = jnp.where(before, jnp.maximum(lower_edge, edge), lower_edge)
        upper_edge = jnp.where(before, upper_edge, jnp.minimum(upper_edge, edge))
    return jnp.maximum(start, lower_edge), jnp.minimum(end, upper_edge)


def select_kernel(
    round_ref, pos_ref, bounds_ref, start_ref, end_ref, own_ref, other_ref,
    rounds_ref, plan_ref, full_ref, *rest, caps, blocks_dev,
):
    reach = len(caps)
    genes, half = own_ref.shape
    chosen_from = sum(cap == genes for cap in caps)
    (slots, edges), pay_refs = rest[-2:], rest[:-2]
    shape = start_ref.shape
    per_row = LANES // genes
    chips = shape[0] * per_row
    chip, core = pos_ref[0], pos_ref[1]
    turn = round_ref[0]
    low, high = window_plan(
        start_ref[...], end_ref[...], bounds_ref, bounds_ref.shape[0], chips * blocks_dev
    )
    edges[0] = low
    edges[1] = high
    at = lax.broadcasted_iota(jnp.int32, shape, 0) * per_row
    at = at + lax.broadcasted_iota(jnp.int32, shape, 1) // genes
    a = lax.broadcasted_iota(jnp.int32, (LANES, LANES), 0)
    b = lax.broadcasted_iota(jnp.int32, (LANES, LANES), 1)
    upto = ((a <= b) & (a // genes == b // genes)).astype(jnp.float32).astype(jnp.bfloat16)
    rounds = jnp.int32(0)
    for way in range(2):
        for k in range(1, reach + 1):
            to = at + (k if way == 0 else -k)
            need = (
                (low < (to + 1) * blocks_dev) & (high > to * blocks_dev)
                & (low < high) & (to >= 0) & (to < chips)
            )
            rank = jnp.dot(
                need.astype(jnp.float32).astype(jnp.bfloat16), upto,
                preferred_element_type=jnp.float32,
            ).astype(jnp.int32)
            cap = caps[k - 1]
            if cap == genes:
                which = lax.broadcasted_iota(jnp.int32, shape, 1) % genes
                slots[way * reach + k - 1] = jnp.where(need, which, -1)
                continue
            slot = rank - 1 - turn * cap
            slots[way * reach + k - 1] = jnp.where(
                need & (slot >= 0) & (slot < cap), slot, -1
            )
            rounds = jnp.maximum(rounds, (jnp.max(rank) + cap - 1) // cap)
    rounds_ref[0] = rounds

    def of_chip(ref, index, which):
        row = ref[index, pl.ds(which // per_row, 1), :]
        out = row[:, :genes]
        for part in range(1, per_row):
            out = jnp.where(
                which % per_row == part, row[:, part * genes : (part + 1) * genes], out
            )
        return out

    used = [lax.broadcasted_iota(jnp.int32, (1, genes), 1)]
    lows = [of_chip(edges, 0, chip)]
    highs = [of_chip(edges, 1, chip)]
    first = genes
    for side in range(2):
        way = core if side == 0 else 1 - core
        for k in range(1, reach + 1):
            source = chip + (2 * way - 1) * k
            valid = (source >= 0) & (source < chips)
            source = jnp.clip(source, 0, chips - 1)
            slot = of_chip(slots, way * reach + k - 1, source)
            used.append(jnp.where(valid & (slot >= 0), slot + first, -1))
            lows.append(of_chip(edges, 0, source))
            highs.append(jnp.where(valid, of_chip(edges, 1, source), 0))
            first += caps[k - 1]
    while len(used) * genes < plan_ref.shape[1]:
        used.append(jnp.full_like(used[0], -1))
        lows.append(jnp.zeros_like(used[0]))
        highs.append(jnp.zeros_like(used[0]))
    plan_ref[...] = jnp.zeros_like(plan_ref)
    for row, parts in enumerate((used, lows, highs)):
        plan_ref[pl.ds(row, 1), :] = jnp.concatenate(parts, axis=1)

    picks = []
    for k in range(chosen_from + 1, reach + 1):
        slot = of_chip(slots, core * reach + k - 1, chip)
        rows = lax.broadcasted_iota(jnp.int32, (caps[k - 1], genes), 0)
        picks.append((rows == slot).astype(jnp.float32))
    if picks:
        picks = jnp.concatenate(picks, axis=0).astype(jnp.bfloat16)
    step = 1024

    def copy(i, carry):
        cols = pl.ds(pl.multiple_of(i * step, step), step)
        late = pl.ds(pl.multiple_of(half + i * step, step), step)
        a, b = own_ref[:, cols], other_ref[:, cols]
        for part, to in ((jnp.where(core == 0, a, b), cols), (jnp.where(core == 0, b, a), late)):
            full_ref[:, to] = part
            if pay_refs:
                chosen = jnp.dot(picks, part, preferred_element_type=jnp.float32)
                chosen = chosen.astype(jnp.bfloat16)
                row = 0
                for pay in pay_refs:
                    pay[:, to] = chosen[row : row + pay.shape[0]]
                    row += pay.shape[0]
        return carry

    lax.fori_loop(0, half // step, copy, 0)


def select(turn, pos, bounds, start, end, own, other, caps, blocks_dev):
    genes, half = own.shape
    all_samples = 2 * half
    reach = len(caps)
    smem = pl.BlockSpec(memory_space=pltpu.SMEM)
    vmem = pl.BlockSpec(memory_space=pltpu.VMEM)
    width = -(-(2 * reach + 1) * genes // LANES) * LANES
    chosen = [cap for cap in caps if cap < genes]
    return pl.pallas_call(
        functools.partial(select_kernel, caps=caps, blocks_dev=blocks_dev),
        out_shape=(
            jax.ShapeDtypeStruct((1,), jnp.int32),
            jax.ShapeDtypeStruct((8, width), jnp.int32),
            jax.ShapeDtypeStruct((genes, all_samples), jnp.bfloat16),
            *[jax.ShapeDtypeStruct((cap, all_samples), jnp.bfloat16) for cap in chosen],
        ),
        in_specs=[smem, smem, smem, vmem, vmem, vmem, vmem],
        out_specs=(smem, vmem, vmem, *[vmem for _ in chosen]),
        scratch_shapes=[
            pltpu.VMEM((2 * reach,) + start.shape, jnp.int32),
            pltpu.VMEM((2,) + start.shape, jnp.int32),
        ],
        compiler_params=pltpu.CompilerParams(vmem_limit_bytes=24 * MIB),
        name="select",
    )(turn, pos, bounds, start, end, own, other)


def product_kernel(
    pos_ref, sums_own, sums_other, plan_ref, *rest, caps, labels, genes, blocks_dev
):
    reach = len(caps)
    n_in = 1 + 2 * reach
    gene_refs = rest[:n_in]
    weight_refs = rest[n_in : n_in + labels + 1]
    out_ref, power_ref, rows, total, power = rest[n_in + labels + 1 :]
    step = pl.program_id(0)
    snp_rows = sums_own.shape[1]
    depth = rows.shape[1]
    used = rows.shape[0]
    chip, core = pos_ref[0], pos_ref[1]

    @pl.when(step == 0)
    def _():
        total[...] = jnp.zeros_like(total)
        power[...] = jnp.zeros_like(power)

    at = 0
    for ref in gene_refs:
        rows[pl.ds(at, ref.shape[0]), :] = ref[...]
        at += ref.shape[0]
    for q, ref in enumerate(weight_refs):
        cols = pl.ds(q * snp_rows, ref.shape[1])
        total[pl.ds(0, used), cols] += jnp.dot(
            rows[...], ref[...], preferred_element_type=jnp.float32
        )
    kept = power[...]
    for t in range(depth // LANES):
        x = rows[pl.ds(0, genes), pl.ds(t * LANES, LANES)].astype(jnp.float32)
        kept = kept + x * x
    power[...] = kept

    @pl.when(step == pl.num_programs(0) - 1)
    def _():
        summed_up(
            chip, core, sums_own, sums_other, plan_ref, out_ref, power_ref, total, power,
            reach=reach, labels=labels, genes=genes, blocks_dev=blocks_dev,
        )


def summed_up(
    chip, core, sums_own, sums_other, plan_ref, out_ref, power_ref, total, power,
    *, reach, labels, genes, blocks_dev,
):
    snp_rows = sums_own.shape[1]
    block = SNP_BLOCK
    n_in = 1 + 2 * reach
    share_blocks = blocks_dev // 2
    sums = sums_own[...] + sums_other[...]
    cross = sums[1:2, :]
    inter = sums[2:3, :]
    inv = 1.0 / (inter - cross * (cross / sums[0:1, :]) + 0.1 * inter)

    def peak(col, inv_block):
        best = None
        for t in range(block // LANES):
            v = total[:, pl.ds(col + t * LANES, LANES)]
            v = v * v * inv_block[:, t * LANES : (t + 1) * LANES]
            best = v if best is None else jnp.maximum(best, v)
        return jnp.max(best.T, axis=0, keepdims=True)

    peaks = []
    for q in range(labels):
        for b in range(blocks_dev):
            peaks.append(peak(q * snp_rows + b * block, inv[:, b * block : (b + 1) * block]))
    for b in range(share_blocks):
        mine = inv[:, b * block : (b + 1) * block]
        late = inv[:, (share_blocks + b) * block : (share_blocks + b + 1) * block]
        peaks.append(peak(labels * snp_rows + b * block, jnp.where(core == 0, mine, late)))
    while len(peaks) % 8:
        peaks.append(jnp.zeros_like(peaks[0]))
    peaks = jnp.concatenate(peaks, axis=0)
    count = peaks.shape[0]
    terms = []
    left = peaks
    for _ in range(3):
        terms.append(left.astype(jnp.bfloat16).astype(jnp.float32))
        left = left - terms[-1]
    terms = jnp.concatenate(terms, axis=0).astype(jnp.bfloat16)
    band = plan_ref.shape[1]
    slot = plan_ref[0:1, :]
    low = plan_ref[1:2, :]
    high = plan_ref[2:3, :]
    place = lax.broadcasted_iota(jnp.int32, (total.shape[0], band), 0) == slot
    spread = jnp.dot(
        terms, place.astype(jnp.float32).astype(jnp.bfloat16),
        preferred_element_type=jnp.float32,
    )
    spread = spread[:count] + spread[count : 2 * count] + spread[2 * count :]

    def masked(row, snp_block):
        inside = (snp_block >= low) & (snp_block < high)
        return jnp.where(inside, spread[row : row + 1], 0.0)

    def highest(row, blocks, first_block):
        best = masked(row, first_block)
        for b in range(1, blocks):
            best = jnp.maximum(best, masked(row + b, first_block + b))
        return best

    out_rows = [highest(labels * blocks_dev, share_blocks, chip * blocks_dev + core * share_blocks)]
    found = [highest(q * blocks_dev, blocks_dev, chip * blocks_dev) for q in range(labels)]
    for c in range(2):
        out_rows += [jnp.where(core == c, v, 0.0) for v in found]
    while len(out_rows) % 8:
        out_rows.append(jnp.zeros_like(out_rows[0]))
    dense = jnp.concatenate(out_rows, axis=0)
    out_ref[...] = jnp.zeros_like(out_ref)
    chips = out_ref.shape[0]
    for i in range(n_in):
        if i == 0:
            target = chip
        else:
            way = core if i <= reach else 1 - core
            target = chip + (2 * way - 1) * ((i - 1) % reach + 1)

        @pl.when((target >= 0) & (target < chips))
        def _(i=i, target=target):
            out_ref[target, :, pl.ds(0, genes)] = dense[:, i * genes : (i + 1) * genes]

    powers = jnp.sum(power[...].T, axis=0, keepdims=True)
    power_ref[...] = jnp.broadcast_to(powers, power_ref.shape)


def products(pos, sums, plan, full, mine, other, weights, caps, labels, chips, blocks_dev):
    genes, all_samples = full.shape
    used = genes + 2 * sum(caps)
    padded = -(-used // LANES) * LANES
    out_rows = -(-(1 + 2 * labels) // 8) * 8
    width = sum(w.shape[1] for w in weights)
    arrays = (full, *mine, *other)

    def whole(x):
        return pl.BlockSpec(x.shape, lambda k: (0,) * len(x.shape))

    outs = (
        jax.ShapeDtypeStruct((chips, out_rows, LANES), jnp.float32),
        jax.ShapeDtypeStruct((8, genes), jnp.float32),
    )
    return pl.pallas_call(
        functools.partial(
            product_kernel, caps=caps, labels=labels, genes=genes, blocks_dev=blocks_dev
        ),
        grid=(all_samples // CHUNK,),
        out_shape=outs,
        in_specs=[
            pl.BlockSpec(memory_space=pltpu.SMEM),
            *[whole(x) for x in (*sums, plan)],
            *[pl.BlockSpec((x.shape[0], CHUNK), lambda k: (0, k)) for x in arrays],
            *[pl.BlockSpec((CHUNK, w.shape[1]), lambda k: (k, 0)) for w in weights],
        ],
        out_specs=tuple(whole(x) for x in outs),
        scratch_shapes=[
            pltpu.VMEM((used, CHUNK), jnp.bfloat16),
            pltpu.VMEM((padded, width), jnp.float32),
            pltpu.VMEM((genes, LANES), jnp.float32),
        ],
        compiler_params=pltpu.CompilerParams(vmem_limit_bytes=48 * MIB),
        cost_estimate=pl.CostEstimate(
            flops=2 * used * all_samples * width,
            bytes_accessed=2 * all_samples * (width + used),
            transcendentals=0,
        ),
        name="products",
    )(pos, *sums, plan, *arrays, *weights)


def finish_kernel(own_ref, other_ref, power_ref, out_ref, *, samples):
    best = jnp.maximum(own_ref[0], other_ref[0])
    for i in range(1, own_ref.shape[0]):
        best = jnp.maximum(best, jnp.maximum(own_ref[i], other_ref[i]))
    labels, genes = out_ref.shape
    peak = best[:labels, :genes]
    out_ref[...] = jnp.sqrt(peak / (power_ref[0:1, :] / samples + 1e-05))


def shards(genotypes, phenotypes, environment, shuffles, window_start, window_end, chrom_bounds):
    snp_rows, half = genotypes.shape
    genes = phenotypes.shape[0]
    perms = shuffles.shape[0]
    chips = lax.axis_size("genome")
    cores = lax.axis_size("sample")
    blocks_dev = snp_rows // SNP_BLOCK
    reach = (HALF_BLK + blocks_dev - 1) // blocks_dev
    all_samples = half * cores
    labels = perms // cores
    caps = tuple(min(genes, genes * 4 >> k) for k in range(1, reach + 1))
    env = environment[None]
    start = window_start.reshape(-1, LANES)
    end = window_end.reshape(-1, LANES)
    pos = jnp.stack([lax.axis_index("genome"), lax.axis_index("sample")]).astype(jnp.int32)

    def travel(k, payload):
        pairs = [(i * cores, (i + k) * cores) for i in range(chips - k)]
        pairs += [((i + k) * cores + 1, i * cores + 1) for i in range(chips - k)]
        return lax.ppermute(payload, ("genome", "sample"), pairs)

    def one_round(turn, pos):
        core = pos[1:]
        other_pheno = swapped(phenotypes)
        own_sums = local_moments(genotypes, env)
        sums = (own_sums, swapped(own_sums))
        late_geno, _ = lax.optimization_barrier((genotypes, other_pheno))
        other_geno = swapped(late_geno)
        other_env = swapped(env)
        other_shuffles = swapped(shuffles)
        rounds, plan, full, *payloads = select(
            turn, pos, chrom_bounds, start, end, phenotypes, other_pheno, caps, blocks_dev
        )
        payloads = [full] * (reach - len(payloads)) + payloads
        mine = [travel(k, x) for k, x in enumerate(payloads, 1)]
        weights = snp_side(
            core, env, other_env, *sums, shuffles, other_shuffles, genotypes, other_geno, labels
        )
        mine, weights = lax.optimization_barrier((mine, weights))
        other = [swapped(x) for x in mine]
        found, power = products(
            pos, sums, plan, full, mine, other, weights, caps, labels, chips, blocks_dev
        )
        return rounds, found, power

    rounds, found, power = one_round(jnp.zeros((1,), jnp.int32), pos)

    def more(carry):
        return carry[0] < rounds[0]

    def again(carry):
        turn, best = carry
        turns, place = lax.optimization_barrier((jnp.full((1,), turn, jnp.int32), pos))
        return turn + 1, jnp.maximum(best, one_round(turns, place)[1])

    _, found = lax.while_loop(more, again, (jnp.int32(1), found))
    gathered = lax.all_to_all(found, "genome", 0, 0, tiled=True)
    return pl.pallas_call(
        functools.partial(finish_kernel, samples=all_samples),
        out_shape=jax.ShapeDtypeStruct((perms + 1, genes), jnp.float32),
        name="finish",
    )(gathered, swapped(gathered), power)


def solution(mesh):
    placed = (
        P("genome", "sample"),
        P("genome", "sample"),
        P("sample"),
        P(None, "sample"),
        P(),
        P(),
        P(),
    )
    return jax.shard_map(
        shards, mesh=mesh, in_specs=placed, out_specs=P(None, "genome"), check_vma=False
    )
```

```python
import functools

import jax
import jax.numpy as jnp
from jax import lax
from jax.experimental import pallas as pl
from jax.experimental.pallas import tpu as pltpu
from jax.sharding import PartitionSpec as P

SNP_BLOCK = 256
HALF_BLK = 7
LANES = 128
ROWS_STEP = 16
UNROLL = 32
SLOT = 8
SIDE = 2 * LANES
CHUNK = 1024
MIB = 2**20


def passed_along(x, axis, by):
    count = lax.axis_size(axis)
    pairs = [(i, i + by) for i in range(count) if 0 <= i + by < count]
    return lax.ppermute(x, axis, pairs)


def swapped(x):
    count = lax.axis_size("sample")
    return lax.ppermute(x, "sample", [(i, (i + 1) % count) for i in range(count)])


def moments_kernel(geno_ref, env_ref, out_ref, sums):
    step = pl.program_id(0)
    snp_rows, chunk = geno_ref.shape

    @pl.when(step == 0)
    def _():
        sums[...] = jnp.zeros_like(sums)

    def add_rows(i, carry):
        first = pl.multiple_of(i * ROWS_STEP, ROWS_STEP)
        held = [sums[m, pl.ds(first, ROWS_STEP), :] for m in range(3)]
        for t in range(chunk // LANES):
            x = geno_ref[pl.ds(first, ROWS_STEP), pl.ds(t * LANES, LANES)].astype(jnp.float32)
            e = env_ref[:, pl.ds(t * LANES, LANES)]
            x = x * x
            held[0] = held[0] + x
            x = x * e
            held[1] = held[1] + x
            held[2] = held[2] + x * e
        for m in range(3):
            sums[m, pl.ds(first, ROWS_STEP), :] = held[m]
        return carry

    lax.fori_loop(0, snp_rows // ROWS_STEP, add_rows, 0, unroll=8)

    @pl.when(step == pl.num_programs(0) - 1)
    def _():
        rows = [jnp.sum(sums[m].T, axis=0, keepdims=True) for m in range(3)]
        rows.append(jnp.zeros((out_ref.shape[0] - 3, snp_rows), jnp.float32))
        out_ref[...] = jnp.concatenate(rows, axis=0)


def local_moments(geno, env):
    snp_rows, half = geno.shape
    chunk = CHUNK
    return pl.pallas_call(
        moments_kernel,
        grid=(half // chunk,),
        out_shape=jax.ShapeDtypeStruct((8, snp_rows), jnp.float32),
        in_specs=[
            pl.BlockSpec((snp_rows, chunk), lambda k: (0, k)),
            pl.BlockSpec((1, chunk), lambda k: (0, k)),
        ],
        out_specs=pl.BlockSpec((8, snp_rows), lambda k: (0, 0)),
        scratch_shapes=[pltpu.VMEM((3, snp_rows, LANES), jnp.float32)],
        compiler_params=pltpu.CompilerParams(vmem_limit_bytes=60 * MIB),
        cost_estimate=pl.CostEstimate(
            flops=10**6, bytes_accessed=10**6, transcendentals=0
        ),
        name="local_moments",
    )(geno, env)


def snp_side_kernel(
    core_ref, env_own, env_other, sums_own, sums_other, shuf_own, shuf_other, own_ref, other_ref,
    *rest, labels,
):
    out_refs, scratch = rest[: labels + 1], rest[labels + 1 :]
    (
        idx, geno, table, dest, stage, first_stage, slope, idx_sems, in_sems, out_sems, first_sems,
    ) = scratch
    snp_rows, half = own_ref.shape
    all_samples = 2 * half
    chunks = all_samples // CHUNK
    words = snp_rows // LANES
    share = snp_rows // 2
    side = SIDE
    per_chunk = CHUNK // side
    core = core_ref[0]
    depth = geno.shape[0]

    def load(k):
        source = own_ref if k * CHUNK < half else other_ref
        return pltpu.make_async_copy(
            source.at[:, pl.ds((k * CHUNK) % half, CHUNK)], geno.at[k % depth],
            in_sems.at[k % depth],
        )

    def load_idx(q, h):
        source = shuf_own if h == 0 else shuf_other
        return pltpu.make_async_copy(
            source.at[core * labels + q],
            idx.at[pl.ds(q * all_samples + h * half, half)],
            idx_sems.at[2 * q + h],
        )

    def save_first(k):
        there = jnp.where(core == 0, k * CHUNK, (k * CHUNK + half) % all_samples)
        rows = pl.ds(pl.multiple_of(there, CHUNK), CHUNK)
        return pltpu.make_async_copy(
            first_stage.at[k % 2, :, pl.ds(pl.multiple_of(core * share, share), share)],
            out_refs[labels].at[rows],
            first_sems.at[k % 2],
        )

    def save(q, k):
        return pltpu.make_async_copy(
            stage.at[k % 2],
            out_refs[q].at[pl.ds(k * CHUNK, CHUNK)],
            out_sems.at[k % 2],
        )

    def read_rows(first):
        base = pl.multiple_of(first * words, UNROLL * words)
        return [table[pl.ds(base + u * SLOT, SLOT), :] for u in range(UNROLL * words // SLOT)]

    def write_rows(q, first, held):
        for u in range(UNROLL):
            to = pl.multiple_of(idx[q * all_samples + first + u] * SLOT, SLOT)
            rows = held[u * words // SLOT]
            turned = (u * words) % SLOT
            dest[pl.ds(to, SLOT), :] = pltpu.roll(rows, SLOT - turned, 0) if turned else rows

    def narrowed(at, rows):
        return [
            dest[pl.ds(at * SLOT + c, rows, stride=SLOT), :].astype(jnp.bfloat16)
            for c in range(words)
        ]

    for k in range(depth):
        load(k).start()
    for q in range(labels):
        for h in range(2):
            load_idx(q, h).start()
    sums = sums_own[...] + sums_other[...]
    slope[...] = jnp.broadcast_to(sums[1:2, :] / sums[0:1, :], (LANES, snp_rows)).T
    unit = (
        lax.broadcasted_iota(jnp.int32, (side, side), 0)
        == lax.broadcasted_iota(jnp.int32, (side, side), 1)
    ).astype(jnp.bfloat16)
    for q in range(labels):
        for h in range(2):
            load_idx(q, h).wait()

    groups = side // UNROLL // words
    for k in range(chunks):
        load(k).wait()
        if k >= 2:
            save_first(k - 2).wait()
        env_ref = env_own if k * CHUNK < half else env_other

        def turn(i, carry, k=k, env_ref=env_ref):
            at = pl.multiple_of(i * side, side)
            e = env_ref[:, pl.ds((k * CHUNK) % half + at, side)]
            behind = pl.multiple_of(jnp.maximum(k * CHUNK + at - side, 0), side)
            for c in range(words):
                rows = pl.ds(c * LANES, LANES)
                x = geno[k % depth, rows, pl.ds(at, side)].astype(jnp.float32)
                r = slope[rows, :]
                a = x * (e - jnp.concatenate([r] * (side // LANES), axis=1))
                t = lax.dot_general(
                    unit, a.astype(jnp.bfloat16), (((1,), (1,)), ((), ())),
                    preferred_element_type=jnp.float32,
                )
                for g in range(groups):
                    first = pl.multiple_of(behind + (c * groups + g) * UNROLL, UNROLL)
                    write_rows(0, first, read_rows(first))
                table[pl.ds((k * CHUNK + at) * words + c, side, stride=words), :] = t
                first_stage[k % 2, pl.ds(at, side), pl.ds(c * LANES, LANES)] = t.astype(
                    jnp.bfloat16
                )
            return carry

        lax.fori_loop(0, per_chunk, turn, 0)
        save_first(k).start()
        if k + depth < chunks:
            load(k + depth).start()

    def last_block(i, carry):
        first = pl.multiple_of(all_samples - side + i * UNROLL, UNROLL)
        write_rows(0, first, read_rows(first))
        return carry

    lax.fori_loop(0, side // UNROLL, last_block, 0)
    for q in range(labels):
        if q > 0:

            def scatter(i, carry, q=q):
                first = pl.multiple_of(i * UNROLL, UNROLL)
                write_rows(q, first, read_rows(first))
                return carry

            lax.fori_loop(0, all_samples // UNROLL, scatter, 0)
        for k in range(chunks):
            if q * chunks + k >= 2:
                save((q * chunks + k - 2) // chunks, (k - 2) % chunks).wait()

            def wide(i, carry, k=k):
                at = pl.multiple_of(i * side, side)
                parts = narrowed(k * CHUNK + at, side)
                for c in range(words):
                    stage[k % 2, pl.ds(at, side), pl.ds(c * LANES, LANES)] = parts[c]
                return carry

            lax.fori_loop(0, CHUNK // side, wide, 0)
            save(q, k).start()
    for k in range(chunks - 2, chunks):
        save_first(k).wait()
        save(labels - 1, k).wait()


def snp_side(core, env_own, env_other, sums_own, sums_other, shuf_own, shuf_other, own, other,
             labels):
    snp_rows, half = own.shape
    all_samples = 2 * half
    words = snp_rows // LANES
    widths = [snp_rows] * labels + [snp_rows // 2]
    any_spec = pl.BlockSpec(memory_space=pl.ANY)
    smem = pl.BlockSpec(memory_space=pltpu.SMEM)
    vmem = pl.BlockSpec(memory_space=pltpu.VMEM)
    return pl.pallas_call(
        functools.partial(snp_side_kernel, labels=labels),
        out_shape=[jax.ShapeDtypeStruct((all_samples, w), jnp.bfloat16) for w in widths],
        in_specs=[smem, vmem, vmem, vmem, vmem, any_spec, any_spec, any_spec, any_spec],
        out_specs=[any_spec for _ in widths],
        scratch_shapes=[
            pltpu.SMEM((labels * all_samples,), jnp.int32),
            pltpu.VMEM((2, snp_rows, CHUNK), jnp.bfloat16),
            pltpu.VMEM((all_samples * words, LANES), jnp.float32),
            pltpu.VMEM((all_samples * SLOT, LANES), jnp.float32),
            pltpu.VMEM((2, CHUNK, snp_rows), jnp.bfloat16),
            pltpu.VMEM((2, CHUNK, snp_rows), jnp.bfloat16),
            pltpu.VMEM((snp_rows, LANES), jnp.float32),
            pltpu.SemaphoreType.DMA((2 * labels,)),
            pltpu.SemaphoreType.DMA((2,)),
            pltpu.SemaphoreType.DMA((2,)),
            pltpu.SemaphoreType.DMA((2,)),
        ],
        compiler_params=pltpu.CompilerParams(vmem_limit_bytes=61 * MIB),
        cost_estimate=pl.CostEstimate(
            flops=40 * 10**9, bytes_accessed=60 * 10**6, transcendentals=0
        ),
        name="snp_side",
    )(core, env_own, env_other, sums_own, sums_other, shuf_own, shuf_other, own, other)


def window_plan(start, end, bounds_ref, n_bounds, total_blocks):
    middle = (start + end - 1) // 2
    lower_edge = jnp.zeros_like(start)
    upper_edge = jnp.full_like(end, total_blocks)
    for i in range(n_bounds):
        edge = bounds_ref[i]
        before = edge <= middle
        lower_edge = jnp.where(before, jnp.maximum(lower_edge, edge), lower_edge)
        upper_edge = jnp.where(before, upper_edge, jnp.minimum(upper_edge, edge))
    return jnp.maximum(start, lower_edge), jnp.minimum(end, upper_edge)


def select_kernel(
    round_ref, pos_ref, bounds_ref, start_ref, end_ref, own_ref, other_ref,
    rounds_ref, plan_ref, full_ref, *rest, caps, blocks_dev,
):
    reach = len(caps)
    genes, half = own_ref.shape
    chosen_from = sum(cap == genes for cap in caps)
    (slots, edges), pay_refs = rest[-2:], rest[:-2]
    shape = start_ref.shape
    per_row = LANES // genes
    chips = shape[0] * per_row
    chip, core = pos_ref[0], pos_ref[1]
    turn = round_ref[0]
    low, high = window_plan(
        start_ref[...], end_ref[...], bounds_ref, bounds_ref.shape[0], chips * blocks_dev
    )
    edges[0] = low
    edges[1] = high
    at = lax.broadcasted_iota(jnp.int32, shape, 0) * per_row
    at = at + lax.broadcasted_iota(jnp.int32, shape, 1) // genes
    a = lax.broadcasted_iota(jnp.int32, (LANES, LANES), 0)
    b = lax.broadcasted_iota(jnp.int32, (LANES, LANES), 1)
    upto = ((a <= b) & (a // genes == b // genes)).astype(jnp.float32).astype(jnp.bfloat16)
    rounds = jnp.int32(0)
    for way in range(2):
        for k in range(1, reach + 1):
            to = at + (k if way == 0 else -k)
            need = (
                (low < (to + 1) * blocks_dev) & (high > to * blocks_dev)
                & (low < high) & (to >= 0) & (to < chips)
            )
            rank = jnp.dot(
                need.astype(jnp.float32).astype(jnp.bfloat16), upto,
                preferred_element_type=jnp.float32,
            ).astype(jnp.int32)
            cap = caps[k - 1]
            if cap == genes:
                which = lax.broadcasted_iota(jnp.int32, shape, 1) % genes
                slots[way * reach + k - 1] = jnp.where(need, which, -1)
                continue
            slot = rank - 1 - turn * cap
            slots[way * reach + k - 1] = jnp.where(
                need & (slot >= 0) & (slot < cap), slot, -1
            )
            rounds = jnp.maximum(rounds, (jnp.max(rank) + cap - 1) // cap)
    rounds_ref[0] = rounds

    def of_chip(ref, index, which):
        row = ref[index, pl.ds(which // per_row, 1), :]
        out = row[:, :genes]
        for part in range(1, per_row):
            out = jnp.where(
                which % per_row == part, row[:, part * genes : (part + 1) * genes], out
            )
        return out

    used = [lax.broadcasted_iota(jnp.int32, (1, genes), 1)]
    lows = [of_chip(edges, 0, chip)]
    highs = [of_chip(edges, 1, chip)]
    first = genes
    for side in range(2):
        way = core if side == 0 else 1 - core
        for k in range(1, reach + 1):
            source = chip + (2 * way - 1) * k
            valid = (source >= 0) & (source < chips)
            source = jnp.clip(source, 0, chips - 1)
            slot = of_chip(slots, way * reach + k - 1, source)
            used.append(jnp.where(valid & (slot >= 0), slot + first, -1))
            lows.append(of_chip(edges, 0, source))
            highs.append(jnp.where(valid, of_chip(edges, 1, source), 0))
            first += caps[k - 1]
    while len(used) * genes < plan_ref.shape[1]:
        used.append(jnp.full_like(used[0], -1))
        lows.append(jnp.zeros_like(used[0]))
        highs.append(jnp.zeros_like(used[0]))
    plan_ref[...] = jnp.zeros_like(plan_ref)
    for row, parts in enumerate((used, lows, highs)):
        plan_ref[pl.ds(row, 1), :] = jnp.concatenate(parts, axis=1)

    picks = []
    for k in range(chosen_from + 1, reach + 1):
        slot = of_chip(slots, core * reach + k - 1, chip)
        rows = lax.broadcasted_iota(jnp.int32, (caps[k - 1], genes), 0)
        picks.append((rows == slot).astype(jnp.float32))
    if picks:
        picks = jnp.concatenate(picks, axis=0).astype(jnp.bfloat16)
    step = 1024

    def copy(i, carry):
        cols = pl.ds(pl.multiple_of(i * step, step), step)
        late = pl.ds(pl.multiple_of(half + i * step, step), step)
        a, b = own_ref[:, cols], other_ref[:, cols]
        for part, to in ((jnp.where(core == 0, a, b), cols), (jnp.where(core == 0, b, a), late)):
            full_ref[:, to] = part
            if pay_refs:
                chosen = jnp.dot(picks, part, preferred_element_type=jnp.float32)
                chosen = chosen.astype(jnp.bfloat16)
                row = 0
                for pay in pay_refs:
                    pay[:, to] = chosen[row : row + pay.shape[0]]
                    row += pay.shape[0]
        return carry

    lax.fori_loop(0, half // step, copy, 0)


def select(turn, pos, bounds, start, end, own, other, caps, blocks_dev):
    genes, half = own.shape
    all_samples = 2 * half
    reach = len(caps)
    smem = pl.BlockSpec(memory_space=pltpu.SMEM)
    vmem = pl.BlockSpec(memory_space=pltpu.VMEM)
    width = -(-(2 * reach + 1) * genes // LANES) * LANES
    chosen = [cap for cap in caps if cap < genes]
    return pl.pallas_call(
        functools.partial(select_kernel, caps=caps, blocks_dev=blocks_dev),
        out_shape=(
            jax.ShapeDtypeStruct((1,), jnp.int32),
            jax.ShapeDtypeStruct((8, width), jnp.int32),
            jax.ShapeDtypeStruct((genes, all_samples), jnp.bfloat16),
            *[jax.ShapeDtypeStruct((cap, all_samples), jnp.bfloat16) for cap in chosen],
        ),
        in_specs=[smem, smem, smem, vmem, vmem, vmem, vmem],
        out_specs=(smem, vmem, vmem, *[vmem for _ in chosen]),
        scratch_shapes=[
            pltpu.VMEM((2 * reach,) + start.shape, jnp.int32),
            pltpu.VMEM((2,) + start.shape, jnp.int32),
        ],
        compiler_params=pltpu.CompilerParams(vmem_limit_bytes=24 * MIB),
        name="select",
    )(turn, pos, bounds, start, end, own, other)


def product_kernel(
    pos_ref, sums_own, sums_other, plan_ref, *rest, caps, labels, genes, blocks_dev
):
    reach = len(caps)
    n_in = 1 + 2 * reach
    gene_refs = rest[:n_in]
    weight_refs = rest[n_in : n_in + labels + 1]
    out_ref, power_ref, rows, total, power = rest[n_in + labels + 1 :]
    step = pl.program_id(0)
    snp_rows = sums_own.shape[1]
    depth = rows.shape[1]
    used = rows.shape[0]
    chip, core = pos_ref[0], pos_ref[1]

    @pl.when(step == 0)
    def _():
        total[...] = jnp.zeros_like(total)
        power[...] = jnp.zeros_like(power)

    at = 0
    for ref in gene_refs:
        rows[pl.ds(at, ref.shape[0]), :] = ref[...]
        at += ref.shape[0]
    for q, ref in enumerate(weight_refs):
        cols = pl.ds(q * snp_rows, ref.shape[1])
        total[pl.ds(0, used), cols] += jnp.dot(
            rows[...], ref[...], preferred_element_type=jnp.float32
        )
    kept = power[...]
    for t in range(depth // LANES):
        x = rows[pl.ds(0, genes), pl.ds(t * LANES, LANES)].astype(jnp.float32)
        kept = kept + x * x
    power[...] = kept

    @pl.when(step == pl.num_programs(0) - 1)
    def _():
        summed_up(
            chip, core, sums_own, sums_other, plan_ref, out_ref, power_ref, total, power,
            reach=reach, labels=labels, genes=genes, blocks_dev=blocks_dev,
        )


def summed_up(
    chip, core, sums_own, sums_other, plan_ref, out_ref, power_ref, total, power,
    *, reach, labels, genes, blocks_dev,
):
    snp_rows = sums_own.shape[1]
    block = SNP_BLOCK
    n_in = 1 + 2 * reach
    share_blocks = blocks_dev // 2
    sums = sums_own[...] + sums_other[...]
    cross = sums[1:2, :]
    inter = sums[2:3, :]
    inv = 1.0 / (inter - cross * (cross / sums[0:1, :]) + 0.1 * inter)

    def peak(col, inv_block):
        best = None
        for t in range(block // LANES):
            v = total[:, pl.ds(col + t * LANES, LANES)]
            v = v * v * inv_block[:, t * LANES : (t + 1) * LANES]
            best = v if best is None else jnp.maximum(best, v)
        return jnp.max(best.T, axis=0, keepdims=True)

    peaks = []
    for q in range(labels):
        for b in range(blocks_dev):
            peaks.append(peak(q * snp_rows + b * block, inv[:, b * block : (b + 1) * block]))
    for b in range(share_blocks):
        mine = inv[:, b * block : (b + 1) * block]
        late = inv[:, (share_blocks + b) * block : (share_blocks + b + 1) * block]
        peaks.append(peak(labels * snp_rows + b * block, jnp.where(core == 0, mine, late)))
    while len(peaks) % 8:
        peaks.append(jnp.zeros_like(peaks[0]))
    peaks = jnp.concatenate(peaks, axis=0)
    count = peaks.shape[0]
    terms = []
    left = peaks
    for _ in range(3):
        terms.append(left.astype(jnp.bfloat16).astype(jnp.float32))
        left = left - terms[-1]
    terms = jnp.concatenate(terms, axis=0).astype(jnp.bfloat16)
    band = plan_ref.shape[1]
    slot = plan_ref[0:1, :]
    low = plan_ref[1:2, :]
    high = plan_ref[2:3, :]
    place = lax.broadcasted_iota(jnp.int32, (total.shape[0], band), 0) == slot
    spread = jnp.dot(
        terms, place.astype(jnp.float32).astype(jnp.bfloat16),
        preferred_element_type=jnp.float32,
    )
    spread = spread[:count] + spread[count : 2 * count] + spread[2 * count :]

    def masked(row, snp_block):
        inside = (snp_block >= low) & (snp_block < high)
        return jnp.where(inside, spread[row : row + 1], 0.0)

    def highest(row, blocks, first_block):
        best = masked(row, first_block)
        for b in range(1, blocks):
            best = jnp.maximum(best, masked(row + b, first_block + b))
        return best

    out_rows = [highest(labels * blocks_dev, share_blocks, chip * blocks_dev + core * share_blocks)]
    found = [highest(q * blocks_dev, blocks_dev, chip * blocks_dev) for q in range(labels)]
    for c in range(2):
        out_rows += [jnp.where(core == c, v, 0.0) for v in found]
    while len(out_rows) % 8:
        out_rows.append(jnp.zeros_like(out_rows[0]))
    dense = jnp.concatenate(out_rows, axis=0)
    out_ref[...] = jnp.zeros_like(out_ref)
    chips = out_ref.shape[0]
    for i in range(n_in):
        if i == 0:
            target = chip
        else:
            way = core if i <= reach else 1 - core
            target = chip + (2 * way - 1) * ((i - 1) % reach + 1)

        @pl.when((target >= 0) & (target < chips))
        def _(i=i, target=target):
            out_ref[target, :, pl.ds(0, genes)] = dense[:, i * genes : (i + 1) * genes]

    powers = jnp.sum(power[...].T, axis=0, keepdims=True)
    power_ref[...] = jnp.broadcast_to(powers, power_ref.shape)


def products(pos, sums, plan, full, mine, other, weights, caps, labels, chips, blocks_dev):
    genes, all_samples = full.shape
    used = genes + 2 * sum(caps)
    padded = -(-used // LANES) * LANES
    out_rows = -(-(1 + 2 * labels) // 8) * 8
    width = sum(w.shape[1] for w in weights)
    arrays = (full, *mine, *other)

    def whole(x):
        return pl.BlockSpec(x.shape, lambda k: (0,) * len(x.shape))

    outs = (
        jax.ShapeDtypeStruct((chips, out_rows, LANES), jnp.float32),
        jax.ShapeDtypeStruct((8, genes), jnp.float32),
    )
    return pl.pallas_call(
        functools.partial(
            product_kernel, caps=caps, labels=labels, genes=genes, blocks_dev=blocks_dev
        ),
        grid=(all_samples // CHUNK,),
        out_shape=outs,
        in_specs=[
            pl.BlockSpec(memory_space=pltpu.SMEM),
            *[whole(x) for x in (*sums, plan)],
            *[pl.BlockSpec((x.shape[0], CHUNK), lambda k: (0, k)) for x in arrays],
            *[pl.BlockSpec((CHUNK, w.shape[1]), lambda k: (k, 0)) for w in weights],
        ],
        out_specs=tuple(whole(x) for x in outs),
        scratch_shapes=[
            pltpu.VMEM((used, CHUNK), jnp.bfloat16),
            pltpu.VMEM((padded, width), jnp.float32),
            pltpu.VMEM((genes, LANES), jnp.float32),
        ],
        compiler_params=pltpu.CompilerParams(vmem_limit_bytes=48 * MIB),
        cost_estimate=pl.CostEstimate(
            flops=2 * used * all_samples * width,
            bytes_accessed=2 * all_samples * (width + used),
            transcendentals=0,
        ),
        name="products",
    )(pos, *sums, plan, *arrays, *weights)


def finish_kernel(own_ref, other_ref, power_ref, out_ref, *, samples):
    best = jnp.maximum(own_ref[0], other_ref[0])
    for i in range(1, own_ref.shape[0]):
        best = jnp.maximum(best, jnp.maximum(own_ref[i], other_ref[i]))
    labels, genes = out_ref.shape
    peak = best[:labels, :genes]
    out_ref[...] = jnp.sqrt(peak / (power_ref[0:1, :] / samples + 1e-05))


def shards(genotypes, phenotypes, environment, shuffles, window_start, window_end, chrom_bounds):
    snp_rows, half = genotypes.shape
    genes = phenotypes.shape[0]
    perms = shuffles.shape[0]
    chips = lax.axis_size("genome")
    cores = lax.axis_size("sample")
    blocks_dev = snp_rows // SNP_BLOCK
    reach = (HALF_BLK + blocks_dev - 1) // blocks_dev
    all_samples = half * cores
    labels = perms // cores
    caps = tuple(min(genes, genes * 4 >> k) for k in range(1, reach + 1))
    env = environment[None]
    start = window_start.reshape(-1, LANES)
    end = window_end.reshape(-1, LANES)
    pos = jnp.stack([lax.axis_index("genome"), lax.axis_index("sample")]).astype(jnp.int32)

    def travel(k, payload):
        pairs = [(i * cores, (i + k) * cores) for i in range(chips - k)]
        pairs += [((i + k) * cores + 1, i * cores + 1) for i in range(chips - k)]
        return lax.ppermute(payload, ("genome", "sample"), pairs)

    def one_round(turn, pos):
        core = pos[1:]
        other_pheno = swapped(phenotypes)
        own_sums = local_moments(genotypes, env)
        sums = (own_sums, swapped(own_sums))
        other_env = swapped(env)
        other_shuffles = swapped(shuffles)
        late_pheno, _ = lax.optimization_barrier((other_pheno, own_sums))
        rounds, plan, full, *payloads = select(
            turn, pos, chrom_bounds, start, end, phenotypes, late_pheno, caps, blocks_dev
        )
        late_geno, plan = lax.optimization_barrier((genotypes, plan))
        other_geno = swapped(late_geno)
        payloads = [full] * (reach - len(payloads)) + payloads
        mine = [travel(k, x) for k, x in enumerate(payloads, 1)]
        weights = snp_side(
            core, env, other_env, *sums, shuffles, other_shuffles, genotypes, other_geno, labels
        )
        mine, weights = lax.optimization_barrier((mine, weights))
        other = [swapped(x) for x in mine]
        found, power = products(
            pos, sums, plan, full, mine, other, weights, caps, labels, chips, blocks_dev
        )
        return rounds, found, power

    rounds, found, power = one_round(jnp.zeros((1,), jnp.int32), pos)

    def more(carry):
        return carry[0] < rounds[0]

    def again(carry):
        turn, best = carry
        turns, place = lax.optimization_barrier((jnp.full((1,), turn, jnp.int32), pos))
        return turn + 1, jnp.maximum(best, one_round(turns, place)[1])

    _, found = lax.while_loop(more, again, (jnp.int32(1), found))
    gathered = lax.all_to_all(found, "genome", 0, 0, tiled=True)
    return pl.pallas_call(
        functools.partial(finish_kernel, samples=all_samples),
        out_shape=jax.ShapeDtypeStruct((perms + 1, genes), jnp.float32),
        name="finish",
    )(gathered, swapped(gathered), power)


def solution(mesh):
    placed = (
        P("genome", "sample"),
        P("genome", "sample"),
        P("sample"),
        P(None, "sample"),
        P(),
        P(),
        P(),
    )
    return jax.shard_map(
        shards, mesh=mesh, in_specs=placed, out_specs=P(None, "genome"), check_vma=False
    )
```

```python
import functools

import jax
import jax.numpy as jnp
from jax import lax
from jax.experimental import pallas as pl
from jax.experimental.pallas import tpu as pltpu
from jax.sharding import PartitionSpec as P

SNP_BLOCK = 256
HALF_BLK = 7
LANES = 128
ROWS_STEP = 16
UNROLL = 32
DEPTH = 2048
SIDE = 2 * LANES
CHUNK = 1024
MIB = 2**20


def passed_along(x, axis, by):
    count = lax.axis_size(axis)
    pairs = [(i, i + by) for i in range(count) if 0 <= i + by < count]
    return lax.ppermute(x, axis, pairs)


def swapped(x):
    count = lax.axis_size("sample")
    return lax.ppermute(x, "sample", [(i, (i + 1) % count) for i in range(count)])


def moments_kernel(geno_ref, env_ref, out_ref, sums):
    step = pl.program_id(0)
    snp_rows, chunk = geno_ref.shape

    @pl.when(step == 0)
    def _():
        sums[...] = jnp.zeros_like(sums)

    def add_rows(i, carry):
        first = pl.multiple_of(i * ROWS_STEP, ROWS_STEP)
        held = [sums[m, pl.ds(first, ROWS_STEP), :] for m in range(3)]
        for t in range(chunk // LANES):
            x = geno_ref[pl.ds(first, ROWS_STEP), pl.ds(t * LANES, LANES)].astype(jnp.float32)
            e = env_ref[:, pl.ds(t * LANES, LANES)]
            x = x * x
            held[0] = held[0] + x
            x = x * e
            held[1] = held[1] + x
            held[2] = held[2] + x * e
        for m in range(3):
            sums[m, pl.ds(first, ROWS_STEP), :] = held[m]
        return carry

    lax.fori_loop(0, snp_rows // ROWS_STEP, add_rows, 0, unroll=4)

    @pl.when(step == pl.num_programs(0) - 1)
    def _():
        rows = [jnp.sum(sums[m].T, axis=0, keepdims=True) for m in range(3)]
        rows.append(jnp.zeros((out_ref.shape[0] - 3, snp_rows), jnp.float32))
        out_ref[...] = jnp.concatenate(rows, axis=0)


def local_moments(geno, env):
    snp_rows, half = geno.shape
    chunk = CHUNK
    return pl.pallas_call(
        moments_kernel,
        grid=(half // chunk,),
        out_shape=jax.ShapeDtypeStruct((8, snp_rows), jnp.float32),
        in_specs=[
            pl.BlockSpec((snp_rows, chunk), lambda k: (0, k)),
            pl.BlockSpec((1, chunk), lambda k: (0, k)),
        ],
        out_specs=pl.BlockSpec((8, snp_rows), lambda k: (0, 0)),
        scratch_shapes=[pltpu.VMEM((3, snp_rows, LANES), jnp.float32)],
        compiler_params=pltpu.CompilerParams(vmem_limit_bytes=60 * MIB),
        cost_estimate=pl.CostEstimate(
            flops=10**6, bytes_accessed=10**6, transcendentals=0
        ),
        name="local_moments",
    )(geno, env)


def snp_side_kernel(
    core_ref, env_own, env_other, sums_own, sums_other, shuf_own, shuf_other, own_ref, other_ref,
    *rest, labels,
):
    out_refs, scratch = rest[: labels + 1], rest[labels + 1 :]
    (
        idx, geno, table, dests, stage, first_stage, slope, idx_sems, in_sems, out_sems, first_sems,
    ) = scratch
    snp_rows, half = own_ref.shape
    all_samples = 2 * half
    chunks = all_samples // CHUNK
    words = snp_rows // LANES
    share = snp_rows // 2
    side = SIDE
    per_chunk = CHUNK // side
    core = core_ref[0]
    depth = geno.shape[0]

    def load(k):
        source = own_ref if k * CHUNK < half else other_ref
        return pltpu.make_async_copy(
            source.at[:, pl.ds((k * CHUNK) % half, CHUNK)], geno.at[k % depth],
            in_sems.at[k % depth],
        )

    def load_idx(q, h):
        source = shuf_own if h == 0 else shuf_other
        return pltpu.make_async_copy(
            source.at[core * labels + q],
            idx.at[pl.ds(q * all_samples + h * half, half)],
            idx_sems.at[2 * q + h],
        )

    def save_first(k):
        there = jnp.where(core == 0, k * CHUNK, (k * CHUNK + half) % all_samples)
        rows = pl.ds(pl.multiple_of(there, CHUNK), CHUNK)
        return pltpu.make_async_copy(
            first_stage.at[k % 2, :, pl.ds(pl.multiple_of(core * share, share), share)],
            out_refs[labels].at[rows],
            first_sems.at[k % 2],
        )

    def save(q, k):
        return pltpu.make_async_copy(
            stage.at[k % 2],
            out_refs[q].at[pl.ds(k * CHUNK, CHUNK)],
            out_sems.at[k % 2],
        )

    def read_rows(first):
        base = pl.multiple_of(first * words, UNROLL * words)
        return [table[pl.ds(base + u * words, words), :] for u in range(UNROLL)]

    def write_rows(q, first, held):
        for u in range(UNROLL):
            to = pl.multiple_of(idx[q * all_samples + first + u] * words, words)
            dests[q][pl.ds(to, words), :] = held[u]

    def narrowed(q, at, rows):
        return [
            dests[q][pl.ds(at * words + c, rows, stride=words), :].astype(jnp.bfloat16)
            for c in range(words)
        ]

    for k in range(depth):
        load(k).start()
    for q in range(labels):
        for h in range(2):
            load_idx(q, h).start()
    sums = sums_own[...] + sums_other[...]
    slope[...] = jnp.broadcast_to(sums[1:2, :] / sums[0:1, :], (LANES, snp_rows)).T
    unit = (
        lax.broadcasted_iota(jnp.int32, (side, side), 0)
        == lax.broadcasted_iota(jnp.int32, (side, side), 1)
    ).astype(jnp.bfloat16)
    for q in range(labels):
        for h in range(2):
            load_idx(q, h).wait()

    groups = side // UNROLL // words
    for k in range(chunks):
        load(k).wait()
        if k >= 2:
            save_first(k - 2).wait()
        env_ref = env_own if k * CHUNK < half else env_other

        def turn(i, carry, k=k, env_ref=env_ref):
            at = pl.multiple_of(i * side, side)
            e = env_ref[:, pl.ds((k * CHUNK) % half + at, side)]
            behind = pl.multiple_of(jnp.maximum(k * CHUNK + at - side, 0), side)
            for c in range(words):
                rows = pl.ds(c * LANES, LANES)
                x = geno[k % depth, rows, pl.ds(at, side)].astype(jnp.float32)
                r = slope[rows, :]
                a = x * (e - jnp.concatenate([r] * (side // LANES), axis=1))
                t = lax.dot_general(
                    unit, a.astype(jnp.bfloat16), (((1,), (1,)), ((), ())),
                    preferred_element_type=jnp.float32,
                )
                for g in range(groups):
                    first = pl.multiple_of(behind + (c * groups + g) * UNROLL, UNROLL)
                    write_rows(0, first, read_rows(first))
                table[pl.ds((k * CHUNK + at) * words + c, side, stride=words), :] = t
                first_stage[k % 2, pl.ds(at, side), pl.ds(c * LANES, LANES)] = t.astype(
                    jnp.bfloat16
                )
            return carry

        lax.fori_loop(0, per_chunk, turn, 0)
        save_first(k).start()
        if k + depth < chunks:
            load(k + depth).start()

    def last_block(i, carry):
        first = pl.multiple_of(all_samples - side + i * UNROLL, UNROLL)
        write_rows(0, first, read_rows(first))
        return carry

    lax.fori_loop(0, side // UNROLL, last_block, 0)

    count = 0
    for q in range(1, labels + 1):
        for k in range(chunks):
            if count >= 2:
                save((count - 2) // chunks, (count - 2) % chunks).wait()

            def step(i, carry, k=k, q=q):
                at = pl.multiple_of(i * UNROLL, UNROLL)
                first = pl.multiple_of(k * CHUNK + at, UNROLL)
                if q < labels:
                    held = read_rows(first)
                parts = narrowed(q - 1, first, UNROLL)
                if q < labels:
                    write_rows(q, first, held)
                for c in range(words):
                    stage[k % 2, pl.ds(at, UNROLL), pl.ds(c * LANES, LANES)] = parts[c]
                return carry

            def wide(i, carry, k=k, q=q):
                at = pl.multiple_of(i * side, side)
                parts = narrowed(q - 1, k * CHUNK + at, side)
                for c in range(words):
                    stage[k % 2, pl.ds(at, side), pl.ds(c * LANES, LANES)] = parts[c]
                return carry

            if q < labels:
                lax.fori_loop(0, CHUNK // UNROLL, step, 0)
            else:
                lax.fori_loop(0, CHUNK // side, wide, 0)
            save(q - 1, k).start()
            count += 1
    for k in range(chunks - 2, chunks):
        save_first(k).wait()
        save(labels - 1, k).wait()


def snp_side(core, env_own, env_other, sums_own, sums_other, shuf_own, shuf_other, own, other,
             labels):
    snp_rows, half = own.shape
    all_samples = 2 * half
    words = snp_rows // LANES
    widths = [snp_rows] * labels + [snp_rows // 2]
    any_spec = pl.BlockSpec(memory_space=pl.ANY)
    smem = pl.BlockSpec(memory_space=pltpu.SMEM)
    vmem = pl.BlockSpec(memory_space=pltpu.VMEM)
    return pl.pallas_call(
        functools.partial(snp_side_kernel, labels=labels),
        out_shape=[jax.ShapeDtypeStruct((all_samples, w), jnp.bfloat16) for w in widths],
        in_specs=[smem, vmem, vmem, vmem, vmem, any_spec, any_spec, any_spec, any_spec],
        out_specs=[any_spec for _ in widths],
        scratch_shapes=[
            pltpu.SMEM((labels * all_samples,), jnp.int32),
            pltpu.VMEM((2, snp_rows, CHUNK), jnp.bfloat16),
            pltpu.VMEM((all_samples * words, LANES), jnp.float32),
            [pltpu.VMEM((all_samples * words, LANES), jnp.float32) for _ in range(labels)],
            pltpu.VMEM((2, CHUNK, snp_rows), jnp.bfloat16),
            pltpu.VMEM((2, CHUNK, snp_rows), jnp.bfloat16),
            pltpu.VMEM((snp_rows, LANES), jnp.float32),
            pltpu.SemaphoreType.DMA((2 * labels,)),
            pltpu.SemaphoreType.DMA((2,)),
            pltpu.SemaphoreType.DMA((2,)),
            pltpu.SemaphoreType.DMA((2,)),
        ],
        compiler_params=pltpu.CompilerParams(vmem_limit_bytes=61 * MIB),
        cost_estimate=pl.CostEstimate(
            flops=40 * 10**9, bytes_accessed=60 * 10**6, transcendentals=0
        ),
        name="snp_side",
    )(core, env_own, env_other, sums_own, sums_other, shuf_own, shuf_other, own, other)


def window_plan(start, end, bounds_ref, n_bounds, total_blocks):
    middle = (start + end - 1) // 2
    lower_edge = jnp.zeros_like(start)
    upper_edge = jnp.full_like(end, total_blocks)
    for i in range(n_bounds):
        edge = bounds_ref[i]
        before = edge <= middle
        lower_edge = jnp.where(before, jnp.maximum(lower_edge, edge), lower_edge)
        upper_edge = jnp.where(before, upper_edge, jnp.minimum(upper_edge, edge))
    return jnp.maximum(start, lower_edge), jnp.minimum(end, upper_edge)


def select_kernel(
    round_ref, pos_ref, bounds_ref, start_ref, end_ref, own_ref, other_ref,
    rounds_ref, plan_ref, full_ref, *rest, caps, blocks_dev,
):
    reach = len(caps)
    genes, half = own_ref.shape
    chosen_from = sum(cap == genes for cap in caps)
    (slots, edges), pay_refs = rest[-2:], rest[:-2]
    shape = start_ref.shape
    per_row = LANES // genes
    chips = shape[0] * per_row
    chip, core = pos_ref[0], pos_ref[1]
    turn = round_ref[0]
    low, high = window_plan(
        start_ref[...], end_ref[...], bounds_ref, bounds_ref.shape[0], chips * blocks_dev
    )
    edges[0] = low
    edges[1] = high
    at = lax.broadcasted_iota(jnp.int32, shape, 0) * per_row
    at = at + lax.broadcasted_iota(jnp.int32, shape, 1) // genes
    a = lax.broadcasted_iota(jnp.int32, (LANES, LANES), 0)
    b = lax.broadcasted_iota(jnp.int32, (LANES, LANES), 1)
    upto = ((a <= b) & (a // genes == b // genes)).astype(jnp.float32).astype(jnp.bfloat16)
    rounds = jnp.int32(0)
    for way in range(2):
        for k in range(1, reach + 1):
            to = at + (k if way == 0 else -k)
            need = (
                (low < (to + 1) * blocks_dev) & (high > to * blocks_dev)
                & (low < high) & (to >= 0) & (to < chips)
            )
            rank = jnp.dot(
                need.astype(jnp.float32).astype(jnp.bfloat16), upto,
                preferred_element_type=jnp.float32,
            ).astype(jnp.int32)
            cap = caps[k - 1]
            if cap == genes:
                which = lax.broadcasted_iota(jnp.int32, shape, 1) % genes
                slots[way * reach + k - 1] = jnp.where(need, which, -1)
                continue
            slot = rank - 1 - turn * cap
            slots[way * reach + k - 1] = jnp.where(
                need & (slot >= 0) & (slot < cap), slot, -1
            )
            rounds = jnp.maximum(rounds, (jnp.max(rank) + cap - 1) // cap)
    rounds_ref[0] = rounds

    def of_chip(ref, index, which):
        row = ref[index, pl.ds(which // per_row, 1), :]
        out = row[:, :genes]
        for part in range(1, per_row):
            out = jnp.where(
                which % per_row == part, row[:, part * genes : (part + 1) * genes], out
            )
        return out

    used = [lax.broadcasted_iota(jnp.int32, (1, genes), 1)]
    lows = [of_chip(edges, 0, chip)]
    highs = [of_chip(edges, 1, chip)]
    first = genes
    for side in range(2):
        way = core if side == 0 else 1 - core
        for k in range(1, reach + 1):
            source = chip + (2 * way - 1) * k
            valid = (source >= 0) & (source < chips)
            source = jnp.clip(source, 0, chips - 1)
            slot = of_chip(slots, way * reach + k - 1, source)
            used.append(jnp.where(valid & (slot >= 0), slot + first, -1))
            lows.append(of_chip(edges, 0, source))
            highs.append(jnp.where(valid, of_chip(edges, 1, source), 0))
            first += caps[k - 1]
    while len(used) * genes < plan_ref.shape[1]:
        used.append(jnp.full_like(used[0], -1))
        lows.append(jnp.zeros_like(used[0]))
        highs.append(jnp.zeros_like(used[0]))
    plan_ref[...] = jnp.zeros_like(plan_ref)
    for row, parts in enumerate((used, lows, highs)):
        plan_ref[pl.ds(row, 1), :] = jnp.concatenate(parts, axis=1)

    picks = []
    for k in range(chosen_from + 1, reach + 1):
        slot = of_chip(slots, core * reach + k - 1, chip)
        rows = lax.broadcasted_iota(jnp.int32, (caps[k - 1], genes), 0)
        picks.append((rows == slot).astype(jnp.float32))
    if picks:
        picks = jnp.concatenate(picks, axis=0).astype(jnp.bfloat16)
    step = 1024

    def copy(i, carry):
        cols = pl.ds(pl.multiple_of(i * step, step), step)
        late = pl.ds(pl.multiple_of(half + i * step, step), step)
        a, b = own_ref[:, cols], other_ref[:, cols]
        for part, to in ((jnp.where(core == 0, a, b), cols), (jnp.where(core == 0, b, a), late)):
            full_ref[:, to] = part
            if pay_refs:
                chosen = jnp.dot(picks, part, preferred_element_type=jnp.float32)
                chosen = chosen.astype(jnp.bfloat16)
                row = 0
                for pay in pay_refs:
                    pay[:, to] = chosen[row : row + pay.shape[0]]
                    row += pay.shape[0]
        return carry

    lax.fori_loop(0, half // step, copy, 0)


def select(turn, pos, bounds, start, end, own, other, caps, blocks_dev):
    genes, half = own.shape
    all_samples = 2 * half
    reach = len(caps)
    smem = pl.BlockSpec(memory_space=pltpu.SMEM)
    vmem = pl.BlockSpec(memory_space=pltpu.VMEM)
    width = -(-(2 * reach + 1) * genes // LANES) * LANES
    chosen = [cap for cap in caps if cap < genes]
    return pl.pallas_call(
        functools.partial(select_kernel, caps=caps, blocks_dev=blocks_dev),
        out_shape=(
            jax.ShapeDtypeStruct((1,), jnp.int32),
            jax.ShapeDtypeStruct((8, width), jnp.int32),
            jax.ShapeDtypeStruct((genes, all_samples), jnp.bfloat16),
            *[jax.ShapeDtypeStruct((cap, all_samples), jnp.bfloat16) for cap in chosen],
        ),
        in_specs=[smem, smem, smem, vmem, vmem, vmem, vmem],
        out_specs=(smem, vmem, vmem, *[vmem for _ in chosen]),
        scratch_shapes=[
            pltpu.VMEM((2 * reach,) + start.shape, jnp.int32),
            pltpu.VMEM((2,) + start.shape, jnp.int32),
        ],
        compiler_params=pltpu.CompilerParams(vmem_limit_bytes=24 * MIB),
        name="select",
    )(turn, pos, bounds, start, end, own, other)


def product_kernel(
    pos_ref, sums_own, sums_other, plan_ref, *rest, caps, labels, genes, blocks_dev
):
    reach = len(caps)
    n_in = 1 + 2 * reach
    gene_refs = rest[:n_in]
    weight_refs = rest[n_in : n_in + labels + 1]
    out_ref, power_ref, rows, total, power = rest[n_in + labels + 1 :]
    step = pl.program_id(0)
    snp_rows = sums_own.shape[1]
    depth = rows.shape[1]
    used = rows.shape[0]
    chip, core = pos_ref[0], pos_ref[1]

    @pl.when(step == 0)
    def _():
        total[...] = jnp.zeros_like(total)
        power[...] = jnp.zeros_like(power)

    at = 0
    for ref in gene_refs:
        rows[pl.ds(at, ref.shape[0]), :] = ref[...]
        at += ref.shape[0]
    for q, ref in enumerate(weight_refs):
        cols = pl.ds(q * snp_rows, ref.shape[1])
        total[pl.ds(0, used), cols] += jnp.dot(
            rows[...], ref[...], preferred_element_type=jnp.float32
        )
    kept = power[...]
    for t in range(depth // LANES):
        x = rows[pl.ds(0, genes), pl.ds(t * LANES, LANES)].astype(jnp.float32)
        kept = kept + x * x
    power[...] = kept

    @pl.when(step == pl.num_programs(0) - 1)
    def _():
        summed_up(
            chip, core, sums_own, sums_other, plan_ref, out_ref, power_ref, total, power,
            reach=reach, labels=labels, genes=genes, blocks_dev=blocks_dev,
        )


def summed_up(
    chip, core, sums_own, sums_other, plan_ref, out_ref, power_ref, total, power,
    *, reach, labels, genes, blocks_dev,
):
    snp_rows = sums_own.shape[1]
    block = SNP_BLOCK
    n_in = 1 + 2 * reach
    share_blocks = blocks_dev // 2
    sums = sums_own[...] + sums_other[...]
    cross = sums[1:2, :]
    inter = sums[2:3, :]
    inv = 1.0 / (inter - cross * (cross / sums[0:1, :]) + 0.1 * inter)

    def peak(col, inv_block):
        best = None
        for t in range(block // LANES):
            v = total[:, pl.ds(col + t * LANES, LANES)]
            v = v * v * inv_block[:, t * LANES : (t + 1) * LANES]
            best = v if best is None else jnp.maximum(best, v)
        return jnp.max(best.T, axis=0, keepdims=True)

    peaks = []
    for q in range(labels):
        for b in range(blocks_dev):
            peaks.append(peak(q * snp_rows + b * block, inv[:, b * block : (b + 1) * block]))
    for b in range(share_blocks):
        mine = inv[:, b * block : (b + 1) * block]
        late = inv[:, (share_blocks + b) * block : (share_blocks + b + 1) * block]
        peaks.append(peak(labels * snp_rows + b * block, jnp.where(core == 0, mine, late)))
    while len(peaks) % 8:
        peaks.append(jnp.zeros_like(peaks[0]))
    peaks = jnp.concatenate(peaks, axis=0)
    count = peaks.shape[0]
    terms = []
    left = peaks
    for _ in range(3):
        terms.append(left.astype(jnp.bfloat16).astype(jnp.float32))
        left = left - terms[-1]
    terms = jnp.concatenate(terms, axis=0).astype(jnp.bfloat16)
    band = plan_ref.shape[1]
    slot = plan_ref[0:1, :]
    low = plan_ref[1:2, :]
    high = plan_ref[2:3, :]
    place = lax.broadcasted_iota(jnp.int32, (total.shape[0], band), 0) == slot
    spread = jnp.dot(
        terms, place.astype(jnp.float32).astype(jnp.bfloat16),
        preferred_element_type=jnp.float32,
    )
    spread = spread[:count] + spread[count : 2 * count] + spread[2 * count :]

    def masked(row, snp_block):
        inside = (snp_block >= low) & (snp_block < high)
        return jnp.where(inside, spread[row : row + 1], 0.0)

    def highest(row, blocks, first_block):
        best = masked(row, first_block)
        for b in range(1, blocks):
            best = jnp.maximum(best, masked(row + b, first_block + b))
        return best

    out_rows = [highest(labels * blocks_dev, share_blocks, chip * blocks_dev + core * share_blocks)]
    found = [highest(q * blocks_dev, blocks_dev, chip * blocks_dev) for q in range(labels)]
    for c in range(2):
        out_rows += [jnp.where(core == c, v, 0.0) for v in found]
    while len(out_rows) % 8:
        out_rows.append(jnp.zeros_like(out_rows[0]))
    dense = jnp.concatenate(out_rows, axis=0)
    out_ref[...] = jnp.zeros_like(out_ref)
    chips = out_ref.shape[0]
    for i in range(n_in):
        if i == 0:
            target = chip
        else:
            way = core if i <= reach else 1 - core
            target = chip + (2 * way - 1) * ((i - 1) % reach + 1)

        @pl.when((target >= 0) & (target < chips))
        def _(i=i, target=target):
            out_ref[target, :, pl.ds(0, genes)] = dense[:, i * genes : (i + 1) * genes]

    powers = jnp.sum(power[...].T, axis=0, keepdims=True)
    power_ref[...] = jnp.broadcast_to(powers, power_ref.shape)


def products(pos, sums, plan, full, mine, other, weights, caps, labels, chips, blocks_dev):
    genes, all_samples = full.shape
    used = genes + 2 * sum(caps)
    padded = -(-used // LANES) * LANES
    out_rows = -(-(1 + 2 * labels) // 8) * 8
    width = sum(w.shape[1] for w in weights)
    arrays = (full, *mine, *other)

    def whole(x):
        return pl.BlockSpec(x.shape, lambda k: (0,) * len(x.shape))

    outs = (
        jax.ShapeDtypeStruct((chips, out_rows, LANES), jnp.float32),
        jax.ShapeDtypeStruct((8, genes), jnp.float32),
    )
    return pl.pallas_call(
        functools.partial(
            product_kernel, caps=caps, labels=labels, genes=genes, blocks_dev=blocks_dev
        ),
        grid=(all_samples // DEPTH,),
        out_shape=outs,
        in_specs=[
            pl.BlockSpec(memory_space=pltpu.SMEM),
            *[whole(x) for x in (*sums, plan)],
            *[pl.BlockSpec((x.shape[0], DEPTH), lambda k: (0, k)) for x in arrays],
            *[pl.BlockSpec((DEPTH, w.shape[1]), lambda k: (k, 0)) for w in weights],
        ],
        out_specs=tuple(whole(x) for x in outs),
        scratch_shapes=[
            pltpu.VMEM((used, DEPTH), jnp.bfloat16),
            pltpu.VMEM((padded, width), jnp.float32),
            pltpu.VMEM((genes, LANES), jnp.float32),
        ],
        compiler_params=pltpu.CompilerParams(vmem_limit_bytes=48 * MIB),
        cost_estimate=pl.CostEstimate(
            flops=2 * used * all_samples * width,
            bytes_accessed=2 * all_samples * (width + used),
            transcendentals=0,
        ),
        name="products",
    )(pos, *sums, plan, *arrays, *weights)


def finish_kernel(own_ref, other_ref, power_ref, out_ref, *, samples):
    best = jnp.maximum(own_ref[0], other_ref[0])
    for i in range(1, own_ref.shape[0]):
        best = jnp.maximum(best, jnp.maximum(own_ref[i], other_ref[i]))
    labels, genes = out_ref.shape
    peak = best[:labels, :genes]
    out_ref[...] = jnp.sqrt(peak / (power_ref[0:1, :] / samples + 1e-05))


def shards(genotypes, phenotypes, environment, shuffles, window_start, window_end, chrom_bounds):
    snp_rows, half = genotypes.shape
    genes = phenotypes.shape[0]
    perms = shuffles.shape[0]
    chips = lax.axis_size("genome")
    cores = lax.axis_size("sample")
    blocks_dev = snp_rows // SNP_BLOCK
    reach = (HALF_BLK + blocks_dev - 1) // blocks_dev
    all_samples = half * cores
    labels = perms // cores
    caps = tuple(min(genes, genes * 4 >> k) for k in range(1, reach + 1))
    env = environment[None]
    start = window_start.reshape(-1, LANES)
    end = window_end.reshape(-1, LANES)
    pos = jnp.stack([lax.axis_index("genome"), lax.axis_index("sample")]).astype(jnp.int32)

    def travel(k, payload):
        pairs = [(i * cores, (i + k) * cores) for i in range(chips - k)]
        pairs += [((i + k) * cores + 1, i * cores + 1) for i in range(chips - k)]
        return lax.ppermute(payload, ("genome", "sample"), pairs)

    def one_round(turn, pos):
        core = pos[1:]
        other_pheno = swapped(phenotypes)
        own_sums = local_moments(genotypes, env)
        sums = (own_sums, swapped(own_sums))
        other_env = swapped(env)
        other_shuffles = swapped(shuffles)
        late_pheno, _ = lax.optimization_barrier((other_pheno, own_sums))
        rounds, plan, full, *payloads = select(
            turn, pos, chrom_bounds, start, end, phenotypes, late_pheno, caps, blocks_dev
        )
        late_geno, plan = lax.optimization_barrier((genotypes, plan))
        other_geno = swapped(late_geno)
        payloads = [full] * (reach - len(payloads)) + payloads
        mine = [travel(k, x) for k, x in enumerate(payloads, 1)]
        weights = snp_side(
            core, env, other_env, *sums, shuffles, other_shuffles, genotypes, other_geno, labels
        )
        mine, weights = lax.optimization_barrier((mine, weights))
        other = [swapped(x) for x in mine]
        found, power = products(
            pos, sums, plan, full, mine, other, weights, caps, labels, chips, blocks_dev
        )
        return rounds, found, power

    rounds, found, power = one_round(jnp.zeros((1,), jnp.int32), pos)

    def more(carry):
        return carry[0] < rounds[0]

    def again(carry):
        turn, best = carry
        turns, place = lax.optimization_barrier((jnp.full((1,), turn, jnp.int32), pos))
        return turn + 1, jnp.maximum(best, one_round(turns, place)[1])

    _, found = lax.while_loop(more, again, (jnp.int32(1), found))
    gathered = lax.all_to_all(found, "genome", 0, 0, tiled=True)
    return pl.pallas_call(
        functools.partial(finish_kernel, samples=all_samples),
        out_shape=jax.ShapeDtypeStruct((perms + 1, genes), jnp.float32),
        name="finish",
    )(gathered, swapped(gathered), power)


def solution(mesh):
    placed = (
        P("genome", "sample"),
        P("genome", "sample"),
        P("sample"),
        P(None, "sample"),
        P(),
        P(),
        P(),
    )
    return jax.shard_map(
        shards, mesh=mesh, in_specs=placed, out_specs=P(None, "genome"), check_vma=False
    )
```

```python
import functools

import jax
import jax.numpy as jnp
from jax import lax
from jax.experimental import pallas as pl
from jax.experimental.pallas import tpu as pltpu
from jax.sharding import PartitionSpec as P

SNP_BLOCK = 256
HALF_BLK = 7
LANES = 128
ROWS_STEP = 16
UNROLL = 32
DEPTH = 2048
SIDE = 2 * LANES
CHUNK = 1024
MIB = 2**20


def passed_along(x, axis, by):
    count = lax.axis_size(axis)
    pairs = [(i, i + by) for i in range(count) if 0 <= i + by < count]
    return lax.ppermute(x, axis, pairs)


def swapped(x):
    count = lax.axis_size("sample")
    return lax.ppermute(x, "sample", [(i, (i + 1) % count) for i in range(count)])


def moments_kernel(geno_ref, env_ref, out_ref, sums):
    step = pl.program_id(0)
    snp_rows, chunk = geno_ref.shape

    @pl.when(step == 0)
    def _():
        sums[...] = jnp.zeros_like(sums)

    def add_rows(i, carry):
        first = pl.multiple_of(i * ROWS_STEP, ROWS_STEP)
        held = [sums[m, pl.ds(first, ROWS_STEP), :] for m in range(3)]
        for t in range(chunk // LANES):
            x = geno_ref[pl.ds(first, ROWS_STEP), pl.ds(t * LANES, LANES)].astype(jnp.float32)
            e = env_ref[:, pl.ds(t * LANES, LANES)]
            x = x * x
            held[0] = held[0] + x
            x = x * e
            held[1] = held[1] + x
            held[2] = held[2] + x * e
        for m in range(3):
            sums[m, pl.ds(first, ROWS_STEP), :] = held[m]
        return carry

    lax.fori_loop(0, snp_rows // ROWS_STEP, add_rows, 0, unroll=4)

    @pl.when(step == pl.num_programs(0) - 1)
    def _():
        rows = [jnp.sum(sums[m].T, axis=0, keepdims=True) for m in range(3)]
        rows.append(jnp.zeros((out_ref.shape[0] - 3, snp_rows), jnp.float32))
        out_ref[...] = jnp.concatenate(rows, axis=0)


def local_moments(geno, env):
    snp_rows, half = geno.shape
    chunk = CHUNK
    return pl.pallas_call(
        moments_kernel,
        grid=(half // chunk,),
        out_shape=jax.ShapeDtypeStruct((8, snp_rows), jnp.float32),
        in_specs=[
            pl.BlockSpec((snp_rows, chunk), lambda k: (0, k)),
            pl.BlockSpec((1, chunk), lambda k: (0, k)),
        ],
        out_specs=pl.BlockSpec((8, snp_rows), lambda k: (0, 0)),
        scratch_shapes=[pltpu.VMEM((3, snp_rows, LANES), jnp.float32)],
        compiler_params=pltpu.CompilerParams(vmem_limit_bytes=60 * MIB),
        cost_estimate=pl.CostEstimate(
            flops=5 * 10**9, bytes_accessed=2 * snp_rows * half, transcendentals=0
        ),
        name="local_moments",
    )(geno, env)


def snp_side_kernel(
    core_ref, env_own, env_other, sums_own, sums_other, shuf_own, shuf_other, own_ref, other_ref,
    *rest, labels,
):
    out_refs, scratch = rest[: labels + 1], rest[labels + 1 :]
    (
        idx, geno, table, dests, stage, first_stage, slope, idx_sems, in_sems, out_sems, first_sems,
    ) = scratch
    snp_rows, half = own_ref.shape
    all_samples = 2 * half
    chunks = all_samples // CHUNK
    words = snp_rows // LANES
    share = snp_rows // 2
    side = SIDE
    per_chunk = CHUNK // side
    core = core_ref[0]
    depth = geno.shape[0]

    def load(k):
        source = own_ref if k * CHUNK < half else other_ref
        return pltpu.make_async_copy(
            source.at[:, pl.ds((k * CHUNK) % half, CHUNK)], geno.at[k % depth],
            in_sems.at[k % depth],
        )

    def load_idx(q, h):
        source = shuf_own if h == 0 else shuf_other
        return pltpu.make_async_copy(
            source.at[core * labels + q],
            idx.at[pl.ds(q * all_samples + h * half, half)],
            idx_sems.at[2 * q + h],
        )

    def save_first(k):
        there = jnp.where(core == 0, k * CHUNK, (k * CHUNK + half) % all_samples)
        rows = pl.ds(pl.multiple_of(there, CHUNK), CHUNK)
        return pltpu.make_async_copy(
            first_stage.at[k % 2, :, pl.ds(pl.multiple_of(core * share, share), share)],
            out_refs[labels].at[rows],
            first_sems.at[k % 2],
        )

    def save(q, k):
        return pltpu.make_async_copy(
            stage.at[k % 2],
            out_refs[q].at[pl.ds(k * CHUNK, CHUNK)],
            out_sems.at[k % 2],
        )

    def read_rows(first):
        base = pl.multiple_of(first * words, UNROLL * words)
        return [table[pl.ds(base + u * words, words), :] for u in range(UNROLL)]

    def write_rows(q, first, held):
        for u in range(UNROLL):
            to = pl.multiple_of(idx[q * all_samples + first + u] * words, words)
            dests[q][pl.ds(to, words), :] = held[u]

    def narrowed(q, at, rows):
        return [
            dests[q][pl.ds(at * words + c, rows, stride=words), :].astype(jnp.bfloat16)
            for c in range(words)
        ]

    for k in range(depth):
        load(k).start()
    for q in range(labels):
        for h in range(2):
            load_idx(q, h).start()
    sums = sums_own[...] + sums_other[...]
    slope[...] = jnp.broadcast_to(sums[1:2, :] / sums[0:1, :], (LANES, snp_rows)).T
    unit = (
        lax.broadcasted_iota(jnp.int32, (side, side), 0)
        == lax.broadcasted_iota(jnp.int32, (side, side), 1)
    ).astype(jnp.bfloat16)
    for q in range(labels):
        for h in range(2):
            load_idx(q, h).wait()

    groups = side // UNROLL // words
    for k in range(chunks):
        load(k).wait()
        if k >= 2:
            save_first(k - 2).wait()
        env_ref = env_own if k * CHUNK < half else env_other

        def turn(i, carry, k=k, env_ref=env_ref):
            at = pl.multiple_of(i * side, side)
            e = env_ref[:, pl.ds((k * CHUNK) % half + at, side)]
            behind = pl.multiple_of(jnp.maximum(k * CHUNK + at - side, 0), side)
            for c in range(words):
                rows = pl.ds(c * LANES, LANES)
                x = geno[k % depth, rows, pl.ds(at, side)].astype(jnp.float32)
                r = slope[rows, :]
                a = x * (e - jnp.concatenate([r] * (side // LANES), axis=1))
                t = lax.dot_general(
                    unit, a.astype(jnp.bfloat16), (((1,), (1,)), ((), ())),
                    preferred_element_type=jnp.float32,
                )
                for g in range(groups):
                    first = pl.multiple_of(behind + (c * groups + g) * UNROLL, UNROLL)
                    write_rows(0, first, read_rows(first))
                table[pl.ds((k * CHUNK + at) * words + c, side, stride=words), :] = t
                first_stage[k % 2, pl.ds(at, side), pl.ds(c * LANES, LANES)] = t.astype(
                    jnp.bfloat16
                )
            return carry

        lax.fori_loop(0, per_chunk, turn, 0)
        save_first(k).start()
        if k + depth < chunks:
            load(k + depth).start()

    def last_block(i, carry):
        first = pl.multiple_of(all_samples - side + i * UNROLL, UNROLL)
        write_rows(0, first, read_rows(first))
        return carry

    lax.fori_loop(0, side // UNROLL, last_block, 0)

    count = 0
    for q in range(1, labels + 1):
        for k in range(chunks):
            if count >= 2:
                save((count - 2) // chunks, (count - 2) % chunks).wait()

            def step(i, carry, k=k, q=q):
                at = pl.multiple_of(i * UNROLL, UNROLL)
                first = pl.multiple_of(k * CHUNK + at, UNROLL)
                if q < labels:
                    held = read_rows(first)
                parts = narrowed(q - 1, first, UNROLL)
                if q < labels:
                    write_rows(q, first, held)
                for c in range(words):
                    stage[k % 2, pl.ds(at, UNROLL), pl.ds(c * LANES, LANES)] = parts[c]
                return carry

            def wide(i, carry, k=k, q=q):
                at = pl.multiple_of(i * side, side)
                parts = narrowed(q - 1, k * CHUNK + at, side)
                for c in range(words):
                    stage[k % 2, pl.ds(at, side), pl.ds(c * LANES, LANES)] = parts[c]
                return carry

            if q < labels:
                lax.fori_loop(0, CHUNK // UNROLL, step, 0)
            else:
                lax.fori_loop(0, CHUNK // side, wide, 0)
            save(q - 1, k).start()
            count += 1
    for k in range(chunks - 2, chunks):
        save_first(k).wait()
        save(labels - 1, k).wait()


def snp_side(core, env_own, env_other, sums_own, sums_other, shuf_own, shuf_other, own, other,
             labels):
    snp_rows, half = own.shape
    all_samples = 2 * half
    words = snp_rows // LANES
    widths = [snp_rows] * labels + [snp_rows // 2]
    any_spec = pl.BlockSpec(memory_space=pl.ANY)
    smem = pl.BlockSpec(memory_space=pltpu.SMEM)
    vmem = pl.BlockSpec(memory_space=pltpu.VMEM)
    return pl.pallas_call(
        functools.partial(snp_side_kernel, labels=labels),
        out_shape=[jax.ShapeDtypeStruct((all_samples, w), jnp.bfloat16) for w in widths],
        in_specs=[smem, vmem, vmem, vmem, vmem, any_spec, any_spec, any_spec, any_spec],
        out_specs=[any_spec for _ in widths],
        scratch_shapes=[
            pltpu.SMEM((labels * all_samples,), jnp.int32),
            pltpu.VMEM((2, snp_rows, CHUNK), jnp.bfloat16),
            pltpu.VMEM((all_samples * words, LANES), jnp.float32),
            [pltpu.VMEM((all_samples * words, LANES), jnp.float32) for _ in range(labels)],
            pltpu.VMEM((2, CHUNK, snp_rows), jnp.bfloat16),
            pltpu.VMEM((2, CHUNK, snp_rows), jnp.bfloat16),
            pltpu.VMEM((snp_rows, LANES), jnp.float32),
            pltpu.SemaphoreType.DMA((2 * labels,)),
            pltpu.SemaphoreType.DMA((2,)),
            pltpu.SemaphoreType.DMA((2,)),
            pltpu.SemaphoreType.DMA((2,)),
        ],
        compiler_params=pltpu.CompilerParams(vmem_limit_bytes=61 * MIB),
        cost_estimate=pl.CostEstimate(
            flops=40 * 10**9, bytes_accessed=60 * 10**6, transcendentals=0
        ),
        name="snp_side",
    )(core, env_own, env_other, sums_own, sums_other, shuf_own, shuf_other, own, other)


def window_plan(start, end, bounds_ref, n_bounds, total_blocks):
    middle = (start + end - 1) // 2
    lower_edge = jnp.zeros_like(start)
    upper_edge = jnp.full_like(end, total_blocks)
    for i in range(n_bounds):
        edge = bounds_ref[i]
        before = edge <= middle
        lower_edge = jnp.where(before, jnp.maximum(lower_edge, edge), lower_edge)
        upper_edge = jnp.where(before, upper_edge, jnp.minimum(upper_edge, edge))
    return jnp.maximum(start, lower_edge), jnp.minimum(end, upper_edge)


def select_kernel(
    round_ref, pos_ref, bounds_ref, start_ref, end_ref, own_ref, other_ref,
    rounds_ref, plan_ref, full_ref, *rest, caps, blocks_dev,
):
    reach = len(caps)
    genes, half = own_ref.shape
    chosen_from = sum(cap == genes for cap in caps)
    (slots, edges), pay_refs = rest[-2:], rest[:-2]
    shape = start_ref.shape
    per_row = LANES // genes
    chips = shape[0] * per_row
    chip, core = pos_ref[0], pos_ref[1]
    turn = round_ref[0]
    low, high = window_plan(
        start_ref[...], end_ref[...], bounds_ref, bounds_ref.shape[0], chips * blocks_dev
    )
    edges[0] = low
    edges[1] = high
    at = lax.broadcasted_iota(jnp.int32, shape, 0) * per_row
    at = at + lax.broadcasted_iota(jnp.int32, shape, 1) // genes
    a = lax.broadcasted_iota(jnp.int32, (LANES, LANES), 0)
    b = lax.broadcasted_iota(jnp.int32, (LANES, LANES), 1)
    upto = ((a <= b) & (a // genes == b // genes)).astype(jnp.float32).astype(jnp.bfloat16)
    rounds = jnp.int32(0)
    for way in range(2):
        for k in range(1, reach + 1):
            to = at + (k if way == 0 else -k)
            need = (
                (low < (to + 1) * blocks_dev) & (high > to * blocks_dev)
                & (low < high) & (to >= 0) & (to < chips)
            )
            rank = jnp.dot(
                need.astype(jnp.float32).astype(jnp.bfloat16), upto,
                preferred_element_type=jnp.float32,
            ).astype(jnp.int32)
            cap = caps[k - 1]
            if cap == genes:
                which = lax.broadcasted_iota(jnp.int32, shape, 1) % genes
                slots[way * reach + k - 1] = jnp.where(need, which, -1)
                continue
            slot = rank - 1 - turn * cap
            slots[way * reach + k - 1] = jnp.where(
                need & (slot >= 0) & (slot < cap), slot, -1
            )
            rounds = jnp.maximum(rounds, (jnp.max(rank) + cap - 1) // cap)
    rounds_ref[0] = rounds

    def of_chip(ref, index, which):
        row = ref[index, pl.ds(which // per_row, 1), :]
        out = row[:, :genes]
        for part in range(1, per_row):
            out = jnp.where(
                which % per_row == part, row[:, part * genes : (part + 1) * genes], out
            )
        return out

    used = [lax.broadcasted_iota(jnp.int32, (1, genes), 1)]
    lows = [of_chip(edges, 0, chip)]
    highs = [of_chip(edges, 1, chip)]
    first = genes
    for side in range(2):
        way = core if side == 0 else 1 - core
        for k in range(1, reach + 1):
            source = chip + (2 * way - 1) * k
            valid = (source >= 0) & (source < chips)
            source = jnp.clip(source, 0, chips - 1)
            slot = of_chip(slots, way * reach + k - 1, source)
            used.append(jnp.where(valid & (slot >= 0), slot + first, -1))
            lows.append(of_chip(edges, 0, source))
            highs.append(jnp.where(valid, of_chip(edges, 1, source), 0))
            first += caps[k - 1]
    while len(used) * genes < plan_ref.shape[1]:
        used.append(jnp.full_like(used[0], -1))
        lows.append(jnp.zeros_like(used[0]))
        highs.append(jnp.zeros_like(used[0]))
    plan_ref[...] = jnp.zeros_like(plan_ref)
    for row, parts in enumerate((used, lows, highs)):
        plan_ref[pl.ds(row, 1), :] = jnp.concatenate(parts, axis=1)

    picks = []
    for k in range(chosen_from + 1, reach + 1):
        slot = of_chip(slots, core * reach + k - 1, chip)
        rows = lax.broadcasted_iota(jnp.int32, (caps[k - 1], genes), 0)
        picks.append((rows == slot).astype(jnp.float32))
    if picks:
        picks = jnp.concatenate(picks, axis=0).astype(jnp.bfloat16)
    step = 1024

    def copy(i, carry):
        cols = pl.ds(pl.multiple_of(i * step, step), step)
        late = pl.ds(pl.multiple_of(half + i * step, step), step)
        a, b = own_ref[:, cols], other_ref[:, cols]
        for part, to in ((jnp.where(core == 0, a, b), cols), (jnp.where(core == 0, b, a), late)):
            full_ref[:, to] = part
            if pay_refs:
                chosen = jnp.dot(picks, part, preferred_element_type=jnp.float32)
                chosen = chosen.astype(jnp.bfloat16)
                row = 0
                for pay in pay_refs:
                    pay[:, to] = chosen[row : row + pay.shape[0]]
                    row += pay.shape[0]
        return carry

    lax.fori_loop(0, half // step, copy, 0)


def select(turn, pos, bounds, start, end, own, other, caps, blocks_dev):
    genes, half = own.shape
    all_samples = 2 * half
    reach = len(caps)
    smem = pl.BlockSpec(memory_space=pltpu.SMEM)
    vmem = pl.BlockSpec(memory_space=pltpu.VMEM)
    width = -(-(2 * reach + 1) * genes // LANES) * LANES
    chosen = [cap for cap in caps if cap < genes]
    return pl.pallas_call(
        functools.partial(select_kernel, caps=caps, blocks_dev=blocks_dev),
        out_shape=(
            jax.ShapeDtypeStruct((1,), jnp.int32),
            jax.ShapeDtypeStruct((8, width), jnp.int32),
            jax.ShapeDtypeStruct((genes, all_samples), jnp.bfloat16),
            *[jax.ShapeDtypeStruct((cap, all_samples), jnp.bfloat16) for cap in chosen],
        ),
        in_specs=[smem, smem, smem, vmem, vmem, vmem, vmem],
        out_specs=(smem, vmem, vmem, *[vmem for _ in chosen]),
        scratch_shapes=[
            pltpu.VMEM((2 * reach,) + start.shape, jnp.int32),
            pltpu.VMEM((2,) + start.shape, jnp.int32),
        ],
        compiler_params=pltpu.CompilerParams(vmem_limit_bytes=24 * MIB),
        name="select",
    )(turn, pos, bounds, start, end, own, other)


def product_kernel(
    pos_ref, sums_own, sums_other, plan_ref, *rest, caps, labels, genes, blocks_dev
):
    reach = len(caps)
    n_in = 1 + 2 * reach
    gene_refs = rest[:n_in]
    weight_refs = rest[n_in : n_in + labels + 1]
    out_ref, power_ref, rows, total, power = rest[n_in + labels + 1 :]
    step = pl.program_id(0)
    snp_rows = sums_own.shape[1]
    depth = rows.shape[1]
    used = rows.shape[0]
    chip, core = pos_ref[0], pos_ref[1]

    @pl.when(step == 0)
    def _():
        total[...] = jnp.zeros_like(total)
        power[...] = jnp.zeros_like(power)

    at = 0
    for ref in gene_refs:
        rows[pl.ds(at, ref.shape[0]), :] = ref[...]
        at += ref.shape[0]
    for q, ref in enumerate(weight_refs):
        cols = pl.ds(q * snp_rows, ref.shape[1])
        total[pl.ds(0, used), cols] += jnp.dot(
            rows[...], ref[...], preferred_element_type=jnp.float32
        )
    kept = power[...]
    for t in range(depth // LANES):
        x = rows[pl.ds(0, genes), pl.ds(t * LANES, LANES)].astype(jnp.float32)
        kept = kept + x * x
    power[...] = kept

    @pl.when(step == pl.num_programs(0) - 1)
    def _():
        summed_up(
            chip, core, sums_own, sums_other, plan_ref, out_ref, power_ref, total, power,
            reach=reach, labels=labels, genes=genes, blocks_dev=blocks_dev,
        )


def summed_up(
    chip, core, sums_own, sums_other, plan_ref, out_ref, power_ref, total, power,
    *, reach, labels, genes, blocks_dev,
):
    snp_rows = sums_own.shape[1]
    block = SNP_BLOCK
    n_in = 1 + 2 * reach
    share_blocks = blocks_dev // 2
    sums = sums_own[...] + sums_other[...]
    cross = sums[1:2, :]
    inter = sums[2:3, :]
    inv = 1.0 / (inter - cross * (cross / sums[0:1, :]) + 0.1 * inter)

    def peak(col, inv_block):
        best = None
        for t in range(block // LANES):
            v = total[:, pl.ds(col + t * LANES, LANES)]
            v = v * v * inv_block[:, t * LANES : (t + 1) * LANES]
            best = v if best is None else jnp.maximum(best, v)
        return jnp.max(best.T, axis=0, keepdims=True)

    peaks = []
    for q in range(labels):
        for b in range(blocks_dev):
            peaks.append(peak(q * snp_rows + b * block, inv[:, b * block : (b + 1) * block]))
    for b in range(share_blocks):
        mine = inv[:, b * block : (b + 1) * block]
        late = inv[:, (share_blocks + b) * block : (share_blocks + b + 1) * block]
        peaks.append(peak(labels * snp_rows + b * block, jnp.where(core == 0, mine, late)))
    while len(peaks) % 8:
        peaks.append(jnp.zeros_like(peaks[0]))
    peaks = jnp.concatenate(peaks, axis=0)
    count = peaks.shape[0]
    terms = []
    left = peaks
    for _ in range(3):
        terms.append(left.astype(jnp.bfloat16).astype(jnp.float32))
        left = left - terms[-1]
    terms = jnp.concatenate(terms, axis=0).astype(jnp.bfloat16)
    band = plan_ref.shape[1]
    slot = plan_ref[0:1, :]
    low = plan_ref[1:2, :]
    high = plan_ref[2:3, :]
    place = lax.broadcasted_iota(jnp.int32, (total.shape[0], band), 0) == slot
    spread = jnp.dot(
        terms, place.astype(jnp.float32).astype(jnp.bfloat16),
        preferred_element_type=jnp.float32,
    )
    spread = spread[:count] + spread[count : 2 * count] + spread[2 * count :]

    def masked(row, snp_block):
        inside = (snp_block >= low) & (snp_block < high)
        return jnp.where(inside, spread[row : row + 1], 0.0)

    def highest(row, blocks, first_block):
        best = masked(row, first_block)
        for b in range(1, blocks):
            best = jnp.maximum(best, masked(row + b, first_block + b))
        return best

    out_rows = [highest(labels * blocks_dev, share_blocks, chip * blocks_dev + core * share_blocks)]
    found = [highest(q * blocks_dev, blocks_dev, chip * blocks_dev) for q in range(labels)]
    for c in range(2):
        out_rows += [jnp.where(core == c, v, 0.0) for v in found]
    while len(out_rows) % 8:
        out_rows.append(jnp.zeros_like(out_rows[0]))
    dense = jnp.concatenate(out_rows, axis=0)
    out_ref[...] = jnp.zeros_like(out_ref)
    chips = out_ref.shape[0]
    for i in range(n_in):
        if i == 0:
            target = chip
        else:
            way = core if i <= reach else 1 - core
            target = chip + (2 * way - 1) * ((i - 1) % reach + 1)

        @pl.when((target >= 0) & (target < chips))
        def _(i=i, target=target):
            out_ref[target, :, pl.ds(0, genes)] = dense[:, i * genes : (i + 1) * genes]

    powers = jnp.sum(power[...].T, axis=0, keepdims=True)
    power_ref[...] = jnp.broadcast_to(powers, power_ref.shape)


def products(pos, sums, plan, full, mine, other, weights, caps, labels, chips, blocks_dev):
    genes, all_samples = full.shape
    used = genes + 2 * sum(caps)
    padded = -(-used // LANES) * LANES
    out_rows = -(-(1 + 2 * labels) // 8) * 8
    width = sum(w.shape[1] for w in weights)
    arrays = (full, *mine, *other)

    def whole(x):
        return pl.BlockSpec(x.shape, lambda k: (0,) * len(x.shape))

    outs = (
        jax.ShapeDtypeStruct((chips, out_rows, LANES), jnp.float32),
        jax.ShapeDtypeStruct((8, genes), jnp.float32),
    )
    return pl.pallas_call(
        functools.partial(
            product_kernel, caps=caps, labels=labels, genes=genes, blocks_dev=blocks_dev
        ),
        grid=(all_samples // DEPTH,),
        out_shape=outs,
        in_specs=[
            pl.BlockSpec(memory_space=pltpu.SMEM),
            *[whole(x) for x in (*sums, plan)],
            *[pl.BlockSpec((x.shape[0], DEPTH), lambda k: (0, k)) for x in arrays],
            *[pl.BlockSpec((DEPTH, w.shape[1]), lambda k: (k, 0)) for w in weights],
        ],
        out_specs=tuple(whole(x) for x in outs),
        scratch_shapes=[
            pltpu.VMEM((used, DEPTH), jnp.bfloat16),
            pltpu.VMEM((padded, width), jnp.float32),
            pltpu.VMEM((genes, LANES), jnp.float32),
        ],
        compiler_params=pltpu.CompilerParams(vmem_limit_bytes=48 * MIB),
        cost_estimate=pl.CostEstimate(
            flops=2 * used * all_samples * width,
            bytes_accessed=2 * all_samples * (width + used),
            transcendentals=0,
        ),
        name="products",
    )(pos, *sums, plan, *arrays, *weights)


def finish_kernel(own_ref, other_ref, power_ref, out_ref, *, samples):
    best = jnp.maximum(own_ref[0], other_ref[0])
    for i in range(1, own_ref.shape[0]):
        best = jnp.maximum(best, jnp.maximum(own_ref[i], other_ref[i]))
    labels, genes = out_ref.shape
    peak = best[:labels, :genes]
    out_ref[...] = jnp.sqrt(peak / (power_ref[0:1, :] / samples + 1e-05))


def shards(genotypes, phenotypes, environment, shuffles, window_start, window_end, chrom_bounds):
    snp_rows, half = genotypes.shape
    genes = phenotypes.shape[0]
    perms = shuffles.shape[0]
    chips = lax.axis_size("genome")
    cores = lax.axis_size("sample")
    blocks_dev = snp_rows // SNP_BLOCK
    reach = (HALF_BLK + blocks_dev - 1) // blocks_dev
    all_samples = half * cores
    labels = perms // cores
    caps = tuple(min(genes, genes * 4 >> k) for k in range(1, reach + 1))
    env = environment[None]
    start = window_start.reshape(-1, LANES)
    end = window_end.reshape(-1, LANES)
    pos = jnp.stack([lax.axis_index("genome"), lax.axis_index("sample")]).astype(jnp.int32)

    def travel(k, payload):
        pairs = [(i * cores, (i + k) * cores) for i in range(chips - k)]
        pairs += [((i + k) * cores + 1, i * cores + 1) for i in range(chips - k)]
        return lax.ppermute(payload, ("genome", "sample"), pairs)

    def one_round(turn, pos):
        core = pos[1:]
        other_pheno = swapped(phenotypes)
        own_sums = local_moments(genotypes, env)
        sums = (own_sums, swapped(own_sums))
        late_geno, _ = lax.optimization_barrier((genotypes, other_pheno))
        other_geno = swapped(late_geno)
        other_env = swapped(env)
        other_shuffles = swapped(shuffles)
        rounds, plan, full, *payloads = select(
            turn, pos, chrom_bounds, start, end, phenotypes, other_pheno, caps, blocks_dev
        )
        payloads = [full] * (reach - len(payloads)) + payloads
        mine = [travel(k, x) for k, x in enumerate(payloads, 1)]
        weights = snp_side(
            core, env, other_env, *sums, shuffles, other_shuffles, genotypes, other_geno, labels
        )
        mine, weights = lax.optimization_barrier((mine, weights))
        other = [swapped(x) for x in mine]
        found, power = products(
            pos, sums, plan, full, mine, other, weights, caps, labels, chips, blocks_dev
        )
        return rounds, found, power

    rounds, found, power = one_round(jnp.zeros((1,), jnp.int32), pos)

    def more(carry):
        return carry[0] < rounds[0]

    def again(carry):
        turn, best = carry
        turns, place = lax.optimization_barrier((jnp.full((1,), turn, jnp.int32), pos))
        return turn + 1, jnp.maximum(best, one_round(turns, place)[1])

    _, found = lax.while_loop(more, again, (jnp.int32(1), found))
    gathered = lax.all_to_all(found, "genome", 0, 0, tiled=True)
    return pl.pallas_call(
        functools.partial(finish_kernel, samples=all_samples),
        out_shape=jax.ShapeDtypeStruct((perms + 1, genes), jnp.float32),
        name="finish",
    )(gathered, swapped(gathered), power)


def solution(mesh):
    placed = (
        P("genome", "sample"),
        P("genome", "sample"),
        P("sample"),
        P(None, "sample"),
        P(),
        P(),
        P(),
    )
    return jax.shard_map(
        shards, mesh=mesh, in_specs=placed, out_specs=P(None, "genome"), check_vma=False
    )
```

```python
import functools

import jax
import jax.numpy as jnp
from jax import lax
from jax.experimental import pallas as pl
from jax.experimental.pallas import tpu as pltpu
from jax.sharding import PartitionSpec as P

SNP_BLOCK = 256
HALF_BLK = 7
LANES = 128
ROWS_STEP = 16
UNROLL = 16
DEPTH = 2048
SIDE = 2 * LANES
CHUNK = 1024
MIB = 2**20


def passed_along(x, axis, by):
    count = lax.axis_size(axis)
    pairs = [(i, i + by) for i in range(count) if 0 <= i + by < count]
    return lax.ppermute(x, axis, pairs)


def swapped(x):
    count = lax.axis_size("sample")
    return lax.ppermute(x, "sample", [(i, (i + 1) % count) for i in range(count)])


def moments_kernel(geno_ref, env_ref, out_ref, sums):
    step = pl.program_id(0)
    snp_rows, chunk = geno_ref.shape

    @pl.when(step == 0)
    def _():
        sums[...] = jnp.zeros_like(sums)

    def add_rows(i, carry):
        first = pl.multiple_of(i * ROWS_STEP, ROWS_STEP)
        held = [sums[m, pl.ds(first, ROWS_STEP), :] for m in range(3)]
        for t in range(chunk // LANES):
            x = geno_ref[pl.ds(first, ROWS_STEP), pl.ds(t * LANES, LANES)].astype(jnp.float32)
            e = env_ref[:, pl.ds(t * LANES, LANES)]
            x = x * x
            held[0] = held[0] + x
            x = x * e
            held[1] = held[1] + x
            held[2] = held[2] + x * e
        for m in range(3):
            sums[m, pl.ds(first, ROWS_STEP), :] = held[m]
        return carry

    lax.fori_loop(0, snp_rows // ROWS_STEP, add_rows, 0, unroll=4)

    @pl.when(step == pl.num_programs(0) - 1)
    def _():
        rows = [jnp.sum(sums[m].T, axis=0, keepdims=True) for m in range(3)]
        rows.append(jnp.zeros((out_ref.shape[0] - 3, snp_rows), jnp.float32))
        out_ref[...] = jnp.concatenate(rows, axis=0)


def local_moments(geno, env):
    snp_rows, half = geno.shape
    chunk = CHUNK
    return pl.pallas_call(
        moments_kernel,
        grid=(half // chunk,),
        out_shape=jax.ShapeDtypeStruct((8, snp_rows), jnp.float32),
        in_specs=[
            pl.BlockSpec((snp_rows, chunk), lambda k: (0, k)),
            pl.BlockSpec((1, chunk), lambda k: (0, k)),
        ],
        out_specs=pl.BlockSpec((8, snp_rows), lambda k: (0, 0)),
        scratch_shapes=[pltpu.VMEM((3, snp_rows, LANES), jnp.float32)],
        compiler_params=pltpu.CompilerParams(vmem_limit_bytes=60 * MIB),
        cost_estimate=pl.CostEstimate(
            flops=5 * 10**9, bytes_accessed=2 * snp_rows * half, transcendentals=0
        ),
        name="local_moments",
    )(geno, env)


def snp_side_kernel(
    core_ref, env_own, env_other, sums_own, sums_other, shuf_own, shuf_other, own_ref, other_ref,
    *rest, labels,
):
    out_refs, scratch = rest[: labels + 1], rest[labels + 1 :]
    (
        idx, geno, table, dests, stage, first_stage, slope, idx_sems, in_sems, out_sems, first_sems,
    ) = scratch
    snp_rows, half = own_ref.shape
    all_samples = 2 * half
    chunks = all_samples // CHUNK
    words = snp_rows // LANES
    share = snp_rows // 2
    side = SIDE
    per_chunk = CHUNK // side
    core = core_ref[0]
    depth = geno.shape[0]

    def load(k):
        source = own_ref if k * CHUNK < half else other_ref
        return pltpu.make_async_copy(
            source.at[:, pl.ds((k * CHUNK) % half, CHUNK)], geno.at[k % depth],
            in_sems.at[k % depth],
        )

    def load_idx(q, h):
        source = shuf_own if h == 0 else shuf_other
        return pltpu.make_async_copy(
            source.at[core * labels + q],
            idx.at[pl.ds(q * all_samples + h * half, half)],
            idx_sems.at[2 * q + h],
        )

    def save_first(k):
        there = jnp.where(core == 0, k * CHUNK, (k * CHUNK + half) % all_samples)
        rows = pl.ds(pl.multiple_of(there, CHUNK), CHUNK)
        return pltpu.make_async_copy(
            first_stage.at[k % 2, :, pl.ds(pl.multiple_of(core * share, share), share)],
            out_refs[labels].at[rows],
            first_sems.at[k % 2],
        )

    def save(q, k):
        return pltpu.make_async_copy(
            stage.at[k % 2],
            out_refs[q].at[pl.ds(k * CHUNK, CHUNK)],
            out_sems.at[k % 2],
        )

    def read_rows(first):
        base = pl.multiple_of(first * words, UNROLL * words)
        return tuple(table[pl.ds(base + u * words, words), :] for u in range(UNROLL))

    def write_rows(q, first, held):
        for u in range(UNROLL):
            to = pl.multiple_of(idx[q * all_samples + first + u] * words, words)
            dests[q][pl.ds(to, words), :] = held[u]

    def narrowed(q, at, rows):
        return [
            dests[q][pl.ds(at * words + c, rows, stride=words), :].astype(jnp.bfloat16)
            for c in range(words)
        ]

    for k in range(depth):
        load(k).start()
    for q in range(labels):
        for h in range(2):
            load_idx(q, h).start()
    sums = sums_own[...] + sums_other[...]
    slope[...] = jnp.broadcast_to(sums[1:2, :] / sums[0:1, :], (LANES, snp_rows)).T
    unit = (
        lax.broadcasted_iota(jnp.int32, (side, side), 0)
        == lax.broadcasted_iota(jnp.int32, (side, side), 1)
    ).astype(jnp.bfloat16)
    for q in range(labels):
        for h in range(2):
            load_idx(q, h).wait()

    groups = side // UNROLL // words
    for k in range(chunks):
        load(k).wait()
        if k >= 2:
            save_first(k - 2).wait()
        env_ref = env_own if k * CHUNK < half else env_other

        def turn(i, carry, k=k, env_ref=env_ref):
            at = pl.multiple_of(i * side, side)
            e = env_ref[:, pl.ds((k * CHUNK) % half + at, side)]
            behind = pl.multiple_of(jnp.maximum(k * CHUNK + at - side, 0), side)
            held = read_rows(behind)
            for c in range(words):
                rows = pl.ds(c * LANES, LANES)
                x = geno[k % depth, rows, pl.ds(at, side)].astype(jnp.float32)
                r = slope[rows, :]
                a = x * (e - jnp.concatenate([r] * (side // LANES), axis=1))
                t = lax.dot_general(
                    unit, a.astype(jnp.bfloat16), (((1,), (1,)), ((), ())),
                    preferred_element_type=jnp.float32,
                )
                for g in range(groups):
                    first = pl.multiple_of(behind + (c * groups + g) * UNROLL, UNROLL)
                    if c * groups + g + 1 < words * groups:
                        later = read_rows(first + UNROLL)
                    write_rows(0, first, held)
                    held = later
                table[pl.ds((k * CHUNK + at) * words + c, side, stride=words), :] = t
                first_stage[k % 2, pl.ds(at, side), pl.ds(c * LANES, LANES)] = t.astype(
                    jnp.bfloat16
                )
            return carry

        lax.fori_loop(0, per_chunk, turn, 0)
        save_first(k).start()
        if k + depth < chunks:
            load(k + depth).start()

    def last_block(i, carry):
        first = pl.multiple_of(all_samples - side + i * UNROLL, UNROLL)
        write_rows(0, first, read_rows(first))
        return carry

    lax.fori_loop(0, side // UNROLL, last_block, 0)

    count = 0
    pair = 2 * UNROLL
    for q in range(1, labels + 1):
        held = read_rows(0)
        for k in range(chunks):
            if count >= 2:
                save((count - 2) // chunks, (count - 2) % chunks).wait()

            def step(i, held, k=k, q=q):
                at = pl.multiple_of(i * pair, pair)
                first = pl.multiple_of(k * CHUNK + at, pair)
                middle = read_rows(first + UNROLL)
                parts = narrowed(q - 1, first, pair)
                write_rows(q, first, held)
                after = jnp.minimum(first + pair, all_samples - UNROLL)
                held = read_rows(pl.multiple_of(after, UNROLL))
                write_rows(q, first + UNROLL, middle)
                for c in range(words):
                    stage[k % 2, pl.ds(at, pair), pl.ds(c * LANES, LANES)] = parts[c]
                return held

            def wide(i, carry, k=k, q=q):
                at = pl.multiple_of(i * side, side)
                parts = narrowed(q - 1, k * CHUNK + at, side)
                for c in range(words):
                    stage[k % 2, pl.ds(at, side), pl.ds(c * LANES, LANES)] = parts[c]
                return carry

            if q < labels:
                held = lax.fori_loop(0, CHUNK // pair, step, held)
            else:
                lax.fori_loop(0, CHUNK // side, wide, 0)
            save(q - 1, k).start()
            count += 1
    for k in range(chunks - 2, chunks):
        save_first(k).wait()
        save(labels - 1, k).wait()


def snp_side(core, env_own, env_other, sums_own, sums_other, shuf_own, shuf_other, own, other,
             labels):
    snp_rows, half = own.shape
    all_samples = 2 * half
    words = snp_rows // LANES
    widths = [snp_rows] * labels + [snp_rows // 2]
    any_spec = pl.BlockSpec(memory_space=pl.ANY)
    smem = pl.BlockSpec(memory_space=pltpu.SMEM)
    vmem = pl.BlockSpec(memory_space=pltpu.VMEM)
    return pl.pallas_call(
        functools.partial(snp_side_kernel, labels=labels),
        out_shape=[jax.ShapeDtypeStruct((all_samples, w), jnp.bfloat16) for w in widths],
        in_specs=[smem, vmem, vmem, vmem, vmem, any_spec, any_spec, any_spec, any_spec],
        out_specs=[any_spec for _ in widths],
        scratch_shapes=[
            pltpu.SMEM((labels * all_samples,), jnp.int32),
            pltpu.VMEM((2, snp_rows, CHUNK), jnp.bfloat16),
            pltpu.VMEM((all_samples * words, LANES), jnp.float32),
            [pltpu.VMEM((all_samples * words, LANES), jnp.float32) for _ in range(labels)],
            pltpu.VMEM((2, CHUNK, snp_rows), jnp.bfloat16),
            pltpu.VMEM((2, CHUNK, snp_rows), jnp.bfloat16),
            pltpu.VMEM((snp_rows, LANES), jnp.float32),
            pltpu.SemaphoreType.DMA((2 * labels,)),
            pltpu.SemaphoreType.DMA((2,)),
            pltpu.SemaphoreType.DMA((2,)),
            pltpu.SemaphoreType.DMA((2,)),
        ],
        compiler_params=pltpu.CompilerParams(vmem_limit_bytes=61 * MIB),
        cost_estimate=pl.CostEstimate(
            flops=40 * 10**9, bytes_accessed=60 * 10**6, transcendentals=0
        ),
        name="snp_side",
    )(core, env_own, env_other, sums_own, sums_other, shuf_own, shuf_other, own, other)


def window_plan(start, end, bounds_ref, n_bounds, total_blocks):
    middle = (start + end - 1) // 2
    lower_edge = jnp.zeros_like(start)
    upper_edge = jnp.full_like(end, total_blocks)
    for i in range(n_bounds):
        edge = bounds_ref[i]
        before = edge <= middle
        lower_edge = jnp.where(before, jnp.maximum(lower_edge, edge), lower_edge)
        upper_edge = jnp.where(before, upper_edge, jnp.minimum(upper_edge, edge))
    return jnp.maximum(start, lower_edge), jnp.minimum(end, upper_edge)


def select_kernel(
    round_ref, pos_ref, bounds_ref, start_ref, end_ref, own_ref, other_ref,
    rounds_ref, plan_ref, full_ref, *rest, caps, blocks_dev,
):
    reach = len(caps)
    genes, half = own_ref.shape
    chosen_from = sum(cap == genes for cap in caps)
    (slots, edges), pay_refs = rest[-2:], rest[:-2]
    shape = start_ref.shape
    per_row = LANES // genes
    chips = shape[0] * per_row
    chip, core = pos_ref[0], pos_ref[1]
    turn = round_ref[0]
    low, high = window_plan(
        start_ref[...], end_ref[...], bounds_ref, bounds_ref.shape[0], chips * blocks_dev
    )
    edges[0] = low
    edges[1] = high
    at = lax.broadcasted_iota(jnp.int32, shape, 0) * per_row
    at = at + lax.broadcasted_iota(jnp.int32, shape, 1) // genes
    a = lax.broadcasted_iota(jnp.int32, (LANES, LANES), 0)
    b = lax.broadcasted_iota(jnp.int32, (LANES, LANES), 1)
    upto = ((a <= b) & (a // genes == b // genes)).astype(jnp.float32).astype(jnp.bfloat16)
    rounds = jnp.int32(0)
    for way in range(2):
        for k in range(1, reach + 1):
            to = at + (k if way == 0 else -k)
            need = (
                (low < (to + 1) * blocks_dev) & (high > to * blocks_dev)
                & (low < high) & (to >= 0) & (to < chips)
            )
            rank = jnp.dot(
                need.astype(jnp.float32).astype(jnp.bfloat16), upto,
                preferred_element_type=jnp.float32,
            ).astype(jnp.int32)
            cap = caps[k - 1]
            if cap == genes:
                which = lax.broadcasted_iota(jnp.int32, shape, 1) % genes
                slots[way * reach + k - 1] = jnp.where(need, which, -1)
                continue
            slot = rank - 1 - turn * cap
            slots[way * reach + k - 1] = jnp.where(
                need & (slot >= 0) & (slot < cap), slot, -1
            )
            rounds = jnp.maximum(rounds, (jnp.max(rank) + cap - 1) // cap)
    rounds_ref[0] = rounds

    def of_chip(ref, index, which):
        row = ref[index, pl.ds(which // per_row, 1), :]
        out = row[:, :genes]
        for part in range(1, per_row):
            out = jnp.where(
                which % per_row == part, row[:, part * genes : (part + 1) * genes], out
            )
        return out

    used = [lax.broadcasted_iota(jnp.int32, (1, genes), 1)]
    lows = [of_chip(edges, 0, chip)]
    highs = [of_chip(edges, 1, chip)]
    first = genes
    for side in range(2):
        way = core if side == 0 else 1 - core
        for k in range(1, reach + 1):
            source = chip + (2 * way - 1) * k
            valid = (source >= 0) & (source < chips)
            source = jnp.clip(source, 0, chips - 1)
            slot = of_chip(slots, way * reach + k - 1, source)
            used.append(jnp.where(valid & (slot >= 0), slot + first, -1))
            lows.append(of_chip(edges, 0, source))
            highs.append(jnp.where(valid, of_chip(edges, 1, source), 0))
            first += caps[k - 1]
    while len(used) * genes < plan_ref.shape[1]:
        used.append(jnp.full_like(used[0], -1))
        lows.append(jnp.zeros_like(used[0]))
        highs.append(jnp.zeros_like(used[0]))
    plan_ref[...] = jnp.zeros_like(plan_ref)
    for row, parts in enumerate((used, lows, highs)):
        plan_ref[pl.ds(row, 1), :] = jnp.concatenate(parts, axis=1)

    picks = []
    for k in range(chosen_from + 1, reach + 1):
        slot = of_chip(slots, core * reach + k - 1, chip)
        rows = lax.broadcasted_iota(jnp.int32, (caps[k - 1], genes), 0)
        picks.append((rows == slot).astype(jnp.float32))
    if picks:
        picks = jnp.concatenate(picks, axis=0).astype(jnp.bfloat16)
    step = 1024

    def copy(i, carry):
        cols = pl.ds(pl.multiple_of(i * step, step), step)
        late = pl.ds(pl.multiple_of(half + i * step, step), step)
        a, b = own_ref[:, cols], other_ref[:, cols]
        for part, to in ((jnp.where(core == 0, a, b), cols), (jnp.where(core == 0, b, a), late)):
            full_ref[:, to] = part
            if pay_refs:
                chosen = jnp.dot(picks, part, preferred_element_type=jnp.float32)
                chosen = chosen.astype(jnp.bfloat16)
                row = 0
                for pay in pay_refs:
                    pay[:, to] = chosen[row : row + pay.shape[0]]
                    row += pay.shape[0]
        return carry

    lax.fori_loop(0, half // step, copy, 0)


def select(turn, pos, bounds, start, end, own, other, caps, blocks_dev):
    genes, half = own.shape
    all_samples = 2 * half
    reach = len(caps)
    smem = pl.BlockSpec(memory_space=pltpu.SMEM)
    vmem = pl.BlockSpec(memory_space=pltpu.VMEM)
    width = -(-(2 * reach + 1) * genes // LANES) * LANES
    chosen = [cap for cap in caps if cap < genes]
    return pl.pallas_call(
        functools.partial(select_kernel, caps=caps, blocks_dev=blocks_dev),
        out_shape=(
            jax.ShapeDtypeStruct((1,), jnp.int32),
            jax.ShapeDtypeStruct((8, width), jnp.int32),
            jax.ShapeDtypeStruct((genes, all_samples), jnp.bfloat16),
            *[jax.ShapeDtypeStruct((cap, all_samples), jnp.bfloat16) for cap in chosen],
        ),
        in_specs=[smem, smem, smem, vmem, vmem, vmem, vmem],
        out_specs=(smem, vmem, vmem, *[vmem for _ in chosen]),
        scratch_shapes=[
            pltpu.VMEM((2 * reach,) + start.shape, jnp.int32),
            pltpu.VMEM((2,) + start.shape, jnp.int32),
        ],
        compiler_params=pltpu.CompilerParams(vmem_limit_bytes=24 * MIB),
        name="select",
    )(turn, pos, bounds, start, end, own, other)


def product_kernel(
    pos_ref, sums_own, sums_other, plan_ref, *rest, caps, labels, genes, blocks_dev
):
    reach = len(caps)
    n_in = 1 + 2 * reach
    gene_refs = rest[:n_in]
    weight_refs = rest[n_in : n_in + labels + 1]
    out_ref, power_ref, rows, total, power = rest[n_in + labels + 1 :]
    step = pl.program_id(0)
    snp_rows = sums_own.shape[1]
    depth = rows.shape[1]
    used = rows.shape[0]
    chip, core = pos_ref[0], pos_ref[1]

    @pl.when(step == 0)
    def _():
        total[...] = jnp.zeros_like(total)
        power[...] = jnp.zeros_like(power)

    at = 0
    for ref in gene_refs:
        rows[pl.ds(at, ref.shape[0]), :] = ref[...]
        at += ref.shape[0]
    for q, ref in enumerate(weight_refs):
        cols = pl.ds(q * snp_rows, ref.shape[1])
        total[pl.ds(0, used), cols] += jnp.dot(
            rows[...], ref[...], preferred_element_type=jnp.float32
        )
    kept = power[...]
    for t in range(depth // LANES):
        x = rows[pl.ds(0, genes), pl.ds(t * LANES, LANES)].astype(jnp.float32)
        kept = kept + x * x
    power[...] = kept

    @pl.when(step == pl.num_programs(0) - 1)
    def _():
        summed_up(
            chip, core, sums_own, sums_other, plan_ref, out_ref, power_ref, total, power,
            reach=reach, labels=labels, genes=genes, blocks_dev=blocks_dev,
        )


def summed_up(
    chip, core, sums_own, sums_other, plan_ref, out_ref, power_ref, total, power,
    *, reach, labels, genes, blocks_dev,
):
    snp_rows = sums_own.shape[1]
    block = SNP_BLOCK
    n_in = 1 + 2 * reach
    share_blocks = blocks_dev // 2
    sums = sums_own[...] + sums_other[...]
    cross = sums[1:2, :]
    inter = sums[2:3, :]
    inv = 1.0 / (inter - cross * (cross / sums[0:1, :]) + 0.1 * inter)

    def peak(col, inv_block):
        best = None
        for t in range(block // LANES):
            v = total[:, pl.ds(col + t * LANES, LANES)]
            v = v * v * inv_block[:, t * LANES : (t + 1) * LANES]
            best = v if best is None else jnp.maximum(best, v)
        return jnp.max(best.T, axis=0, keepdims=True)

    peaks = []
    for q in range(labels):
        for b in range(blocks_dev):
            peaks.append(peak(q * snp_rows + b * block, inv[:, b * block : (b + 1) * block]))
    for b in range(share_blocks):
        mine = inv[:, b * block : (b + 1) * block]
        late = inv[:, (share_blocks + b) * block : (share_blocks + b + 1) * block]
        peaks.append(peak(labels * snp_rows + b * block, jnp.where(core == 0, mine, late)))
    while len(peaks) % 8:
        peaks.append(jnp.zeros_like(peaks[0]))
    peaks = jnp.concatenate(peaks, axis=0)
    count = peaks.shape[0]
    terms = []
    left = peaks
    for _ in range(3):
        terms.append(left.astype(jnp.bfloat16).astype(jnp.float32))
        left = left - terms[-1]
    terms = jnp.concatenate(terms, axis=0).astype(jnp.bfloat16)
    band = plan_ref.shape[1]
    slot = plan_ref[0:1, :]
    low = plan_ref[1:2, :]
    high = plan_ref[2:3, :]
    place = lax.broadcasted_iota(jnp.int32, (total.shape[0], band), 0) == slot
    spread = jnp.dot(
        terms, place.astype(jnp.float32).astype(jnp.bfloat16),
        preferred_element_type=jnp.float32,
    )
    spread = spread[:count] + spread[count : 2 * count] + spread[2 * count :]

    def masked(row, snp_block):
        inside = (snp_block >= low) & (snp_block < high)
        return jnp.where(inside, spread[row : row + 1], 0.0)

    def highest(row, blocks, first_block):
        best = masked(row, first_block)
        for b in range(1, blocks):
            best = jnp.maximum(best, masked(row + b, first_block + b))
        return best

    out_rows = [highest(labels * blocks_dev, share_blocks, chip * blocks_dev + core * share_blocks)]
    found = [highest(q * blocks_dev, blocks_dev, chip * blocks_dev) for q in range(labels)]
    for c in range(2):
        out_rows += [jnp.where(core == c, v, 0.0) for v in found]
    while len(out_rows) % 8:
        out_rows.append(jnp.zeros_like(out_rows[0]))
    dense = jnp.concatenate(out_rows, axis=0)
    out_ref[...] = jnp.zeros_like(out_ref)
    chips = out_ref.shape[0]
    for i in range(n_in):
        if i == 0:
            target = chip
        else:
            way = core if i <= reach else 1 - core
            target = chip + (2 * way - 1) * ((i - 1) % reach + 1)

        @pl.when((target >= 0) & (target < chips))
        def _(i=i, target=target):
            out_ref[target, :, pl.ds(0, genes)] = dense[:, i * genes : (i + 1) * genes]

    powers = jnp.sum(power[...].T, axis=0, keepdims=True)
    power_ref[...] = jnp.broadcast_to(powers, power_ref.shape)


def products(pos, sums, plan, full, mine, other, weights, caps, labels, chips, blocks_dev):
    genes, all_samples = full.shape
    used = genes + 2 * sum(caps)
    padded = -(-used // LANES) * LANES
    out_rows = -(-(1 + 2 * labels) // 8) * 8
    width = sum(w.shape[1] for w in weights)
    arrays = (full, *mine, *other)

    def whole(x):
        return pl.BlockSpec(x.shape, lambda k: (0,) * len(x.shape))

    outs = (
        jax.ShapeDtypeStruct((chips, out_rows, LANES), jnp.float32),
        jax.ShapeDtypeStruct((8, genes), jnp.float32),
    )
    return pl.pallas_call(
        functools.partial(
            product_kernel, caps=caps, labels=labels, genes=genes, blocks_dev=blocks_dev
        ),
        grid=(all_samples // DEPTH,),
        out_shape=outs,
        in_specs=[
            pl.BlockSpec(memory_space=pltpu.SMEM),
            *[whole(x) for x in (*sums, plan)],
            *[pl.BlockSpec((x.shape[0], DEPTH), lambda k: (0, k)) for x in arrays],
            *[pl.BlockSpec((DEPTH, w.shape[1]), lambda k: (k, 0)) for w in weights],
        ],
        out_specs=tuple(whole(x) for x in outs),
        scratch_shapes=[
            pltpu.VMEM((used, DEPTH), jnp.bfloat16),
            pltpu.VMEM((padded, width), jnp.float32),
            pltpu.VMEM((genes, LANES), jnp.float32),
        ],
        compiler_params=pltpu.CompilerParams(vmem_limit_bytes=48 * MIB),
        cost_estimate=pl.CostEstimate(
            flops=2 * used * all_samples * width,
            bytes_accessed=2 * all_samples * (width + used),
            transcendentals=0,
        ),
        name="products",
    )(pos, *sums, plan, *arrays, *weights)


def finish_kernel(own_ref, other_ref, power_ref, out_ref, *, samples):
    best = jnp.maximum(own_ref[0], other_ref[0])
    for i in range(1, own_ref.shape[0]):
        best = jnp.maximum(best, jnp.maximum(own_ref[i], other_ref[i]))
    labels, genes = out_ref.shape
    peak = best[:labels, :genes]
    out_ref[...] = jnp.sqrt(peak / (power_ref[0:1, :] / samples + 1e-05))


def shards(genotypes, phenotypes, environment, shuffles, window_start, window_end, chrom_bounds):
    snp_rows, half = genotypes.shape
    genes = phenotypes.shape[0]
    perms = shuffles.shape[0]
    chips = lax.axis_size("genome")
    cores = lax.axis_size("sample")
    blocks_dev = snp_rows // SNP_BLOCK
    reach = (HALF_BLK + blocks_dev - 1) // blocks_dev
    all_samples = half * cores
    labels = perms // cores
    caps = tuple(min(genes, genes * 4 >> k) for k in range(1, reach + 1))
    env = environment[None]
    start = window_start.reshape(-1, LANES)
    end = window_end.reshape(-1, LANES)
    pos = jnp.stack([lax.axis_index("genome"), lax.axis_index("sample")]).astype(jnp.int32)

    def travel(k, payload):
        pairs = [(i * cores, (i + k) * cores) for i in range(chips - k)]
        pairs += [((i + k) * cores + 1, i * cores + 1) for i in range(chips - k)]
        return lax.ppermute(payload, ("genome", "sample"), pairs)

    def one_round(turn, pos):
        core = pos[1:]
        other_pheno = swapped(phenotypes)
        own_sums = local_moments(genotypes, env)
        sums = (own_sums, swapped(own_sums))
        late_geno, _ = lax.optimization_barrier((genotypes, other_pheno))
        other_geno = swapped(late_geno)
        other_env = swapped(env)
        other_shuffles = swapped(shuffles)
        rounds, plan, full, *payloads = select(
            turn, pos, chrom_bounds, start, end, phenotypes, other_pheno, caps, blocks_dev
        )
        payloads = [full] * (reach - len(payloads)) + payloads
        mine = [travel(k, x) for k, x in enumerate(payloads, 1)]
        weights = snp_side(
            core, env, other_env, *sums, shuffles, other_shuffles, genotypes, other_geno, labels
        )
        mine, weights = lax.optimization_barrier((mine, weights))
        other = [swapped(x) for x in mine]
        found, power = products(
            pos, sums, plan, full, mine, other, weights, caps, labels, chips, blocks_dev
        )
        return rounds, found, power

    rounds, found, power = one_round(jnp.zeros((1,), jnp.int32), pos)

    def more(carry):
        return carry[0] < rounds[0]

    def again(carry):
        turn, best = carry
        turns, place = lax.optimization_barrier((jnp.full((1,), turn, jnp.int32), pos))
        return turn + 1, jnp.maximum(best, one_round(turns, place)[1])

    _, found = lax.while_loop(more, again, (jnp.int32(1), found))
    gathered = lax.all_to_all(found, "genome", 0, 0, tiled=True)
    return pl.pallas_call(
        functools.partial(finish_kernel, samples=all_samples),
        out_shape=jax.ShapeDtypeStruct((perms + 1, genes), jnp.float32),
        name="finish",
    )(gathered, swapped(gathered), power)


def solution(mesh):
    placed = (
        P("genome", "sample"),
        P("genome", "sample"),
        P("sample"),
        P(None, "sample"),
        P(),
        P(),
        P(),
    )
    return jax.shard_map(
        shards, mesh=mesh, in_specs=placed, out_specs=P(None, "genome"), check_vma=False
    )
```

```python
import functools

import jax
import jax.numpy as jnp
from jax import lax
from jax.experimental import pallas as pl
from jax.experimental.pallas import tpu as pltpu
from jax.sharding import PartitionSpec as P

SNP_BLOCK = 256
HALF_BLK = 7
LANES = 128
ROWS_STEP = 16
UNROLL = 32
DEPTH = 2048
SIDE = 2 * LANES
CHUNK = 1024
MIB = 2**20


def passed_along(x, axis, by):
    count = lax.axis_size(axis)
    pairs = [(i, i + by) for i in range(count) if 0 <= i + by < count]
    return lax.ppermute(x, axis, pairs)


def swapped(x):
    count = lax.axis_size("sample")
    return lax.ppermute(x, "sample", [(i, (i + 1) % count) for i in range(count)])


def moments_kernel(geno_ref, env_ref, out_ref, sums):
    step = pl.program_id(0)
    snp_rows, chunk = geno_ref.shape

    @pl.when(step == 0)
    def _():
        sums[...] = jnp.zeros_like(sums)

    def add_rows(i, carry):
        first = pl.multiple_of(i * ROWS_STEP, ROWS_STEP)
        held = [sums[m, pl.ds(first, ROWS_STEP), :] for m in range(3)]
        for t in range(chunk // LANES):
            x = geno_ref[pl.ds(first, ROWS_STEP), pl.ds(t * LANES, LANES)].astype(jnp.float32)
            e = env_ref[:, pl.ds(t * LANES, LANES)]
            x = x * x
            held[0] = held[0] + x
            x = x * e
            held[1] = held[1] + x
            held[2] = held[2] + x * e
        for m in range(3):
            sums[m, pl.ds(first, ROWS_STEP), :] = held[m]
        return carry

    lax.fori_loop(0, snp_rows // ROWS_STEP, add_rows, 0, unroll=4)

    @pl.when(step == pl.num_programs(0) - 1)
    def _():
        rows = [jnp.sum(sums[m].T, axis=0, keepdims=True) for m in range(3)]
        rows.append(jnp.zeros((out_ref.shape[0] - 3, snp_rows), jnp.float32))
        out_ref[...] = jnp.concatenate(rows, axis=0)


def local_moments(geno, env):
    snp_rows, half = geno.shape
    chunk = CHUNK
    return pl.pallas_call(
        moments_kernel,
        grid=(half // chunk,),
        out_shape=jax.ShapeDtypeStruct((8, snp_rows), jnp.float32),
        in_specs=[
            pl.BlockSpec((snp_rows, chunk), lambda k: (0, k)),
            pl.BlockSpec((1, chunk), lambda k: (0, k)),
        ],
        out_specs=pl.BlockSpec((8, snp_rows), lambda k: (0, 0)),
        scratch_shapes=[pltpu.VMEM((3, snp_rows, LANES), jnp.float32)],
        compiler_params=pltpu.CompilerParams(vmem_limit_bytes=60 * MIB),
        cost_estimate=pl.CostEstimate(
            flops=5 * 10**9, bytes_accessed=2 * snp_rows * half, transcendentals=0
        ),
        name="local_moments",
    )(geno, env)


def snp_side_kernel(
    core_ref, env_own, env_other, sums_own, sums_other, shuf_own, shuf_other, own_ref, other_ref,
    *rest, labels,
):
    out_refs, scratch = rest[: labels + 1], rest[labels + 1 :]
    (
        idx, geno, table, dests, stage, first_stage, slope, idx_sems, in_sems, out_sems, first_sems,
    ) = scratch
    snp_rows, half = own_ref.shape
    all_samples = 2 * half
    chunks = all_samples // CHUNK
    words = snp_rows // LANES
    share = snp_rows // 2
    side = SIDE
    per_chunk = CHUNK // side
    core = core_ref[0]
    depth = geno.shape[0]

    def load(k):
        source = own_ref if k * CHUNK < half else other_ref
        return pltpu.make_async_copy(
            source.at[:, pl.ds((k * CHUNK) % half, CHUNK)], geno.at[k % depth],
            in_sems.at[k % depth],
        )

    def load_idx(q, h):
        source = shuf_own if h == 0 else shuf_other
        return pltpu.make_async_copy(
            source.at[core * labels + q],
            idx.at[pl.ds(q * all_samples + h * half, half)],
            idx_sems.at[2 * q + h],
        )

    def save_first(k):
        there = jnp.where(core == 0, k * CHUNK, (k * CHUNK + half) % all_samples)
        rows = pl.ds(pl.multiple_of(there, CHUNK), CHUNK)
        return pltpu.make_async_copy(
            first_stage.at[k % 2, :, pl.ds(pl.multiple_of(core * share, share), share)],
            out_refs[labels].at[rows],
            first_sems.at[k % 2],
        )

    def save(q, k):
        return pltpu.make_async_copy(
            stage.at[k % 2],
            out_refs[q].at[pl.ds(k * CHUNK, CHUNK)],
            out_sems.at[k % 2],
        )

    def read_rows(first):
        base = pl.multiple_of(first * words, UNROLL * words)
        return [table[pl.ds(base + u * words, words), :] for u in range(UNROLL)]

    def write_rows(q, first, held):
        for u in range(UNROLL):
            to = pl.multiple_of(idx[q * all_samples + first + u] * words, words)
            dests[q][pl.ds(to, words), :] = held[u]

    def narrowed(q, at, rows):
        return [
            dests[q][pl.ds(at * words + c, rows, stride=words), :].astype(jnp.bfloat16)
            for c in range(words)
        ]

    for k in range(depth):
        load(k).start()
    for q in range(labels):
        for h in range(2):
            load_idx(q, h).start()
    sums = sums_own[...] + sums_other[...]
    slope[...] = jnp.broadcast_to(sums[1:2, :] / sums[0:1, :], (LANES, snp_rows)).T
    unit = (
        lax.broadcasted_iota(jnp.int32, (side, side), 0)
        == lax.broadcasted_iota(jnp.int32, (side, side), 1)
    ).astype(jnp.bfloat16)
    for q in range(labels):
        for h in range(2):
            load_idx(q, h).wait()

    per_turn = side // LANES
    groups = side // UNROLL // (words // per_turn)
    for k in range(chunks):
        load(k).wait()
        if k >= 2:
            save_first(k - 2).wait()
        env_ref = env_own if k * CHUNK < half else env_other

        def turn(i, carry, k=k, env_ref=env_ref):
            at = pl.multiple_of(i * side, side)
            e = env_ref[:, pl.ds((k * CHUNK) % half + at, side)]
            behind = pl.multiple_of(jnp.maximum(k * CHUNK + at - side, 0), side)
            for j in range(words // per_turn):
                rows = pl.ds(j * side, side)
                x = geno[k % depth, rows, pl.ds(at, side)].astype(jnp.float32)
                r = slope[rows, :]
                a = x * (e - jnp.concatenate([r] * per_turn, axis=1))
                t = lax.dot_general(
                    unit, a.astype(jnp.bfloat16), (((1,), (1,)), ((), ())),
                    preferred_element_type=jnp.float32,
                )
                for g in range(groups):
                    first = pl.multiple_of(behind + (j * groups + g) * UNROLL, UNROLL)
                    write_rows(0, first, read_rows(first))
                for c in range(per_turn):
                    word = j * per_turn + c
                    table[pl.ds((k * CHUNK + at) * words + word, side, stride=words), :] = t[
                        :, c * LANES : (c + 1) * LANES
                    ]
                first_stage[k % 2, pl.ds(at, side), rows] = t.astype(jnp.bfloat16)
            return carry

        lax.fori_loop(0, per_chunk, turn, 0)
        save_first(k).start()
        if k + depth < chunks:
            load(k + depth).start()

    def last_block(i, carry):
        first = pl.multiple_of(all_samples - side + i * UNROLL, UNROLL)
        write_rows(0, first, read_rows(first))
        return carry

    lax.fori_loop(0, side // UNROLL, last_block, 0)

    count = 0
    for q in range(1, labels + 1):
        for k in range(chunks):
            if count >= 2:
                save((count - 2) // chunks, (count - 2) % chunks).wait()

            def step(i, carry, k=k, q=q):
                at = pl.multiple_of(i * UNROLL, UNROLL)
                first = pl.multiple_of(k * CHUNK + at, UNROLL)
                if q < labels:
                    held = read_rows(first)
                parts = narrowed(q - 1, first, UNROLL)
                if q < labels:
                    write_rows(q, first, held)
                for c in range(words):
                    stage[k % 2, pl.ds(at, UNROLL), pl.ds(c * LANES, LANES)] = parts[c]
                return carry

            def wide(i, carry, k=k, q=q):
                at = pl.multiple_of(i * side, side)
                parts = narrowed(q - 1, k * CHUNK + at, side)
                for c in range(words):
                    stage[k % 2, pl.ds(at, side), pl.ds(c * LANES, LANES)] = parts[c]
                return carry

            if q < labels:
                lax.fori_loop(0, CHUNK // UNROLL, step, 0)
            else:
                lax.fori_loop(0, CHUNK // side, wide, 0)
            save(q - 1, k).start()
            count += 1
    for k in range(chunks - 2, chunks):
        save_first(k).wait()
        save(labels - 1, k).wait()


def snp_side(core, env_own, env_other, sums_own, sums_other, shuf_own, shuf_other, own, other,
             labels):
    snp_rows, half = own.shape
    all_samples = 2 * half
    words = snp_rows // LANES
    widths = [snp_rows] * labels + [snp_rows // 2]
    any_spec = pl.BlockSpec(memory_space=pl.ANY)
    smem = pl.BlockSpec(memory_space=pltpu.SMEM)
    vmem = pl.BlockSpec(memory_space=pltpu.VMEM)
    return pl.pallas_call(
        functools.partial(snp_side_kernel, labels=labels),
        out_shape=[jax.ShapeDtypeStruct((all_samples, w), jnp.bfloat16) for w in widths],
        in_specs=[smem, vmem, vmem, vmem, vmem, any_spec, any_spec, any_spec, any_spec],
        out_specs=[any_spec for _ in widths],
        scratch_shapes=[
            pltpu.SMEM((labels * all_samples,), jnp.int32),
            pltpu.VMEM((2, snp_rows, CHUNK), jnp.bfloat16),
            pltpu.VMEM((all_samples * words, LANES), jnp.float32),
            [pltpu.VMEM((all_samples * words, LANES), jnp.float32) for _ in range(labels)],
            pltpu.VMEM((2, CHUNK, snp_rows), jnp.bfloat16),
            pltpu.VMEM((2, CHUNK, snp_rows), jnp.bfloat16),
            pltpu.VMEM((snp_rows, LANES), jnp.float32),
            pltpu.SemaphoreType.DMA((2 * labels,)),
            pltpu.SemaphoreType.DMA((2,)),
            pltpu.SemaphoreType.DMA((2,)),
            pltpu.SemaphoreType.DMA((2,)),
        ],
        compiler_params=pltpu.CompilerParams(vmem_limit_bytes=61 * MIB),
        cost_estimate=pl.CostEstimate(
            flops=40 * 10**9, bytes_accessed=60 * 10**6, transcendentals=0
        ),
        name="snp_side",
    )(core, env_own, env_other, sums_own, sums_other, shuf_own, shuf_other, own, other)


def window_plan(start, end, bounds_ref, n_bounds, total_blocks):
    middle = (start + end - 1) // 2
    lower_edge = jnp.zeros_like(start)
    upper_edge = jnp.full_like(end, total_blocks)
    for i in range(n_bounds):
        edge = bounds_ref[i]
        before = edge <= middle
        lower_edge = jnp.where(before, jnp.maximum(lower_edge, edge), lower_edge)
        upper_edge = jnp.where(before, upper_edge, jnp.minimum(upper_edge, edge))
    return jnp.maximum(start, lower_edge), jnp.minimum(end, upper_edge)


def select_kernel(
    round_ref, pos_ref, bounds_ref, start_ref, end_ref, own_ref, other_ref,
    rounds_ref, plan_ref, full_ref, *rest, caps, blocks_dev,
):
    reach = len(caps)
    genes, half = own_ref.shape
    chosen_from = sum(cap == genes for cap in caps)
    (slots, edges), pay_refs = rest[-2:], rest[:-2]
    shape = start_ref.shape
    per_row = LANES // genes
    chips = shape[0] * per_row
    chip, core = pos_ref[0], pos_ref[1]
    turn = round_ref[0]
    low, high = window_plan(
        start_ref[...], end_ref[...], bounds_ref, bounds_ref.shape[0], chips * blocks_dev
    )
    edges[0] = low
    edges[1] = high
    at = lax.broadcasted_iota(jnp.int32, shape, 0) * per_row
    at = at + lax.broadcasted_iota(jnp.int32, shape, 1) // genes
    a = lax.broadcasted_iota(jnp.int32, (LANES, LANES), 0)
    b = lax.broadcasted_iota(jnp.int32, (LANES, LANES), 1)
    upto = ((a <= b) & (a // genes == b // genes)).astype(jnp.float32).astype(jnp.bfloat16)
    rounds = jnp.int32(0)
    for way in range(2):
        for k in range(1, reach + 1):
            to = at + (k if way == 0 else -k)
            need = (
                (low < (to + 1) * blocks_dev) & (high > to * blocks_dev)
                & (low < high) & (to >= 0) & (to < chips)
            )
            rank = jnp.dot(
                need.astype(jnp.float32).astype(jnp.bfloat16), upto,
                preferred_element_type=jnp.float32,
            ).astype(jnp.int32)
            cap = caps[k - 1]
            if cap == genes:
                which = lax.broadcasted_iota(jnp.int32, shape, 1) % genes
                slots[way * reach + k - 1] = jnp.where(need, which, -1)
                continue
            slot = rank - 1 - turn * cap
            slots[way * reach + k - 1] = jnp.where(
                need & (slot >= 0) & (slot < cap), slot, -1
            )
            rounds = jnp.maximum(rounds, (jnp.max(rank) + cap - 1) // cap)
    rounds_ref[0] = rounds

    def of_chip(ref, index, which):
        row = ref[index, pl.ds(which // per_row, 1), :]
        out = row[:, :genes]
        for part in range(1, per_row):
            out = jnp.where(
                which % per_row == part, row[:, part * genes : (part + 1) * genes], out
            )
        return out

    used = [lax.broadcasted_iota(jnp.int32, (1, genes), 1)]
    lows = [of_chip(edges, 0, chip)]
    highs = [of_chip(edges, 1, chip)]
    first = genes
    for side in range(2):
        way = core if side == 0 else 1 - core
        for k in range(1, reach + 1):
            source = chip + (2 * way - 1) * k
            valid = (source >= 0) & (source < chips)
            source = jnp.clip(source, 0, chips - 1)
            slot = of_chip(slots, way * reach + k - 1, source)
            used.append(jnp.where(valid & (slot >= 0), slot + first, -1))
            lows.append(of_chip(edges, 0, source))
            highs.append(jnp.where(valid, of_chip(edges, 1, source), 0))
            first += caps[k - 1]
    while len(used) * genes < plan_ref.shape[1]:
        used.append(jnp.full_like(used[0], -1))
        lows.append(jnp.zeros_like(used[0]))
        highs.append(jnp.zeros_like(used[0]))
    plan_ref[...] = jnp.zeros_like(plan_ref)
    for row, parts in enumerate((used, lows, highs)):
        plan_ref[pl.ds(row, 1), :] = jnp.concatenate(parts, axis=1)

    picks = []
    for k in range(chosen_from + 1, reach + 1):
        slot = of_chip(slots, core * reach + k - 1, chip)
        rows = lax.broadcasted_iota(jnp.int32, (caps[k - 1], genes), 0)
        picks.append((rows == slot).astype(jnp.float32))
    if picks:
        picks = jnp.concatenate(picks, axis=0).astype(jnp.bfloat16)
    step = 1024

    def copy(i, carry):
        cols = pl.ds(pl.multiple_of(i * step, step), step)
        late = pl.ds(pl.multiple_of(half + i * step, step), step)
        a, b = own_ref[:, cols], other_ref[:, cols]
        for part, to in ((jnp.where(core == 0, a, b), cols), (jnp.where(core == 0, b, a), late)):
            full_ref[:, to] = part
            if pay_refs:
                chosen = jnp.dot(picks, part, preferred_element_type=jnp.float32)
                chosen = chosen.astype(jnp.bfloat16)
                row = 0
                for pay in pay_refs:
                    pay[:, to] = chosen[row : row + pay.shape[0]]
                    row += pay.shape[0]
        return carry

    lax.fori_loop(0, half // step, copy, 0)


def select(turn, pos, bounds, start, end, own, other, caps, blocks_dev):
    genes, half = own.shape
    all_samples = 2 * half
    reach = len(caps)
    smem = pl.BlockSpec(memory_space=pltpu.SMEM)
    vmem = pl.BlockSpec(memory_space=pltpu.VMEM)
    width = -(-(2 * reach + 1) * genes // LANES) * LANES
    chosen = [cap for cap in caps if cap < genes]
    return pl.pallas_call(
        functools.partial(select_kernel, caps=caps, blocks_dev=blocks_dev),
        out_shape=(
            jax.ShapeDtypeStruct((1,), jnp.int32),
            jax.ShapeDtypeStruct((8, width), jnp.int32),
            jax.ShapeDtypeStruct((genes, all_samples), jnp.bfloat16),
            *[jax.ShapeDtypeStruct((cap, all_samples), jnp.bfloat16) for cap in chosen],
        ),
        in_specs=[smem, smem, smem, vmem, vmem, vmem, vmem],
        out_specs=(smem, vmem, vmem, *[vmem for _ in chosen]),
        scratch_shapes=[
            pltpu.VMEM((2 * reach,) + start.shape, jnp.int32),
            pltpu.VMEM((2,) + start.shape, jnp.int32),
        ],
        compiler_params=pltpu.CompilerParams(vmem_limit_bytes=24 * MIB),
        name="select",
    )(turn, pos, bounds, start, end, own, other)


def product_kernel(
    pos_ref, sums_own, sums_other, plan_ref, *rest, caps, labels, genes, blocks_dev
):
    reach = len(caps)
    n_in = 1 + 2 * reach
    gene_refs = rest[:n_in]
    weight_refs = rest[n_in : n_in + labels + 1]
    out_ref, power_ref, rows, total, power = rest[n_in + labels + 1 :]
    step = pl.program_id(0)
    snp_rows = sums_own.shape[1]
    depth = rows.shape[1]
    used = rows.shape[0]
    chip, core = pos_ref[0], pos_ref[1]

    @pl.when(step == 0)
    def _():
        total[...] = jnp.zeros_like(total)
        power[...] = jnp.zeros_like(power)

    at = 0
    for ref in gene_refs:
        rows[pl.ds(at, ref.shape[0]), :] = ref[...]
        at += ref.shape[0]
    for q, ref in enumerate(weight_refs):
        cols = pl.ds(q * snp_rows, ref.shape[1])
        total[pl.ds(0, used), cols] += jnp.dot(
            rows[...], ref[...], preferred_element_type=jnp.float32
        )
    kept = power[...]
    for t in range(depth // LANES):
        x = rows[pl.ds(0, genes), pl.ds(t * LANES, LANES)].astype(jnp.float32)
        kept = kept + x * x
    power[...] = kept

    @pl.when(step == pl.num_programs(0) - 1)
    def _():
        summed_up(
            chip, core, sums_own, sums_other, plan_ref, out_ref, power_ref, total, power,
            reach=reach, labels=labels, genes=genes, blocks_dev=blocks_dev,
        )


def summed_up(
    chip, core, sums_own, sums_other, plan_ref, out_ref, power_ref, total, power,
    *, reach, labels, genes, blocks_dev,
):
    snp_rows = sums_own.shape[1]
    block = SNP_BLOCK
    n_in = 1 + 2 * reach
    share_blocks = blocks_dev // 2
    sums = sums_own[...] + sums_other[...]
    cross = sums[1:2, :]
    inter = sums[2:3, :]
    inv = 1.0 / (inter - cross * (cross / sums[0:1, :]) + 0.1 * inter)

    def peak(col, inv_block):
        best = None
        for t in range(block // LANES):
            v = total[:, pl.ds(col + t * LANES, LANES)]
            v = v * v * inv_block[:, t * LANES : (t + 1) * LANES]
            best = v if best is None else jnp.maximum(best, v)
        return jnp.max(best.T, axis=0, keepdims=True)

    peaks = []
    for q in range(labels):
        for b in range(blocks_dev):
            peaks.append(peak(q * snp_rows + b * block, inv[:, b * block : (b + 1) * block]))
    for b in range(share_blocks):
        mine = inv[:, b * block : (b + 1) * block]
        late = inv[:, (share_blocks + b) * block : (share_blocks + b + 1) * block]
        peaks.append(peak(labels * snp_rows + b * block, jnp.where(core == 0, mine, late)))
    while len(peaks) % 8:
        peaks.append(jnp.zeros_like(peaks[0]))
    peaks = jnp.concatenate(peaks, axis=0)
    count = peaks.shape[0]
    terms = []
    left = peaks
    for _ in range(3):
        terms.append(left.astype(jnp.bfloat16).astype(jnp.float32))
        left = left - terms[-1]
    terms = jnp.concatenate(terms, axis=0).astype(jnp.bfloat16)
    band = plan_ref.shape[1]
    slot = plan_ref[0:1, :]
    low = plan_ref[1:2, :]
    high = plan_ref[2:3, :]
    place = lax.broadcasted_iota(jnp.int32, (total.shape[0], band), 0) == slot
    spread = jnp.dot(
        terms, place.astype(jnp.float32).astype(jnp.bfloat16),
        preferred_element_type=jnp.float32,
    )
    spread = spread[:count] + spread[count : 2 * count] + spread[2 * count :]

    def masked(row, snp_block):
        inside = (snp_block >= low) & (snp_block < high)
        return jnp.where(inside, spread[row : row + 1], 0.0)

    def highest(row, blocks, first_block):
        best = masked(row, first_block)
        for b in range(1, blocks):
            best = jnp.maximum(best, masked(row + b, first_block + b))
        return best

    out_rows = [highest(labels * blocks_dev, share_blocks, chip * blocks_dev + core * share_blocks)]
    found = [highest(q * blocks_dev, blocks_dev, chip * blocks_dev) for q in range(labels)]
    for c in range(2):
        out_rows += [jnp.where(core == c, v, 0.0) for v in found]
    while len(out_rows) % 8:
        out_rows.append(jnp.zeros_like(out_rows[0]))
    dense = jnp.concatenate(out_rows, axis=0)
    out_ref[...] = jnp.zeros_like(out_ref)
    chips = out_ref.shape[0]
    for i in range(n_in):
        if i == 0:
            target = chip
        else:
            way = core if i <= reach else 1 - core
            target = chip + (2 * way - 1) * ((i - 1) % reach + 1)

        @pl.when((target >= 0) & (target < chips))
        def _(i=i, target=target):
            out_ref[target, :, pl.ds(0, genes)] = dense[:, i * genes : (i + 1) * genes]

    powers = jnp.sum(power[...].T, axis=0, keepdims=True)
    power_ref[...] = jnp.broadcast_to(powers, power_ref.shape)


def products(pos, sums, plan, full, mine, other, weights, caps, labels, chips, blocks_dev):
    genes, all_samples = full.shape
    used = genes + 2 * sum(caps)
    padded = -(-used // LANES) * LANES
    out_rows = -(-(1 + 2 * labels) // 8) * 8
    width = sum(w.shape[1] for w in weights)
    arrays = (full, *mine, *other)

    def whole(x):
        return pl.BlockSpec(x.shape, lambda k: (0,) * len(x.shape))

    outs = (
        jax.ShapeDtypeStruct((chips, out_rows, LANES), jnp.float32),
        jax.ShapeDtypeStruct((8, genes), jnp.float32),
    )
    return pl.pallas_call(
        functools.partial(
            product_kernel, caps=caps, labels=labels, genes=genes, blocks_dev=blocks_dev
        ),
        grid=(all_samples // DEPTH,),
        out_shape=outs,
        in_specs=[
            pl.BlockSpec(memory_space=pltpu.SMEM),
            *[whole(x) for x in (*sums, plan)],
            *[pl.BlockSpec((x.shape[0], DEPTH), lambda k: (0, k)) for x in arrays],
            *[pl.BlockSpec((DEPTH, w.shape[1]), lambda k: (k, 0)) for w in weights],
        ],
        out_specs=tuple(whole(x) for x in outs),
        scratch_shapes=[
            pltpu.VMEM((used, DEPTH), jnp.bfloat16),
            pltpu.VMEM((padded, width), jnp.float32),
            pltpu.VMEM((genes, LANES), jnp.float32),
        ],
        compiler_params=pltpu.CompilerParams(vmem_limit_bytes=48 * MIB),
        cost_estimate=pl.CostEstimate(
            flops=2 * used * all_samples * width,
            bytes_accessed=2 * all_samples * (width + used),
            transcendentals=0,
        ),
        name="products",
    )(pos, *sums, plan, *arrays, *weights)


def finish_kernel(own_ref, other_ref, power_ref, out_ref, *, samples):
    best = jnp.maximum(own_ref[0], other_ref[0])
    for i in range(1, own_ref.shape[0]):
        best = jnp.maximum(best, jnp.maximum(own_ref[i], other_ref[i]))
    labels, genes = out_ref.shape
    peak = best[:labels, :genes]
    out_ref[...] = jnp.sqrt(peak / (power_ref[0:1, :] / samples + 1e-05))


def shards(genotypes, phenotypes, environment, shuffles, window_start, window_end, chrom_bounds):
    snp_rows, half = genotypes.shape
    genes = phenotypes.shape[0]
    perms = shuffles.shape[0]
    chips = lax.axis_size("genome")
    cores = lax.axis_size("sample")
    blocks_dev = snp_rows // SNP_BLOCK
    reach = (HALF_BLK + blocks_dev - 1) // blocks_dev
    all_samples = half * cores
    labels = perms // cores
    caps = tuple(min(genes, genes * 4 >> k) for k in range(1, reach + 1))
    env = environment[None]
    start = window_start.reshape(-1, LANES)
    end = window_end.reshape(-1, LANES)
    pos = jnp.stack([lax.axis_index("genome"), lax.axis_index("sample")]).astype(jnp.int32)

    def travel(k, payload):
        pairs = [(i * cores, (i + k) * cores) for i in range(chips - k)]
        pairs += [((i + k) * cores + 1, i * cores + 1) for i in range(chips - k)]
        return lax.ppermute(payload, ("genome", "sample"), pairs)

    def one_round(turn, pos):
        core = pos[1:]
        other_pheno = swapped(phenotypes)
        own_sums = local_moments(genotypes, env)
        sums = (own_sums, swapped(own_sums))
        late_geno, _ = lax.optimization_barrier((genotypes, other_pheno))
        other_geno = swapped(late_geno)
        other_env = swapped(env)
        other_shuffles = swapped(shuffles)
        rounds, plan, full, *payloads = select(
            turn, pos, chrom_bounds, start, end, phenotypes, other_pheno, caps, blocks_dev
        )
        payloads = [full] * (reach - len(payloads)) + payloads
        mine = [travel(k, x) for k, x in enumerate(payloads, 1)]
        weights = snp_side(
            core, env, other_env, *sums, shuffles, other_shuffles, genotypes, other_geno, labels
        )
        mine, weights = lax.optimization_barrier((mine, weights))
        other = [swapped(x) for x in mine]
        found, power = products(
            pos, sums, plan, full, mine, other, weights, caps, labels, chips, blocks_dev
        )
        return rounds, found, power

    rounds, found, power = one_round(jnp.zeros((1,), jnp.int32), pos)

    def more(carry):
        return carry[0] < rounds[0]

    def again(carry):
        turn, best = carry
        turns, place = lax.optimization_barrier((jnp.full((1,), turn, jnp.int32), pos))
        return turn + 1, jnp.maximum(best, one_round(turns, place)[1])

    _, found = lax.while_loop(more, again, (jnp.int32(1), found))
    gathered = lax.all_to_all(found, "genome", 0, 0, tiled=True)
    return pl.pallas_call(
        functools.partial(finish_kernel, samples=all_samples),
        out_shape=jax.ShapeDtypeStruct((perms + 1, genes), jnp.float32),
        name="finish",
    )(gathered, swapped(gathered), power)


def solution(mesh):
    placed = (
        P("genome", "sample"),
        P("genome", "sample"),
        P("sample"),
        P(None, "sample"),
        P(),
        P(),
        P(),
    )
    return jax.shard_map(
        shards, mesh=mesh, in_specs=placed, out_specs=P(None, "genome"), check_vma=False
    )
```
